32 devices in a mesh: dp: 16 (over z, x, core), tensor: 2 (over y).
Axes of the slice: x: 2, y: 2, z: 4, core: 2. Of those that a mesh axis runs over, the one named last changes fastest.
Arguments:
- hidden_in: bfloat16 [64, 512, 768], P(('dp', 'tensor')), may hold values from -6 to 6
- lengths: int32 [64], P('dp'), may hold values from 32 to 512, as said below
- queries: bfloat16 [64, 768], P(('dp', 'tensor')), may hold values from -6 to 6
- positives: int32 [64], P(('dp', 'tensor')), may hold values from 0 to 63, each once
- gain_attn: float32 [768], replicated, may hold values from 0.5 to 1.5
- w_query: bfloat16 [768, 768], P(None, 'tensor'), may hold values from -0.0546875 to 0.0546875
- w_key: bfloat16 [768, 768], P(None, 'tensor'), may hold values from -0.21875 to 0.21875
- w_value: bfloat16 [768, 768], P(None, 'tensor'), may hold values from -0.21875 to 0.21875
- w_out: bfloat16 [768, 768], P('tensor'), may hold values from -1.25 to 1.25
- rel_table: float32 [32, 12], P(None, 'tensor'), may hold values from -6 to 6
- gain_ffn: float32 [768], replicated, may hold values from 0.5 to 1.5
- w_inner: bfloat16 [768, 3072], P(None, 'tensor'), may hold values from -0.21875 to 0.21875
- w_outer: bfloat16 [3072, 768], P('tensor'), may hold values from -0.109375 to 0.109375
- w_proj: bfloat16 [768, 768], replicated, may hold values from -0.21875 to 0.21875
Outputs:
- layer_out: bfloat16 [64, 512, 768], P(('dp', 'tensor'))
- query_loss: float32 [64], P(('dp', 'tensor'))
- input_grad: float32 [64, 512, 768], P(('dp', 'tensor'))
- gain_attn_grad: float32 [768], replicated
- query_w_grad: float32 [768, 768], P(None, 'tensor')
- key_w_grad: float32 [768, 768], P(None, 'tensor')
- value_w_grad: float32 [768, 768], P(None, 'tensor')
- out_w_grad: float32 [768, 768], P('tensor')
- table_grad: float32 [32, 12], P(None, 'tensor')
- gain_ffn_grad: float32 [768], replicated
- inner_w_grad: float32 [768, 3072], P(None, 'tensor')
- outer_w_grad: float32 [3072, 768], P('tensor')
- proj_w_grad: float32 [768, 768], replicated
The draws below stay inside these ranges and needn't reach their ends.
Inputs may be any that keep to these rules, and one draw needn't show every extreme that they name: `lengths`: among the 4 passages of each index of dp one has exactly 512 tokens. `positives`: each passage is the positive of exactly one query.
All inputs are finite; a program needn't handle non-finite values.
Results may differ from the reference program's by a relative error of at most 0.028.
Values may be sent and summed in bfloat16 or wider, within the bound.
No kernel may reach another device: no remote copies, remote signals or barrier semaphores. Data moves between devices by JAX's collectives and lax.ppermute only.
A program may use at most 192 MiB of HBM per device.

```python
from functools import partial
import jax
import jax.numpy as jnp
from jax import lax

D = 768
HEADS = 12
HEAD_DIM = 64
FF = 3072
BUCKETS = 32
EMBED = 768
SEQ = 512
MINLEN = 32
SEQ_DEV = 4
BATCH = 64


def draw_lengths(key, part):
    key = jax.random.fold_in(key, 11)
    subkeys = jax.random.split(key, 3)
    blocks = BATCH // SEQ_DEV
    drawn_len = jax.random.randint(subkeys[0], (blocks, SEQ_DEV), MINLEN, SEQ + 1)
    full_column = jax.random.randint(subkeys[1], (blocks, 1), 0, SEQ_DEV)
    column_ids = jnp.arange(SEQ_DEV, dtype=jnp.int32)[None, :]
    drawn_len = jnp.where(column_ids == full_column, SEQ, drawn_len)
    short_block = jax.random.randint(subkeys[2], (), 0, blocks)
    block_ids = jnp.arange(blocks, dtype=jnp.int32)[:, None]
    short_column = (full_column + 1) % SEQ_DEV
    drawn_len = jnp.where((block_ids == short_block) & (column_ids == short_column), MINLEN, drawn_len)
    return drawn_len.reshape(BATCH).astype(jnp.int32)


def steps_of(rng, extent, pieces, least, largest):
    def one(axis_at, parts):
        heights = jax.random.uniform(jax.random.fold_in(jax.random.fold_in(rng, 6), axis_at), (parts,), jnp.float32, least / len(pieces), largest / len(pieces))
        return jnp.repeat(jnp.exp(heights), extent[axis_at] // parts).reshape((-1,) + (1,) * (len(extent) - axis_at - 1))

    loudness = one(*pieces[0])
    for cut in pieces[1:]:
        loudness = loudness * one(*cut)
    return loudness


def gaussian(rng, shape, width, limit, cuts=(), kind=jnp.bfloat16):
    entries = jax.random.normal(rng, shape, jnp.float32) * width
    if len(cuts) > 0:
        entries = steps_of(rng, shape, cuts, -0.22, 0.18) * entries
    return jnp.clip(entries, min=-limit, max=limit).astype(kind)


def setup_inputs(seed: int = 0) -> dict:
    seeds = jax.random.split(jax.random.key(seed), 15)
    hidden_in = gaussian(seeds[0], (BATCH, SEQ, D), 1.0, 6.0, ((0, 32),))
    lengths = draw_lengths(jax.random.fold_in(seeds[14], 71), 0)
    queries = gaussian(seeds[2], (BATCH, EMBED), 1.0, 6.0, ((0, 32),))
    positives = jax.random.permutation(seeds[3], BATCH).astype(jnp.int32)
    gain_attn = jnp.clip(1.0 + 0.1 * jax.random.normal(seeds[4], (D,), jnp.float32), 0.5, 1.5)
    w_query = gaussian(seeds[5], (D, HEADS * HEAD_DIM), (16 * D) ** -0.5, 0.0546875, ((1, 2),))
    w_key = gaussian(seeds[6], (D, HEADS * HEAD_DIM), D ** -0.5, 0.21875, ((1, 2),))
    w_value = gaussian(seeds[7], (D, HEADS * HEAD_DIM), D ** -0.5, 0.21875, ((1, 2),))
    w_out = gaussian(seeds[8], (HEADS * HEAD_DIM, D), (D // 32) ** -0.5, 1.25, ((0, 2),))
    rel_table = gaussian(seeds[9], (BUCKETS, HEADS), 1.0, 6.0, ((1, 2),), jnp.float32)
    gain_ffn = jnp.clip(1.0 + 0.1 * jax.random.normal(seeds[10], (D,), jnp.float32), 0.5, 1.5)
    w_inner = gaussian(seeds[11], (D, FF), D ** -0.5, 0.21875, ((1, 2),))
    w_outer = gaussian(seeds[12], (FF, D), FF ** -0.5, 0.109375, ((0, 2),))
    w_proj = gaussian(seeds[13], (D, EMBED), D ** -0.5, 0.21875)
    return {"hidden_in": hidden_in, "lengths": lengths, "queries": queries, "positives": positives, "gain_attn": gain_attn, "w_query": w_query, "w_key": w_key, "w_value": w_value, "w_out": w_out, "rel_table": rel_table, "gain_ffn": gain_ffn, "w_inner": w_inner, "w_outer": w_outer, "w_proj": w_proj}


@jax.custom_vjp
def low(v):
    return lax.optimization_barrier(v.astype(jnp.bfloat16)).astype(jnp.float32)

@jax.custom_vjp
def low_back(v):
    return v

def low_keep(v):
    return (low(v), None)

def low_pass(kept, grad):
    return (grad,)

def back_keep(v):
    return (v, None)

def back_low(kept, grad):
    return (low(grad),)
low.defvjp(low_keep, low_pass)
low_back.defvjp(back_keep, back_low)
large_steps = (12, 16, 23, 32, 46, 64, 91)
contrast_sharpness = 0.02
loss_scale = 256.0
stabilizer_floor = 1e-06
highest = lax.Precision.HIGHEST

def bucket_table(seq_len, bucket_count):
    places = jnp.arange(seq_len, dtype=jnp.int32)
    offset = places[None, :] - places[:, None]
    distance = jnp.abs(offset)
    half_count = bucket_count // 2
    exact_count = half_count // 2
    far_part = exact_count + sum(((distance >= bound_at).astype(jnp.int32) for bound_at in large_steps))
    return jnp.where(offset > 0, half_count, 0) + jnp.where(distance < exact_count, distance, far_part)

def rms_apply(values, gain_vec):
    inv_rms = lax.rsqrt(lax.optimization_barrier(jnp.mean(values * values, axis=-1, keepdims=True)) + stabilizer_floor)
    return values * inv_rms * gain_vec

def exact_matmul_helper(left, right):
    return jnp.matmul(left, right, precision=highest)

def encode_block(weights, block_in, block_len):
    gain_attn, w_query, w_key, w_value, w_out, rel_table, gain_ffn, w_inner, w_outer = weights
    seq_count, seq_len, model_dim = block_in.shape
    head_count = rel_table.shape[1]
    head_dim = w_query.shape[1] // head_count
    reshaped_tensor = (seq_count, seq_len, head_count, head_dim)
    normed = low(rms_apply(block_in, gain_attn))
    query_rows = low(low_back(exact_matmul_helper(normed, w_query))).reshape(reshaped_tensor)
    key_rows = low(low_back(exact_matmul_helper(normed, w_key))).reshape(reshaped_tensor)
    value_rows = low(low_back(exact_matmul_helper(normed, w_value))).reshape(reshaped_tensor)
    rel_bias = jnp.transpose(jnp.take(rel_table, bucket_table(seq_len, rel_table.shape[0]), axis=0), (2, 0, 1))
    scores = jnp.einsum('bihd,bjhd->bhij', query_rows, key_rows, precision=highest) + rel_bias[None]
    scores = low_back(scores)
    is_valid = jnp.arange(seq_len, dtype=jnp.int32)[None, :] < block_len[:, None]
    scores = jnp.where(is_valid[:, None, None, :], scores, -1e+30)
    attn_probs = jax.nn.softmax(scores, axis=-1)
    context = jnp.einsum('bhij,bjhd->bihd', low(attn_probs), value_rows, precision=highest)
    context = low(low_back(context)).reshape(seq_count, seq_len, head_count * head_dim)
    residual = block_in + low_back(exact_matmul_helper(context, w_out))
    normed_two = low(rms_apply(residual, gain_ffn))
    inner_pre = low_back(exact_matmul_helper(normed_two, w_inner))
    activated = low(jax.nn.gelu(inner_pre, approximate=True))
    layer_full = residual + low_back(exact_matmul_helper(activated, w_outer))
    pooled = lax.optimization_barrier(jnp.sum(jnp.where(is_valid[:, :, None], layer_full, 0.0), axis=1)) / block_len[:, None].astype(jnp.float32)
    return (layer_full, pooled)

def forward(lengths, positives, queries, hidden, *params):
    weights = params[:-1]
    w_proj = params[-1]
    seq_total, seq_len, model_dim = hidden.shape
    block_seqs = 8
    blocked = jax.checkpoint(encode_block)

    def one_block(block_items):
        return blocked(weights, block_items[0], block_items[1])
    block_outs, pooled = lax.map(one_block, (hidden.reshape(seq_total // block_seqs, block_seqs, seq_len, model_dim), lengths.reshape(seq_total // block_seqs, block_seqs)))
    layer_full = block_outs.reshape(seq_total, seq_len, model_dim)
    pooled = pooled.reshape(seq_total, model_dim)
    embedding = low_back(exact_matmul_helper(low(pooled), w_proj))
    sphere_embedding_rows = low(embedding * lax.rsqrt(lax.optimization_barrier(jnp.sum(embedding * embedding, axis=-1, keepdims=True)) + stabilizer_floor))
    question_sphere_rows = low(queries * lax.rsqrt(lax.optimization_barrier(jnp.sum(queries * queries, axis=-1, keepdims=True)) + stabilizer_floor))
    cosine_score_matrix = low_back(exact_matmul_helper(question_sphere_rows, sphere_embedding_rows.T) / contrast_sharpness)
    losses = jax.nn.logsumexp(cosine_score_matrix, axis=-1) - jnp.take_along_axis(cosine_score_matrix, positives[:, None], axis=1)[:, 0]
    return (loss_scale * jnp.sum(losses), (layer_full, losses))

def reference(hidden_in, lengths, queries, positives, gain_attn, w_query, w_key, w_value, w_out, rel_table, gain_ffn, w_inner, w_outer, w_proj):
    floats = [array_in.astype(jnp.float32) for array_in in (hidden_in, gain_attn, w_query, w_key, w_value, w_out, rel_table, gain_ffn, w_inner, w_outer, w_proj)]
    objective, pullback, aux_out = jax.vjp(partial(forward, lengths, positives, queries.astype(jnp.float32)), *floats, has_aux=True)
    layer_full, losses = aux_out
    gradients = pullback(jnp.ones((), jnp.float32))
    return (layer_full.astype(jnp.bfloat16), losses, gradients[0], gradients[1], gradients[2], gradients[3], gradients[4], gradients[5], gradients[6], gradients[7], gradients[8], gradients[9], gradients[10])
```

```python
import functools

import numpy as np

import jax
import jax.numpy as jnp
from jax import lax
from jax.experimental import pallas as pl
from jax.experimental.pallas import tpu as pltpu
from jax.sharding import PartitionSpec as P

LARGE_STEPS = (12, 16, 23, 32, 46, 64, 91)
SHARPNESS = 0.02
LOSS_SCALE = 256.0
EPS = 1e-06
NEG = -1e30
BF = jnp.bfloat16
F32 = jnp.float32
TILE = 128
GELU_A = 0.7978845608028654
GELU_B = 0.044715
MIB = 1024 * 1024

NN = (((1,), (0,)), ((), ()))
NT = (((1,), (1,)), ((), ()))
TN = (((0,), (0,)), ((), ()))


def mm(a, b, dims=NN):
    return lax.dot_general(a, b, dims, preferred_element_type=F32)


def bucket_of(r):
    a = np.abs(r)
    far = 8 + sum((a >= t).astype(np.int32) for t in LARGE_STEPS)
    return np.where(r > 0, 16, 0) + np.where(a < 8, a, far)


def diag_onehot(buckets):
    lane = np.arange(2 * TILE)
    rows = [bucket_of(TILE * d + TILE - 1 - lane) for d in (-1, 0, 1)]
    idx = np.concatenate(rows)
    hot = (idx[:, None] == np.arange(buckets)[None, :]).astype(np.float32)
    hot[2 * TILE - 1 :: 2 * TILE] = 0.0
    return hot


def bias_pieces(nb_ref, far_ref, h, bj, bi):
    d = bj - bi
    if abs(d) <= 1:
        return nb_ref[3 * h + d + 1]
    return far_ref[h, 1 if d > 0 else 0]


def attn_fwd_kernel(first, heads, *refs):
    if first:
        (lens, x_ref, gain_ref, w_ref, bv_ref, far_ref) = refs[:6]
        (an_ref, q_ref, k_ref, v_ref, ctx_ref, ctxt_ref, lse_ref, nb_ref, mask_ref) = refs[6:]
    else:
        (lens, x_ref, w_ref, bv_ref, far_ref) = refs[:5]
        (q_ref, k_ref, v_ref, ctx_ref, ctxt_ref, lse_ref, nb_ref, mask_ref) = refs[5:]
    b = pl.program_id(0)
    seq = x_ref.shape[1]
    nblk = seq // TILE
    width = heads * 64

    @pl.when(b == 0)
    def _():
        for t in range(3 * heads):
            v = jnp.broadcast_to(bv_ref[t : t + 1, :], (TILE, 2 * TILE))
            nb_ref[t] = pltpu.roll(v, TILE + 1, 1, stride=1, stride_axis=0)[:, :TILE]

    row = lax.broadcasted_iota(jnp.int32, (seq, TILE), 0)
    mask_ref[...] = jnp.where(row < lens[b], 0.0, NEG)
    if first:
        x = x_ref[0].astype(F32)
        inv = lax.rsqrt(jnp.mean(x * x, axis=-1, keepdims=True) + EPS)
        an = (x * inv * gain_ref[...]).astype(BF)
        an_ref[0] = an
    else:
        an = x_ref[0]
    lane = lax.broadcasted_iota(jnp.int32, (1, TILE), 1)
    low = (lane < 64).astype(F32)
    for pair in range(heads // 2):
        cols = slice(TILE * pair, TILE * (pair + 1))
        qp = mm(an, w_ref[:, TILE * pair : TILE * (pair + 1)])
        kp = mm(an, w_ref[:, width + TILE * pair : width + TILE * (pair + 1)])
        vp = mm(an, w_ref[:, 2 * width + TILE * pair : 2 * width + TILE * (pair + 1)])
        q_ref[0, :, cols] = qp.astype(BF)
        kb = kp.astype(BF)
        k_ref[0, :, cols] = kb
        v_ref[0, :, cols] = vp.astype(BF)
        vt = jnp.transpose(vp).astype(BF)
        ctx_cols = []
        for ib in range(seq // 256):
            halves = []
            for e in range(2):
                h = 2 * pair + e
                sel = low if e == 0 else 1.0 - low
                qm = (qp[256 * ib : 256 * (ib + 1)] * sel).astype(BF)
                s = mm(kb, qm, NT)
                parts = []
                for bj in range(nblk):
                    for t in range(2):
                        piece = s[TILE * bj : TILE * (bj + 1), TILE * t : TILE * (t + 1)]
                        piece = piece + bias_pieces(nb_ref, far_ref, h, bj, 2 * ib + t)
                        parts.append(piece + mask_ref[TILE * bj : TILE * (bj + 1), :])
                s = jnp.concatenate(
                    [jnp.concatenate(parts[2 * bj : 2 * bj + 2], axis=1) for bj in range(nblk)],
                    axis=0,
                )
                top = jnp.max(s, axis=0, keepdims=True)
                p = jnp.exp(s - top)
                total = jnp.sum(p, axis=0, keepdims=True)
                lse_ref[0, h : h + 1, 256 * ib : 256 * (ib + 1)] = top + jnp.log(total)
                c = mm(vt[64 * e : 64 * (e + 1), :], p.astype(BF))
                halves.append(c * (1.0 / total))
            ctx_cols.append(jnp.concatenate(halves, axis=0))
        ct = jnp.concatenate(ctx_cols, axis=1)
        ctxt_ref[0, cols, :] = ct.astype(BF)
        ctx_ref[0, :, cols] = jnp.transpose(ct).astype(BF)


def const_spec(shape):
    zeros = (0,) * len(shape)
    return pl.BlockSpec(shape, lambda b: zeros, pipeline_mode=pl.Buffered(1))


def row_spec(shape):
    tail = (0,) * (len(shape) - 1)
    return pl.BlockSpec((1,) + tuple(shape[1:]), lambda b: (b,) + tail)


SMEM_SPEC = pl.BlockSpec(memory_space=pltpu.SMEM)


def attn_fwd(x, lens, w, bv, far, gain=None):
    n, seq, d = x.shape
    width = w.shape[1] // 3
    heads = width // 64
    first = gain is not None
    args = [lens, x] + ([gain.reshape(1, d)] if first else []) + [w, bv, far]
    specs = (
        [SMEM_SPEC, row_spec(x.shape)]
        + ([const_spec((1, d))] if first else [])
        + [const_spec(w.shape), const_spec(bv.shape), SMEM_SPEC]
    )
    tok = jax.ShapeDtypeStruct((n, seq, width), BF)
    outs = ([jax.ShapeDtypeStruct((n, seq, d), BF)] if first else []) + [
        tok,
        tok,
        tok,
        tok,
        jax.ShapeDtypeStruct((n, width, seq), BF),
        jax.ShapeDtypeStruct((n, 8, seq), F32),
    ]
    out_specs = [row_spec(o.shape) for o in outs]
    nb = jax.ShapeDtypeStruct((3 * heads, TILE, TILE), F32)
    return pl.pallas_call(
        functools.partial(attn_fwd_kernel, first, heads),
        grid=(n,),
        in_specs=specs,
        out_specs=out_specs + [pl.BlockSpec(nb.shape, lambda b: (0, 0, 0))],
        out_shape=outs + [nb],
        scratch_shapes=[pltpu.VMEM((seq, TILE), F32)],
        compiler_params=pltpu.CompilerParams(vmem_limit_bytes=40 * MIB),
        cost_estimate=pl.CostEstimate(
            flops=2 * n * seq * (d * 3 * width + 2 * seq * width * 4),
            bytes_accessed=8 * n * seq * d,
            transcendentals=n * heads * seq * seq,
        ),
        name="attn_fwd",
    )(*args)


def attn_bwd_kernel(heads, *refs):
    (lens, q_ref, k_ref, v_ref, dc_ref, lse_ref, nb_ref, far_ref) = refs[:8]
    (dq_ref, dk_ref, dv_ref, diag_ref, fsum_ref, mask_ref, t_ref) = refs[8:]
    b = pl.program_id(0)
    seq = q_ref.shape[1]
    nblk = seq // TILE

    @pl.when(b == 0)
    def _():
        t_ref[...] = jnp.zeros_like(t_ref)
        fsum_ref[...] = jnp.zeros_like(fsum_ref)

    row = lax.broadcasted_iota(jnp.int32, (seq, TILE), 0)
    mask_ref[...] = jnp.where(row < lens[b], 0.0, NEG)
    lane = lax.broadcasted_iota(jnp.int32, (1, TILE), 1)
    low = (lane < 64).astype(F32)
    for pair in range(heads // 2):
        cols = slice(TILE * pair, TILE * (pair + 1))
        kb = k_ref[0, :, cols]
        vb = v_ref[0, :, cols]
        kt = jnp.transpose(kb.astype(F32)).astype(BF)
        qf = q_ref[0, :, cols].astype(F32)
        df = dc_ref[0, :, cols].astype(F32)
        dk = jnp.zeros((seq, TILE), F32)
        dv = jnp.zeros((seq, TILE), F32)
        dq_cols = []
        for ib in range(seq // 256):
            halves = []
            for e in range(2):
                h = 2 * pair + e
                sel = low if e == 0 else 1.0 - low
                qm = (qf[256 * ib : 256 * (ib + 1)] * sel).astype(BF)
                dm = (df[256 * ib : 256 * (ib + 1)] * sel).astype(BF)
                s = mm(kb, qm, NT)
                lse = lse_ref[0, h : h + 1, 256 * ib : 256 * (ib + 1)]
                parts = []
                for bj in range(nblk):
                    for t in range(2):
                        piece = s[TILE * bj : TILE * (bj + 1), TILE * t : TILE * (t + 1)]
                        piece = piece + bias_pieces(nb_ref, far_ref, h, bj, 2 * ib + t)
                        parts.append(piece + mask_ref[TILE * bj : TILE * (bj + 1), :])
                s = jnp.concatenate(
                    [jnp.concatenate(parts[2 * bj : 2 * bj + 2], axis=1) for bj in range(nblk)],
                    axis=0,
                )
                p = jnp.exp(s - lse)
                dp = mm(vb, dm, NT)
                t1 = p * dp
                along = jnp.sum(t1, axis=0, keepdims=True)
                ds = t1 - p * along
                pb = p.astype(BF)
                db = ds.astype(BF)
                dv = dv + mm(pb, dm)
                dk = dk + mm(db, qm)
                halves.append(mm(kt[64 * e : 64 * (e + 1), :], db))
                far_sum = [None, None]
                for bj in range(nblk):
                    for t in range(2):
                        d = bj - (2 * ib + t)
                        piece = ds[TILE * bj : TILE * (bj + 1), TILE * t : TILE * (t + 1)]
                        if abs(d) <= 1:
                            t_ref[3 * h + d + 1] += piece
                        else:
                            side = 1 if d > 0 else 0
                            one = jnp.sum(piece, axis=0, keepdims=True)
                            far_sum[side] = one if far_sum[side] is None else far_sum[side] + one
                for side in range(2):
                    if far_sum[side] is not None:
                        fsum_ref[2 * h + side : 2 * h + side + 1, :] += far_sum[side]
            dq_cols.append(jnp.concatenate(halves, axis=0))
        dqt = jnp.concatenate(dq_cols, axis=1)
        dq_ref[0, :, cols] = jnp.transpose(dqt).astype(BF)
        dk_ref[0, :, cols] = dk.astype(BF)
        dv_ref[0, :, cols] = dv.astype(BF)

    @pl.when(b == pl.num_programs(0) - 1)
    def _():
        bits = lax.broadcasted_iota(jnp.int32, (TILE, 2 * TILE), 0)
        for t in range(3 * heads):
            x = jnp.concatenate([t_ref[t], jnp.zeros((TILE, TILE), F32)], axis=1)
            x = pltpu.roll(x, TILE - 1, 1)
            for s in range(7):
                x = jnp.where((bits >> s) & 1 == 1, pltpu.roll(x, 2 * TILE - (1 << s), 1), x)
            diag_ref[t : t + 1, :] = jnp.sum(x, axis=0, keepdims=True)


def attn_bwd(lens, q, k, v, dctx, lse, nb, far):
    n, seq, width = q.shape
    heads = width // 64
    tok = jax.ShapeDtypeStruct((n, seq, width), BF)
    full = lambda s: pl.BlockSpec(s, lambda b: (0,) * len(s))
    return pl.pallas_call(
        functools.partial(attn_bwd_kernel, heads),
        grid=(n,),
        in_specs=[SMEM_SPEC]
        + [row_spec(q.shape)] * 4
        + [row_spec(lse.shape), const_spec(nb.shape), SMEM_SPEC],
        out_specs=[row_spec(q.shape)] * 3 + [full((3 * heads, 2 * TILE)), full((2 * heads, TILE))],
        out_shape=[
            tok,
            tok,
            tok,
            jax.ShapeDtypeStruct((3 * heads, 2 * TILE), F32),
            jax.ShapeDtypeStruct((2 * heads, TILE), F32),
        ],
        scratch_shapes=[
            pltpu.VMEM((seq, TILE), F32),
            pltpu.VMEM((3 * heads, TILE, TILE), F32),
        ],
        compiler_params=pltpu.CompilerParams(vmem_limit_bytes=40 * MIB),
        cost_estimate=pl.CostEstimate(
            flops=2 * n * 5 * seq * seq * width * 4,
            bytes_accessed=16 * n * seq * width,
            transcendentals=n * heads * seq * seq,
        ),
        name="attn_bwd",
    )(lens, q, k, v, dctx, lse, nb, far)


def ffn_fwd_kernel(chunk, *refs):
    (lens, x_ref, ca_ref, cb_ref, wa_ref, wb_ref, gain_ref, ia_ref, ib_ref) = refs[:9]
    (res_ref, fin_ref, act_ref, gp_ref, asum_ref, rsum_ref) = refs[9:]
    b = pl.program_id(0)
    seq = x_ref.shape[1]
    res = x_ref[0].astype(F32) + mm(ca_ref[0], wa_ref[...]) + mm(cb_ref[0], wb_ref[...])
    res_ref[0] = res
    inv = lax.rsqrt(jnp.mean(res * res, axis=-1, keepdims=True) + EPS)
    fin = (res * inv * gain_ref[...]).astype(BF)
    fin_ref[0] = fin
    valid = lax.broadcasted_iota(jnp.int32, (seq, TILE), 0) < lens[b]
    col = lax.broadcasted_iota(jnp.int32, (8, seq), 1)
    vrow = (col < lens[b]).astype(F32).astype(BF)
    vcol = valid.astype(F32)[:, :1]
    rsum_ref[0] = jnp.sum(res * vcol, axis=0, keepdims=True)
    half = ia_ref.shape[1]
    for side, w_ref in enumerate((ia_ref, ib_ref)):
        for c in range(half // chunk):
            src = slice(c * chunk, (c + 1) * chunk)
            dst = slice(side * half + c * chunk, side * half + (c + 1) * chunk)
            v = mm(fin, w_ref[:, src])
            v2 = v * v
            th = jnp.tanh(v * (GELU_A + (GELU_A * GELU_B) * v2))
            hh = 0.5 + 0.5 * th
            act = (v * hh).astype(BF)
            slope = hh + (v * (0.5 - 0.5 * th * th)) * (GELU_A + (3.0 * GELU_A * GELU_B) * v2)
            act_ref[0, :, dst] = act
            gp_ref[0, :, dst] = (slope * vcol).astype(BF)
            asum_ref[0, :, dst] = mm(vrow, act)[:1]


def ffn_fwd(lens, x, ctx_a, ctx_b, wo_a, wo_b, gain, wi_a, wi_b):
    n, seq, d = x.shape
    half = wi_a.shape[1]
    outs = [
        jax.ShapeDtypeStruct((n, seq, d), F32),
        jax.ShapeDtypeStruct((n, seq, d), BF),
        jax.ShapeDtypeStruct((n, seq, 2 * half), BF),
        jax.ShapeDtypeStruct((n, seq, 2 * half), BF),
        jax.ShapeDtypeStruct((n, 1, 2 * half), F32),
        jax.ShapeDtypeStruct((n, 1, d), F32),
    ]
    return pl.pallas_call(
        functools.partial(ffn_fwd_kernel, 512),
        grid=(n,),
        in_specs=[SMEM_SPEC, row_spec(x.shape), row_spec(ctx_a.shape), row_spec(ctx_b.shape)]
        + [const_spec(wo_a.shape)] * 2
        + [const_spec((1, d))]
        + [const_spec(wi_a.shape)] * 2,
        out_specs=[row_spec(o.shape) for o in outs],
        out_shape=outs,
        compiler_params=pltpu.CompilerParams(vmem_limit_bytes=48 * MIB),
        cost_estimate=pl.CostEstimate(
            flops=2 * n * seq * d * (d + 2 * half),
            bytes_accessed=n * seq * (8 * d + 8 * half) + 8 * d * half,
            transcendentals=n * seq * 2 * half,
        ),
        name="ffn_fwd",
    )(lens, x, ctx_a, ctx_b, wo_a, wo_b, gain.reshape(1, d), wi_a, wi_b)


def bits_of(n):
    return [1 << i for i in range(n.bit_length() - 1)]


def swap(x, axis, bit, size):
    return lax.ppermute(x, axis, [(i, i ^ bit) for i in range(size)])


def two(up, first, second):
    return jnp.where(up, jnp.concatenate([second, first]), jnp.concatenate([first, second]))


class Place:
    def __init__(self, dp, tensor):
        self.dp, self.tensor = dp, tensor
        self.di = lax.axis_index("dp")
        self.ti = lax.axis_index("tensor")
        self.bits = bits_of(dp)

    def up(self, bit):
        return (self.di & bit) > 0

    def across(self, x):
        return swap(x, "tensor", 1, self.tensor)

    def dp_swap(self, x, bit):
        return swap(x, "dp", bit, self.dp)

    def gather(self, x):
        x = two(self.ti > 0, x, self.across(x))
        for bit in self.bits:
            x = two(self.up(bit), x, self.dp_swap(x, bit))
        return x

    def total(self, x):
        x = x + self.across(x)
        for bit in self.bits:
            x = x + self.dp_swap(x, bit)
        return x

    def fetch(self, w):
        rows = w.shape[0] // 4
        core, xb = self.bits[0], self.bits[1]
        at = 2 * (self.di & 1) + ((self.di >> 1) & 1)
        mine = self.across(lax.dynamic_slice_in_dim(w, at * rows, rows, 0))
        pair = two(self.up(xb), mine, self.dp_swap(mine, xb))
        return two(self.up(core), pair, self.dp_swap(pair, core))

    def reduce(self, own, other):
        core = self.bits[0]
        half = own.shape[0] // 2
        both = jnp.stack([own, other])
        lo, hi = both[:, :half], both[:, half:]
        up = self.up(core)
        cur = jnp.where(up, hi, lo) + self.dp_swap(jnp.where(up, lo, hi), core)
        cur = cur[0] + self.across(cur[1])
        done = [core]
        for bit in self.bits[1:]:
            rows = cur.shape[0]
            if rows % 32 == 0:
                lo, hi = cur[: rows // 2], cur[rows // 2 :]
                up = self.up(bit)
                cur = jnp.where(up, hi, lo) + self.dp_swap(jnp.where(up, lo, hi), bit)
                done.append(bit)
            else:
                cur = cur + self.dp_swap(cur, bit)
        for bit in reversed(done):
            cur = two(self.up(bit), cur, self.dp_swap(cur, bit))
        return cur


def body(
    mesh_shape,
    hidden_in,
    lengths,
    queries,
    positives,
    gain_attn,
    w_query,
    w_key,
    w_value,
    w_out,
    rel_table,
    gain_ffn,
    w_inner,
    w_outer,
    w_proj,
):
    pc = Place(mesh_shape["dp"], mesh_shape["tensor"])
    n, seq, d = hidden_in.shape
    half = w_inner.shape[1]
    buckets = rel_table.shape[0]
    lens = lax.dynamic_slice_in_dim(lengths, pc.ti * n, n, 0)
    hot = jnp.asarray(diag_onehot(buckets))

    qf = queries.astype(F32)
    q_unit = (qf * lax.rsqrt(jnp.sum(qf * qf, axis=-1, keepdims=True) + EPS)).astype(BF)
    ints = jnp.stack([positives // 256, positives % 256, lens // 256, lens % 256], axis=1)
    ints = jnp.pad(ints.astype(BF), ((0, 0), (0, TILE - 4)))
    pack = pc.gather(jnp.concatenate([q_unit, ints], axis=1))
    q_all = pack[:, :d]
    ints = pack[:, d : d + 4].astype(jnp.int32)
    pos_all = ints[:, 0] * 256 + ints[:, 1]
    len_all = ints[:, 2] * 256 + ints[:, 3]

    w_qkv = jnp.concatenate([w_query, w_key, w_value], axis=1)
    o_qkv = pc.fetch(w_qkv)
    o_out = pc.fetch(w_out)
    o_inner = pc.fetch(w_inner)
    o_outer = pc.fetch(w_outer)
    o_table = pc.across(rel_table)

    def bias_of(table):
        bv = jnp.dot(hot, table, precision=lax.Precision.HIGHEST)
        bv = bv.T.reshape(table.shape[1] * 3, 2 * TILE)
        far = jnp.stack([table[buckets // 2 - 1], table[buckets - 1]], axis=1)
        return bv, far

    bv_a, far_a = bias_of(rel_table)
    bv_b, far_b = bias_of(o_table)

    an, q_a, k_a, v_a, ctx_a, ctxt_a, lse_a, nb_a = attn_fwd(
        hidden_in, lens, w_qkv, bv_a, far_a, gain_attn
    )
    q_b, k_b, v_b, ctx_b, ctxt_b, lse_b, nb_b = attn_fwd(an, lens, o_qkv, bv_b, far_b)
    res, fin, act, gp, asum, rsum = ffn_fwd(
        lens, hidden_in, ctx_a, ctx_b, w_out, o_out, gain_ffn, w_inner, o_inner
    )
    asum = asum[:, 0]
    a_hi = asum.astype(BF)
    a_lo = (asum - a_hi.astype(F32)).astype(BF)
    a_two = jnp.concatenate([a_hi, a_lo])
    branch = mm(a_two[:, :half], w_outer) + mm(a_two[:, half:], o_outer)
    flen = lens[:, None].astype(F32)
    pooled = (rsum[:, 0] + branch[:n] + branch[n:]) / flen
    pooled_all = pc.gather(pooled.astype(BF))

    count = pooled_all.shape[0]
    emb = mm(pooled_all, w_proj)
    inv_emb = lax.rsqrt(jnp.sum(emb * emb, axis=-1, keepdims=True) + EPS)
    unit = (emb * inv_emb).astype(BF)
    logits = mm(q_all, unit, NT) / SHARPNESS
    top = jnp.max(logits, axis=-1, keepdims=True)
    log_total = top + jnp.log(jnp.sum(jnp.exp(logits - top), axis=-1, keepdims=True))
    hit = jnp.arange(count, dtype=jnp.int32)[None, :] == pos_all[:, None]
    loss_all = log_total[:, 0] - jnp.sum(jnp.where(hit, logits, 0.0), axis=1)
    d_logits = (LOSS_SCALE * (jnp.exp(logits - log_total) - hit.astype(F32))).astype(BF)
    d_unit = mm(d_logits, q_all, TN) / SHARPNESS
    along = jnp.sum(emb * d_unit, axis=-1, keepdims=True)
    d_emb = (inv_emb * d_unit - inv_emb * inv_emb * inv_emb * along * emb).astype(BF)
    d_rows = mm(d_emb, w_proj, NT) / len_all[:, None].astype(F32)
    first = (pc.di * pc.tensor + pc.ti) * n
    query_loss = lax.dynamic_slice_in_dim(loss_all, first, n, 0)
    d_row = lax.dynamic_slice_in_dim(d_rows, first, n, 0)
    d_row_b = d_row.astype(BF)
    g = jnp.concatenate([mm(d_row_b, w_outer, NT), mm(d_row_b, o_outer, NT)], axis=1)

    d_inner = (gp.astype(F32) * g[:, None, :]).astype(BF)
    di_a, di_b = d_inner[:, :, :half], d_inner[:, :, half:]
    flat = lambda t: t.reshape(n * seq, t.shape[-1])
    gi_a = mm(flat(fin), flat(di_a), TN).astype(BF)
    gi_b = mm(flat(fin), flat(di_b), TN).astype(BF)
    inner_grad = pc.reduce(gi_a, gi_b)
    d_two = (mm(flat(di_a), w_inner, NT) + mm(flat(di_b), o_inner, NT)).reshape(n, seq, d)
    inv_two = lax.rsqrt(jnp.mean(res * res, axis=-1, keepdims=True) + EPS)
    gain_ffn_part = jnp.sum(d_two * res * inv_two, axis=(0, 1))
    scaled = d_two * gain_ffn
    inner_sum = jnp.sum(scaled * res, axis=-1, keepdims=True)
    valid = jnp.arange(seq, dtype=jnp.int32)[None, :] < lens[:, None]
    d_layer = jnp.where(valid[:, :, None], d_row[:, None, :], 0.0)
    d_res = d_layer + scaled * inv_two - res * (inv_two * inv_two * inv_two) * inner_sum / d
    d_attn = d_res.astype(BF)
    dctx_a = mm(flat(d_attn), w_out, NT).astype(BF).reshape(n, seq, -1)
    dctx_b = mm(flat(d_attn), o_out, NT).astype(BF).reshape(n, seq, -1)
    out_mm = lambda ct: jnp.einsum("bks,bsd->kd", ct, d_attn, preferred_element_type=F32)
    go_a, go_b = out_mm(ctxt_a), out_mm(ctxt_b)

    dq_b, dk_b, dv_b, diag_b, fsum_b = attn_bwd(lens, q_b, k_b, v_b, dctx_b, lse_b, nb_b, far_b)
    dq_a, dk_a, dv_a, diag_a, fsum_a = attn_bwd(lens, q_a, k_a, v_a, dctx_a, lse_a, nb_a, far_a)
    an_f = flat(an)

    def grads(dq, dk, dv, go):
        cols = [mm(an_f, flat(t), TN) for t in (dq, dk, dv)]
        wide = jnp.concatenate([go[:, : d // 2], go[:, d // 2 :]], axis=0)
        return jnp.concatenate(cols + [wide], axis=1).astype(BF)

    attn_grad = pc.reduce(grads(dq_a, dk_a, dv_a, go_a), grads(dq_b, dk_b, dv_b, go_b))
    width = w_query.shape[1]

    def back(dq, dk, dv, w):
        return (
            mm(flat(dq), w[:, :width], NT)
            + mm(flat(dk), w[:, width : 2 * width], NT)
            + mm(flat(dv), w[:, 2 * width :], NT)
        )

    d_one = (back(dq_a, dk_a, dv_a, w_qkv) + back(dq_b, dk_b, dv_b, o_qkv)).reshape(n, seq, d)
    x = hidden_in.astype(F32)
    inv_one = lax.rsqrt(jnp.mean(x * x, axis=-1, keepdims=True) + EPS)
    gain_attn_part = jnp.sum(d_one * x * inv_one, axis=(0, 1))
    scaled = d_one * gain_attn
    in_sum = jnp.sum(scaled * x, axis=-1, keepdims=True)
    input_grad = d_res + scaled * inv_one - x * (inv_one * inv_one * inv_one) * in_sum / d

    def table_of(diag, fsum):
        heads = fsum.shape[0] // 2
        t = jnp.dot(diag.reshape(heads, -1), hot, precision=lax.Precision.HIGHEST)
        f = jnp.sum(fsum, axis=1).reshape(heads, 2)
        t = t.at[:, buckets // 2 - 1].add(f[:, 0])
        return t.at[:, buckets - 1].add(f[:, 1])

    t_a, t_b = table_of(diag_a, fsum_a), table_of(diag_b, fsum_b)
    table_both = jnp.where(pc.ti > 0, jnp.stack([t_b, t_a]), jnp.stack([t_a, t_b]))
    small = jnp.concatenate([gain_attn_part, gain_ffn_part, table_both.reshape(-1)])
    small = pc.total(small.reshape(-1, TILE)).reshape(-1)
    gain_attn_grad, gain_ffn_grad = small[:d], small[d : 2 * d]
    table_sum = small[2 * d :].reshape(2, -1, buckets)
    table_grad = lax.dynamic_index_in_dim(table_sum, pc.ti, 0, keepdims=False).T

    layer = res.reshape(n * seq, d) + mm(flat(act[:, :, :half]), w_outer)
    layer = (layer + mm(flat(act[:, :, half:]), o_outer)).reshape(n, seq, d).astype(BF)
    asum_b = asum.astype(BF)
    sides = jnp.where(pc.ti > 0, asum_b[:, half:], asum_b[:, :half])
    del sides
    mine, theirs = asum_b[:, :half], asum_b[:, half:]
    a_all = two(pc.ti > 0, mine, pc.across(theirs))
    for bit in pc.bits:
        a_all = two(pc.up(bit), a_all, pc.dp_swap(a_all, bit))
    outer_grad = mm(a_all, d_rows.astype(BF), TN)
    proj_grad = mm(pooled_all, d_emb, TN)

    attn_f = attn_grad.astype(F32)
    out_wide = attn_f[:, 3 * width :]
    out_grad = jnp.concatenate([out_wide[: d // 2], out_wide[d // 2 :]], axis=1)
    return (
        layer,
        query_loss,
        input_grad,
        gain_attn_grad,
        attn_f[:, :width],
        attn_f[:, width : 2 * width],
        attn_f[:, 2 * width : 3 * width],
        out_grad,
        table_grad,
        gain_ffn_grad,
        inner_grad.astype(F32),
        outer_grad,
        proj_grad,
    )


def solution(mesh):
    both = ("dp", "tensor")
    return jax.shard_map(
        functools.partial(body, dict(mesh.shape)),
        mesh=mesh,
        in_specs=(
            P(both, None, None),
            P("dp"),
            P(both, None),
            P(both),
            P(),
            P(None, "tensor"),
            P(None, "tensor"),
            P(None, "tensor"),
            P("tensor", None),
            P(None, "tensor"),
            P(),
            P(None, "tensor"),
            P("tensor", None),
            P(),
        ),
        out_specs=(
            P(both, None, None),
            P(both),
            P(both, None, None),
            P(),
            P(None, "tensor"),
            P(None, "tensor"),
            P(None, "tensor"),
            P("tensor", None),
            P(None, "tensor"),
            P(),
            P(None, "tensor"),
            P("tensor", None),
            P(),
        ),
        check_vma=False,
    )
```

```python
import functools

import numpy as np

import jax
import jax.numpy as jnp
from jax import lax
from jax.experimental import pallas as pl
from jax.experimental.pallas import tpu as pltpu
from jax.sharding import PartitionSpec as P

LARGE_STEPS = (12, 16, 23, 32, 46, 64, 91)
SHARPNESS = 0.02
LOSS_SCALE = 256.0
EPS = 1e-06
NEG = -1e30
BF = jnp.bfloat16
F32 = jnp.float32
TILE = 128
GELU_A = 0.7978845608028654
GELU_B = 0.044715
MIB = 1024 * 1024

NN = (((1,), (0,)), ((), ()))
NT = (((1,), (1,)), ((), ()))
TN = (((0,), (0,)), ((), ()))


def mm(a, b, dims=NN):
    return lax.dot_general(a, b, dims, preferred_element_type=F32)


def bucket_of(r):
    a = np.abs(r)
    far = 8 + sum((a >= t).astype(np.int32) for t in LARGE_STEPS)
    return np.where(r > 0, 16, 0) + np.where(a < 8, a, far)


def diag_onehot(buckets):
    lane = np.arange(2 * TILE)
    rows = [bucket_of(TILE * d + TILE - 1 - lane) for d in (-1, 0, 1)]
    idx = np.concatenate(rows)
    hot = (idx[:, None] == np.arange(buckets)[None, :]).astype(np.float32)
    hot[2 * TILE - 1 :: 2 * TILE] = 0.0
    return hot

def params(**kw):
    return pltpu.CompilerParams(vmem_limit_bytes=60 * MIB, **kw)


def cost(us):
    return pl.CostEstimate(flops=0, bytes_accessed=int(us * 3.6e6), transcendentals=0)

ANY = pl.BlockSpec(memory_space=pl.ANY)
SMEM_SPEC = pl.BlockSpec(memory_space=pltpu.SMEM)


def const_spec(shape):
    zeros = (0,) * len(shape)
    return pl.BlockSpec(tuple(shape), lambda b: zeros, pipeline_mode=pl.Buffered(1))


def out_const(shape):
    zeros = (0,) * len(shape)
    return pl.BlockSpec(tuple(shape), lambda b: zeros)


def row_spec(shape):
    tail = (0,) * (len(shape) - 1)
    return pl.BlockSpec((1,) + tuple(shape[1:]), lambda b: (b,) + tail)


def sds(shape, dtype):
    return jax.ShapeDtypeStruct(tuple(shape), dtype)


def split3(t):
    hi = t.astype(BF)
    rest = t - hi.astype(F32)
    mid = rest.astype(BF)
    return hi, mid, (rest - mid.astype(F32)).astype(BF)


def run_copies(copies):
    for c in copies:
        c.start()
    for c in copies:
        c.wait()


def pack_kernel(at_ref, tab_ref, wq, wk, wv, wo, wi, wu, s0, s1, s2, sem):
    at = at_ref[0]
    d, width = wq.shape
    rows = d // 4
    half = wo.shape[0] // 4
    urows = wu.shape[0] // 8
    qrow = pl.ds(pl.multiple_of(at * rows, rows), rows)
    orow = pl.ds(pl.multiple_of(at * half, half), half)
    u0 = pl.ds(pl.multiple_of(at * 2 * urows, urows), urows)
    u1 = pl.ds(pl.multiple_of(at * 2 * urows + urows, urows), urows)
    top = pl.ds(0, rows)
    pairs = [
        (wq.at[qrow], s0.at[top, 0:width]),
        (wk.at[qrow], s0.at[top, width : 2 * width]),
        (wv.at[qrow], s0.at[top, 2 * width : 3 * width]),
        (wo.at[orow, 0:width], s0.at[pl.ds(0, half), 3 * width : 4 * width]),
        (wo.at[orow, width : 2 * width], s0.at[pl.ds(half, half), 3 * width : 4 * width]),
        (wi.at[qrow], s1),
        (wu.at[u0], s2.at[:, 0:d]),
        (wu.at[u1], s2.at[:, d : 2 * d]),
    ]
    copies = [pltpu.make_async_copy(a, b, sem.at[i]) for i, (a, b) in enumerate(pairs)]
    for c in copies:
        c.start()
    s0[rows:, :] = jnp.zeros((16, s0.shape[1]), BF)
    heads = tab_ref.shape[1]
    for k, part in enumerate(split3(tab_ref[...])):
        for s in range(2):
            lane = (2 * k + s) * TILE
            s0[rows:, lane : lane + heads] = part[16 * s : 16 * s + 16]
    for c in copies:
        c.wait()


def pack_weights(at, table, wq, wk, wv, wo, wi, wu):
    d, half = wi.shape
    rows = d // 4
    return pl.pallas_call(
        pack_kernel,
        in_specs=[SMEM_SPEC, pl.BlockSpec(memory_space=pltpu.VMEM)] + [ANY] * 6,
        out_specs=[pl.BlockSpec(memory_space=pltpu.VMEM)] * 3,
        out_shape=[sds((rows + 16, half), BF), sds((rows, half), BF), sds((rows, half), BF)],
        scratch_shapes=[pltpu.SemaphoreType.DMA((8,))],
        compiler_params=params(),
        cost_estimate=cost(3),
        name="pack_weights",
    )(at, table, wq, wk, wv, wo, wi, wu)


def spots(at):
    core, xb = at // 2, at % 2
    return [at, 2 * core + 1 - xb, 2 * (1 - core) + xb, 2 * (1 - core) + 1 - xb]


def qkv_copies(at, packs, dst, sem):
    width = dst.shape[1]
    rows = dst.shape[0] // 4
    out = []
    for i, (p, s) in enumerate(zip(packs, spots(at))):
        to = dst.at[pl.ds(pl.multiple_of(s * rows, rows), rows)]
        out.append(pltpu.make_async_copy(p.at[pl.ds(0, rows), 0:width], to, sem.at[i]))
    return out


def out_copies(at, packs, dst, sem):
    width = dst.shape[1] // 2
    rows = dst.shape[0] // 4
    out = []
    for i, (p, s) in enumerate(zip(packs, spots(at))):
        to = pl.ds(pl.multiple_of(s * rows, rows), rows)
        for e in range(2):
            src = p.at[pl.ds(e * rows, rows), 3 * width : 4 * width]
            dst_e = dst.at[to, e * width : (e + 1) * width]
            out.append(pltpu.make_async_copy(src, dst_e, sem.at[2 * i + e]))
    return out


def inner_copies(at, packs, dst, sem):
    rows = dst.shape[0] // 4
    out = []
    for i, (p, s) in enumerate(zip(packs, spots(at))):
        to = dst.at[pl.ds(pl.multiple_of(s * rows, rows), rows)]
        out.append(pltpu.make_async_copy(p.at[pl.ds(0, rows)], to, sem.at[i]))
    return out


def outer_copies(at, packs, dst, sem):
    rows = dst.shape[0] // 8
    d = dst.shape[1]
    out = []
    for i, (p, s) in enumerate(zip(packs, spots(at))):
        for e in range(2):
            to = dst.at[pl.ds(pl.multiple_of(s * 2 * rows + e * rows, rows), rows)]
            src = p.at[pl.ds(0, rows), e * d : (e + 1) * d]
            out.append(pltpu.make_async_copy(src, to, sem.at[2 * i + e]))
    return out


def bias_piece(nb_ref, tf_ref, h, bj, bi):
    d = bj - bi
    if abs(d) <= 1:
        return nb_ref[3 * h + d + 1]
    last = tf_ref.shape[0] - 1 if d > 0 else tf_ref.shape[0] // 2 - 1
    return tf_ref[last : last + 1, h : h + 1]


def biased_scores(s, nb_ref, tf_ref, mask_ref, h, ib):
    rows = []
    for bj in range(s.shape[0] // TILE):
        parts = []
        for t in range(2):
            piece = s[TILE * bj : TILE * (bj + 1), TILE * t : TILE * (t + 1)]
            piece = piece + bias_piece(nb_ref, tf_ref, h, bj, 2 * ib + t)
            parts.append(piece + mask_ref[TILE * bj : TILE * (bj + 1), :])
        rows.append(jnp.concatenate(parts, axis=1))
    return jnp.concatenate(rows, axis=0)


def set_mask(mask_ref, length):
    row = lax.broadcasted_iota(jnp.int32, mask_ref.shape, 0)
    mask_ref[...] = jnp.where(row < length, 0.0, NEG)


def set_bias(parts, hot_ref, tf_ref, nb_ref):
    tf_ref[...] = parts[0].astype(F32) + parts[1].astype(F32) + parts[2].astype(F32)
    hot = hot_ref[...]
    bv = mm(parts[0], hot, TN) + mm(parts[1], hot, TN) + mm(parts[2], hot, TN)
    for t in range(nb_ref.shape[0]):
        h, k = t // 3, t % 3
        v = jnp.broadcast_to(bv[h : h + 1, 2 * TILE * k : 2 * TILE * (k + 1)], (TILE, 2 * TILE))
        nb_ref[t] = pltpu.roll(v, TILE + 1, 1, stride=1, stride_axis=0)[:, :TILE]


def attn_rows(an, wq, wk, wv, nb_ref, tf_ref, mask_ref, q_ref, k_ref, v_ref, ctx_ref, ctxt_ref, lse_ref):
    seq = an.shape[0]
    width = q_ref.shape[2]
    low = (lax.broadcasted_iota(jnp.int32, (1, TILE), 1) < 64).astype(F32)
    for pair in range(width // TILE):
        cols = slice(TILE * pair, TILE * (pair + 1))
        qp = mm(an, wq[:, cols])
        kb = mm(an, wk[:, cols]).astype(BF)
        vp = mm(an, wv[:, cols])
        q_ref[0, :, cols] = qp.astype(BF)
        k_ref[0, :, cols] = kb
        v_ref[0, :, cols] = vp.astype(BF)
        vt = jnp.transpose(vp).astype(BF)
        ctx_cols = []
        for ib in range(seq // 256):
            halves = []
            for e in range(2):
                h = 2 * pair + e
                sel = low if e == 0 else 1.0 - low
                qm = (qp[256 * ib : 256 * (ib + 1)] * sel).astype(BF)
                s = biased_scores(mm(kb, qm, NT), nb_ref, tf_ref, mask_ref, h, ib)
                top = jnp.max(s, axis=0, keepdims=True)
                p = jnp.exp(s - top)
                total = jnp.sum(p, axis=0, keepdims=True)
                lse_ref[0, h : h + 1, 256 * ib : 256 * (ib + 1)] = top + jnp.log(total)
                c = mm(vt[64 * e : 64 * (e + 1), :], p.astype(BF))
                halves.append(c * (1.0 / total))
            ctx_cols.append(jnp.concatenate(halves, axis=0))
        ct = jnp.concatenate(ctx_cols, axis=1)
        ctxt_ref[0, cols, :] = ct.astype(BF)
        ctx_ref[0, :, cols] = jnp.transpose(ct).astype(BF)


def attn_own_kernel(lens, x_ref, gain_ref, wq, wk, wv, tab_ref, hot_ref, an_ref, *refs):
    outs, (nb_ref, tf_ref, mask_ref) = refs[:6], refs[6:]
    b = pl.program_id(0)

    @pl.when(b == 0)
    def _():
        pad = jnp.zeros((tab_ref.shape[0], TILE - tab_ref.shape[1]), F32)
        set_bias(split3(jnp.concatenate([tab_ref[...], pad], axis=1)), hot_ref, tf_ref, nb_ref)

    set_mask(mask_ref, lens[b])
    x = x_ref[0].astype(F32)
    inv = lax.rsqrt(jnp.mean(x * x, axis=-1, keepdims=True) + EPS)
    an = (x * inv * gain_ref[...]).astype(BF)
    an_ref[0] = an
    attn_rows(an, wq, wk, wv, nb_ref, tf_ref, mask_ref, *outs)


def attn_other_kernel(lens, at_ref, an_ref, hot_ref, p0, p1, p2, p3, *refs):
    outs, (nb_ref, tf_ref, mask_ref, w_ref, tab_ref, sem) = refs[:6], refs[6:]
    b = pl.program_id(0)

    @pl.when(b == 0)
    def _():
        rows = w_ref.shape[0] // 4
        copies = qkv_copies(at_ref[0], (p0, p1, p2, p3), w_ref, sem)
        copies.append(pltpu.make_async_copy(p0.at[pl.ds(rows, 16)], tab_ref, sem.at[4]))
        run_copies(copies)
        side = lambda i: tab_ref[:, TILE * i : TILE * (i + 1)]
        parts = [jnp.concatenate([side(2 * k), side(2 * k + 1)], axis=0) for k in range(3)]
        set_bias(parts, hot_ref, tf_ref, nb_ref)

    set_mask(mask_ref, lens[b])
    width = outs[0].shape[2]
    w = [w_ref.at[:, width * k : width * (k + 1)] for k in range(3)]
    attn_rows(an_ref[0], *w, nb_ref, tf_ref, mask_ref, *outs)


def attn_outs(n, seq, width, buckets):
    heads = width // 64
    tok = sds((n, seq, width), BF)
    rows = [tok, tok, tok, tok, sds((n, width, seq), BF), sds((n, 8, seq), F32)]
    flat = [sds((3 * heads, TILE, TILE), F32), sds((buckets, TILE), F32)]
    return rows + flat, [row_spec(o.shape) for o in rows] + [out_const(o.shape) for o in flat]


def attn_own(lens, x, gain, wq, wk, wv, table, hot):
    n, seq, d = x.shape
    outs, specs = attn_outs(n, seq, wq.shape[1], table.shape[0])
    an = sds((n, seq, d), BF)
    return pl.pallas_call(
        attn_own_kernel,
        grid=(n,),
        in_specs=[SMEM_SPEC, row_spec(x.shape), const_spec((1, d))]
        + [const_spec(wq.shape)] * 3
        + [const_spec(table.shape), const_spec(hot.shape)],
        out_specs=[row_spec(an.shape)] + specs,
        out_shape=[an] + outs,
        scratch_shapes=[pltpu.VMEM((seq, TILE), F32)],
        compiler_params=params(),
        cost_estimate=cost(16),
        name="attn_own",
    )(lens, x, gain.reshape(1, d), wq, wk, wv, table, hot)


def attn_other(lens, at, an, hot, packs, width):
    n, seq, d = an.shape
    outs, specs = attn_outs(n, seq, width, hot.shape[0])
    return pl.pallas_call(
        attn_other_kernel,
        grid=(n,),
        in_specs=[SMEM_SPEC, SMEM_SPEC, row_spec(an.shape), const_spec(hot.shape)] + [ANY] * 4,
        out_specs=specs,
        out_shape=outs,
        scratch_shapes=[
            pltpu.VMEM((seq, TILE), F32),
            pltpu.VMEM((d, 3 * width), BF),
            pltpu.VMEM((16, packs[0].shape[1]), BF),
            pltpu.SemaphoreType.DMA((5,)),
        ],
        compiler_params=params(),
        cost_estimate=cost(16),
        name="attn_other",
    )(lens, at, an, hot, *packs)


def attn_bwd_kernel(lens, at_ref, q_ref, k_ref, v_ref, dc_ref, lse_ref, nb_ref, tf_ref, an_ref, go_ref, *refs):
    (dq_ref, dk_ref, dv_ref, send_ref, keep_ref, diag_ref, fsum_ref, mask_ref, t_ref, wg_ref) = refs
    b = pl.program_id(0)
    seq, width = q_ref.shape[1], q_ref.shape[2]
    heads = width // 64
    nblk = seq // TILE

    @pl.when(b == 0)
    def _():
        t_ref[...] = jnp.zeros_like(t_ref)
        fsum_ref[...] = jnp.zeros_like(fsum_ref)

    set_mask(mask_ref, lens[b])
    low = (lax.broadcasted_iota(jnp.int32, (1, TILE), 1) < 64).astype(F32)
    for pair in range(heads // 2):
        cols = slice(TILE * pair, TILE * (pair + 1))
        kb = k_ref[0, :, cols]
        vb = v_ref[0, :, cols]
        kt = jnp.transpose(kb.astype(F32)).astype(BF)
        qf = q_ref[0, :, cols].astype(F32)
        df = dc_ref[0, :, cols].astype(F32)
        dk = jnp.zeros((seq, TILE), F32)
        dv = jnp.zeros((seq, TILE), F32)
        dq_cols = []
        for ib in range(seq // 256):
            halves = []
            for e in range(2):
                h = 2 * pair + e
                sel = low if e == 0 else 1.0 - low
                qm = (qf[256 * ib : 256 * (ib + 1)] * sel).astype(BF)
                dm = (df[256 * ib : 256 * (ib + 1)] * sel).astype(BF)
                s = biased_scores(mm(kb, qm, NT), nb_ref, tf_ref, mask_ref, h, ib)
                p = jnp.exp(s - lse_ref[0, h : h + 1, 256 * ib : 256 * (ib + 1)])
                t1 = p * mm(vb, dm, NT)
                ds = t1 - p * jnp.sum(t1, axis=0, keepdims=True)
                db = ds.astype(BF)
                dv = dv + mm(p.astype(BF), dm)
                dk = dk + mm(db, qm)
                halves.append(mm(kt[64 * e : 64 * (e + 1), :], db))
                far_sum = [None, None]
                for bj in range(nblk):
                    for t in range(2):
                        d = bj - (2 * ib + t)
                        piece = ds[TILE * bj : TILE * (bj + 1), TILE * t : TILE * (t + 1)]
                        if abs(d) <= 1:
                            t_ref[3 * h + d + 1] += piece
                        else:
                            side = 1 if d > 0 else 0
                            one = jnp.sum(piece, axis=0, keepdims=True)
                            far_sum[side] = one if far_sum[side] is None else far_sum[side] + one
                for side in range(2):
                    if far_sum[side] is not None:
                        fsum_ref[2 * h + side : 2 * h + side + 1, :] += far_sum[side]
            dq_cols.append(jnp.concatenate(halves, axis=0))
        dq_ref[0, :, cols] = jnp.transpose(jnp.concatenate(dq_cols, axis=1)).astype(BF)
        dk_ref[0, :, cols] = dk.astype(BF)
        dv_ref[0, :, cols] = dv.astype(BF)

    ant = jnp.transpose(an_ref[0].astype(F32)).astype(BF)
    for i, ref in enumerate((dq_ref, dk_ref, dv_ref)):
        part = mm(ant, ref[0])
        at = slice(width * i, width * (i + 1))

        @pl.when(b == 0)
        def _():
            wg_ref[:, at] = part

        @pl.when(b > 0)
        def _():
            wg_ref[:, at] += part

    @pl.when(b == pl.num_programs(0) - 1)
    def _():
        rows = wg_ref.shape[0] // 2
        wg_ref[:, 3 * width :] = go_ref[...]
        core = at_ref[0] // 2
        keep_ref[...] = wg_ref[pl.ds(pl.multiple_of(core * rows, rows), rows), :].astype(BF)
        send_ref[...] = wg_ref[pl.ds(pl.multiple_of((1 - core) * rows, rows), rows), :].astype(BF)
        bits = lax.broadcasted_iota(jnp.int32, (TILE, 2 * TILE), 0)
        for t in range(3 * heads):
            x = jnp.concatenate([t_ref[t], jnp.zeros((TILE, TILE), F32)], axis=1)
            x = pltpu.roll(x, TILE - 1, 1)
            for s in range(7):
                x = jnp.where((bits >> s) & 1 == 1, pltpu.roll(x, 2 * TILE - (1 << s), 1), x)
            diag_ref[t : t + 1, :] = jnp.sum(x, axis=0, keepdims=True)


def attn_bwd(lens, at, q, k, v, dctx, lse, nb, tf, an, go):
    n, seq, width = q.shape
    d = an.shape[2]
    heads = width // 64
    tok = sds((n, seq, width), BF)
    flat = [
        sds((d // 2, 4 * width), BF),
        sds((d // 2, 4 * width), BF),
        sds((3 * heads, 2 * TILE), F32),
        sds((2 * heads, TILE), F32),
    ]
    return pl.pallas_call(
        attn_bwd_kernel,
        grid=(n,),
        in_specs=[SMEM_SPEC, SMEM_SPEC]
        + [row_spec(q.shape)] * 4
        + [row_spec(lse.shape), const_spec(nb.shape), const_spec(tf.shape), row_spec(an.shape), const_spec(go.shape)],
        out_specs=[row_spec(q.shape)] * 3 + [out_const(o.shape) for o in flat],
        out_shape=[tok, tok, tok] + flat,
        scratch_shapes=[
            pltpu.VMEM((seq, TILE), F32),
            pltpu.VMEM((3 * heads, TILE, TILE), F32),
            pltpu.VMEM((d, 4 * width), F32),
        ],
        compiler_params=params(),
        cost_estimate=cost(32),
        name="attn_bwd",
    )(lens, at, q, k, v, dctx, lse, nb, tf, an, go)


def gelu_parts(v):
    v2 = v * v
    th = jnp.tanh(v * (GELU_A + (GELU_A * GELU_B) * v2))
    hh = 0.5 + 0.5 * th
    slope = hh + (v * (0.5 - 0.5 * th * th)) * (GELU_A + (3.0 * GELU_A * GELU_B) * v2)
    return v * hh, slope


def ffn_rows(fin, w_ref, length, act_ref, gp_ref, asum_ref):
    seq = fin.shape[0]
    vcol = (lax.broadcasted_iota(jnp.int32, (seq, TILE), 0) < length).astype(F32)[:, :1]
    vrow = (lax.broadcasted_iota(jnp.int32, (8, seq), 1) < length).astype(F32).astype(BF)
    chunk = 512
    for c in range(w_ref.shape[1] // chunk):
        at = slice(c * chunk, (c + 1) * chunk)
        act, slope = gelu_parts(mm(fin, w_ref[:, at]))
        act = act.astype(BF)
        act_ref[0, :, at] = act
        gp_ref[0, :, at] = (slope * vcol).astype(BF)
        asum_ref[0, :, at] = mm(vrow, act)[:1]
    return vcol


def ffn_own_kernel(lens, at_ref, x_ref, ca_ref, cb_ref, wa_ref, gain_ref, w_ref, p0, p1, p2, p3, *refs):
    (res_ref, fin_ref, rsum_ref, act_ref, gp_ref, asum_ref, wb_ref, sem) = refs
    b = pl.program_id(0)

    @pl.when(b == 0)
    def _():
        run_copies(out_copies(at_ref[0], (p0, p1, p2, p3), wb_ref, sem))

    res = x_ref[0].astype(F32) + mm(ca_ref[0], wa_ref[...]) + mm(cb_ref[0], wb_ref[...])
    res_ref[0] = res
    inv = lax.rsqrt(jnp.mean(res * res, axis=-1, keepdims=True) + EPS)
    fin = (res * inv * gain_ref[...]).astype(BF)
    fin_ref[0] = fin
    vcol = ffn_rows(fin, w_ref, lens[b], act_ref, gp_ref, asum_ref)
    rsum_ref[0] = jnp.sum(res * vcol, axis=0, keepdims=True)


def ffn_other_kernel(lens, at_ref, fin_ref, p0, p1, p2, p3, act_ref, gp_ref, asum_ref, w_ref, sem):
    b = pl.program_id(0)

    @pl.when(b == 0)
    def _():
        run_copies(inner_copies(at_ref[0], (p0, p1, p2, p3), w_ref, sem))

    ffn_rows(fin_ref[0], w_ref, lens[b], act_ref, gp_ref, asum_ref)


def ffn_own(lens, at, x, ctx_a, ctx_b, wo, gain, wi, packs):
    n, seq, d = x.shape
    half = wi.shape[1]
    outs = [
        sds((n, seq, d), F32),
        sds((n, seq, d), BF),
        sds((n, 1, d), F32),
        sds((n, seq, half), BF),
        sds((n, seq, half), BF),
        sds((n, 1, half), F32),
    ]
    return pl.pallas_call(
        ffn_own_kernel,
        grid=(n,),
        in_specs=[SMEM_SPEC, SMEM_SPEC, row_spec(x.shape), row_spec(ctx_a.shape), row_spec(ctx_b.shape)]
        + [const_spec(wo.shape), const_spec((1, d)), const_spec(wi.shape)]
        + [ANY] * 4,
        out_specs=[row_spec(o.shape) for o in outs],
        out_shape=outs,
        scratch_shapes=[pltpu.VMEM(wo.shape, BF), pltpu.SemaphoreType.DMA((8,))],
        compiler_params=params(),
        cost_estimate=cost(13),
        name="ffn_own",
    )(lens, at, x, ctx_a, ctx_b, wo, gain.reshape(1, d), wi, *packs)


def ffn_other(lens, at, fin, packs):
    n, seq, d = fin.shape
    half = packs[0].shape[1]
    outs = [sds((n, seq, half), BF), sds((n, seq, half), BF), sds((n, 1, half), F32)]
    return pl.pallas_call(
        ffn_other_kernel,
        grid=(n,),
        in_specs=[SMEM_SPEC, SMEM_SPEC, row_spec(fin.shape)] + [ANY] * 4,
        out_specs=[row_spec(o.shape) for o in outs],
        out_shape=outs,
        scratch_shapes=[pltpu.VMEM((d, half), BF), pltpu.SemaphoreType.DMA((4,))],
        compiler_params=params(),
        cost_estimate=cost(11),
        name="ffn_other",
    )(lens, at, fin, *packs)


def pool_kernel(lens, at_ref, aa_ref, ab_ref, rs_ref, w_ref, p0, p1, p2, p3, out_ref, wb_ref, sem):
    run_copies(outer_copies(at_ref[0], (p0, p1, p2, p3), wb_ref, sem))
    n = aa_ref.shape[0]

    def stacked(ref):
        rows = [ref[i] for i in range(n)]
        hi = [r.astype(BF) for r in rows]
        lo = [(r - h.astype(F32)).astype(BF) for r, h in zip(rows, hi)]
        pad = jnp.zeros((16 - 2 * n, rows[0].shape[1]), F32)
        return jnp.concatenate([t.astype(F32) for t in hi + lo] + [pad], axis=0).astype(BF)

    br = mm(stacked(aa_ref), w_ref[...]) + mm(stacked(ab_ref), wb_ref[...])
    for i in range(n):
        total = rs_ref[i] + br[i : i + 1] + br[n + i : n + i + 1]
        out_ref[i : i + 1, :] = total / lens[i].astype(F32)


def pool(lens, at, asum_a, asum_b, rsum, wu, packs):
    n = asum_a.shape[0]
    d = wu.shape[1]
    vm = pl.BlockSpec(memory_space=pltpu.VMEM)
    return pl.pallas_call(
        pool_kernel,
        in_specs=[SMEM_SPEC, SMEM_SPEC, vm, vm, vm, vm] + [ANY] * 4,
        out_specs=vm,
        out_shape=sds((8, d), F32),
        scratch_shapes=[pltpu.VMEM(wu.shape, BF), pltpu.SemaphoreType.DMA((8,))],
        compiler_params=params(),
        cost_estimate=cost(5),
        name="pool",
    )(lens, at, asum_a, asum_b, rsum, wu, *packs)


def loss_kernel(me_ref, at_ref, got_ref, wp_ref, wu_ref, p0, p1, p2, p3, *refs):
    (loss_ref, row_ref, g_ref, gn_ref, drow_ref, demb_ref, wb_ref, sem) = refs
    copies = outer_copies(at_ref[0], (p0, p1, p2, p3), wb_ref, sem)
    for c in copies:
        c.start()
    d = wp_ref.shape[0]
    count = got_ref.shape[0]
    pooled = got_ref[:, :d]
    qs = got_ref[:, d : 2 * d]
    ints = got_ref[:, 2 * d : 2 * d + TILE].astype(F32)
    pos = (ints[:, 0:1] * 256.0 + ints[:, 1:2]).astype(jnp.int32)
    length = ints[:, 2:3] * 256.0 + ints[:, 3:4]
    wp = wp_ref[...]
    emb = mm(pooled, wp)
    inv = lax.rsqrt(jnp.sum(emb * emb, axis=-1, keepdims=True) + EPS)
    unit = (emb * inv).astype(BF)
    logits = mm(qs, unit, NT) / SHARPNESS
    top = jnp.max(logits, axis=-1, keepdims=True)
    total = top + jnp.log(jnp.sum(jnp.exp(logits - top), axis=-1, keepdims=True))
    hit = lax.broadcasted_iota(jnp.int32, (count, count), 1) == pos
    loss = total - jnp.sum(jnp.where(hit, logits, 0.0), axis=1, keepdims=True)
    d_logits = (LOSS_SCALE * (jnp.exp(logits - total) - jnp.where(hit, 1.0, 0.0))).astype(BF)
    d_unit = mm(d_logits, qs, TN) / SHARPNESS
    along = jnp.sum(emb * d_unit, axis=-1, keepdims=True)
    d_emb = (inv * d_unit - inv * inv * inv * along * emb).astype(BF)
    demb_ref[...] = d_emb
    rows = mm(d_emb, wp, NT) / length
    drow_ref[...] = rows.astype(BF)
    index = lax.broadcasted_iota(jnp.int32, (count, 1), 0)
    pick = lambda t, i: jnp.sum(jnp.where(index == i, t, 0.0), axis=0, keepdims=True)
    own = [pick(rows, me_ref[i]) for i in range(2)]
    near = [pick(rows, me_ref[2 + i]) for i in range(2)]
    lost = jnp.broadcast_to(loss, (count, TILE))
    pad = jnp.zeros((6, d), F32)
    row_ref[...] = jnp.concatenate(own + [pad], axis=0)
    loss_ref[...] = jnp.concatenate([pick(lost, me_ref[i]) for i in range(2)] + [pad[:, :TILE]], axis=0)
    four = jnp.concatenate(own + near + [jnp.zeros((12, d), F32)], axis=0).astype(BF)
    for c in copies:
        c.wait()
    half = wu_ref.shape[0]
    ga = mm(four, wu_ref[...], NT)
    gb = mm(four, wb_ref[...], NT)
    g_ref[:, :half] = ga[:8]
    g_ref[:, half:] = gb[:8]
    gn_ref[...] = ga[:8]


def loss_all(me, at, got, wp, wu, packs):
    half, d = wu.shape
    count = got.shape[0]
    vm = pl.BlockSpec(memory_space=pltpu.VMEM)
    return pl.pallas_call(
        loss_kernel,
        in_specs=[SMEM_SPEC, SMEM_SPEC, vm, vm, vm] + [ANY] * 4,
        out_specs=[vm] * 6,
        out_shape=[
            sds((8, TILE), F32),
            sds((8, d), F32),
            sds((8, 2 * half), F32),
            sds((8, half), F32),
            sds((count, d), BF),
            sds((count, d), BF),
        ],
        scratch_shapes=[pltpu.VMEM(wu.shape, BF), pltpu.SemaphoreType.DMA((8,))],
        compiler_params=params(),
        cost_estimate=cost(7),
        name="loss",
    )(me, at, got, wp, wu, *packs)


def inner_grad_kernel(lens, at_ref, fin_ref, gp_ref, fnb_ref, g_ref, gn_ref, w_ref, send_ref, keep_ref, acc_ref):
    b = pl.program_id(0)
    n = pl.num_programs(0) // 2
    half = w_ref.shape[1]
    seq = fin_ref.shape[1]
    chunk = 512

    def add(fin, d_of):
        fin_t = jnp.transpose(fin.astype(F32)).astype(BF)
        for c in range(half // chunk):
            at = slice(c * chunk, (c + 1) * chunk)
            part = mm(fin_t, d_of(at))

            @pl.when(b == 0)
            def _():
                acc_ref[:, at] = part

            @pl.when(b > 0)
            def _():
                acc_ref[:, at] += part

    @pl.when(b < n)
    def _():
        add(fin_ref[0], lambda at: (gp_ref[0, :, at].astype(F32) * g_ref[pl.ds(b, 1), at]).astype(BF))

    @pl.when(b >= n)
    def _():
        fin = fnb_ref[0]
        valid = lax.broadcasted_iota(jnp.int32, (seq, TILE), 0) < lens[jnp.maximum(b, n)]
        vcol = valid.astype(F32)[:, :1]

        def d_of(at):
            slope = gelu_parts(mm(fin, w_ref[:, at]))[1]
            return (slope * vcol * gn_ref[pl.ds(b, 1), at]).astype(BF)

        add(fin, d_of)

    @pl.when(b == 2 * n - 1)
    def _():
        rows = acc_ref.shape[0] // 2
        core = at_ref[0] // 2
        keep_ref[...] = acc_ref[pl.ds(pl.multiple_of(core * rows, rows), rows), :].astype(BF)
        send_ref[...] = acc_ref[pl.ds(pl.multiple_of((1 - core) * rows, rows), rows), :].astype(BF)


def inner_grad(lens4, at, fin, gp, fin_nb, g, gn, wi):
    n, seq, d = fin.shape
    half = wi.shape[1]
    own = lambda shape: pl.BlockSpec((1,) + shape[1:], lambda b: (jnp.minimum(b, n - 1), 0, 0))
    near = lambda shape: pl.BlockSpec((1,) + shape[1:], lambda b: (jnp.maximum(b - n, 0), 0, 0))
    return pl.pallas_call(
        inner_grad_kernel,
        grid=(2 * n,),
        in_specs=[SMEM_SPEC, SMEM_SPEC, own(fin.shape), own(gp.shape), near(fin.shape)]
        + [const_spec(g.shape), const_spec(gn.shape), const_spec(wi.shape)],
        out_specs=[out_const((d // 2, half))] * 2,
        out_shape=[sds((d // 2, half), BF)] * 2,
        scratch_shapes=[pltpu.VMEM(wi.shape, F32)],
        compiler_params=params(),
        cost_estimate=cost(18),
        name="inner_grad",
    )(lens4, at, fin, gp, fin_nb, g, gn, wi)


def ffn_bwd_kernel(lens, at_ref, res_ref, gpa_ref, gpb_ref, g_ref, row_ref, gain_ref, wi_ref, wo_ref, cta_ref, ctb_ref, *refs):
    packs0, packs1 = refs[:4], refs[4:8]
    (dres_ref, dca_ref, dcb_ref, gain_out, goa_ref, gob_ref, wib_ref, wob_ref, sa_ref, sb_ref, sem0, sem1) = refs[8:]
    b = pl.program_id(0)
    last = pl.num_programs(0) - 1

    @pl.when(b == 0)
    def _():
        run_copies(
            out_copies(at_ref[0], packs0, wob_ref, sem0) + inner_copies(at_ref[0], packs1, wib_ref, sem1)
        )
        gain_out[...] = jnp.zeros_like(gain_out)
        sa_ref[...] = jnp.zeros_like(sa_ref)
        sb_ref[...] = jnp.zeros_like(sb_ref)

    res = res_ref[0]
    seq, d = res.shape
    half = wi_ref.shape[1]
    g = g_ref[pl.ds(b, 1), :]
    da = (gpa_ref[0].astype(F32) * g[:, :half]).astype(BF)
    db = (gpb_ref[0].astype(F32) * g[:, half:]).astype(BF)
    d_two = mm(da, wi_ref[...], NT) + mm(db, wib_ref[...], NT)
    inv = lax.rsqrt(jnp.mean(res * res, axis=-1, keepdims=True) + EPS)
    dr = d_two * res
    gain_out[...] += jnp.sum(dr * inv, axis=0, keepdims=True)
    gain = gain_ref[...]
    along = jnp.sum(dr * gain, axis=-1, keepdims=True)
    valid = lax.broadcasted_iota(jnp.int32, (seq, TILE), 0) < lens[b]
    vcol = valid.astype(F32)[:, :1]
    d_res = vcol * row_ref[pl.ds(b, 1), :] + d_two * gain * inv - res * (inv * inv * inv * along / d)
    dres_ref[0] = d_res
    d_attn = d_res.astype(BF)
    dca_ref[0] = mm(d_attn, wo_ref[...], NT).astype(BF)
    dcb_ref[0] = mm(d_attn, wob_ref[...], NT).astype(BF)
    sa_ref[...] += mm(cta_ref[0], d_attn)
    sb_ref[...] += mm(ctb_ref[0], d_attn)

    @pl.when(b == last)
    def _():
        rows = sa_ref.shape[0]
        for s_ref, o_ref in ((sa_ref, goa_ref), (sb_ref, gob_ref)):
            o_ref[:rows, :] = s_ref[:, :rows]
            o_ref[rows:, :] = s_ref[:, rows:]


def ffn_bwd(lens, at, res, gpa, gpb, g, row, gain, wi, wo, cta, ctb, packs0, packs1):
    n, seq, d = res.shape
    width = wo.shape[0]
    outs = [sds((n, seq, d), F32), sds((n, seq, width), BF), sds((n, seq, width), BF)]
    flat = [sds((1, d), F32), sds((d, width), F32), sds((d, width), F32)]
    return pl.pallas_call(
        ffn_bwd_kernel,
        grid=(n,),
        in_specs=[SMEM_SPEC, SMEM_SPEC, row_spec(res.shape), row_spec(gpa.shape), row_spec(gpb.shape)]
        + [const_spec(g.shape), const_spec(row.shape), const_spec((1, d)), const_spec(wi.shape), const_spec(wo.shape)]
        + [row_spec(cta.shape), row_spec(ctb.shape)]
        + [ANY] * 8,
        out_specs=[row_spec(o.shape) for o in outs] + [out_const(o.shape) for o in flat],
        out_shape=outs + flat,
        scratch_shapes=[
            pltpu.VMEM(wi.shape, BF),
            pltpu.VMEM(wo.shape, BF),
            pltpu.VMEM((width, d), F32),
            pltpu.VMEM((width, d), F32),
            pltpu.SemaphoreType.DMA((8,)),
            pltpu.SemaphoreType.DMA((4,)),
        ],
        compiler_params=params(),
        cost_estimate=cost(20),
        name="ffn_bwd",
    )(lens, at, res, gpa, gpb, g, row, gain.reshape(1, d), wi, wo, cta, ctb, *packs0, *packs1)


def input_kernel(at_ref, x_ref, dres_ref, gain_ref, qa, ka, va, qb, kb, vb, wq, wk, wv, p0, p1, p2, p3, out_ref, gain_out, w_ref, sem):
    b = pl.program_id(0)

    @pl.when(b == 0)
    def _():
        run_copies(qkv_copies(at_ref[0], (p0, p1, p2, p3), w_ref, sem))
        gain_out[...] = jnp.zeros_like(gain_out)

    width = wq.shape[1]
    d_one = mm(qa[0], wq[...], NT) + mm(ka[0], wk[...], NT) + mm(va[0], wv[...], NT)
    for i, t in enumerate((qb, kb, vb)):
        d_one = d_one + mm(t[0], w_ref[:, width * i : width * (i + 1)], NT)
    x = x_ref[0].astype(F32)
    inv = lax.rsqrt(jnp.mean(x * x, axis=-1, keepdims=True) + EPS)
    dx = d_one * x
    gain_out[...] += jnp.sum(dx * inv, axis=0, keepdims=True)
    gain = gain_ref[...]
    along = jnp.sum(dx * gain, axis=-1, keepdims=True)
    out_ref[0] = dres_ref[0] + d_one * gain * inv - x * (inv * inv * inv * along / x.shape[1])


def input_part(at, x, dres, gain, toks, wq, wk, wv, packs):
    n, seq, d = x.shape
    width = wq.shape[1]
    return pl.pallas_call(
        input_kernel,
        grid=(n,),
        in_specs=[SMEM_SPEC, row_spec(x.shape), row_spec(dres.shape), const_spec((1, d))]
        + [row_spec(toks[0].shape)] * 6
        + [const_spec(wq.shape)] * 3
        + [ANY] * 4,
        out_specs=[row_spec(x.shape), out_const((1, d))],
        out_shape=[sds(x.shape, F32), sds((1, d), F32)],
        scratch_shapes=[pltpu.VMEM((d, 3 * width), BF), pltpu.SemaphoreType.DMA((4,))],
        compiler_params=params(),
        cost_estimate=cost(12),
        name="input_part",
    )(at, x, dres, gain.reshape(1, d), *toks, wq, wk, wv, *packs)


def layer_kernel(at_ref, res_ref, aa_ref, ab_ref, w_ref, p0, p1, p2, p3, out_ref, wb_ref, sem):
    @pl.when(pl.program_id(0) == 0)
    def _():
        run_copies(outer_copies(at_ref[0], (p0, p1, p2, p3), wb_ref, sem))

    out_ref[0] = (res_ref[0] + mm(aa_ref[0], w_ref[...]) + mm(ab_ref[0], wb_ref[...])).astype(BF)


def layer_part(at, res, act_a, act_b, wu, packs):
    n, seq, d = res.shape
    return pl.pallas_call(
        layer_kernel,
        grid=(n,),
        in_specs=[SMEM_SPEC, row_spec(res.shape), row_spec(act_a.shape), row_spec(act_b.shape), const_spec(wu.shape)]
        + [ANY] * 4,
        out_specs=row_spec(res.shape),
        out_shape=sds(res.shape, BF),
        scratch_shapes=[pltpu.VMEM(wu.shape, BF), pltpu.SemaphoreType.DMA((8,))],
        compiler_params=params(),
        cost_estimate=cost(12),
        name="layer_part",
    )(at, res, act_a, act_b, wu, *packs)


def after(*xs):
    return lax.optimization_barrier(xs)


def bits_of(n):
    return [1 << i for i in range(n.bit_length() - 1)]


def swap(x, axis, bit, size):
    return lax.ppermute(x, axis, [(i, i ^ bit) for i in range(size)])


def two(up, first, second):
    return jnp.where(up, jnp.concatenate([second, first]), jnp.concatenate([first, second]))


class Place:
    def __init__(self, chips, tensor):
        self.chips, self.tensor = chips, tensor
        self.chip = lax.axis_index("chip")
        self.core = lax.axis_index("core")
        self.ti = lax.axis_index("tensor")

    def across(self, x):
        return swap(x, "tensor", 1, self.tensor)

    def core_swap(self, x):
        return swap(x, "core", 1, 2)

    def share(self, x):
        return lax.all_to_all(x, ("chip", "core", "tensor"), 0, 0, tiled=True)

    def side(self, mine):
        return swap(mine, "chip", 1, self.chips)

    def spread(self, mine, side):
        return [mine, side, self.core_swap(mine), self.core_swap(side)]

    def exchange(self, x):
        rows, width = x.shape
        return lax.all_to_all(x.reshape(self.chips, rows // self.chips, width), "chip", 0, 0, tiled=True)

    def add(self, got):
        return jnp.sum(got.astype(F32), axis=0).astype(BF)

    def gather(self, x):
        got = lax.all_to_all(jnp.broadcast_to(x[None], (self.chips,) + x.shape), "chip", 0, 0, tiled=True)
        return got.reshape(-1, x.shape[1])

    def join(self, x):
        return two(self.core > 0, x, self.core_swap(x))


def body(
    mesh_shape,
    hidden_in,
    lengths,
    queries,
    positives,
    gain_attn,
    w_query,
    w_key,
    w_value,
    w_out,
    rel_table,
    gain_ffn,
    w_inner,
    w_outer,
    w_proj,
):
    pc = Place(mesh_shape["chip"], mesh_shape["tensor"])
    n, seq, d = hidden_in.shape
    half = w_inner.shape[1]
    width = w_query.shape[1]
    buckets = rel_table.shape[0]
    lens = lax.dynamic_slice_in_dim(lengths, pc.ti * n, n, 0)
    near_lens = lax.dynamic_slice_in_dim(lengths, (1 - pc.ti) * n, n, 0)
    lens4 = jnp.concatenate([lens, near_lens])
    at = (2 * pc.core + (pc.chip & 1)).reshape(1)
    devices = pc.chips * 2 * pc.tensor
    hot = diag_onehot(buckets)
    hot_t = jnp.asarray(hot.T, BF)

    packs = pack_weights(at, rel_table, w_query, w_key, w_value, w_out, w_inner, w_outer)
    y_attn, y_inner, y_outer = [pc.across(p) for p in packs]

    an, q_a, k_a, v_a, ctx_a, ctxt_a, lse_a, nb_a, tf_a = attn_own(
        lens, hidden_in, gain_attn, w_query, w_key, w_value, rel_table, hot_t
    )
    y_attn, an = after(y_attn, an)
    p_attn = pc.spread(y_attn, pc.side(y_attn))
    x_inner = pc.side(y_inner)
    q_b, k_b, v_b, ctx_b, ctxt_b, lse_b, nb_b, tf_b = attn_other(lens, at, an, hot_t, p_attn, width)
    y_inner, x_inner, y_outer, ctx_b = after(y_inner, x_inner, y_outer, ctx_b)
    p_inner = pc.spread(y_inner, x_inner)
    x_outer = pc.side(y_outer)
    res, fin, rsum, act_a, gp_a, asum_a = ffn_own(
        lens, at, hidden_in, ctx_a, ctx_b, w_out, gain_ffn, w_inner, p_attn
    )
    fin_nb = pc.across(fin)
    act_b, gp_b, asum_b = ffn_other(lens, at, fin, p_inner)
    y_outer, x_outer, asum_b = after(y_outer, x_outer, asum_b)
    p_outer = pc.spread(y_outer, x_outer)
    pooled = pool(lens, at, asum_a, asum_b, rsum, w_outer, p_outer)[:n]

    qf = queries.astype(F32)
    q_unit = (qf * lax.rsqrt(jnp.sum(qf * qf, axis=-1, keepdims=True) + EPS)).astype(BF)
    ints = jnp.stack([positives // 256, positives % 256, lens // 256, lens % 256], axis=1)
    ints = jnp.pad(ints.astype(BF), ((0, 0), (0, TILE - 4)))
    common = jnp.concatenate([pooled.astype(BF), q_unit, ints], axis=1)
    common = jnp.broadcast_to(common[None], (devices,) + common.shape)
    got = pc.share(common).reshape(devices * n, -1)
    base = (2 * pc.chip + pc.core) * pc.tensor * n
    me = jnp.stack([base + pc.ti * n, base + pc.ti * n + 1, base + (1 - pc.ti) * n, base + (1 - pc.ti) * n + 1])
    loss8, row8, g8, gn8, d_rows, d_emb = loss_all(me, at, got, w_proj, w_outer, p_outer)
    query_loss = loss8[:n, 0]

    sums_a, sums_b = asum_a[:, 0].astype(BF), asum_b[:, 0].astype(BF)
    sums = jnp.where(pc.ti > 0, jnp.stack([sums_b, sums_a]), jnp.stack([sums_a, sums_b]))
    sums = jnp.broadcast_to(sums[None], (2 * pc.chips,) + sums.shape).reshape((devices,) + sums.shape[1:])
    sums, g8 = after(sums, g8)
    sums = pc.share(sums)

    gi_send, gi_keep = inner_grad(lens4, at, fin, gp_a, fin_nb, g8, gn8, w_inner)
    gi_send, gp_a = after(gi_send, gp_a)
    d_res, dctx_a, dctx_b, gain_ffn_part, go_a, go_b = ffn_bwd(
        lens, at, res, gp_a, gp_b, g8, row8, gain_ffn, w_inner, w_out, ctxt_a, ctxt_b, p_attn, p_inner
    )
    inner_half, sums, dctx_b = after(gi_keep + pc.core_swap(gi_send), sums, dctx_b)
    dq_b, dk_b, dv_b, send_b, keep_b, diag_b, fsum_b = attn_bwd(
        lens, at, q_b, k_b, v_b, dctx_b, lse_b, nb_b, tf_b, an, go_b
    )
    half_b, inner_part, dctx_a = after(keep_b + pc.core_swap(send_b), pc.add(pc.exchange(inner_half)), dctx_a)
    far_part = pc.across(half_b)
    dq_a, dk_a, dv_a, send_a, keep_a, diag_a, fsum_a = attn_bwd(
        lens, at, q_a, k_a, v_a, dctx_a, lse_a, nb_a, tf_a, an, go_a
    )
    inner_all, far_part, send_a = after(pc.gather(inner_part), far_part, send_a)
    parts = pc.exchange(keep_a + far_part + pc.core_swap(send_a))
    layer = layer_part(at, res, act_a, act_b, w_outer, p_outer)
    parts, layer, inner_all = after(parts, layer, inner_all)
    inner_sum = pc.join(inner_all)
    attn_all = pc.gather(pc.add(parts))
    toks = (dq_a, dk_a, dv_a, dq_b, dk_b, dv_b)
    input_grad, gain_attn_part = input_part(
        at, hidden_in, d_res, gain_attn, toks, w_query, w_key, w_value, p_attn
    )

    attn_all, input_grad = after(attn_all, input_grad)
    attn_sum = pc.join(attn_all)

    def table_of(diag, fsum):
        heads = fsum.shape[0] // 2
        t = jnp.dot(diag.reshape(heads, -1), jnp.asarray(hot), precision=lax.Precision.HIGHEST)
        f = jnp.sum(fsum, axis=1).reshape(heads, 2)
        t = t.at[:, buckets // 2 - 1].add(f[:, 0])
        return t.at[:, buckets - 1].add(f[:, 1])

    t_a, t_b = table_of(diag_a, fsum_a), table_of(diag_b, fsum_b)
    table_both = jnp.where(pc.ti > 0, jnp.stack([t_b, t_a]), jnp.stack([t_a, t_b]))
    small = jnp.concatenate([gain_attn_part[0], gain_ffn_part[0], table_both.reshape(-1)])
    small = jnp.broadcast_to(small.reshape(1, -1, TILE), (devices, small.shape[0] // TILE, TILE))
    small = jnp.sum(pc.share(small), axis=0).reshape(-1)
    gain_attn_grad, gain_ffn_grad = small[:d], small[d : 2 * d]
    table_sum = small[2 * d :].reshape(2, -1, buckets)
    table_grad = lax.dynamic_index_in_dim(table_sum, pc.ti, 0, keepdims=False).T

    outer_grad = mm(sums.reshape(devices * n, -1), d_rows, TN)
    proj_grad = mm(got[:, :d], d_emb, TN)

    attn_f = attn_sum.astype(F32)
    out_wide = attn_f[:, 3 * width :]
    out_grad = jnp.concatenate([out_wide[: d // 2], out_wide[d // 2 :]], axis=1)
    return (
        layer,
        query_loss,
        input_grad,
        gain_attn_grad,
        attn_f[:, :width],
        attn_f[:, width : 2 * width],
        attn_f[:, 2 * width : 3 * width],
        out_grad,
        table_grad,
        gain_ffn_grad,
        inner_sum.astype(F32),
        outer_grad,
        proj_grad,
    )


def solution(mesh):
    dp, tensor = mesh.shape["dp"], mesh.shape["tensor"]
    fine = jax.sharding.Mesh(mesh.devices.reshape(dp // 2, 2, tensor), ("chip", "core", "tensor"))
    rows = ("chip", "core")
    both = rows + ("tensor",)
    return jax.shard_map(
        functools.partial(body, dict(fine.shape)),
        mesh=fine,
        in_specs=(
            P(both, None, None),
            P(rows),
            P(both, None),
            P(both),
            P(),
            P(None, "tensor"),
            P(None, "tensor"),
            P(None, "tensor"),
            P("tensor", None),
            P(None, "tensor"),
            P(),
            P(None, "tensor"),
            P("tensor", None),
            P(),
        ),
        out_specs=(
            P(both, None, None),
            P(both),
            P(both, None, None),
            P(),
            P(None, "tensor"),
            P(None, "tensor"),
            P(None, "tensor"),
            P("tensor", None),
            P(None, "tensor"),
            P(),
            P(None, "tensor"),
            P("tensor", None),
            P(),
        ),
        check_vma=False,
    )
```

```python
import functools

import numpy as np

import jax
import jax.numpy as jnp
from jax import lax
from jax.experimental import pallas as pl
from jax.experimental.pallas import tpu as pltpu
from jax.sharding import PartitionSpec as P

LARGE_STEPS = (12, 16, 23, 32, 46, 64, 91)
SHARPNESS = 0.02
LOSS_SCALE = 256.0
EPS = 1e-06
NEG = -1e30
BF = jnp.bfloat16
F32 = jnp.float32
TILE = 128
BUCKETS = 32
GELU_A = 0.7978845608028654
GELU_B = 0.044715
MIB = 1024 * 1024

NN = (((1,), (0,)), ((), ()))
NT = (((1,), (1,)), ((), ()))
TN = (((0,), (0,)), ((), ()))


def mm(a, b, dims=NN):
    return lax.dot_general(a, b, dims, preferred_element_type=F32)


def bucket_of(r):
    a = np.abs(r)
    far = 8 + sum((a >= t).astype(np.int32) for t in LARGE_STEPS)
    return np.where(r > 0, 16, 0) + np.where(a < 8, a, far)


def diag_onehot(buckets, back):
    lane = np.arange(2 * TILE)
    at = lane - TILE + 1 if back else TILE - 1 - lane
    idx = np.concatenate([bucket_of(TILE * d + at) for d in (-1, 0, 1)])
    hot = (idx[:, None] == np.arange(buckets)[None, :]).astype(np.float32)
    hot[2 * TILE - 1 :: 2 * TILE] = 0.0
    return hot


def params(**kw):
    return pltpu.CompilerParams(vmem_limit_bytes=60 * MIB, **kw)


def cost(us):
    return pl.CostEstimate(flops=0, bytes_accessed=int(us * 3.6e6), transcendentals=0)

ANY = pl.BlockSpec(memory_space=pl.ANY)
SMEM_SPEC = pl.BlockSpec(memory_space=pltpu.SMEM)


def const_spec(shape):
    zeros = (0,) * len(shape)
    return pl.BlockSpec(tuple(shape), lambda b: zeros, pipeline_mode=pl.Buffered(1))


def out_const(shape):
    zeros = (0,) * len(shape)
    return pl.BlockSpec(tuple(shape), lambda b: zeros)


def row_spec(shape):
    tail = (0,) * (len(shape) - 1)
    return pl.BlockSpec((1,) + tuple(shape[1:]), lambda b: (b,) + tail)


def sds(shape, dtype):
    return jax.ShapeDtypeStruct(tuple(shape), dtype)


def split3(t):
    hi = t.astype(BF)
    rest = t - hi.astype(F32)
    mid = rest.astype(BF)
    return hi, mid, (rest - mid.astype(F32)).astype(BF)


def run_copies(copies):
    for c in copies:
        c.start()
    for c in copies:
        c.wait()


def pack_kernel(at_ref, tab_ref, wq, wk, wv, wo, wi, wu, s0, s1, s2, s3, sem):
    at = at_ref[0]
    width = wq.shape[1]
    rows = s2.shape[0]

    def part(w, dst, i, spot, count):
        src = w.at[pl.ds(pl.multiple_of(spot * count, count), count)]
        return pltpu.make_async_copy(src, dst, sem.at[i])

    spread = [(w, s0.at[pl.ds(0, rows), width * i : width * (i + 1)]) for i, w in enumerate((wq, wk, wv))]
    copies = [part(w, dst, i, at, rows) for i, (w, dst) in enumerate(spread + [(wi, s2)])]
    copies += [part(w, dst, 4 + i, at // 2, dst.shape[0]) for i, (w, dst) in enumerate(((wo, s1), (wu, s3)))]
    for c in copies:
        c.start()
    s0[rows:, :] = jnp.zeros((16, s0.shape[1]), BF)
    heads, buckets = tab_ref.shape
    for k, t in enumerate(split3(tab_ref[...])):
        s0[rows : rows + heads, TILE * k : TILE * k + buckets] = t
    for c in copies:
        c.wait()


def pack_weights(at, table, wq, wk, wv, wo, wi, wu):
    d, half = wi.shape
    width = wq.shape[1]
    vm = pl.BlockSpec(memory_space=pltpu.VMEM)
    return pl.pallas_call(
        pack_kernel,
        in_specs=[SMEM_SPEC, vm] + [ANY] * 6,
        out_specs=[vm] * 4,
        out_shape=[
            sds((d // 4 + 16, 3 * width), BF),
            sds((width // 2, d), BF),
            sds((d // 4, half), BF),
            sds((half // 2, d), BF),
        ],
        scratch_shapes=[pltpu.SemaphoreType.DMA((6,))],
        compiler_params=params(),
        cost_estimate=cost(3),
        name="pack_weights",
    )(at, table, wq, wk, wv, wo, wi, wu)


def join_copies(at, packs, dst, sem):
    core, xb = at // 2, at % 2
    spots = [at, 2 * core + 1 - xb, 2 * (1 - core) + xb, 2 * (1 - core) + 1 - xb]
    if len(packs) == 2:
        spots = [core, 1 - core]
    rows = dst.shape[0] // len(packs)
    out = []
    for i, (p, s) in enumerate(zip(packs, spots)):
        to = dst.at[pl.ds(pl.multiple_of(s * rows, rows), rows)]
        out.append(pltpu.make_async_copy(p.at[pl.ds(0, rows)], to, sem.at[i]))
    return out


EXTRA = 16


def key_extras(length, rows):
    row = lax.broadcasted_iota(jnp.int32, (rows, TILE), 0)
    lane = lax.broadcasted_iota(jnp.int32, (rows, TILE), 1) & 63
    blk = (lane - 1) & 3
    hot = (lane >= 1) & (lane < 13) & (blk == row // TILE)
    one = ((lane == 0) & (row >= length)) | hot | ((lane >= 13) & (lane < EXTRA))
    return jnp.where(one, 1.0, 0.0)


def far_rows(tf_ref, h, seq):
    row = lax.broadcasted_iota(jnp.int32, (EXTRA, seq), 0)
    diff = ((row - 1) & 3) - lax.broadcasted_iota(jnp.int32, (EXTRA, seq), 1) // TILE
    out = jnp.where(row == 0, NEG, 0.0)
    last, mid = BUCKETS - 1, BUCKETS // 2 - 1
    for k in range(3):
        mine = (row >= 1 + 4 * k) & (row < 5 + 4 * k)
        out = out + jnp.where(mine & (diff >= 2), tf_ref[k, h : h + 1, last : last + 1], 0.0)
        out = out + jnp.where(mine & (diff <= -2), tf_ref[k, h : h + 1, mid : mid + 1], 0.0)
    return out


def stack_rows(e, main, extra):
    pad = jnp.zeros((64 - extra.shape[0], extra.shape[1]), BF)
    return jnp.concatenate([main, extra, pad] if e == 0 else [extra, pad, main], axis=0)


def near_bias(s, nb_ref, h, ib):
    rows = []
    for bj in range(s.shape[0] // TILE):
        parts = []
        for t in range(2):
            piece = s[TILE * bj : TILE * (bj + 1), TILE * t : TILE * (t + 1)]
            d = bj - (2 * ib + t)
            parts.append(piece + nb_ref[3 * h + d + 1] if abs(d) <= 1 else piece)
        rows.append(jnp.concatenate(parts, axis=1))
    return rows


def set_bias(parts, hot_ref, tf_ref, nb_ref):
    for k in range(3):
        tf_ref[k] = parts[k].astype(F32)
    hot = hot_ref[...]
    bv = mm(parts[0], hot) + mm(parts[1], hot) + mm(parts[2], hot)
    for t in range(nb_ref.shape[0]):
        h, k = t // 3, t % 3
        v = jnp.broadcast_to(bv[h : h + 1, 2 * TILE * k : 2 * TILE * (k + 1)], (TILE, 2 * TILE))
        nb_ref[t] = pltpu.roll(v, TILE + 1, 1, stride=1, stride_axis=0)[:, :TILE]


def attn_rows(an, length, ws, outs, nb_ref, tf_ref, s_ref, p_ref):
    q_ref, qt_ref, k_ref, v_ref, ctx_ref, ctxt_ref, lse_ref = outs
    seq = an.shape[0]
    width = q_ref.shape[2]
    for ref, w in zip((q_ref, k_ref, v_ref), ws):
        ref[0] = mm(an, w[...]).astype(BF)
    kx = key_extras(length, seq)
    lane = lax.broadcasted_iota(jnp.int32, (seq, TILE), 1)
    blocks = [(h, ib) for h in range(width // 64) for ib in range(seq // 256)]
    keys, queries, values, tops, sums, rows = {}, {}, {}, {}, {}, {}

    def prepare(h):
        pair, e = h // 2, h % 2
        cols = slice(TILE * pair, TILE * (pair + 1))
        if e == 0:
            qt_ref[0, cols, :] = jnp.transpose(q_ref[0, :, cols])
            values[pair] = jnp.transpose(v_ref[0, :, cols])
        mine = lane < 64 if e == 0 else lane >= 64
        keys[h] = jnp.where(mine, k_ref[0, :, cols].astype(F32), kx).astype(BF)
        qt = qt_ref[0, 64 * h : 64 * (h + 1), :]
        queries[h] = stack_rows(e, qt, far_rows(tf_ref, h, seq).astype(BF))

    def score(t):
        h, ib = blocks[t]
        if ib == 0:
            prepare(h)
        s = mm(keys[h], queries[h][:, 256 * ib : 256 * (ib + 1)])
        top = None
        for bj, piece in enumerate(near_bias(s, nb_ref, h, ib)):
            s_ref[t % 2, TILE * bj : TILE * (bj + 1), :] = piece
            m = jnp.max(piece.reshape(TILE // 8, 8, 256), axis=0)
            top = m if top is None else jnp.maximum(top, m)
        tops[t] = jnp.max(top, axis=0, keepdims=True)

    def soft(t):
        h, ib = blocks[t]
        total = None
        for bj in range(seq // TILE):
            at = slice(TILE * bj, TILE * (bj + 1))
            p = jnp.exp(s_ref[t % 2, at, :] - tops[t])
            one = jnp.sum(p.reshape(TILE // 8, 8, 256), axis=0)
            total = one if total is None else total + one
            p_ref[h % 2, at, 256 * ib : 256 * (ib + 1)] = p.astype(BF)
        sums[t] = jnp.sum(total, axis=0, keepdims=True)
        lse_ref[0, h : h + 1, 256 * ib : 256 * (ib + 1)] = tops[t] + jnp.log(sums[t])

    def combine(h):
        per = seq // 256
        total = jnp.concatenate([sums[per * h + i] for i in range(per)], axis=1)
        vt = values[h // 2][64 * (h % 2) : 64 * (h % 2 + 1), :]
        rows[h] = mm(vt, p_ref[h % 2]) * (1.0 / total)
        if h % 2 == 1:
            pair = h // 2
            cols = slice(TILE * pair, TILE * (pair + 1))
            ct = jnp.concatenate([rows[h - 1], rows[h]], axis=0).astype(BF)
            ctxt_ref[0, cols, :] = ct
            ctx_ref[0, :, cols] = jnp.transpose(ct)

    score(0)
    for t, (h, ib) in enumerate(blocks):
        if t + 1 < len(blocks):
            score(t + 1)
        soft(t)
        if ib == seq // 256 - 1:
            combine(h)


def attn_own_kernel(lens, x_ref, gain_ref, wq, wk, wv, tab_ref, hot_ref, an_ref, ant_ref, *refs):
    outs, (nb_ref, tf_ref, s_ref, p_ref) = refs[:7], refs[7:]
    b = pl.program_id(0)

    @pl.when(b == 0)
    def _():
        heads, buckets = tab_ref.shape
        wide = jnp.concatenate([tab_ref[...], jnp.zeros((heads, TILE - buckets), F32)], axis=1)
        wide = jnp.concatenate([wide, jnp.zeros((16 - heads, TILE), F32)], axis=0)
        set_bias(split3(wide), hot_ref, tf_ref, nb_ref)

    x = x_ref[0].astype(F32)
    inv = lax.rsqrt(jnp.mean(x * x, axis=-1, keepdims=True) + EPS)
    an = (x * inv * gain_ref[...]).astype(BF)
    an_ref[0] = an
    ant_ref[...] = jnp.transpose(an)
    attn_rows(an, lens[b], (wq, wk, wv), outs, nb_ref, tf_ref, s_ref, p_ref)


def attn_other_kernel(lens, at_ref, an_ref, hot_ref, x_ref, ca_ref, wo_ref, gain_ref, p0, p1, p2, p3, o0, o1, *refs):
    outs, (nb_ref, tf_ref, res_ref, fin_ref, fint_ref, rsum_ref) = refs[:7], refs[7:13]
    (s_ref, p_ref, w_ref, tab_ref, wb_ref, sem, sem1) = refs[13:]
    b = pl.program_id(0)
    late = join_copies(at_ref[0], (o0, o1), wb_ref, sem1)

    @pl.when(b == 0)
    def _():
        rows = w_ref.shape[0] // 4
        copies = join_copies(at_ref[0], (p0, p1, p2, p3), w_ref, sem)
        copies.append(pltpu.make_async_copy(p0.at[pl.ds(rows, 16)], tab_ref, sem.at[4]))
        for c in copies + late:
            c.start()
        for c in copies:
            c.wait()
        parts = [tab_ref[:, TILE * k : TILE * (k + 1)] for k in range(3)]
        set_bias(parts, hot_ref, tf_ref, nb_ref)

    width = outs[0].shape[2]
    ws = [w_ref.at[:, width * k : width * (k + 1)] for k in range(3)]
    attn_rows(an_ref[0], lens[b], ws, outs, nb_ref, tf_ref, s_ref, p_ref)

    @pl.when(b == 0)
    def _():
        for c in late:
            c.wait()

    res = x_ref[0].astype(F32) + mm(ca_ref[0], wo_ref[...]) + mm(outs[4][0], wb_ref[...])
    res_ref[0] = res
    inv = lax.rsqrt(jnp.mean(res * res, axis=-1, keepdims=True) + EPS)
    fin = (res * inv * gain_ref[...]).astype(BF)
    fin_ref[0] = fin
    fint_ref[...] = jnp.transpose(fin)
    vcol = (lax.broadcasted_iota(jnp.int32, (res.shape[0], TILE), 0) < lens[b]).astype(F32)[:, :1]
    rsum_ref[0] = jnp.sum(res * vcol, axis=0, keepdims=True)


def attn_outs(n, seq, width):
    heads = width // 64
    tok, turned = sds((n, seq, width), BF), sds((n, width, seq), BF)
    rows = [tok, turned, tok, tok, tok, turned, sds((n, 8, seq), F32)]
    flat = [sds((3 * heads, TILE, TILE), F32), sds((3, 16, TILE), F32)]
    scratch = [pltpu.VMEM((2, seq, 256), F32), pltpu.VMEM((2, seq, seq), BF)]
    return rows + flat, [row_spec(o.shape) for o in rows] + [out_const(o.shape) for o in flat], scratch


def attn_own(lens, x, gain, wq, wk, wv, table, hot):
    n, seq, d = x.shape
    outs, specs, scratch = attn_outs(n, seq, wq.shape[1])
    return pl.pallas_call(
        attn_own_kernel,
        grid=(n,),
        in_specs=[SMEM_SPEC, row_spec(x.shape), const_spec((1, d))]
        + [const_spec(wq.shape)] * 3
        + [const_spec(table.shape), const_spec(hot.shape)],
        out_specs=[row_spec(x.shape), pl.BlockSpec((d, seq), lambda b: (0, b))] + specs,
        out_shape=[sds((n, seq, d), BF), sds((d, n * seq), BF)] + outs,
        scratch_shapes=scratch,
        compiler_params=params(),
        cost_estimate=cost(12),
        name="attn_own",
    )(lens, x, gain.reshape(1, d), wq, wk, wv, table, hot)


def attn_other(lens, at, an, hot, x, ctx_a, wo, gain, packs, packs_o):
    n, seq, d = an.shape
    width = wo.shape[0]
    outs, specs, scratch = attn_outs(n, seq, width)
    more = [sds((n, seq, d), F32), sds((n, seq, d), BF), sds((d, n * seq), BF), sds((n, 1, d), F32)]
    more_specs = [row_spec(o.shape) for o in more]
    more_specs[2] = pl.BlockSpec((d, seq), lambda b: (0, b))
    return pl.pallas_call(
        attn_other_kernel,
        grid=(n,),
        in_specs=[SMEM_SPEC, SMEM_SPEC, row_spec(an.shape), const_spec(hot.shape), row_spec(x.shape)]
        + [row_spec(ctx_a.shape), const_spec(wo.shape), const_spec((1, d))]
        + [ANY] * 6,
        out_specs=specs + more_specs,
        out_shape=outs + more,
        scratch_shapes=scratch
        + [
            pltpu.VMEM((d, 3 * width), BF),
            pltpu.VMEM((16, 3 * width), BF),
            pltpu.VMEM(wo.shape, BF),
            pltpu.SemaphoreType.DMA((5,)),
            pltpu.SemaphoreType.DMA((2,)),
        ],
        compiler_params=params(),
        cost_estimate=cost(15),
        name="attn_other",
    )(lens, at, an, hot, x, ctx_a, wo, gain.reshape(1, d), *packs, *packs_o)


def attn_bwd_kernel(lens, at_ref, *refs):
    (q_ref, qt_ref, k_ref, v_ref, dc_ref, dct_ref, ct_ref, lse_ref, nb_ref, tf_ref, hot_ref, ant_hbm, go_hbm) = refs[:13]
    (dq_ref, dk_ref, dv_ref, send_ref, keep_ref, table_ref) = refs[13:19]
    (t_ref, fsum_ref, p_ref, ds_ref, all_ref, ant_ref, go_ref, sem) = refs[19:]
    b = pl.program_id(0)
    seq, width = q_ref.shape[1], q_ref.shape[2]
    heads = width // 64
    nblk = seq // TILE

    late = [pltpu.make_async_copy(ant_hbm, ant_ref, sem.at[0]), pltpu.make_async_copy(go_hbm, go_ref, sem.at[1])]

    @pl.when(b == 0)
    def _():
        for c in late:
            c.start()
        t_ref[...] = jnp.zeros_like(t_ref)
        fsum_ref[...] = jnp.zeros_like(fsum_ref)
        table_ref[...] = jnp.zeros_like(table_ref)

    kx = key_extras(lens[b], seq)
    lane = lax.broadcasted_iota(jnp.int32, (seq, TILE), 1)
    vx = jnp.where((lane & 63) < 3, 1.0, 0.0)
    keys, values, queries, grads, turned = {}, {}, {}, {}, {}

    def prepare(h):
        pair, e = h // 2, h % 2
        cols = slice(TILE * pair, TILE * (pair + 1))
        mine = lane < 64 if e == 0 else lane >= 64
        if e == 0:
            turned[pair] = jnp.transpose(k_ref[0, :, cols])
        keys[h] = jnp.where(mine, k_ref[0, :, cols].astype(F32), kx).astype(BF)
        values[h] = jnp.where(mine, v_ref[0, :, cols].astype(F32), vx).astype(BF)
        at = slice(64 * h, 64 * (h + 1))
        lse = split3(-lse_ref[0, h : h + 1, :])
        extra = far_rows(tf_ref, h, seq)
        row = lax.broadcasted_iota(jnp.int32, (EXTRA, seq), 0)
        for k in range(3):
            extra = jnp.where(row == 13 + k, lse[k].astype(F32), extra)
        queries[h] = stack_rows(e, qt_ref[0, at, :], extra.astype(BF))
        along = jnp.sum(dct_ref[0, at, :].astype(F32) * ct_ref[0, at, :].astype(F32), axis=0, keepdims=True)
        extra = jnp.zeros((EXTRA, seq), F32)
        for k, part in enumerate(split3(-along)):
            extra = jnp.where(row == k, part.astype(F32), extra)
        grads[h] = stack_rows(e, dct_ref[0, at, :], extra.astype(BF))

    def block(h, ib):
        pair, e = h // 2, h % 2
        at = slice(256 * ib, 256 * (ib + 1))
        to = slice(seq * e + 256 * ib, seq * e + 256 * (ib + 1))
        s = mm(keys[h], queries[h][:, at])
        dp = mm(values[h], grads[h][:, at])
        near, far = {}, {}
        for bj, piece in enumerate(near_bias(s, nb_ref, h, ib)):
            rows = slice(TILE * bj, TILE * (bj + 1))
            p = jnp.exp(piece)
            ds = p * dp[rows, :]
            p_ref[pair % 2, rows, to] = p.astype(BF)
            ds_ref[pair % 2, rows, to] = ds.astype(BF)
            for t in range(2):
                d = bj - (2 * ib + t)
                one = ds[:, TILE * t : TILE * (t + 1)]
                if abs(d) <= 1:
                    near[d] = near[d] + one if d in near else one
                else:
                    one = jnp.sum(one.reshape(TILE // 8, 8, TILE), axis=0)
                    side = 1 if d > 0 else 0
                    far[side] = far[side] + one if side in far else one
        for d, one in near.items():
            t_ref[3 * h + d + 1] += one
        for side, one in far.items():
            fsum_ref[2 * h + side] += one

    def finish(pair, part):
        slot = pair % 2
        cols = slice(TILE * pair, TILE * (pair + 1))
        rows = pl.ds(pl.multiple_of(b * seq, seq), seq)
        if part < 2:
            src, other, out_ref = ((p_ref, dc_ref, dv_ref), (ds_ref, q_ref, dk_ref))[part]
            rhs = other[0, :, cols]
            one = jnp.where(lane < 64, mm(src[slot, :, :seq], rhs), mm(src[slot, :, seq:], rhs)).astype(BF)
            out_ref[0, :, cols] = one
            base = width * (2 - part)
            all_ref[rows, base + TILE * pair : base + TILE * (pair + 1)] = one
        if part == 2:
            kt = turned[pair]
            dqt = [mm(kt[64 * e : 64 * (e + 1), :], ds_ref[slot, :, seq * e : seq * (e + 1)]) for e in range(2)]
            one = jnp.transpose(jnp.concatenate(dqt, axis=0).astype(BF))
            dq_ref[0, :, cols] = one
            all_ref[rows, TILE * pair : TILE * (pair + 1)] = one

    for pair in range(heads // 2):
        step = 0
        for e in range(2):
            prepare(2 * pair + e)
            for ib in range(seq // 256):
                block(2 * pair + e, ib)
                if pair > 0 and step < 3:
                    finish(pair - 1, step)
                step += 1
    for part in range(3):
        finish(heads // 2 - 1, part)

    @pl.when(b == pl.num_programs(0) - 1)
    def _():
        for c in late:
            c.wait()
        rows = ant_ref.shape[0] // 2
        core = at_ref[0] // 2
        for ref, half in ((send_ref, 1 - core), (keep_ref, core)):
            at = pl.ds(pl.multiple_of(half * rows, rows), rows)
            ref[:, : 3 * width] = mm(ant_ref[at, :], all_ref[...]).astype(BF)
            ref[:, 3 * width :] = go_ref[at, :].astype(BF)
        turn = lax.broadcasted_iota(jnp.int32, (TILE, TILE), 0) + lax.broadcasted_iota(jnp.int32, (TILE, TILE), 1)
        turn = jnp.where(turn == TILE - 1, 1.0, 0.0).astype(BF)
        tiles = t_ref.shape[0]
        parts = split3(t_ref[...].reshape(tiles * TILE, TILE))
        back = mm(parts[0], turn) + mm(parts[1], turn) + mm(parts[2], turn)
        diag = []
        for t in range(tiles):
            x = jnp.concatenate([back[TILE * t : TILE * (t + 1)], jnp.zeros((TILE, TILE), F32)], axis=1)
            x = pltpu.roll(x, 0, 1, stride=1, stride_axis=0)
            diag.append(jnp.sum(x, axis=0, keepdims=True))
        rows = [jnp.concatenate(diag[3 * h : 3 * h + 3], axis=1) for h in range(heads)]
        rows.append(jnp.zeros((16 - heads, rows[0].shape[1]), F32))
        near = [mm(part, hot_ref[...]) for part in split3(jnp.concatenate(rows, axis=0))]
        lane = lax.broadcasted_iota(jnp.int32, (1, TILE), 1)
        for h in range(heads):
            one = near[0][h : h + 1] + near[1][h : h + 1] + near[2][h : h + 1]
            for side, bucket in ((0, BUCKETS // 2 - 1), (1, BUCKETS - 1)):
                far = jnp.sum(jnp.sum(fsum_ref[2 * h + side], axis=0, keepdims=True), axis=1, keepdims=True)
                one = one + jnp.where(lane == bucket, far, 0.0)
            table_ref[h : h + 1, :] = one


def attn_bwd(lens, at, q, qt, k, v, dctx, dctxt, ctxt, lse, nb, tf, hot, ant, go):
    n, seq, width = q.shape
    d = ant.shape[0]
    heads = width // 64
    tok = sds((n, seq, width), BF)
    flat = [
        sds((d // 2, 4 * width), BF),
        sds((d // 2, 4 * width), BF),
        sds((8, TILE), F32),
    ]
    ins = [q, qt, k, v, dctx, dctxt, ctxt, lse]
    return pl.pallas_call(
        attn_bwd_kernel,
        grid=(n,),
        in_specs=[SMEM_SPEC, SMEM_SPEC]
        + [row_spec(x.shape) for x in ins]
        + [const_spec(nb.shape), const_spec(tf.shape), const_spec(hot.shape), ANY, ANY],
        out_specs=[row_spec(q.shape)] * 3 + [out_const(o.shape) for o in flat],
        out_shape=[tok, tok, tok] + flat,
        scratch_shapes=[
            pltpu.VMEM((3 * heads, TILE, TILE), F32),
            pltpu.VMEM((2 * heads, 8, TILE), F32),
            pltpu.VMEM((2, seq, 2 * seq), BF),
            pltpu.VMEM((2, seq, 2 * seq), BF),
            pltpu.VMEM((n * seq, 3 * width), BF),
            pltpu.VMEM(ant.shape, BF),
            pltpu.VMEM(go.shape, F32),
            pltpu.SemaphoreType.DMA((2,)),
        ],
        compiler_params=params(),
        cost_estimate=cost(20),
        name="attn_bwd",
    )(lens, at, *ins, nb, tf, hot, ant, go)


def gelu_parts(v):
    v2 = v * v
    th = jnp.tanh(v * (GELU_A + (GELU_A * GELU_B) * v2))
    hh = 0.5 + 0.5 * th
    slope = hh + (v * (0.5 - 0.5 * th * th)) * (GELU_A + (3.0 * GELU_A * GELU_B) * v2)
    return v * hh, slope


def ffn_fwd_kernel(lens, at_ref, fin_ref, rs_ref, wi_ref, wu_ref, p0, p1, p2, p3, *refs):
    (act_ref, gp_ref, actb_ref, gpb_ref, asum_ref, rsum_ref) = refs[:6]
    (wib_ref, wu_buf, v_ref, sem1, sem2) = refs[6:]
    b = pl.program_id(0)
    late = join_copies(at_ref[0], (p0, p1, p2, p3), wib_ref, sem1) + [pltpu.make_async_copy(wu_ref, wu_buf, sem2)]

    @pl.when(b == 0)
    def _():
        for c in late:
            c.start()

    fin = fin_ref[0]
    seq = fin.shape[0]
    half = wi_ref.shape[1]
    chunk = v_ref.shape[2]
    length = lens[b]
    vrow = (lax.broadcasted_iota(jnp.int32, (8, seq), 1) < length).astype(F32).astype(BF)
    vcol = (lax.broadcasted_iota(jnp.int32, (seq, TILE), 0) < length).astype(F32)[:, :1]
    spot = lambda c: slice(c * chunk, (c + 1) * chunk)
    parts = [(w, a, g, c) for w, a, g in ((wi_ref, act_ref, gp_ref), (wib_ref, actb_ref, gpb_ref)) for c in range(half // chunk)]

    def project(t):
        w, _, _, c = parts[t]
        v_ref[t % 2] = mm(fin, w[:, spot(c)])

    project(0)
    for t, (_, a_ref, g_ref, c) in enumerate(parts):
        if t + 1 == half // chunk:

            @pl.when(b == 0)
            def _():
                for copy in late:
                    copy.wait()

        if t + 1 < len(parts):
            project(t + 1)
        for r in range(seq // TILE):
            rows = slice(TILE * r, TILE * (r + 1))
            act, slope = gelu_parts(v_ref[t % 2, rows, :])
            a_ref[0, rows, spot(c)] = act.astype(BF)
            g_ref[0, rows, spot(c)] = (slope * vcol[rows]).astype(BF)
        asum_ref[0, :, spot(t)] = mm(vrow, a_ref[0, :, spot(c)])[:1]
    own = asum_ref[0, :, :half]
    hi = own.astype(BF)
    lo = (own - hi.astype(F32)).astype(BF)
    two_rows = jnp.concatenate([hi.astype(F32), lo.astype(F32), jnp.zeros((14, half), F32)], axis=0).astype(BF)
    branch = mm(two_rows, wu_buf[...])
    rsum_ref[0] = rs_ref[0] + branch[0:1] + branch[1:2]


def ffn_fwd(lens, at, fin, rsum, wi, wu, packs):
    n, seq, d = fin.shape
    half = wi.shape[1]
    wide = sds((n, seq, half), BF)
    outs = [wide, wide, wide, wide, sds((n, 1, 2 * half), F32), sds((n, 1, d), F32)]
    return pl.pallas_call(
        ffn_fwd_kernel,
        grid=(n,),
        in_specs=[SMEM_SPEC, SMEM_SPEC, row_spec(fin.shape), row_spec(rsum.shape), const_spec(wi.shape)] + [ANY] * 5,
        out_specs=[row_spec(o.shape) for o in outs],
        out_shape=outs,
        scratch_shapes=[
            pltpu.VMEM(wi.shape, BF),
            pltpu.VMEM(wu.shape, BF),
            pltpu.VMEM((2, seq, 512), F32),
            pltpu.SemaphoreType.DMA((4,)),
            pltpu.SemaphoreType.DMA,
        ],
        compiler_params=params(),
        cost_estimate=cost(16),
        name="ffn_fwd",
    )(lens, at, fin, rsum, wi, wu, *packs)


def pool_kernel(lens, at_ref, asum_ref, rs_ref, p0, p1, out_ref, wb_ref, sem):
    run_copies(join_copies(at_ref[0], (p0, p1), wb_ref, sem))
    n = asum_ref.shape[0]
    half = wb_ref.shape[0]
    rows = [asum_ref[i, :, half:] for i in range(n)]
    hi = [r.astype(BF) for r in rows]
    lo = [(r - h.astype(F32)).astype(BF) for r, h in zip(rows, hi)]
    pad = jnp.zeros((16 - 2 * n, half), F32)
    br = mm(jnp.concatenate([t.astype(F32) for t in hi + lo] + [pad], axis=0).astype(BF), wb_ref[...])
    for i in range(n):
        total = rs_ref[i] + br[i : i + 1] + br[n + i : n + i + 1]
        out_ref[i : i + 1, :] = total / lens[i].astype(F32)


def pool(lens, at, asum, rsum, packs):
    n, _, d = rsum.shape
    half = asum.shape[2] // 2
    vm = pl.BlockSpec(memory_space=pltpu.VMEM)
    return pl.pallas_call(
        pool_kernel,
        in_specs=[SMEM_SPEC, SMEM_SPEC, vm, vm] + [ANY] * 2,
        out_specs=vm,
        out_shape=sds((8, d), F32),
        scratch_shapes=[pltpu.VMEM((half, d), BF), pltpu.SemaphoreType.DMA((4,))],
        compiler_params=params(),
        cost_estimate=cost(4),
        name="pool",
    )(lens, at, asum, rsum, *packs)


def loss_kernel(me_ref, at_ref, lens, pool_ref, q_ref, wp_ref, fint_hbm, gp_hbm, fn0, fn1, wi_hbm, wu_hbm, p0, p1, *refs):
    (loss_ref, row_ref, g_ref, drow_ref, demb_ref, send_ref, keep_ref) = refs[:7]
    (wu_ref, wb_ref, fint_ref, gp_ref, fnb_ref, wi_ref, ft_ref, gn_ref, v_ref, d_ref, dn_ref, sem, sem2) = refs[7:]
    copies = join_copies(at_ref[0], (p0, p1), wb_ref, sem)
    moves = [(wu_hbm, wu_ref), (wi_hbm, wi_ref), (gp_hbm, gp_ref), (fint_hbm, fint_ref)]
    moves += [(f, fnb_ref.at[pl.ds(i, 1)]) for i, f in enumerate((fn0, fn1))]
    loads = [pltpu.make_async_copy(a, b, sem2.at[i]) for i, (a, b) in enumerate(moves)]
    for c in [loads[0]] + copies + loads[1:]:
        c.start()
    d = wp_ref.shape[0]
    count = pool_ref.shape[0]
    pooled = pool_ref[...]
    qs = q_ref[:, :d]
    ints = q_ref[:, d : d + TILE].astype(F32)
    pos = (ints[:, 0:1] * 256.0 + ints[:, 1:2]).astype(jnp.int32)
    length = ints[:, 2:3] * 256.0 + ints[:, 3:4]
    wp = wp_ref[...]
    emb = mm(pooled, wp)
    inv = lax.rsqrt(jnp.sum(emb * emb, axis=-1, keepdims=True) + EPS)
    unit = (emb * inv).astype(BF)
    logits = mm(qs, unit, NT) / SHARPNESS
    top = jnp.max(logits, axis=-1, keepdims=True)
    total = top + jnp.log(jnp.sum(jnp.exp(logits - top), axis=-1, keepdims=True))
    hit = lax.broadcasted_iota(jnp.int32, (count, count), 1) == pos
    loss = total - jnp.sum(jnp.where(hit, logits, 0.0), axis=1, keepdims=True)
    d_logits = (LOSS_SCALE * (jnp.exp(logits - total) - jnp.where(hit, 1.0, 0.0))).astype(BF)
    d_unit = mm(d_logits, qs, TN) / SHARPNESS
    along = jnp.sum(emb * d_unit, axis=-1, keepdims=True)
    d_emb = (inv * d_unit - inv * inv * inv * along * emb).astype(BF)
    demb_ref[...] = d_emb
    rows = mm(d_emb, wp, NT) / length
    drow_ref[...] = rows.astype(BF)
    index = lax.broadcasted_iota(jnp.int32, (count, 1), 0)
    pick = lambda t, i: jnp.sum(jnp.where(index == i, t, 0.0), axis=0, keepdims=True)
    n, seq, half = gp_ref.shape
    own = [pick(rows, me_ref[i]) for i in range(n)]
    near = [pick(rows, me_ref[n + i]) for i in range(n)]
    lost = jnp.broadcast_to(loss, (count, TILE))
    pad = jnp.zeros((8 - n, d), F32)
    row_ref[...] = jnp.concatenate(own + [pad], axis=0)
    loss_ref[...] = jnp.concatenate([pick(lost, me_ref[i]) for i in range(n)] + [pad[:, :TILE]], axis=0)
    four = jnp.concatenate(own + near + [jnp.zeros((16 - 2 * n, d), F32)], axis=0).astype(BF)
    loads[0].wait()
    ga = mm(four, wu_ref[...], NT)
    gn_ref[...] = ga[:8]
    for c in copies:
        c.wait()
    g_ref[:, :half] = ga[:8]
    g_ref[:, half:] = mm(four, wb_ref[...], NT)[:8]
    for c in loads[1:]:
        c.wait()

    for i in range(n):
        ft_ref[:, seq * i : seq * (i + 1)] = jnp.transpose(fnb_ref[i])
    chunk = v_ref.shape[3]
    steps = half // chunk
    spot = lambda c: slice(c * chunk, (c + 1) * chunk)

    def project(c):
        for i in range(n):
            v_ref[c % 2, i] = mm(fnb_ref[i], wi_ref[:, spot(c)])

    def scale(c):
        for i in range(n):
            at = slice(seq * i, seq * (i + 1))
            d_ref[c % 2, at, :] = (gp_ref[i, :, spot(c)].astype(F32) * gn_ref[i : i + 1, spot(c)]).astype(BF)
            for r in range(seq // TILE):
                part = slice(TILE * r, TILE * (r + 1))
                valid = lax.broadcasted_iota(jnp.int32, (TILE, TILE), 0) + TILE * r < lens[n + i]
                slope = gelu_parts(v_ref[c % 2, i, part, :])[1]
                one = slope * valid.astype(F32)[:, :1] * gn_ref[n + i : n + i + 1, spot(c)]
                dn_ref[c % 2, seq * i + TILE * r : seq * i + TILE * (r + 1), :] = one.astype(BF)

    rows2 = d // 2
    core = at_ref[0] // 2
    project(0)
    scale(0)
    for c in range(steps):
        if c + 1 < steps:
            project(c + 1)
        for ref, side in ((send_ref, 1 - core), (keep_ref, core)):
            at = pl.ds(pl.multiple_of(side * rows2, rows2), rows2)
            one = mm(fint_ref[at, :], d_ref[c % 2]) + mm(ft_ref[at, :], dn_ref[c % 2])
            ref[:, spot(c)] = one.astype(BF)
        if c + 1 < steps:
            scale(c + 1)


def loss_all(me, at, lens4, pooled, queries, wp, fint, gp, fin_nb, wi, wu, packs):
    half, d = wu.shape
    n, seq, _ = gp.shape
    count = pooled.shape[0]
    chunk = 512
    vm = pl.BlockSpec(memory_space=pltpu.VMEM)
    return pl.pallas_call(
        loss_kernel,
        in_specs=[SMEM_SPEC] * 3 + [vm] * 3 + [ANY] * 8,
        out_specs=[vm] * 7,
        out_shape=[
            sds((8, TILE), F32),
            sds((8, d), F32),
            sds((8, 2 * half), F32),
            sds((count, d), BF),
            sds((count, d), BF),
            sds((d // 2, half), BF),
            sds((d // 2, half), BF),
        ],
        scratch_shapes=[
            pltpu.VMEM(wu.shape, BF),
            pltpu.VMEM(wu.shape, BF),
            pltpu.VMEM(fint.shape, BF),
            pltpu.VMEM(gp.shape, BF),
            pltpu.VMEM((n, seq, d), BF),
            pltpu.VMEM(wi.shape, BF),
            pltpu.VMEM(fint.shape, BF),
            pltpu.VMEM((8, half), F32),
            pltpu.VMEM((2, n, seq, chunk), F32),
            pltpu.VMEM((2, n * seq, chunk), BF),
            pltpu.VMEM((2, n * seq, chunk), BF),
            pltpu.SemaphoreType.DMA((4,)),
            pltpu.SemaphoreType.DMA((6,)),
        ],
        compiler_params=params(),
        cost_estimate=cost(17),
        name="loss_inner",
    )(me, at, lens4, pooled, queries, wp, fint, gp, *fin_nb, wi, wu, *packs)


def ffn_bwd_kernel(lens, at_ref, res_ref, gpa_ref, gpb_ref, g_ref, row_ref, gain_ref, wi_ref, wo_ref, cta_ref, ctb_ref, *refs):
    packs0, packs1 = refs[:2], refs[2:6]
    (dres_ref, dca_ref, dta_ref, dcb_ref, dtb_ref, goa_ref, gob_ref) = refs[6:13]
    (wib_ref, wob_ref, cta_buf, ctb_buf, d_ref, da_ref, sem0, sem1, sem2) = refs[13:]
    b = pl.program_id(0)
    n = pl.num_programs(0)
    res = res_ref[0]
    seq, d = res.shape
    half = wi_ref.shape[1]
    chunk = d_ref.shape[2]
    copies0 = join_copies(at_ref[0], packs0, wob_ref, sem0)
    copies1 = join_copies(at_ref[0], packs1, wib_ref, sem1)
    late = [pltpu.make_async_copy(cta_ref, cta_buf, sem2.at[0]), pltpu.make_async_copy(ctb_ref, ctb_buf, sem2.at[1])]

    @pl.when(b == 0)
    def _():
        for c in copies1 + copies0 + late:
            c.start()
        for c in copies1 + copies0:
            c.wait()

    parts = [(gp, w, c) for gp, w in ((gpa_ref, wi_ref), (gpb_ref, wib_ref)) for c in range(half // chunk)]

    def scale(t):
        gp, _, c = parts[t]
        base = half if gp is gpb_ref else 0
        g = g_ref[pl.ds(b, 1), base + c * chunk : base + (c + 1) * chunk]
        d_ref[t % 2] = (gp[0, :, c * chunk : (c + 1) * chunk].astype(F32) * g).astype(BF)

    d_two = None
    scale(0)
    for t, (_, w, c) in enumerate(parts):
        if t + 1 < len(parts):
            scale(t + 1)
        one = mm(d_ref[t % 2], w[:, c * chunk : (c + 1) * chunk], NT)
        d_two = one if d_two is None else d_two + one
    inv = lax.rsqrt(jnp.mean(res * res, axis=-1, keepdims=True) + EPS)
    dr = d_two * res
    gain = gain_ref[...]
    along = jnp.sum(dr * gain, axis=-1, keepdims=True)
    valid = lax.broadcasted_iota(jnp.int32, (seq, TILE), 0) < lens[b]
    vcol = valid.astype(F32)[:, :1]
    d_res = vcol * row_ref[pl.ds(b, 1), :] + d_two * gain * inv - res * (inv * inv * inv * along / d)
    dres_ref[0] = d_res
    d_attn = d_res.astype(BF)
    da_ref[pl.ds(pl.multiple_of(b * seq, seq), seq), :] = d_attn
    for w, o_ref, t_ref in ((wo_ref, dca_ref, dta_ref), (wob_ref, dcb_ref, dtb_ref)):
        turned = mm(w[...], d_attn, NT).astype(BF)
        t_ref[0] = turned
        o_ref[0] = jnp.transpose(turned)

    @pl.when(b == n - 1)
    def _():
        for c in late:
            c.wait()
        rows = cta_buf.shape[1]
        for ct_ref, o_ref in ((cta_buf, goa_ref), (ctb_buf, gob_ref)):
            total = None
            for i in range(cta_buf.shape[0]):
                one = mm(ct_ref[i], da_ref[seq * i : seq * (i + 1), :])
                total = one if total is None else total + one
            o_ref[:rows, :] = total[:, :rows]
            o_ref[rows:, :] = total[:, rows:]


def ffn_bwd(lens, at, res, gpa, gpb, g, row, gain, wi, wo, cta, ctb, packs0, packs1):
    n, seq, d = res.shape
    width = wo.shape[0]
    outs = [sds((n, seq, d), F32)] + [sds((n, seq, width), BF), sds((n, width, seq), BF)] * 2
    flat = [sds((d, width), F32), sds((d, width), F32)]
    return pl.pallas_call(
        ffn_bwd_kernel,
        grid=(n,),
        in_specs=[SMEM_SPEC, SMEM_SPEC, row_spec(res.shape), row_spec(gpa.shape), row_spec(gpb.shape)]
        + [const_spec(g.shape), const_spec(row.shape), const_spec((1, d)), const_spec(wi.shape), const_spec(wo.shape)]
        + [ANY] * 8,
        out_specs=[row_spec(o.shape) for o in outs] + [out_const(o.shape) for o in flat],
        out_shape=outs + flat,
        scratch_shapes=[
            pltpu.VMEM(wi.shape, BF),
            pltpu.VMEM(wo.shape, BF),
            pltpu.VMEM(cta.shape, BF),
            pltpu.VMEM(ctb.shape, BF),
            pltpu.VMEM((2, seq, 512), BF),
            pltpu.VMEM((n * seq, d), BF),
            pltpu.SemaphoreType.DMA((4,)),
            pltpu.SemaphoreType.DMA((4,)),
            pltpu.SemaphoreType.DMA((2,)),
        ],
        compiler_params=params(),
        cost_estimate=cost(15),
        name="ffn_bwd",
    )(lens, at, res, gpa, gpb, g, row, gain.reshape(1, d), wi, wo, cta, ctb, *packs0, *packs1)


def input_kernel(at_ref, x_ref, dres_ref, gain_ref, qa, ka, va, qb, kb, vb, wq, wk, wv, p0, p1, p2, p3, out_ref, w_ref, sem):
    @pl.when(pl.program_id(0) == 0)
    def _():
        run_copies(join_copies(at_ref[0], (p0, p1, p2, p3), w_ref, sem))

    width = wq.shape[1]
    d_one = mm(qa[0], wq[...], NT) + mm(ka[0], wk[...], NT) + mm(va[0], wv[...], NT)
    for i, t in enumerate((qb, kb, vb)):
        d_one = d_one + mm(t[0], w_ref[:, width * i : width * (i + 1)], NT)
    x = x_ref[0].astype(F32)
    inv = lax.rsqrt(jnp.mean(x * x, axis=-1, keepdims=True) + EPS)
    dx = d_one * x
    gain = gain_ref[...]
    along = jnp.sum(dx * gain, axis=-1, keepdims=True)
    out_ref[0] = dres_ref[0] + d_one * gain * inv - x * (inv * inv * inv * along / x.shape[1])


def input_part(at, x, dres, gain, toks, wq, wk, wv, packs):
    n, seq, d = x.shape
    width = wq.shape[1]
    return pl.pallas_call(
        input_kernel,
        grid=(n,),
        in_specs=[SMEM_SPEC, row_spec(x.shape), row_spec(dres.shape), const_spec((1, d))]
        + [row_spec(toks[0].shape)] * 6
        + [const_spec(wq.shape)] * 3
        + [ANY] * 4,
        out_specs=row_spec(x.shape),
        out_shape=sds(x.shape, F32),
        scratch_shapes=[pltpu.VMEM((d, 3 * width), BF), pltpu.SemaphoreType.DMA((4,))],
        compiler_params=params(),
        cost_estimate=cost(12),
        name="input_part",
    )(at, x, dres, gain.reshape(1, d), *toks, wq, wk, wv, *packs)


def layer_kernel(at_ref, res_ref, aa_ref, ab_ref, w_ref, p0, p1, out_ref, wb_ref, sem):
    @pl.when(pl.program_id(0) == 0)
    def _():
        run_copies(join_copies(at_ref[0], (p0, p1), wb_ref, sem))

    out_ref[0] = (res_ref[0] + mm(aa_ref[0], w_ref[...]) + mm(ab_ref[0], wb_ref[...])).astype(BF)


def layer_part(at, res, act_a, act_b, wu, packs):
    n, seq, d = res.shape
    return pl.pallas_call(
        layer_kernel,
        grid=(n,),
        in_specs=[SMEM_SPEC, row_spec(res.shape), row_spec(act_a.shape), row_spec(act_b.shape), const_spec(wu.shape)]
        + [ANY] * 2,
        out_specs=row_spec(res.shape),
        out_shape=sds(res.shape, BF),
        scratch_shapes=[pltpu.VMEM(wu.shape, BF), pltpu.SemaphoreType.DMA((4,))],
        compiler_params=params(),
        cost_estimate=cost(12),
        name="layer_part",
    )(at, res, act_a, act_b, wu, *packs)


def gain_row(prod):
    ones = jnp.ones((16, prod.shape[1]), BF)
    return sum(mm(ones, part, NT)[:1] for part in split3(prod))


def inner_done_kernel(at_ref, own_ref, near_ref, w_ref, out_ref, gain_ref):
    rows = own_ref.shape[0]
    core = at_ref[0] // 2
    halves = [own_ref[...].astype(F32), near_ref[...].astype(F32)]
    for half in range(2):
        one = jnp.where(core == half, halves[0], halves[1])
        at = slice(rows * half, rows * (half + 1))
        out_ref[at, :] = one
        gain_ref[:, at] = jnp.broadcast_to(gain_row(one * w_ref[at, :].astype(F32)), (8, rows))


def inner_done(at, own, near, w):
    d, half = w.shape
    chunk = 512
    cols = lambda r: pl.BlockSpec((r, chunk), lambda c: (0, c))
    return pl.pallas_call(
        inner_done_kernel,
        grid=(half // chunk,),
        in_specs=[SMEM_SPEC, cols(d // 2), cols(d // 2), cols(d)],
        out_specs=[cols(d), pl.BlockSpec((8, d), lambda c: (c, 0))],
        out_shape=[sds((d, half), F32), sds((8 * (half // chunk), d), F32)],
        compiler_params=params(),
        cost_estimate=cost(5),
        name="inner_done",
    )(at, own, near, w)


def attn_done_kernel(at_ref, own_ref, near_ref, wq, wk, wv, q_ref, k_ref, v_ref, o_ref, gain_ref):
    rows = own_ref.shape[0]
    width = wq.shape[1]
    core = at_ref[0] // 2
    for half in range(2):
        at = slice(rows * half, rows * (half + 1))
        total = None
        for i, (w, out) in enumerate(((wq, q_ref), (wk, k_ref), (wv, v_ref), (None, o_ref))):
            cols = slice(width * i, width * (i + 1))
            one = jnp.where(core == half, own_ref[:, cols].astype(F32), near_ref[:, cols].astype(F32))
            if w is None:
                out[:, at] = one
            else:
                out[at, :] = one
                prod = one * w[at, :].astype(F32)
                total = prod if total is None else total + prod
        gain_ref[:, at] = jnp.broadcast_to(gain_row(total), (8, rows))


def attn_done(at, own, near, wq, wk, wv):
    d, width = wq.shape
    vm = pl.BlockSpec(memory_space=pltpu.VMEM)
    grad = sds((d, width), F32)
    return pl.pallas_call(
        attn_done_kernel,
        in_specs=[SMEM_SPEC] + [vm] * 5,
        out_specs=[vm] * 5,
        out_shape=[grad, grad, grad, sds((width, d), F32), sds((8, d), F32)],
        compiler_params=params(),
        cost_estimate=cost(5),
        name="attn_done",
    )(at, own, near, wq, wk, wv)


def after(*xs):
    return lax.optimization_barrier(xs)


def swap(x, axis, bit, size):
    return lax.ppermute(x, axis, [(i, i ^ bit) for i in range(size)])


class Place:
    def __init__(self, chips, tensor):
        self.chips, self.tensor = chips, tensor
        self.chip = lax.axis_index("chip")
        self.core = lax.axis_index("core")
        self.ti = lax.axis_index("tensor")

    def across(self, x):
        return swap(x, "tensor", 1, self.tensor)

    def core_swap(self, x):
        return swap(x, "core", 1, 2)

    def share(self, x):
        return lax.all_to_all(x, ("chip", "core", "tensor"), 0, 0, tiled=True)

    def side(self, mine):
        return swap(mine, "chip", 1, self.chips)

    def spread(self, mine, side):
        return [mine, side, self.core_swap(mine), self.core_swap(side)]

    def exchange(self, x):
        rows, width = x.shape
        return lax.all_to_all(x.reshape(self.chips, rows // self.chips, width), "chip", 0, 0, tiled=True)

    def add(self, got):
        return jnp.sum(got.astype(F32), axis=0).astype(BF)

    def gather(self, x):
        got = lax.all_to_all(jnp.broadcast_to(x[None], (self.chips,) + x.shape), "chip", 0, 0, tiled=True)
        return got.reshape(-1, x.shape[1])

    def total(self, x):
        x = x + self.core_swap(x)
        for i in range(self.chips.bit_length() - 1):
            x = x + swap(x, "chip", 1 << i, self.chips)
        return x


def body(
    mesh_shape,
    hidden_in,
    lengths,
    queries,
    positives,
    gain_attn,
    w_query,
    w_key,
    w_value,
    w_out,
    rel_table,
    gain_ffn,
    w_inner,
    w_outer,
    w_proj,
):
    pc = Place(mesh_shape["chip"], mesh_shape["tensor"])
    n, seq, d = hidden_in.shape
    half = w_inner.shape[1]
    width = w_query.shape[1]
    buckets = rel_table.shape[0]
    lens = lax.dynamic_slice_in_dim(lengths, pc.ti * n, n, 0)
    near_lens = lax.dynamic_slice_in_dim(lengths, (1 - pc.ti) * n, n, 0)
    lens4 = jnp.concatenate([lens, near_lens])
    at = (2 * pc.core + (pc.chip & 1)).reshape(1)
    devices = pc.chips * 2 * pc.tensor
    hot_t = jnp.asarray(np.pad(diag_onehot(buckets, False).T, ((0, TILE - buckets), (0, 0))), BF)
    hot_back = jnp.asarray(np.pad(diag_onehot(buckets, True), ((0, 0), (0, TILE - buckets))), BF)

    turned = rel_table.T
    packs = pack_weights(at, turned, w_query, w_key, w_value, w_out, w_inner, w_outer)
    y_attn, y_out, y_inner, y_outer = [pc.across(p) for p in packs]

    qf = queries.astype(F32)
    q_unit = (qf * lax.rsqrt(jnp.sum(qf * qf, axis=-1, keepdims=True) + EPS)).astype(BF)
    ints = jnp.stack([positives // 256, positives % 256, lens // 256, lens % 256], axis=1)
    ints = jnp.pad(ints.astype(BF), ((0, 0), (0, TILE - 4)))
    q_all = jnp.concatenate([q_unit, ints], axis=1)

    an, ant, q_a, qt_a, k_a, v_a, ctx_a, ctxt_a, lse_a, nb_a, tf_a = attn_own(
        lens, hidden_in, gain_attn, w_query, w_key, w_value, turned, hot_t
    )
    y_attn, an, q_all = after(y_attn, an, q_all)
    x_attn = pc.side(y_attn)
    q_all = pc.share(jnp.broadcast_to(q_all[None], (devices,) + q_all.shape))
    x_attn, y_out, q_all = after(x_attn, y_out, q_all)
    p_attn = pc.spread(y_attn, x_attn)
    p_out = [y_out, pc.core_swap(y_out)]
    y_inner, an = after(y_inner, an)
    x_inner = pc.side(y_inner)
    q_b, qt_b, k_b, v_b, ctx_b, ctxt_b, lse_b, nb_b, tf_b, res, fin, fint, rsum = attn_other(
        lens, at, an, hot_t, hidden_in, ctx_a, w_out, gain_ffn, p_attn, p_out
    )
    y_inner, x_inner, fin = after(y_inner, x_inner, fin)
    p_inner = pc.spread(y_inner, x_inner)
    fin_nb = [pc.across(fin[i : i + 1]) for i in range(n)]
    act_a, gp_a, act_b, gp_b, asum, rsum = ffn_fwd(lens, at, fin, rsum, w_inner, w_outer, p_inner)
    y_outer, asum, fin_nb[0] = after(y_outer, asum, fin_nb[0])
    p_outer = [y_outer, pc.core_swap(y_outer)]
    pooled = pool(lens, at, asum, rsum, p_outer)[:n].astype(BF)

    sums_a, sums_b = asum[:, 0, :half].astype(BF), asum[:, 0, half:].astype(BF)
    sums = jnp.where(pc.ti > 0, jnp.stack([sums_b, sums_a]), jnp.stack([sums_a, sums_b]))
    msg = jnp.concatenate([jnp.broadcast_to(pooled[None], (2,) + pooled.shape), sums], axis=2)
    msg = jnp.broadcast_to(msg[None], (2 * pc.chips,) + msg.shape).reshape((devices,) + msg.shape[1:])
    got = pc.share(msg).reshape(devices * n, -1)
    pooled = got[:, :d]
    base = (2 * pc.chip + pc.core) * pc.tensor * n
    me = jnp.stack([base + pc.ti * n, base + pc.ti * n + 1, base + (1 - pc.ti) * n, base + (1 - pc.ti) * n + 1])
    loss8, row8, g8, d_rows, d_emb, gi_send, gi_keep = loss_all(
        me, at, lens4, pooled, q_all.reshape(devices * n, -1), w_proj, fint, gp_a, fin_nb, w_inner, w_outer, p_outer
    )
    query_loss = loss8[:n, 0]

    inner_half, gp_a = after(gi_keep + pc.core_swap(gi_send), gp_a)
    inner_parts = pc.exchange(inner_half)
    d_res, dctx_a, dctxt_a, dctx_b, dctxt_b, go_a, go_b = ffn_bwd(
        lens, at, res, gp_a, gp_b, g8, row8, gain_ffn, w_inner, w_out, ctxt_a, ctxt_b, p_out, p_inner
    )
    dq_b, dk_b, dv_b, send_b, keep_b, table_b = attn_bwd(
        lens, at, q_b, qt_b, k_b, v_b, dctx_b, dctxt_b, ctxt_b, lse_b, nb_b, tf_b, hot_back, ant, go_b
    )
    half_b, dctx_a = after(keep_b + pc.core_swap(send_b), dctx_a)
    far_part = pc.across(half_b)
    inner_part, dctx_a = after(pc.add(inner_parts), dctx_a)
    dq_a, dk_a, dv_a, send_a, keep_a, table_a = attn_bwd(
        lens, at, q_a, qt_a, k_a, v_a, dctx_a, dctxt_a, ctxt_a, lse_a, nb_a, tf_a, hot_back, ant, go_a
    )
    inner_all, far_part, send_a = after(pc.gather(inner_part), far_part, send_a)
    parts = pc.exchange(keep_a + far_part + pc.core_swap(send_a))
    toks = (dq_a, dk_a, dv_a, dq_b, dk_b, dv_b)
    input_grad = input_part(at, hidden_in, d_res, gain_attn, toks, w_query, w_key, w_value, p_attn)

    table_sum = pc.total(table_a + pc.across(table_b))

    layer = layer_part(at, res, act_a, act_b, w_outer, p_outer)
    parts, input_grad, layer, inner_all = after(parts, input_grad, layer, inner_all)
    attn_all = pc.gather(pc.add(parts))
    inner_sum, gain_ffn_part = inner_done(at, inner_all, pc.core_swap(inner_all), w_inner)
    gain_ffn_part = jnp.sum(gain_ffn_part[::8], axis=0)
    gain_ffn_grad = (gain_ffn_part + pc.across(gain_ffn_part)) / gain_ffn
    proj_grad = mm(pooled, d_emb, TN)
    outer_grad = mm(got[:, d:], d_rows, TN)
    attn_all, proj_grad, outer_grad, gain_ffn_grad, inner_sum, table_sum = after(
        attn_all, proj_grad, outer_grad, gain_ffn_grad, inner_sum, table_sum
    )
    q_grad, k_grad, v_grad, out_grad, gain_attn_part = attn_done(
        at, attn_all, pc.core_swap(attn_all), w_query, w_key, w_value
    )
    gain_attn_part = gain_attn_part[0]
    gain_attn_grad = (gain_attn_part + pc.across(gain_attn_part)) / gain_attn
    return (
        layer,
        query_loss,
        input_grad,
        gain_attn_grad,
        q_grad,
        k_grad,
        v_grad,
        out_grad,
        table_sum[: rel_table.shape[1], :buckets].T,
        gain_ffn_grad,
        inner_sum,
        outer_grad,
        proj_grad,
    )


def solution(mesh):
    dp, tensor = mesh.shape["dp"], mesh.shape["tensor"]
    fine = jax.sharding.Mesh(mesh.devices.reshape(dp // 2, 2, tensor), ("chip", "core", "tensor"))
    rows = ("chip", "core")
    both = rows + ("tensor",)
    return jax.shard_map(
        functools.partial(body, dict(fine.shape)),
        mesh=fine,
        in_specs=(
            P(both, None, None),
            P(rows),
            P(both, None),
            P(both),
            P(),
            P(None, "tensor"),
            P(None, "tensor"),
            P(None, "tensor"),
            P("tensor", None),
            P(None, "tensor"),
            P(),
            P(None, "tensor"),
            P("tensor", None),
            P(),
        ),
        out_specs=(
            P(both, None, None),
            P(both),
            P(both, None, None),
            P(),
            P(None, "tensor"),
            P(None, "tensor"),
            P(None, "tensor"),
            P("tensor", None),
            P(None, "tensor"),
            P(),
            P(None, "tensor"),
            P("tensor", None),
            P(),
        ),
        check_vma=False,
    )
```

```python
import functools

import numpy as np

import jax
import jax.numpy as jnp
from jax import lax
from jax.experimental import pallas as pl
from jax.experimental.pallas import tpu as pltpu
from jax.sharding import PartitionSpec as P

LARGE_STEPS = (12, 16, 23, 32, 46, 64, 91)
SHARPNESS = 0.02
LOSS_SCALE = 256.0
EPS = 1e-06
NEG = -1e30
BF = jnp.bfloat16
F32 = jnp.float32
TILE = 128
BUCKETS = 32
GELU_A = 0.7978845608028654
GELU_B = 0.044715
MIB = 1024 * 1024

NN = (((1,), (0,)), ((), ()))
NT = (((1,), (1,)), ((), ()))
TN = (((0,), (0,)), ((), ()))


def mm(a, b, dims=NN):
    return lax.dot_general(a, b, dims, preferred_element_type=F32)


def bucket_of(r):
    a = np.abs(r)
    far = 8 + sum((a >= t).astype(np.int32) for t in LARGE_STEPS)
    return np.where(r > 0, 16, 0) + np.where(a < 8, a, far)


def diag_onehot(buckets, back):
    lane = np.arange(2 * TILE)
    at = lane - TILE + 1 if back else TILE - 1 - lane
    idx = np.concatenate([bucket_of(TILE * d + at) for d in (-1, 0, 1)])
    hot = (idx[:, None] == np.arange(buckets)[None, :]).astype(np.float32)
    hot[2 * TILE - 1 :: 2 * TILE] = 0.0
    return hot


def params(**kw):
    return pltpu.CompilerParams(vmem_limit_bytes=60 * MIB, **kw)


def cost(us):
    return pl.CostEstimate(flops=0, bytes_accessed=int(us * 3.6e6), transcendentals=0)

ANY = pl.BlockSpec(memory_space=pl.ANY)
SMEM_SPEC = pl.BlockSpec(memory_space=pltpu.SMEM)


def const_spec(shape):
    zeros = (0,) * len(shape)
    return pl.BlockSpec(tuple(shape), lambda b: zeros, pipeline_mode=pl.Buffered(1))


def out_const(shape):
    zeros = (0,) * len(shape)
    return pl.BlockSpec(tuple(shape), lambda b: zeros)


def row_spec(shape):
    tail = (0,) * (len(shape) - 1)
    return pl.BlockSpec((1,) + tuple(shape[1:]), lambda b: (b,) + tail)


def sds(shape, dtype):
    return jax.ShapeDtypeStruct(tuple(shape), dtype)


def split3(t):
    hi = t.astype(BF)
    rest = t - hi.astype(F32)
    mid = rest.astype(BF)
    return hi, mid, (rest - mid.astype(F32)).astype(BF)


def run_copies(copies):
    for c in copies:
        c.start()
    for c in copies:
        c.wait()


def out_pieces(width, d):
    rows, tall = width // 4, width // 6
    rest = rows - tall
    out = [((0, tall, 0, d), (0, tall, 0, d))]
    for i in range(2):
        out.append(((tall, rest, i * width, width), (i * rest, rest, d, width)))
    return out


def pack_kernel(at_ref, tab_ref, wq, wk, wv, wo, wi, wu, s0, s1, s2, sem):
    at = at_ref[0]
    d, width = wq.shape
    rows = d // 4

    def part(w, dst, i):
        count = w.shape[0] // 4
        src = w.at[pl.ds(pl.multiple_of(at * count, count), count)]
        return pltpu.make_async_copy(src, dst, sem.at[i])

    copies = [part(w, s0.at[pl.ds(0, rows), width * i : width * (i + 1)], i) for i, w in enumerate((wq, wk, wv))]
    copies += [part(wi, s1, 3), part(wu, s2, 4)]
    for i, (a, b) in enumerate(out_pieces(width, d)):
        src = wo.at[pl.ds(pl.multiple_of(at * (width // 4) + a[0], 32), a[1]), a[2] : a[2] + a[3]]
        dst = s0.at[pl.ds(rows + 16 + b[0], b[1]), b[2] : b[2] + b[3]]
        copies.append(pltpu.make_async_copy(src, dst, sem.at[5 + i]))
    for c in copies:
        c.start()
    s0[rows : rows + 16, :] = jnp.zeros((16, s0.shape[1]), BF)
    heads, buckets = tab_ref.shape
    for k, t in enumerate(split3(tab_ref[...])):
        s0[rows : rows + heads, TILE * k : TILE * k + buckets] = t
    for c in copies:
        c.wait()


def pack_weights(at, table, wq, wk, wv, wo, wi, wu):
    d, half = wi.shape
    width = wq.shape[1]
    vm = pl.BlockSpec(memory_space=pltpu.VMEM)
    return pl.pallas_call(
        pack_kernel,
        in_specs=[SMEM_SPEC, vm] + [ANY] * 6,
        out_specs=[vm] * 3,
        out_shape=[
            sds((d // 4 + 16 + width // 6, 3 * width), BF),
            sds((d // 4, half), BF),
            sds((half // 4, d), BF),
        ],
        scratch_shapes=[pltpu.SemaphoreType.DMA((8,))],
        compiler_params=params(),
        cost_estimate=cost(3),
        name="pack_weights",
    )(at, table, wq, wk, wv, wo, wi, wu)


def quarter_spots(at):
    core, xb = at // 2, at % 2
    return [at, 2 * core + 1 - xb, 2 * (1 - core) + xb, 2 * (1 - core) + 1 - xb]


def out_copies(at, packs, dst, sem):
    width, d = dst.shape
    base = d // 4 + 16
    out = []
    for i, (p, s) in enumerate(zip(packs, quarter_spots(at))):
        for j, (a, b) in enumerate(out_pieces(width, d)):
            src = p.at[pl.ds(base + b[0], b[1]), b[2] : b[2] + b[3]]
            to = dst.at[pl.ds(pl.multiple_of(s * (width // 4) + a[0], 32), a[1]), a[2] : a[2] + a[3]]
            out.append(pltpu.make_async_copy(src, to, sem.at[3 * i + j]))
    return out


def join_copies(at, packs, dst, sem):
    rows = dst.shape[0] // 4
    out = []
    for i, (p, s) in enumerate(zip(packs, quarter_spots(at))):
        to = dst.at[pl.ds(pl.multiple_of(s * rows, rows), rows)]
        out.append(pltpu.make_async_copy(p.at[pl.ds(0, rows)], to, sem.at[i]))
    return out


EXTRA = 16


def key_extras(length, rows):
    row = lax.broadcasted_iota(jnp.int32, (rows, TILE), 0)
    lane = lax.broadcasted_iota(jnp.int32, (rows, TILE), 1) & 63
    blk = (lane - 1) & 3
    hot = (lane >= 1) & (lane < 13) & (blk == row // TILE)
    one = ((lane == 0) & (row >= length)) | hot | ((lane >= 13) & (lane < EXTRA))
    return jnp.where(one, 1.0, 0.0)


def far_rows(tf_ref, h, seq):
    row = lax.broadcasted_iota(jnp.int32, (EXTRA, seq), 0)
    diff = ((row - 1) & 3) - lax.broadcasted_iota(jnp.int32, (EXTRA, seq), 1) // TILE
    out = jnp.where(row == 0, NEG, 0.0)
    last, mid = BUCKETS - 1, BUCKETS // 2 - 1
    for k in range(3):
        mine = (row >= 1 + 4 * k) & (row < 5 + 4 * k)
        out = out + jnp.where(mine & (diff >= 2), tf_ref[k, h : h + 1, last : last + 1], 0.0)
        out = out + jnp.where(mine & (diff <= -2), tf_ref[k, h : h + 1, mid : mid + 1], 0.0)
    return out


def stack_rows(e, main, extra):
    pad = jnp.zeros((64 - extra.shape[0], extra.shape[1]), BF)
    return jnp.concatenate([main, extra, pad] if e == 0 else [extra, pad, main], axis=0)


def near_bias(s, nb_ref, h, ib):
    rows = []
    for bj in range(s.shape[0] // TILE):
        parts = []
        for t in range(2):
            piece = s[TILE * bj : TILE * (bj + 1), TILE * t : TILE * (t + 1)]
            d = bj - (2 * ib + t)
            parts.append(piece + nb_ref[3 * h + d + 1] if abs(d) <= 1 else piece)
        rows.append(jnp.concatenate(parts, axis=1))
    return rows


def set_bias(parts, hot_ref, tf_ref, nb_ref):
    for k in range(3):
        tf_ref[k] = parts[k].astype(F32)
    hot = hot_ref[...]
    bv = mm(parts[0], hot) + mm(parts[1], hot) + mm(parts[2], hot)
    for t in range(nb_ref.shape[0]):
        h, k = t // 3, t % 3
        v = jnp.broadcast_to(bv[h : h + 1, 2 * TILE * k : 2 * TILE * (k + 1)], (TILE, 2 * TILE))
        nb_ref[t] = pltpu.roll(v, TILE + 1, 1, stride=1, stride_axis=0)[:, :TILE]


def attn_rows(an, length, ws, outs, nb_ref, tf_ref, s_ref, p_ref):
    q_ref, qt_ref, k_ref, v_ref, ctx_ref, ctxt_ref, lse_ref = outs
    seq = an.shape[0]
    width = q_ref.shape[2]
    for ref, w in zip((q_ref, k_ref, v_ref), ws):
        ref[0] = mm(an, w[...]).astype(BF)
    kx = key_extras(length, seq)
    lane = lax.broadcasted_iota(jnp.int32, (seq, TILE), 1)
    blocks = [(h, ib) for h in range(width // 64) for ib in range(seq // 256)]
    keys, queries, values, tops, sums, rows = {}, {}, {}, {}, {}, {}

    def prepare(h):
        pair, e = h // 2, h % 2
        cols = slice(TILE * pair, TILE * (pair + 1))
        if e == 0:
            qt_ref[0, cols, :] = jnp.transpose(q_ref[0, :, cols])
            values[pair] = jnp.transpose(v_ref[0, :, cols])
        mine = lane < 64 if e == 0 else lane >= 64
        keys[h] = jnp.where(mine, k_ref[0, :, cols].astype(F32), kx).astype(BF)
        qt = qt_ref[0, 64 * h : 64 * (h + 1), :]
        queries[h] = stack_rows(e, qt, far_rows(tf_ref, h, seq).astype(BF))

    def start(t):
        h, ib = blocks[t]
        if ib == 0:
            prepare(h)
        s = mm(keys[h], queries[h][:, 256 * ib : 256 * (ib + 1)])
        return near_bias(s, nb_ref, h, ib)

    def score(t, bj, pieces):
        piece = pieces[bj]
        s_ref[t % 2, TILE * bj : TILE * (bj + 1), :] = piece
        m = jnp.max(piece.reshape(TILE // 8, 8, 256), axis=0)
        tops[t] = m if bj == 0 else jnp.maximum(tops[t], m)
        if bj == seq // TILE - 1:
            tops[t] = jnp.max(tops[t], axis=0, keepdims=True)

    def soft(t, bj):
        h, ib = blocks[t]
        at = slice(TILE * bj, TILE * (bj + 1))
        p = jnp.exp(s_ref[t % 2, at, :] - tops[t])
        one = jnp.sum(p.reshape(TILE // 8, 8, 256), axis=0)
        sums[t] = one if bj == 0 else sums[t] + one
        p_ref[h % 2, at, 256 * ib : 256 * (ib + 1)] = p.astype(BF)
        if bj == seq // TILE - 1:
            sums[t] = jnp.sum(sums[t], axis=0, keepdims=True)
            lse_ref[0, h : h + 1, 256 * ib : 256 * (ib + 1)] = tops[t] + jnp.log(sums[t])

    def combine(h):
        per = seq // 256
        total = jnp.concatenate([sums[per * h + i] for i in range(per)], axis=1)
        vt = values[h // 2][64 * (h % 2) : 64 * (h % 2 + 1), :]
        rows[h] = mm(vt, p_ref[h % 2]) * (1.0 / total)
        if h % 2 == 1:
            pair = h // 2
            cols = slice(TILE * pair, TILE * (pair + 1))
            ct = jnp.concatenate([rows[h - 1], rows[h]], axis=0).astype(BF)
            ctxt_ref[0, cols, :] = ct
            ctx_ref[0, :, cols] = jnp.transpose(ct)

    for t in range(len(blocks) + 1):
        if t < len(blocks):
            pieces = start(t)
            for bj in range(seq // TILE):
                score(t, bj, pieces)
        if t > 0:
            for bj in range(seq // TILE):
                soft(t - 1, bj)
            if blocks[t - 1][1] == seq // 256 - 1:
                combine(blocks[t - 1][0])


def attn_own_kernel(lens, x_ref, gain_ref, wq, wk, wv, tab_ref, hot_ref, an_ref, ant_ref, *refs):
    outs, (nb_ref, tf_ref, s_ref, p_ref) = refs[:7], refs[7:]
    b = pl.program_id(0)

    @pl.when(b == 0)
    def _():
        heads, buckets = tab_ref.shape
        wide = jnp.concatenate([tab_ref[...], jnp.zeros((heads, TILE - buckets), F32)], axis=1)
        wide = jnp.concatenate([wide, jnp.zeros((16 - heads, TILE), F32)], axis=0)
        set_bias(split3(wide), hot_ref, tf_ref, nb_ref)

    x = x_ref[0].astype(F32)
    inv = lax.rsqrt(jnp.mean(x * x, axis=-1, keepdims=True) + EPS)
    an = (x * inv * gain_ref[...]).astype(BF)
    an_ref[0] = an
    ant_ref[...] = jnp.transpose(an)
    attn_rows(an, lens[b], (wq, wk, wv), outs, nb_ref, tf_ref, s_ref, p_ref)


def attn_other_kernel(lens, at_ref, an_ref, hot_ref, x_ref, ca_ref, wo_ref, gain_ref, p0, p1, p2, p3, *refs):
    outs, (nb_ref, tf_ref, res_ref, fin_ref, fint_ref, rsum_ref, f0_ref, f1_ref) = list(refs[:6]), refs[6:14]
    (s_ref, p_ref, w_ref, tab_ref, wb_ref, c_ref, sem, sem1) = refs[14:]
    outs.insert(4, c_ref)
    b = pl.program_id(0)
    late = out_copies(at_ref[0], (p0, p1, p2, p3), wb_ref, sem1)

    @pl.when(b == 0)
    def _():
        rows = w_ref.shape[0] // 4
        copies = join_copies(at_ref[0], (p0, p1, p2, p3), w_ref, sem)
        copies.append(pltpu.make_async_copy(p0.at[pl.ds(rows, 16)], tab_ref, sem.at[4]))
        for c in copies + late:
            c.start()
        for c in copies:
            c.wait()
        parts = [tab_ref[:, TILE * k : TILE * (k + 1)] for k in range(3)]
        set_bias(parts, hot_ref, tf_ref, nb_ref)

    width = outs[0].shape[2]
    ws = [w_ref.at[:, width * k : width * (k + 1)] for k in range(3)]
    attn_rows(an_ref[0], lens[b], ws, outs, nb_ref, tf_ref, s_ref, p_ref)

    @pl.when(b == 0)
    def _():
        for c in late:
            c.wait()

    res = x_ref[0].astype(F32) + mm(ca_ref[0], wo_ref[...]) + mm(outs[4][0], wb_ref[...])
    res_ref[0] = res
    inv = lax.rsqrt(jnp.mean(res * res, axis=-1, keepdims=True) + EPS)
    fin = (res * inv * gain_ref[...]).astype(BF)
    fin_ref[0] = fin
    for i, f_ref in enumerate((f0_ref, f1_ref)):

        @pl.when(b == i)
        def _():
            f_ref[0] = fin

    vcol = (lax.broadcasted_iota(jnp.int32, (res.shape[0], TILE), 0) < lens[b]).astype(F32)[:, :1]
    fint_ref[...] = jnp.transpose((fin.astype(F32) * vcol).astype(BF))
    rsum_ref[0] = jnp.sum(res * vcol, axis=0, keepdims=True)


def attn_outs(n, seq, width):
    heads = width // 64
    tok, turned = sds((n, seq, width), BF), sds((n, width, seq), BF)
    rows = [tok, turned, tok, tok, tok, turned, sds((n, 8, seq), F32)]
    flat = [sds((3 * heads, TILE, TILE), F32), sds((3, 16, TILE), F32)]
    scratch = [pltpu.VMEM((2, seq, 256), F32), pltpu.VMEM((2, seq, seq), BF)]
    return rows + flat, [row_spec(o.shape) for o in rows] + [out_const(o.shape) for o in flat], scratch


def attn_own(lens, x, gain, wq, wk, wv, table, hot):
    n, seq, d = x.shape
    outs, specs, scratch = attn_outs(n, seq, wq.shape[1])
    return pl.pallas_call(
        attn_own_kernel,
        grid=(n,),
        in_specs=[SMEM_SPEC, row_spec(x.shape), const_spec((1, d))]
        + [const_spec(wq.shape)] * 3
        + [const_spec(table.shape), const_spec(hot.shape)],
        out_specs=[row_spec(x.shape), pl.BlockSpec((d, seq), lambda b: (0, b))] + specs,
        out_shape=[sds((n, seq, d), BF), sds((d, n * seq), BF)] + outs,
        scratch_shapes=scratch,
        compiler_params=params(),
        cost_estimate=cost(12),
        name="attn_own",
    )(lens, x, gain.reshape(1, d), wq, wk, wv, table, hot)


def attn_other(lens, at, an, hot, x, ctx_a, wo, gain, packs):
    n, seq, d = an.shape
    width = wo.shape[0]
    outs, specs, scratch = attn_outs(n, seq, width)
    del outs[4], specs[4]
    more = [sds((n, seq, d), F32), sds((n, seq, d), BF), sds((d, n * seq), BF), sds((n, 1, d), F32)]
    more_specs = [row_spec(o.shape) for o in more]
    more_specs[2] = pl.BlockSpec((d, seq), lambda b: (0, b))
    more += [sds((1, seq, d), BF)] * n
    more_specs += [out_const((1, seq, d))] * n
    return pl.pallas_call(
        attn_other_kernel,
        grid=(n,),
        in_specs=[SMEM_SPEC, SMEM_SPEC, row_spec(an.shape), const_spec(hot.shape), row_spec(x.shape)]
        + [row_spec(ctx_a.shape), const_spec(wo.shape), const_spec((1, d))]
        + [ANY] * 4,
        out_specs=specs + more_specs,
        out_shape=outs + more,
        scratch_shapes=scratch
        + [
            pltpu.VMEM((d, 3 * width), BF),
            pltpu.VMEM((16, 3 * width), BF),
            pltpu.VMEM(wo.shape, BF),
            pltpu.VMEM((1, seq, width), BF),
            pltpu.SemaphoreType.DMA((5,)),
            pltpu.SemaphoreType.DMA((12,)),
        ],
        compiler_params=params(),
        cost_estimate=cost(15),
        name="attn_other",
    )(lens, at, an, hot, x, ctx_a, wo, gain.reshape(1, d), *packs)


def attn_back(b, n, length, core, w, d_attn, ins, outs, scratch, late):
    (q_ref, qt_ref, k_ref, v_ref, ct_ref, lse_ref, nb_ref, tf_ref, ant_ref, hot_ref) = ins
    (dq_ref, dk_ref, dv_ref, send_ref, keep_ref, table_ref) = outs
    (dc_ref, dct_ref, t_ref, fsum_ref, p_ref, ds_ref, all_ref, da_ref, go_ref) = scratch
    seq, width = q_ref.shape[1], q_ref.shape[2]
    heads = width // 64
    nblk = seq // TILE
    here = pl.ds(pl.multiple_of(b * seq, seq), seq)

    @pl.when(b == 0)
    def _():
        t_ref[...] = jnp.zeros_like(t_ref)
        fsum_ref[...] = jnp.zeros_like(fsum_ref)
        table_ref[...] = jnp.zeros_like(table_ref)

    da_ref[here, :] = d_attn
    dct_ref[...] = mm(w, d_attn, NT).astype(BF)
    dc_ref[...] = jnp.transpose(dct_ref[...])
    kx = key_extras(length, seq)
    lane = lax.broadcasted_iota(jnp.int32, (seq, TILE), 1)
    vx = jnp.where((lane & 63) < 3, 1.0, 0.0)
    keys, values, queries, grads, turned = {}, {}, {}, {}, {}

    def prepare(h):
        pair, e = h // 2, h % 2
        cols = slice(TILE * pair, TILE * (pair + 1))
        mine = lane < 64 if e == 0 else lane >= 64
        if e == 0:
            turned[pair] = jnp.transpose(k_ref[b, :, cols])
        keys[h] = jnp.where(mine, k_ref[b, :, cols].astype(F32), kx).astype(BF)
        values[h] = jnp.where(mine, v_ref[b, :, cols].astype(F32), vx).astype(BF)
        at = slice(64 * h, 64 * (h + 1))
        lse = split3(-lse_ref[b, h : h + 1, :])
        extra = far_rows(tf_ref, h, seq)
        row = lax.broadcasted_iota(jnp.int32, (EXTRA, seq), 0)
        for k in range(3):
            extra = jnp.where(row == 13 + k, lse[k].astype(F32), extra)
        queries[h] = stack_rows(e, qt_ref[b, at, :], extra.astype(BF))
        along = jnp.sum(dct_ref[at, :].astype(F32) * ct_ref[b, at, :].astype(F32), axis=0, keepdims=True)
        extra = jnp.zeros((EXTRA, seq), F32)
        for k, part in enumerate(split3(-along)):
            extra = jnp.where(row == k, part.astype(F32), extra)
        grads[h] = stack_rows(e, dct_ref[at, :], extra.astype(BF))

    def block(h, ib):
        pair, e = h // 2, h % 2
        at = slice(256 * ib, 256 * (ib + 1))
        to = slice(seq * e + 256 * ib, seq * e + 256 * (ib + 1))
        s = mm(keys[h], queries[h][:, at])
        dp = mm(values[h], grads[h][:, at])
        near, far = {}, {}
        for bj, piece in enumerate(near_bias(s, nb_ref, h, ib)):
            rows = slice(TILE * bj, TILE * (bj + 1))
            p = jnp.exp(piece)
            ds = p * dp[rows, :]
            p_ref[pair % 2, rows, to] = p.astype(BF)
            ds_ref[pair % 2, rows, to] = ds.astype(BF)
            for t in range(2):
                d = bj - (2 * ib + t)
                one = ds[:, TILE * t : TILE * (t + 1)]
                if abs(d) <= 1:
                    near[d] = near[d] + one if d in near else one
                else:
                    one = jnp.sum(one.reshape(TILE // 8, 8, TILE), axis=0)
                    side = 1 if d > 0 else 0
                    far[side] = far[side] + one if side in far else one
        for d, one in near.items():
            t_ref[3 * h + d + 1] += one
        for side, one in far.items():
            fsum_ref[2 * h + side] += one

    def finish(pair, part):
        slot = pair % 2
        cols = slice(TILE * pair, TILE * (pair + 1))
        if part < 2:
            src, rhs, out_ref = ((p_ref, dc_ref[:, cols], dv_ref), (ds_ref, q_ref[b, :, cols], dk_ref))[part]
            one = jnp.where(lane < 64, mm(src[slot, :, :seq], rhs), mm(src[slot, :, seq:], rhs)).astype(BF)
            out_ref[0, :, cols] = one
            base = width * (2 - part)
            all_ref[here, base + TILE * pair : base + TILE * (pair + 1)] = one
        if part == 2:
            kt = turned[pair]
            dqt = [mm(kt[64 * e : 64 * (e + 1), :], ds_ref[slot, :, seq * e : seq * (e + 1)]) for e in range(2)]
            one = jnp.transpose(jnp.concatenate(dqt, axis=0).astype(BF))
            dq_ref[0, :, cols] = one
            all_ref[here, TILE * pair : TILE * (pair + 1)] = one

    for pair in range(heads // 2):
        step = 0
        for e in range(2):
            prepare(2 * pair + e)
            for ib in range(seq // 256):
                block(2 * pair + e, ib)
                if pair > 0 and step < 3:
                    finish(pair - 1, step)
                step += 1
    for part in range(3):
        finish(heads // 2 - 1, part)

    @pl.when(b == n - 1)
    def _():
        for c in late:
            c.wait()
        rows = ant_ref.shape[0] // 2
        out = None
        for i in range(n):
            one = mm(ct_ref[i], da_ref[seq * i : seq * (i + 1), :])
            out = one if out is None else out + one
        go_ref[:width, :] = out[:, :width].astype(BF)
        go_ref[width:, :] = out[:, width:].astype(BF)
        for ref, half in ((send_ref, 1 - core), (keep_ref, core)):
            at = pl.ds(pl.multiple_of(half * rows, rows), rows)
            ref[:, : 3 * width] = mm(ant_ref[at, :], all_ref[...]).astype(BF)
            ref[:, 3 * width :] = go_ref[at, :]
        turn = lax.broadcasted_iota(jnp.int32, (TILE, TILE), 0) + lax.broadcasted_iota(jnp.int32, (TILE, TILE), 1)
        turn = jnp.where(turn == TILE - 1, 1.0, 0.0).astype(BF)
        tiles = t_ref.shape[0]
        parts = split3(t_ref[...].reshape(tiles * TILE, TILE))
        back = mm(parts[0], turn) + mm(parts[1], turn) + mm(parts[2], turn)
        diag = []
        for t in range(tiles):
            x = jnp.concatenate([back[TILE * t : TILE * (t + 1)], jnp.zeros((TILE, TILE), F32)], axis=1)
            x = pltpu.roll(x, 0, 1, stride=1, stride_axis=0)
            diag.append(jnp.sum(x, axis=0, keepdims=True))
        lines = [jnp.concatenate(diag[3 * h : 3 * h + 3], axis=1) for h in range(heads)]
        lines.append(jnp.zeros((16 - heads, lines[0].shape[1]), F32))
        near = [mm(part, hot_ref[...]) for part in split3(jnp.concatenate(lines, axis=0))]
        spot = lax.broadcasted_iota(jnp.int32, (1, TILE), 1)
        for h in range(heads):
            one = near[0][h : h + 1] + near[1][h : h + 1] + near[2][h : h + 1]
            for side, bucket in ((0, BUCKETS // 2 - 1), (1, BUCKETS - 1)):
                far = jnp.sum(jnp.sum(fsum_ref[2 * h + side], axis=0, keepdims=True), axis=1, keepdims=True)
                one = one + jnp.where(spot == bucket, far, 0.0)
            table_ref[h : h + 1, :] = one


def back_outs(n, seq, width, d):
    tok = sds((n, seq, width), BF)
    half = sds((d // 2, 4 * width), BF)
    outs = [tok, tok, tok, half, half, sds((8, TILE), F32)]
    return outs, [row_spec(tok.shape)] * 3 + [out_const(o.shape) for o in outs[3:]]


def back_scratch(n, seq, width, d):
    heads = width // 64
    return [
        pltpu.VMEM((seq, width), BF),
        pltpu.VMEM((width, seq), BF),
        pltpu.VMEM((3 * heads, TILE, TILE), F32),
        pltpu.VMEM((2 * heads, 8, TILE), F32),
        pltpu.VMEM((2, seq, 2 * seq), BF),
        pltpu.VMEM((2, seq, 2 * seq), BF),
        pltpu.VMEM((n * seq, 3 * width), BF),
        pltpu.VMEM((n * seq, d), BF),
        pltpu.VMEM((d, width), BF),
    ]


def attn_bwd_kernel(lens, at_ref, da_blk, wo_ref, hot_ref, lse_ref, tf_ref, *refs):
    hbm, outs, scratch = refs[:7], refs[7:13], refs[13:22]
    bufs, sem = refs[22:29], refs[29]
    b = pl.program_id(0)
    n = da_blk.shape[0] * lse_ref.shape[0]
    copies = [pltpu.make_async_copy(x, y, sem.at[i]) for i, (x, y) in enumerate(zip(hbm, bufs))]

    @pl.when(b == 0)
    def _():
        for c in copies:
            c.start()
        for c in copies[:-1]:
            c.wait()

    q, qt, k, v, ct, nb, ant = bufs
    ins = (q, qt, k, v, ct, lse_ref, nb, tf_ref, ant, hot_ref)
    attn_back(b, n, lens[b], at_ref[0] // 2, wo_ref[...], da_blk[0], ins, outs, scratch, copies[-1:])


def attn_bwd(lens, at, d_attn, wo, hot, lse, tf, *arrays):
    n, seq, d = d_attn.shape
    width = wo.shape[0]
    outs, specs = back_outs(n, seq, width, d)
    return pl.pallas_call(
        attn_bwd_kernel,
        grid=(n,),
        in_specs=[SMEM_SPEC, SMEM_SPEC, row_spec(d_attn.shape)]
        + [const_spec(x.shape) for x in (wo, hot, lse, tf)]
        + [ANY] * 7,
        out_specs=specs,
        out_shape=outs,
        scratch_shapes=back_scratch(n, seq, width, d)
        + [pltpu.VMEM(x.shape, x.dtype) for x in arrays]
        + [pltpu.SemaphoreType.DMA((7,))],
        compiler_params=params(),
        cost_estimate=cost(16),
        name="attn_bwd",
    )(lens, at, d_attn, wo, hot, lse, tf, *arrays)


def gelu_parts(v):
    v2 = v * v
    half = 0.5 + 0.5 * jnp.tanh(v * (GELU_A + (GELU_A * GELU_B) * v2))
    act = v * half
    return act, half + (act - act * half) * (2.0 * GELU_A + (6.0 * GELU_A * GELU_B) * v2)


def ffn_fwd_kernel(lens, at_ref, fin_ref, rs_ref, wi_ref, wu_ref, p0, p1, p2, p3, *refs):
    (act_ref, gp_ref, actb_ref, gpb_ref, asum_ref, rsum_ref) = refs[:6]
    (wib_ref, wu_buf, v_ref, sem1, sem2) = refs[6:]
    b = pl.program_id(0)
    late = join_copies(at_ref[0], (p0, p1, p2, p3), wib_ref, sem1) + [pltpu.make_async_copy(wu_ref, wu_buf, sem2)]

    @pl.when(b == 0)
    def _():
        for c in late:
            c.start()

    fin = fin_ref[0]
    seq = fin.shape[0]
    half = wi_ref.shape[1]
    chunk = v_ref.shape[2]
    length = lens[b]
    vrow = (lax.broadcasted_iota(jnp.int32, (8, seq), 1) < length).astype(F32).astype(BF)
    spot = lambda c: slice(c * chunk, (c + 1) * chunk)
    parts = [(w, a, g, c) for w, a, g in ((wi_ref, act_ref, gp_ref), (wib_ref, actb_ref, gpb_ref)) for c in range(half // chunk)]

    def project(t):
        w, _, _, c = parts[t]
        v_ref[t % 2] = mm(fin, w[:, spot(c)])

    project(0)
    for t, (_, a_ref, g_ref, c) in enumerate(parts):
        if t + 1 == half // chunk:

            @pl.when(b == 0)
            def _():
                for copy in late:
                    copy.wait()

        if t + 1 < len(parts):
            project(t + 1)
        for r in range(seq // TILE):
            rows = slice(TILE * r, TILE * (r + 1))
            act, slope = gelu_parts(v_ref[t % 2, rows, :])
            a_ref[0, rows, spot(c)] = act.astype(BF)
            g_ref[0, rows, spot(c)] = slope.astype(BF)
        asum_ref[0, :, spot(t)] = mm(vrow, a_ref[0, :, spot(c)])[:1]
    own = asum_ref[0, :, :half]
    hi = own.astype(BF)
    lo = (own - hi.astype(F32)).astype(BF)
    two_rows = jnp.concatenate([hi.astype(F32), lo.astype(F32), jnp.zeros((14, half), F32)], axis=0).astype(BF)
    branch = mm(two_rows, wu_buf[...])
    rsum_ref[0] = rs_ref[0] + branch[0:1] + branch[1:2]


def ffn_fwd(lens, at, fin, rsum, wi, wu, packs):
    n, seq, d = fin.shape
    half = wi.shape[1]
    wide = sds((n, seq, half), BF)
    outs = [wide, wide, wide, wide, sds((n, 1, 2 * half), F32), sds((n, 1, d), F32)]
    return pl.pallas_call(
        ffn_fwd_kernel,
        grid=(n,),
        in_specs=[SMEM_SPEC, SMEM_SPEC, row_spec(fin.shape), row_spec(rsum.shape), const_spec(wi.shape)] + [ANY] * 5,
        out_specs=[row_spec(o.shape) for o in outs],
        out_shape=outs,
        scratch_shapes=[
            pltpu.VMEM(wi.shape, BF),
            pltpu.VMEM(wu.shape, BF),
            pltpu.VMEM((2, seq, 512), F32),
            pltpu.SemaphoreType.DMA((4,)),
            pltpu.SemaphoreType.DMA,
        ],
        compiler_params=params(),
        cost_estimate=cost(16),
        name="ffn_fwd",
    )(lens, at, fin, rsum, wi, wu, *packs)


def pool_kernel(lens, at_ref, asum_ref, rs_ref, p0, p1, p2, p3, out_ref, wb_ref, sem):
    run_copies(join_copies(at_ref[0], (p0, p1, p2, p3), wb_ref, sem))
    n = asum_ref.shape[0]
    half = wb_ref.shape[0]
    rows = [asum_ref[i, :, half:] for i in range(n)]
    hi = [r.astype(BF) for r in rows]
    lo = [(r - h.astype(F32)).astype(BF) for r, h in zip(rows, hi)]
    pad = jnp.zeros((16 - 2 * n, half), F32)
    br = mm(jnp.concatenate([t.astype(F32) for t in hi + lo] + [pad], axis=0).astype(BF), wb_ref[...])
    for i in range(n):
        total = rs_ref[i] + br[i : i + 1] + br[n + i : n + i + 1]
        out_ref[i : i + 1, :] = total / lens[i].astype(F32)


def pool(lens, at, asum, rsum, packs):
    n, _, d = rsum.shape
    half = asum.shape[2] // 2
    vm = pl.BlockSpec(memory_space=pltpu.VMEM)
    return pl.pallas_call(
        pool_kernel,
        in_specs=[SMEM_SPEC, SMEM_SPEC, vm, vm] + [ANY] * 4,
        out_specs=vm,
        out_shape=sds((8, d), F32),
        scratch_shapes=[pltpu.VMEM((half, d), BF), pltpu.SemaphoreType.DMA((4,))],
        compiler_params=params(),
        cost_estimate=cost(4),
        name="pool",
    )(lens, at, asum, rsum, *packs)


def loss_kernel(me_ref, at_ref, lens, pool_ref, q_ref, wp_ref, fint_hbm, gp_hbm, fn0, fn1, wi_hbm, wu_hbm, p0, p1, p2, p3, *refs):
    (loss_ref, row_ref, g_ref, drow_ref, demb_ref, send_ref, keep_ref) = refs[:7]
    (wu_ref, wb_ref, gp_ref, fnb_ref, wi_ref, ft_ref, gn_ref, v_ref, d_ref, sum_ref, sem, sem2) = refs[7:]
    copies = join_copies(at_ref[0], (p0, p1, p2, p3), wb_ref, sem)
    moves = [(wu_hbm, wu_ref), (wi_hbm, wi_ref), (gp_hbm, gp_ref)]
    moves.append((fint_hbm, ft_ref.at[:, pl.ds(0, fint_hbm.shape[1])]))
    moves += [(f, fnb_ref.at[pl.ds(i, 1)]) for i, f in enumerate((fn0, fn1))]
    loads = [pltpu.make_async_copy(a, b, sem2.at[i]) for i, (a, b) in enumerate(moves)]
    for c in [loads[0]] + copies + loads[1:]:
        c.start()
    d = wp_ref.shape[0]
    count = pool_ref.shape[0]
    pooled = pool_ref[...]
    qs = q_ref[:, :d]
    ints = q_ref[:, d : d + TILE].astype(F32)
    pos = (ints[:, 0:1] * 256.0 + ints[:, 1:2]).astype(jnp.int32)
    length = ints[:, 2:3] * 256.0 + ints[:, 3:4]
    wp = wp_ref[...]
    emb = mm(pooled, wp)
    inv = lax.rsqrt(jnp.sum(emb * emb, axis=-1, keepdims=True) + EPS)
    unit = (emb * inv).astype(BF)
    logits = mm(qs, unit, NT) / SHARPNESS
    top = jnp.max(logits, axis=-1, keepdims=True)
    total = top + jnp.log(jnp.sum(jnp.exp(logits - top), axis=-1, keepdims=True))
    hit = lax.broadcasted_iota(jnp.int32, (count, count), 1) == pos
    loss = total - jnp.sum(jnp.where(hit, logits, 0.0), axis=1, keepdims=True)
    d_logits = (LOSS_SCALE * (jnp.exp(logits - total) - jnp.where(hit, 1.0, 0.0))).astype(BF)
    d_unit = mm(d_logits, qs, TN) / SHARPNESS
    along = jnp.sum(emb * d_unit, axis=-1, keepdims=True)
    d_emb = (inv * d_unit - inv * inv * inv * along * emb).astype(BF)
    demb_ref[...] = d_emb
    rows = mm(d_emb, wp, NT) / length
    drow_ref[...] = rows.astype(BF)
    index = lax.broadcasted_iota(jnp.int32, (count, 1), 0)
    pick = lambda t, i: jnp.sum(jnp.where(index == i, t, 0.0), axis=0, keepdims=True)
    n, seq, half = gp_ref.shape
    own = [pick(rows, me_ref[i]) for i in range(n)]
    near = [pick(rows, me_ref[n + i]) for i in range(n)]
    lost = jnp.broadcast_to(loss, (count, TILE))
    pad = jnp.zeros((8 - n, d), F32)
    row_ref[...] = jnp.concatenate(own + [pad], axis=0)
    loss_ref[...] = jnp.concatenate([pick(lost, me_ref[i]) for i in range(n)] + [pad[:, :TILE]], axis=0)
    four = jnp.concatenate(own + near + [jnp.zeros((16 - 2 * n, d), F32)], axis=0).astype(BF)
    loads[0].wait()
    ga = mm(four, wu_ref[...], NT)
    gn_ref[...] = ga[:8]
    for c in copies:
        c.wait()
    g_ref[:, :half] = ga[:8]
    g_ref[:, half:] = mm(four, wb_ref[...], NT)[:8]
    for c in loads[1:]:
        c.wait()

    tokens = n * seq
    for i in range(n):
        valid = lax.broadcasted_iota(jnp.int32, (seq, TILE), 0) < lens[n + i]
        fin = (fnb_ref[i].astype(F32) * valid.astype(F32)[:, :1]).astype(BF)
        ft_ref[:, tokens + seq * i : tokens + seq * (i + 1)] = jnp.transpose(fin)
    chunk = v_ref.shape[3]
    steps = half // chunk
    spot = lambda c: slice(c * chunk, (c + 1) * chunk)

    def project(c):
        for i in range(n):
            v_ref[c % 2, i] = mm(fnb_ref[i], wi_ref[:, spot(c)])

    def scale(c):
        for i in range(n):
            at = slice(seq * i, seq * (i + 1))
            d_ref[c % 2, at, :] = (gp_ref[i, :, spot(c)].astype(F32) * gn_ref[i : i + 1, spot(c)]).astype(BF)
            for r in range(seq // TILE):
                part = slice(TILE * r, TILE * (r + 1))
                slope = gelu_parts(v_ref[c % 2, i, part, :])[1]
                one = slope * gn_ref[n + i : n + i + 1, spot(c)]
                base = tokens + seq * i + TILE * r
                d_ref[c % 2, base : base + TILE, :] = one.astype(BF)

    rows2 = d // 2
    core = at_ref[0] // 2
    project(0)
    scale(0)
    for c in range(steps):
        if c + 1 < steps:
            project(c + 1)
        sum_ref[...] = mm(ft_ref[...], d_ref[c % 2]).astype(BF)
        for ref, side in ((send_ref, 1 - core), (keep_ref, core)):
            ref[:, spot(c)] = sum_ref[pl.ds(pl.multiple_of(side * rows2, rows2), rows2), :]
        if c + 1 < steps:
            scale(c + 1)


def loss_all(me, at, lens4, pooled, queries, wp, fint, gp, fin_nb, wi, wu, packs):
    half, d = wu.shape
    n, seq, _ = gp.shape
    count = pooled.shape[0]
    chunk = 512
    vm = pl.BlockSpec(memory_space=pltpu.VMEM)
    return pl.pallas_call(
        loss_kernel,
        in_specs=[SMEM_SPEC] * 3 + [vm] * 3 + [ANY] * 10,
        out_specs=[vm] * 7,
        out_shape=[
            sds((8, TILE), F32),
            sds((8, d), F32),
            sds((8, 2 * half), F32),
            sds((count, d), BF),
            sds((count, d), BF),
            sds((d // 2, half), BF),
            sds((d // 2, half), BF),
        ],
        scratch_shapes=[
            pltpu.VMEM(wu.shape, BF),
            pltpu.VMEM(wu.shape, BF),
            pltpu.VMEM(gp.shape, BF),
            pltpu.VMEM((n, seq, d), BF),
            pltpu.VMEM(wi.shape, BF),
            pltpu.VMEM((d, 2 * n * seq), BF),
            pltpu.VMEM((8, half), F32),
            pltpu.VMEM((2, n, seq, chunk), F32),
            pltpu.VMEM((2, 2 * n * seq, chunk), BF),
            pltpu.VMEM((d, chunk), BF),
            pltpu.SemaphoreType.DMA((4,)),
            pltpu.SemaphoreType.DMA((6,)),
        ],
        compiler_params=params(),
        cost_estimate=cost(17),
        name="loss_inner",
    )(me, at, lens4, pooled, queries, wp, fint, gp, *fin_nb, wi, wu, *packs)


def mid_bwd_kernel(lens, at_ref, g_ref, row_ref, gain_ref, hot_ref, lse_ref, tf_ref, *refs):
    hbm, packs0, packs1 = refs[:11], refs[11:15], refs[15:19]
    (dres_ref, dattn_ref), outs, scratch = refs[19:21], refs[21:27], refs[27:36]
    bufs, (wib_ref, wob_ref, d_ref, sem, sem0, sem1) = refs[36:47], refs[47:]
    wi_ref, gpa_ref, gpb_ref, res_all, q, qt, k, v, ct, nb, ant = bufs
    b = pl.program_id(0)
    n = lse_ref.shape[0]
    copies = [pltpu.make_async_copy(x, y, sem.at[i]) for i, (x, y) in enumerate(zip(hbm, bufs))]
    copies0 = out_copies(at_ref[0], packs0, wob_ref, sem0)
    copies1 = join_copies(at_ref[0], packs1, wib_ref, sem1)

    def first(group):
        @pl.when(b == 0)
        def _():
            for c in group:
                c.wait()

    @pl.when(b == 0)
    def _():
        for c in copies[:2] + copies1 + copies[2:4] + copies0 + copies[4:]:
            c.start()

    first(copies[:2])
    _, seq, d = res_all.shape
    half = wi_ref.shape[1]
    chunk = d_ref.shape[2]
    steps = half // chunk
    parts = [(gp, w, c) for gp, w in ((gpa_ref, wi_ref), (gpb_ref, wib_ref)) for c in range(steps)]

    def scale(t):
        gp, _, c = parts[t]
        g = g_ref[pl.ds(b, 1), t * chunk : (t + 1) * chunk]
        d_ref[t % 2] = (gp[b, :, c * chunk : (c + 1) * chunk].astype(F32) * g).astype(BF)

    d_two = None
    scale(0)
    for t, (_, w, c) in enumerate(parts):
        if t + 1 == steps:
            first(copies[2:4] + copies1)
        if t + 1 < len(parts):
            scale(t + 1)
        one = mm(d_ref[t % 2], w[:, c * chunk : (c + 1) * chunk], NT)
        d_two = one if d_two is None else d_two + one
    res = res_all[b]
    inv = lax.rsqrt(jnp.mean(res * res, axis=-1, keepdims=True) + EPS)
    scaled = d_two * gain_ref[...]
    along = jnp.sum(scaled * res, axis=-1, keepdims=True)
    valid = lax.broadcasted_iota(jnp.int32, (seq, TILE), 0) < lens[b]
    vcol = valid.astype(F32)[:, :1]
    inv = inv * vcol
    d_res = vcol * row_ref[pl.ds(b, 1), :] + scaled * inv - res * (inv * inv * inv * along / d)
    dres_ref[0] = d_res
    d_attn = d_res.astype(BF)
    dattn_ref[0] = d_attn
    first(copies0 + copies[4:-1])
    ins = (q, qt, k, v, ct, lse_ref, nb, tf_ref, ant, hot_ref)
    attn_back(b, n, lens[b], at_ref[0] // 2, wob_ref[...], d_attn, ins, outs, scratch, copies[-1:])


def mid_bwd(lens, at, g, row, gain, hot, lse, tf, arrays, packs0, packs1):
    wi, _, _, res = arrays[:4]
    n, seq, d = res.shape
    half = wi.shape[1]
    width = packs0[0].shape[1] // 3
    outs, specs = back_outs(n, seq, width, d)
    more = [sds((n, seq, d), F32), sds((n, seq, d), BF)]
    return pl.pallas_call(
        mid_bwd_kernel,
        grid=(n,),
        in_specs=[SMEM_SPEC, SMEM_SPEC]
        + [const_spec(x.shape) for x in (g, row)]
        + [const_spec((1, d))]
        + [const_spec(x.shape) for x in (hot, lse, tf)]
        + [ANY] * 19,
        out_specs=[row_spec(o.shape) for o in more] + specs,
        out_shape=more + outs,
        scratch_shapes=back_scratch(n, seq, width, d)
        + [pltpu.VMEM(x.shape, x.dtype) for x in arrays]
        + [
            pltpu.VMEM((d, half), BF),
            pltpu.VMEM((width, d), BF),
            pltpu.VMEM((2, seq, 512), BF),
            pltpu.SemaphoreType.DMA((11,)),
            pltpu.SemaphoreType.DMA((12,)),
            pltpu.SemaphoreType.DMA((4,)),
        ],
        compiler_params=params(),
        cost_estimate=cost(32),
        name="mid_bwd",
    )(lens, at, g, row, gain.reshape(1, d), hot, lse, tf, *arrays, *packs0, *packs1)


def input_kernel(at_ref, x_ref, dres_ref, gain_ref, qa, ka, va, qb, kb, vb, wq, wk, wv, p0, p1, p2, p3, out_ref, w_ref, sem):
    @pl.when(pl.program_id(0) == 0)
    def _():
        run_copies(join_copies(at_ref[0], (p0, p1, p2, p3), w_ref, sem))

    width = wq.shape[1]
    d_one = mm(qa[0], wq[...], NT) + mm(ka[0], wk[...], NT) + mm(va[0], wv[...], NT)
    for i, t in enumerate((qb, kb, vb)):
        d_one = d_one + mm(t[0], w_ref[:, width * i : width * (i + 1)], NT)
    x = x_ref[0].astype(F32)
    inv = lax.rsqrt(jnp.mean(x * x, axis=-1, keepdims=True) + EPS)
    dx = d_one * x
    gain = gain_ref[...]
    along = jnp.sum(dx * gain, axis=-1, keepdims=True)
    out_ref[0] = dres_ref[0] + d_one * gain * inv - x * (inv * inv * inv * along / x.shape[1])


def input_part(at, x, dres, gain, toks, wq, wk, wv, packs):
    n, seq, d = x.shape
    width = wq.shape[1]
    return pl.pallas_call(
        input_kernel,
        grid=(n,),
        in_specs=[SMEM_SPEC, row_spec(x.shape), row_spec(dres.shape), const_spec((1, d))]
        + [row_spec(toks[0].shape)] * 6
        + [const_spec(wq.shape)] * 3
        + [ANY] * 4,
        out_specs=row_spec(x.shape),
        out_shape=sds(x.shape, F32),
        scratch_shapes=[pltpu.VMEM((d, 3 * width), BF), pltpu.SemaphoreType.DMA((4,))],
        compiler_params=params(),
        cost_estimate=cost(12),
        name="input_part",
    )(at, x, dres, gain.reshape(1, d), *toks, wq, wk, wv, *packs)


def layer_kernel(at_ref, res_ref, aa_ref, ab_ref, w_ref, p0, p1, p2, p3, out_ref, wb_ref, sem):
    @pl.when(pl.program_id(0) == 0)
    def _():
        run_copies(join_copies(at_ref[0], (p0, p1, p2, p3), wb_ref, sem))

    out_ref[0] = (res_ref[0] + mm(aa_ref[0], w_ref[...]) + mm(ab_ref[0], wb_ref[...])).astype(BF)


def layer_part(at, res, act_a, act_b, wu, packs):
    n, seq, d = res.shape
    return pl.pallas_call(
        layer_kernel,
        grid=(n,),
        in_specs=[SMEM_SPEC, row_spec(res.shape), row_spec(act_a.shape), row_spec(act_b.shape), const_spec(wu.shape)]
        + [ANY] * 4,
        out_specs=row_spec(res.shape),
        out_shape=sds(res.shape, BF),
        scratch_shapes=[pltpu.VMEM(wu.shape, BF), pltpu.SemaphoreType.DMA((4,))],
        compiler_params=params(),
        cost_estimate=cost(12),
        name="layer_part",
    )(at, res, act_a, act_b, wu, *packs)


def gain_row(prod):
    ones = jnp.ones((16, prod.shape[1]), BF)
    return sum(mm(ones, part, NT)[:1] for part in split3(prod))


def inner_done_kernel(at_ref, own_ref, near_ref, w_ref, out_ref, gain_ref):
    rows = own_ref.shape[0]
    core = at_ref[0] // 2
    halves = [own_ref[...].astype(F32), near_ref[...].astype(F32)]
    for half in range(2):
        one = jnp.where(core == half, halves[0], halves[1])
        at = slice(rows * half, rows * (half + 1))
        out_ref[at, :] = one
        gain_ref[:, at] = jnp.broadcast_to(gain_row(one * w_ref[at, :].astype(F32)), (8, rows))


def inner_done(at, own, near, w):
    d, half = w.shape
    chunk = 512
    cols = lambda r: pl.BlockSpec((r, chunk), lambda c: (0, c))
    return pl.pallas_call(
        inner_done_kernel,
        grid=(half // chunk,),
        in_specs=[SMEM_SPEC, cols(d // 2), cols(d // 2), cols(d)],
        out_specs=[cols(d), pl.BlockSpec((8, d), lambda c: (c, 0))],
        out_shape=[sds((d, half), F32), sds((8 * (half // chunk), d), F32)],
        compiler_params=params(),
        cost_estimate=cost(5),
        name="inner_done",
    )(at, own, near, w)


def attn_done_kernel(half_ref, sum_ref, wq, wk, wv, *refs):
    q_ref, k_ref, v_ref, o_ref, gain_ref = refs[-5:]
    width = wq.shape[1]
    total = None
    for i, (w, out) in enumerate(((wq, q_ref), (wk, k_ref), (wv, v_ref))):
        one = sum_ref[:, width * i : width * (i + 1)].astype(F32)
        out[...] = one
        prod = one * w[...].astype(F32)
        total = prod if total is None else total + prod
    o_ref[...] = sum_ref[:, 3 * width :].astype(F32)
    gain_ref[...] = jnp.broadcast_to(gain_row(total), gain_ref.shape)


def attn_done(half, sums, wq, wk, wv, into=()):
    d, width = wq.shape
    rows = d // 2
    grad = sds((d, width), F32)
    block = pl.BlockSpec((rows, width), lambda b, half: (half[0], 0))
    across = pl.BlockSpec((width, rows), lambda b, half: (0, half[0]))
    return pl.pallas_call(
        attn_done_kernel,
        grid_spec=pltpu.PrefetchScalarGridSpec(
            num_scalar_prefetch=1,
            grid=(1,),
            in_specs=[pl.BlockSpec(sums.shape, lambda b, half: (0, 0))] + [block] * 3 + [ANY] * len(into),
            out_specs=[block] * 3 + [across, pl.BlockSpec((8, rows), lambda b, half: (0, 0))],
        ),
        out_shape=[grad, grad, grad, sds((width, d), F32), sds((8, rows), F32)],
        input_output_aliases={5 + i: i for i in range(len(into))},
        compiler_params=params(),
        cost_estimate=cost(3),
        name="attn_done",
    )(half, sums, wq, wk, wv, *into)


def after(*xs):
    return lax.optimization_barrier(xs)


def swap(x, axis, bit, size):
    return lax.ppermute(x, axis, [(i, i ^ bit) for i in range(size)])


class Place:
    def __init__(self, chips, tensor):
        self.chips, self.tensor = chips, tensor
        self.chip = lax.axis_index("chip")
        self.core = lax.axis_index("core")
        self.ti = lax.axis_index("tensor")

    def across(self, x):
        return swap(x, "tensor", 1, self.tensor)

    def core_swap(self, x):
        return swap(x, "core", 1, 2)

    def share(self, x):
        return lax.all_to_all(x, ("chip", "core", "tensor"), 0, 0, tiled=True)

    def side(self, mine):
        return swap(mine, "chip", 1, self.chips)

    def spread(self, mine, side):
        return [mine, side, self.core_swap(mine), self.core_swap(side)]

    def exchange(self, x):
        rows, width = x.shape
        return lax.all_to_all(x.reshape(self.chips, rows // self.chips, width), "chip", 0, 0, tiled=True)

    def add(self, got):
        return jnp.sum(got.astype(F32), axis=0).astype(BF)

    def gather(self, x):
        got = lax.all_to_all(jnp.broadcast_to(x[None], (self.chips,) + x.shape), "chip", 0, 0, tiled=True)
        return got.reshape(-1, x.shape[1])

    def total(self, x):
        for i in range(self.chips.bit_length() - 1):
            x = x + swap(x, "chip", 1 << i, self.chips)
        return x


def body(
    mesh_shape,
    hidden_in,
    lengths,
    queries,
    positives,
    gain_attn,
    w_query,
    w_key,
    w_value,
    w_out,
    rel_table,
    gain_ffn,
    w_inner,
    w_outer,
    w_proj,
):
    pc = Place(mesh_shape["chip"], mesh_shape["tensor"])
    n, seq, d = hidden_in.shape
    half = w_inner.shape[1]
    width = w_query.shape[1]
    buckets = rel_table.shape[0]
    lens = lax.dynamic_slice_in_dim(lengths, pc.ti * n, n, 0)
    near_lens = lax.dynamic_slice_in_dim(lengths, (1 - pc.ti) * n, n, 0)
    lens4 = jnp.concatenate([lens, near_lens])
    at = (2 * pc.core + (pc.chip & 1)).reshape(1)
    devices = pc.chips * 2 * pc.tensor
    hot_t = jnp.asarray(np.pad(diag_onehot(buckets, False).T, ((0, TILE - buckets), (0, 0))), BF)
    hot_back = jnp.asarray(np.pad(diag_onehot(buckets, True), ((0, 0), (0, TILE - buckets))), BF)

    turned = rel_table.T
    packs = pack_weights(at, turned, w_query, w_key, w_value, w_out, w_inner, w_outer)
    y_attn = pc.across(packs[0])

    qf = queries.astype(F32)
    q_unit = (qf * lax.rsqrt(jnp.sum(qf * qf, axis=-1, keepdims=True) + EPS)).astype(BF)
    ints = jnp.stack([positives // 256, positives % 256, lens // 256, lens % 256], axis=1)
    ints = jnp.pad(ints.astype(BF), ((0, 0), (0, TILE - 4)))
    q_all = jnp.concatenate([q_unit, ints], axis=1)

    an, ant, q_a, qt_a, k_a, v_a, ctx_a, ctxt_a, lse_a, nb_a, tf_a = attn_own(
        lens, hidden_in, gain_attn, w_query, w_key, w_value, turned, hot_t
    )
    y_attn, an, q_all, *packs = after(y_attn, an, q_all, *packs[1:])
    y_inner, y_outer = [pc.across(p) for p in packs]
    x_attn = pc.side(y_attn)
    q_all = pc.share(jnp.broadcast_to(q_all[None], (devices,) + q_all.shape))
    x_attn, q_all = after(x_attn, q_all)
    p_attn = pc.spread(y_attn, x_attn)
    y_inner, an = after(y_inner, an)
    x_inner = pc.side(y_inner)
    q_b, qt_b, k_b, v_b, ctxt_b, lse_b, nb_b, tf_b, res, fin, fint, rsum, *fins = attn_other(
        lens, at, an, hot_t, hidden_in, ctx_a, w_out, gain_ffn, p_attn
    )
    y_inner, x_inner, y_outer, fin, *fins = after(y_inner, x_inner, y_outer, fin, *fins)
    x_outer = pc.side(y_outer)
    p_inner = pc.spread(y_inner, x_inner)
    fin_nb = [pc.across(f) for f in fins]
    act_a, gp_a, act_b, gp_b, asum, rsum = ffn_fwd(lens, at, fin, rsum, w_inner, w_outer, p_inner)
    y_outer, x_outer, asum, fin_nb[0] = after(y_outer, x_outer, asum, fin_nb[0])
    p_outer = pc.spread(y_outer, x_outer)
    pooled = pool(lens, at, asum, rsum, p_outer)[:n].astype(BF)

    sums_a, sums_b = asum[:, 0, :half].astype(BF), asum[:, 0, half:].astype(BF)
    sums = jnp.where(pc.ti > 0, jnp.stack([sums_b, sums_a]), jnp.stack([sums_a, sums_b]))
    msg = jnp.concatenate([jnp.broadcast_to(pooled[None], (2,) + pooled.shape), sums], axis=2)
    msg = jnp.broadcast_to(msg[None], (2 * pc.chips,) + msg.shape).reshape((devices,) + msg.shape[1:])
    got = pc.share(msg).reshape(devices * n, -1)
    pooled = got[:, :d]
    base = (2 * pc.chip + pc.core) * pc.tensor * n
    me = jnp.stack([base + pc.ti * n, base + pc.ti * n + 1, base + (1 - pc.ti) * n, base + (1 - pc.ti) * n + 1])
    loss8, row8, g8, d_rows, d_emb, gi_send, gi_keep = loss_all(
        me, at, lens4, pooled, q_all.reshape(devices * n, -1), w_proj, fint, gp_a, fin_nb, w_inner, w_outer, p_outer
    )
    query_loss = loss8[:n, 0]

    inner_half, gp_a = after(gi_keep + pc.core_swap(gi_send), gp_a)
    inner_parts = pc.exchange(inner_half)
    arrays = [w_inner, gp_a, gp_b, res, q_b, qt_b, k_b, v_b, ctxt_b, nb_b, ant]
    d_res, d_attn, dq_b, dk_b, dv_b, send_b, keep_b, table_b = mid_bwd(
        lens, at, g8, row8, gain_ffn, hot_back, lse_b, tf_b, arrays, p_attn, p_inner
    )
    half_b, d_attn = after(keep_b + pc.core_swap(send_b), d_attn)
    far_part = pc.across(half_b)
    inner_part, d_attn = after(pc.add(inner_parts), d_attn)
    dq_a, dk_a, dv_a, send_a, keep_a, table_a = attn_bwd(
        lens, at, d_attn, w_out, hot_back, lse_a, tf_a, q_a, qt_a, k_a, v_a, ctxt_a, nb_a, ant
    )
    proj_grad = mm(pooled, d_emb, TN)
    outer_grad = mm(got[:, d:], d_rows, TN)
    inner_all, far_part, far_table, send_a, proj_grad, outer_grad = after(
        pc.gather(inner_part), far_part, pc.across(table_b), send_a, proj_grad, outer_grad
    )
    table = table_a + far_table
    near_a, near_table = after(pc.core_swap(send_a), pc.core_swap(table))
    parts = pc.exchange(keep_a + far_part + near_a)
    toks = (dq_a, dk_a, dv_a, dq_b, dk_b, dv_b)
    input_grad = input_part(at, hidden_in, d_res, gain_attn, toks, w_query, w_key, w_value, p_attn)

    inner_sum, gain_ffn_part = inner_done(at, inner_all, pc.core_swap(inner_all), w_inner)
    layer = layer_part(at, res, act_a, act_b, w_outer, p_outer)
    parts, input_grad, layer = after(parts, input_grad, layer)
    attn_all = pc.gather(pc.add(parts))
    table_sum = pc.total(table + near_table)
    gain_ffn_part = jnp.sum(gain_ffn_part[::8], axis=0)
    gain_ffn_grad = (gain_ffn_part + pc.across(gain_ffn_part)) / gain_ffn
    attn_all, gain_ffn_grad, table_sum, inner_sum = after(attn_all, gain_ffn_grad, table_sum, inner_sum)
    half = pc.core.reshape(1)
    near = pc.core_swap(attn_all)
    *grads, gain_own = attn_done(half, attn_all, w_query, w_key, w_value)
    near, *grads = after(near, *grads)
    gain_own = gain_own[0] + pc.across(gain_own[0])
    *grads, _ = attn_done(1 - half, near, w_query, w_key, w_value, grads)
    gain_own, *grads = after(gain_own, *grads)
    q_grad, k_grad, v_grad, out_grad = grads
    gain_near = pc.core_swap(gain_own)
    gain_attn_grad = jnp.where(
        pc.core > 0, jnp.concatenate([gain_near, gain_own]), jnp.concatenate([gain_own, gain_near])
    ) / gain_attn
    return (
        layer,
        query_loss,
        input_grad,
        gain_attn_grad,
        q_grad,
        k_grad,
        v_grad,
        out_grad,
        table_sum[: rel_table.shape[1], :buckets].T,
        gain_ffn_grad,
        inner_sum,
        outer_grad,
        proj_grad,
    )


def solution(mesh):
    dp, tensor = mesh.shape["dp"], mesh.shape["tensor"]
    fine = jax.sharding.Mesh(mesh.devices.reshape(dp // 2, 2, tensor), ("chip", "core", "tensor"))
    rows = ("chip", "core")
    both = rows + ("tensor",)
    return jax.shard_map(
        functools.partial(body, dict(fine.shape)),
        mesh=fine,
        in_specs=(
            P(both, None, None),
            P(rows),
            P(both, None),
            P(both),
            P(),
            P(None, "tensor"),
            P(None, "tensor"),
            P(None, "tensor"),
            P("tensor", None),
            P(None, "tensor"),
            P(),
            P(None, "tensor"),
            P("tensor", None),
            P(),
        ),
        out_specs=(
            P(both, None, None),
            P(both),
            P(both, None, None),
            P(),
            P(None, "tensor"),
            P(None, "tensor"),
            P(None, "tensor"),
            P("tensor", None),
            P(None, "tensor"),
            P(),
            P(None, "tensor"),
            P("tensor", None),
            P(),
        ),
        check_vma=False,
    )
```

```python
import functools

import numpy as np

import jax
import jax.numpy as jnp
from jax import lax
from jax.experimental import pallas as pl
from jax.experimental.pallas import tpu as pltpu
from jax.sharding import PartitionSpec as P

LARGE_STEPS = (12, 16, 23, 32, 46, 64, 91)
SHARPNESS = 0.02
LOSS_SCALE = 256.0
EPS = 1e-06
NEG = -1e30
BF = jnp.bfloat16
F32 = jnp.float32
TILE = 128
BUCKETS = 32
GELU_A = 0.7978845608028654
GELU_B = 0.044715
MIB = 1024 * 1024

NN = (((1,), (0,)), ((), ()))
NT = (((1,), (1,)), ((), ()))
TN = (((0,), (0,)), ((), ()))


def mm(a, b, dims=NN):
    return lax.dot_general(a, b, dims, preferred_element_type=F32)


def bucket_of(r):
    a = np.abs(r)
    far = 8 + sum((a >= t).astype(np.int32) for t in LARGE_STEPS)
    return np.where(r > 0, 16, 0) + np.where(a < 8, a, far)


def diag_onehot(buckets, back):
    lane = np.arange(2 * TILE)
    at = lane - TILE + 1 if back else TILE - 1 - lane
    idx = np.concatenate([bucket_of(TILE * d + at) for d in (-1, 0, 1)])
    hot = (idx[:, None] == np.arange(buckets)[None, :]).astype(np.float32)
    hot[2 * TILE - 1 :: 2 * TILE] = 0.0
    return hot


def params(mib=60):
    return pltpu.CompilerParams(vmem_limit_bytes=mib * MIB)


def cost(us):
    return pl.CostEstimate(flops=0, bytes_accessed=int(us * 3.6e6), transcendentals=0)

ANY = pl.BlockSpec(memory_space=pl.ANY)
SMEM_SPEC = pl.BlockSpec(memory_space=pltpu.SMEM)


def const_spec(shape):
    zeros = (0,) * len(shape)
    return pl.BlockSpec(tuple(shape), lambda b: zeros, pipeline_mode=pl.Buffered(1))


def out_const(shape):
    zeros = (0,) * len(shape)
    return pl.BlockSpec(tuple(shape), lambda b: zeros)


def row_spec(shape):
    tail = (0,) * (len(shape) - 1)
    return pl.BlockSpec((1,) + tuple(shape[1:]), lambda b: (b,) + tail)


def sds(shape, dtype):
    return jax.ShapeDtypeStruct(tuple(shape), dtype)


def split3(t):
    hi = t.astype(BF)
    rest = t - hi.astype(F32)
    mid = rest.astype(BF)
    return hi, mid, (rest - mid.astype(F32)).astype(BF)


def run_copies(copies):
    for c in copies:
        c.start()
    for c in copies:
        c.wait()


def out_pieces(width, d):
    rows, tall = width // 4, width // 6
    rest = rows - tall
    out = [((0, tall, 0, d), (0, tall, 0, d))]
    for i in range(2):
        out.append(((tall, rest, i * width, width), (i * rest, rest, d, width)))
    return out


def pack_kernel(at_ref, tab_ref, wq, wk, wv, wo, wi, wu, s0, s1, s2, sem):
    at = at_ref[0]
    d, width = wq.shape
    rows = d // 4

    def part(w, dst, i):
        count = w.shape[0] // 4
        src = w.at[pl.ds(pl.multiple_of(at * count, count), count)]
        return pltpu.make_async_copy(src, dst, sem.at[i])

    copies = [part(w, s0.at[pl.ds(0, rows), width * i : width * (i + 1)], i) for i, w in enumerate((wq, wk, wv))]
    copies += [part(wi, s1, 3), part(wu, s2, 4)]
    for i, (a, b) in enumerate(out_pieces(width, d)):
        src = wo.at[pl.ds(pl.multiple_of(at * (width // 4) + a[0], 32), a[1]), a[2] : a[2] + a[3]]
        dst = s0.at[pl.ds(rows + 16 + b[0], b[1]), b[2] : b[2] + b[3]]
        copies.append(pltpu.make_async_copy(src, dst, sem.at[5 + i]))
    for c in copies:
        c.start()
    s0[rows : rows + 16, :] = jnp.zeros((16, s0.shape[1]), BF)
    heads, buckets = tab_ref.shape
    for k, t in enumerate(split3(tab_ref[...])):
        s0[rows : rows + heads, TILE * k : TILE * k + buckets] = t
    for c in copies:
        c.wait()


def pack_weights(at, table, wq, wk, wv, wo, wi, wu):
    d, half = wi.shape
    width = wq.shape[1]
    vm = pl.BlockSpec(memory_space=pltpu.VMEM)
    return pl.pallas_call(
        pack_kernel,
        in_specs=[SMEM_SPEC, vm] + [ANY] * 6,
        out_specs=[vm] * 3,
        out_shape=[
            sds((d // 4 + 16 + width // 6, 3 * width), BF),
            sds((d // 4, half), BF),
            sds((half // 4, d), BF),
        ],
        scratch_shapes=[pltpu.SemaphoreType.DMA((8,))],
        compiler_params=params(),
        cost_estimate=cost(3),
        name="pack_weights",
    )(at, table, wq, wk, wv, wo, wi, wu)


def quarter_spots(at):
    core, xb = at // 2, at % 2
    return [at, 2 * core + 1 - xb, 2 * (1 - core) + xb, 2 * (1 - core) + 1 - xb]


def out_copies(at, packs, dst, sem):
    width, d = dst.shape
    base = d // 4 + 16
    out = []
    for i, (p, s) in enumerate(zip(packs, quarter_spots(at))):
        for j, (a, b) in enumerate(out_pieces(width, d)):
            src = p.at[pl.ds(base + b[0], b[1]), b[2] : b[2] + b[3]]
            to = dst.at[pl.ds(pl.multiple_of(s * (width // 4) + a[0], 32), a[1]), a[2] : a[2] + a[3]]
            out.append(pltpu.make_async_copy(src, to, sem.at[3 * i + j]))
    return out


def join_copies(at, packs, dst, sem):
    rows = dst.shape[0] // 4
    out = []
    for i, (p, s) in enumerate(zip(packs, quarter_spots(at))):
        to = dst.at[pl.ds(pl.multiple_of(s * rows, rows), rows)]
        out.append(pltpu.make_async_copy(p.at[pl.ds(0, rows)], to, sem.at[i]))
    return out


EXTRA = 16


def key_extras(length, rows):
    row = lax.broadcasted_iota(jnp.int32, (rows, TILE), 0)
    lane = lax.broadcasted_iota(jnp.int32, (rows, TILE), 1) & 63
    blk = (lane - 1) & 3
    hot = (lane >= 1) & (lane < 13) & (blk == row // TILE)
    one = ((lane == 0) & (row >= length)) | hot | ((lane >= 13) & (lane < EXTRA))
    return jnp.where(one, 1.0, 0.0)


def far_rows(tf_ref, h, seq):
    row = lax.broadcasted_iota(jnp.int32, (EXTRA, seq), 0)
    diff = ((row - 1) & 3) - lax.broadcasted_iota(jnp.int32, (EXTRA, seq), 1) // TILE
    out = jnp.where(row == 0, NEG, 0.0)
    last, mid = BUCKETS - 1, BUCKETS // 2 - 1
    for k in range(3):
        mine = (row >= 1 + 4 * k) & (row < 5 + 4 * k)
        out = out + jnp.where(mine & (diff >= 2), tf_ref[k, h : h + 1, last : last + 1], 0.0)
        out = out + jnp.where(mine & (diff <= -2), tf_ref[k, h : h + 1, mid : mid + 1], 0.0)
    return out


def stack_rows(e, main, extra):
    pad = jnp.zeros((64 - extra.shape[0], extra.shape[1]), BF)
    return jnp.concatenate([main, extra, pad] if e == 0 else [extra, pad, main], axis=0)


def near_bias(s, nb_ref, h, ib):
    rows = []
    for bj in range(s.shape[0] // TILE):
        parts = []
        for t in range(2):
            piece = s[TILE * bj : TILE * (bj + 1), TILE * t : TILE * (t + 1)]
            d = bj - (2 * ib + t)
            parts.append(piece + nb_ref[3 * h + d + 1] if abs(d) <= 1 else piece)
        rows.append(jnp.concatenate(parts, axis=1))
    return rows


def set_bias(parts, hot_ref, tf_ref, nb_ref):
    for k in range(3):
        tf_ref[k] = parts[k].astype(F32)
    hot = hot_ref[...]
    bv = mm(parts[0], hot) + mm(parts[1], hot) + mm(parts[2], hot)
    for t in range(nb_ref.shape[0]):
        h, k = t // 3, t % 3
        v = jnp.broadcast_to(bv[h : h + 1, 2 * TILE * k : 2 * TILE * (k + 1)], (TILE, 2 * TILE))
        nb_ref[t] = pltpu.roll(v, TILE + 1, 1, stride=1, stride_axis=0)[:, :TILE]


def attn_rows(an, length, ws, outs, nb_ref, tf_ref, s_ref, p_ref, between=None):
    q_ref, qt_ref, k_ref, v_ref, ctx_ref, ctxt_ref, lse_ref = outs
    seq = an.shape[0]
    width = q_ref.shape[2]
    for ref, w in zip((q_ref, k_ref), ws):
        ref[0] = mm(an, w[...]).astype(BF)
    kx = key_extras(length, seq)
    lane = lax.broadcasted_iota(jnp.int32, (seq, TILE), 1)
    blocks = [(h, ib) for h in range(width // 64) for ib in range(seq // 256)]
    keys, queries, values, tops, rows = {}, {}, {}, {}, {}

    def prepare(h):
        pair, e = h // 2, h % 2
        cols = slice(TILE * pair, TILE * (pair + 1))
        if e == 0:
            qt_ref[0, cols, :] = jnp.transpose(q_ref[0, :, cols])
        mine = lane < 64 if e == 0 else lane >= 64
        keys[h] = jnp.where(mine, k_ref[0, :, cols].astype(F32), kx).astype(BF)
        qt = qt_ref[0, 64 * h : 64 * (h + 1), :]
        queries[h] = stack_rows(e, qt, far_rows(tf_ref, h, seq).astype(BF))

    def start(t):
        h, ib = blocks[t]
        if ib == 0:
            prepare(h)
        s = mm(keys[h], queries[h][:, 256 * ib : 256 * (ib + 1)])
        return near_bias(s, nb_ref, h, ib)

    def score(t, bj, pieces):
        piece = pieces[bj]
        s_ref[t % 2, TILE * bj : TILE * (bj + 1), :] = piece
        m = jnp.max(piece.reshape(TILE // 8, 8, 256), axis=0)
        tops[t] = m if bj == 0 else jnp.maximum(tops[t], m)
        if bj == seq // TILE - 1:
            tops[t] = jnp.max(tops[t], axis=0, keepdims=True)

    def soft(t, bj):
        h, ib = blocks[t]
        at = slice(TILE * bj, TILE * (bj + 1))
        p_ref[h % 2, at, 256 * ib : 256 * (ib + 1)] = jnp.exp(s_ref[t % 2, at, :] - tops[t]).astype(BF)

    def combine(h):
        per = seq // 256
        top = jnp.concatenate([tops[per * h + i] for i in range(per)], axis=1)
        if h % 2 == 0:
            values[h // 2] = jnp.transpose(v_ref[0, :, TILE * (h // 2) : TILE * (h // 2 + 1)])
        vt = values[h // 2][64 * (h % 2) : 64 * (h % 2 + 1), :]
        got = mm(jnp.concatenate([vt, jnp.ones((16, seq), BF)], axis=0), p_ref[h % 2])
        total = got[64:65]
        lse_ref[0, h : h + 1, :] = top + jnp.log(total)
        rows[h] = got[:64] * (1.0 / total)
        if h % 2 == 1:
            pair = h // 2
            cols = slice(TILE * pair, TILE * (pair + 1))
            ct = jnp.concatenate([rows[h - 1], rows[h]], axis=0).astype(BF)
            ctxt_ref[0, cols, :] = ct
            ctx_ref[0, :, cols] = jnp.transpose(ct)

    for t in range(len(blocks) + 1):
        if t < len(blocks):
            pieces = start(t)
            for bj in range(seq // TILE):
                score(t, bj, pieces)
        if t == 0:
            v_ref[0] = mm(an, ws[2][...]).astype(BF)
        if t == 5 and between is not None:
            between()
        if t > 0:
            for bj in range(seq // TILE):
                soft(t - 1, bj)
            if blocks[t - 1][1] == seq // 256 - 1:
                combine(blocks[t - 1][0])


def attn_own_kernel(lens, x_ref, gain_ref, wq, wk, wv, tab_ref, hot_ref, an_ref, ant_ref, *refs):
    outs, (nb_ref, tf_ref, s_ref, p_ref) = refs[:7], refs[7:]
    b = pl.program_id(0)

    @pl.when(b == 0)
    def _():
        heads, buckets = tab_ref.shape
        wide = jnp.concatenate([tab_ref[...], jnp.zeros((heads, TILE - buckets), F32)], axis=1)
        wide = jnp.concatenate([wide, jnp.zeros((16 - heads, TILE), F32)], axis=0)
        set_bias(split3(wide), hot_ref, tf_ref, nb_ref)

    x = x_ref[0].astype(F32)
    inv = lax.rsqrt(jnp.mean(x * x, axis=-1, keepdims=True) + EPS)
    an = (x * inv * gain_ref[...]).astype(BF)
    an_ref[0] = an
    ant_ref[...] = jnp.transpose(an)
    attn_rows(an, lens[b], (wq, wk, wv), outs, nb_ref, tf_ref, s_ref, p_ref)


def attn_other_kernel(lens, at_ref, an_ref, hot_ref, gain_ref, x_hbm, ca_hbm, wo_hbm, p0, p1, p2, p3, *refs):
    outs, (nb_ref, tf_ref, res_ref, fin_ref, fint_ref, rsum_ref, f0_ref, f1_ref) = list(refs[:6]), refs[6:14]
    (s_ref, p_ref, w_ref, tab_ref, wb_ref, c_ref, x_ref, ca_ref, wo_ref, sem, sem1, sem2) = refs[14:]
    outs.insert(4, c_ref)
    b = pl.program_id(0)
    late = out_copies(at_ref[0], (p0, p1, p2, p3), wb_ref, sem1)
    moves = ((x_hbm, x_ref), (ca_hbm, ca_ref), (wo_hbm, wo_ref))
    more = [pltpu.make_async_copy(x, y, sem2.at[i]) for i, (x, y) in enumerate(moves)]

    @pl.when(b == 0)
    def _():
        rows = w_ref.shape[0] // 4
        copies = join_copies(at_ref[0], (p0, p1, p2, p3), w_ref, sem)
        copies.append(pltpu.make_async_copy(p0.at[pl.ds(rows, 16)], tab_ref, sem.at[4]))
        for c in copies + more + late:
            c.start()
        for c in copies:
            c.wait()
        parts = [tab_ref[:, TILE * k : TILE * (k + 1)] for k in range(3)]
        set_bias(parts, hot_ref, tf_ref, nb_ref)
        for c in more:
            c.wait()

    width = outs[0].shape[2]
    ws = [w_ref.at[:, width * k : width * (k + 1)] for k in range(3)]

    def between():
        res_ref[0] = x_ref[b].astype(F32) + mm(ca_ref[b], wo_ref[...])

    attn_rows(an_ref[0], lens[b], ws, outs, nb_ref, tf_ref, s_ref, p_ref, between)

    @pl.when(b == 0)
    def _():
        for c in late:
            c.wait()

    res = res_ref[0] + mm(outs[4][0], wb_ref[...])
    res_ref[0] = res
    inv = lax.rsqrt(jnp.mean(res * res, axis=-1, keepdims=True) + EPS)
    fin = (res * inv * gain_ref[...]).astype(BF)
    fin_ref[0] = fin
    for i, f_ref in enumerate((f0_ref, f1_ref)):

        @pl.when(b == i)
        def _():
            f_ref[0] = fin

    vcol = (lax.broadcasted_iota(jnp.int32, (res.shape[0], TILE), 0) < lens[b]).astype(F32)[:, :1]
    fint_ref[...] = jnp.transpose((fin.astype(F32) * vcol).astype(BF))
    rsum_ref[0] = jnp.sum(res * vcol, axis=0, keepdims=True)


def attn_outs(n, seq, width):
    heads = width // 64
    tok, turned = sds((n, seq, width), BF), sds((n, width, seq), BF)
    rows = [tok, turned, tok, tok, tok, turned, sds((n, 8, seq), F32)]
    flat = [sds((3 * heads, TILE, TILE), F32), sds((3, 16, TILE), F32)]
    scratch = [pltpu.VMEM((2, seq, 256), F32), pltpu.VMEM((2, seq, seq), BF)]
    return rows + flat, [row_spec(o.shape) for o in rows] + [out_const(o.shape) for o in flat], scratch


def attn_own(lens, x, gain, wq, wk, wv, table, hot):
    n, seq, d = x.shape
    outs, specs, scratch = attn_outs(n, seq, wq.shape[1])
    return pl.pallas_call(
        attn_own_kernel,
        grid=(n,),
        in_specs=[SMEM_SPEC, row_spec(x.shape), const_spec((1, d))]
        + [const_spec(wq.shape)] * 3
        + [const_spec(table.shape), const_spec(hot.shape)],
        out_specs=[row_spec(x.shape), pl.BlockSpec((d, seq), lambda b: (0, b))] + specs,
        out_shape=[sds((n, seq, d), BF), sds((d, n * seq), BF)] + outs,
        scratch_shapes=scratch,
        compiler_params=params(),
        cost_estimate=cost(12),
        name="attn_own",
    )(lens, x, gain.reshape(1, d), wq, wk, wv, table, hot)


def attn_other(lens, at, an, hot, x, ctx_a, wo, gain, packs):
    n, seq, d = an.shape
    width = wo.shape[0]
    outs, specs, scratch = attn_outs(n, seq, width)
    del outs[4], specs[4]
    more = [sds((n, seq, d), F32), sds((n, seq, d), BF), sds((d, n * seq), BF), sds((n, 1, d), F32)]
    more_specs = [row_spec(o.shape) for o in more]
    more_specs[2] = pl.BlockSpec((d, seq), lambda b: (0, b))
    more += [sds((1, seq, d), BF)] * n
    more_specs += [out_const((1, seq, d))] * n
    return pl.pallas_call(
        attn_other_kernel,
        grid=(n,),
        in_specs=[SMEM_SPEC, SMEM_SPEC, row_spec(an.shape), const_spec(hot.shape), const_spec((1, d))]
        + [ANY] * 7,
        out_specs=specs + more_specs,
        out_shape=outs + more,
        scratch_shapes=scratch
        + [
            pltpu.VMEM((d, 3 * width), BF),
            pltpu.VMEM((16, 3 * width), BF),
            pltpu.VMEM(wo.shape, BF),
            pltpu.VMEM((1, seq, width), BF),
            pltpu.VMEM(x.shape, BF),
            pltpu.VMEM(ctx_a.shape, BF),
            pltpu.VMEM(wo.shape, BF),
            pltpu.SemaphoreType.DMA((5,)),
            pltpu.SemaphoreType.DMA((12,)),
            pltpu.SemaphoreType.DMA((3,)),
        ],
        compiler_params=params(),
        cost_estimate=cost(15),
        name="attn_other",
    )(lens, at, an, hot, gain.reshape(1, d), x, ctx_a, wo, *packs)


def attn_back(b, n, length, core, w, d_attn, ins, outs, scratch, late):
    (q_ref, qt_ref, k_ref, v_ref, ct_ref, lse_ref, nb_ref, tf_ref, ant_ref, hot_ref) = ins
    (all_hbm, send_ref, keep_ref, table_ref) = outs
    (dc_ref, dct_ref, t_ref, fsum_ref, p_ref, ds_ref, all_ref, da_ref, go_ref, out_sem) = scratch
    seq, width = q_ref.shape[1], q_ref.shape[2]
    heads = width // 64
    nblk = seq // TILE
    here = pl.ds(pl.multiple_of(b * seq, seq), seq)

    @pl.when(b == 0)
    def _():
        t_ref[...] = jnp.zeros_like(t_ref)
        fsum_ref[...] = jnp.zeros_like(fsum_ref)
        table_ref[...] = jnp.zeros_like(table_ref)

    dct_ref[...] = mm(w, d_attn, NT).astype(BF)
    dc_ref[...] = jnp.transpose(dct_ref[...])
    kx = key_extras(length, seq)
    lane = lax.broadcasted_iota(jnp.int32, (seq, TILE), 1)
    vx = jnp.where((lane & 63) < 3, 1.0, 0.0)
    keys, values, queries, grads, turned = {}, {}, {}, {}, {}

    def prepare(h):
        pair, e = h // 2, h % 2
        cols = slice(TILE * pair, TILE * (pair + 1))
        mine = lane < 64 if e == 0 else lane >= 64
        if e == 0:
            turned[pair] = jnp.transpose(k_ref[b, :, cols])
        keys[h] = jnp.where(mine, k_ref[b, :, cols].astype(F32), kx).astype(BF)
        values[h] = jnp.where(mine, v_ref[b, :, cols].astype(F32), vx).astype(BF)
        at = slice(64 * h, 64 * (h + 1))
        lse = split3(-lse_ref[b, h : h + 1, :])
        extra = far_rows(tf_ref, h, seq)
        row = lax.broadcasted_iota(jnp.int32, (EXTRA, seq), 0)
        for k in range(3):
            extra = jnp.where(row == 13 + k, lse[k].astype(F32), extra)
        queries[h] = stack_rows(e, qt_ref[b, at, :], extra.astype(BF))
        along = jnp.sum(dct_ref[at, :].astype(F32) * ct_ref[b, at, :].astype(F32), axis=0, keepdims=True)
        extra = jnp.zeros((EXTRA, seq), F32)
        for k, part in enumerate(split3(-along)):
            extra = jnp.where(row == k, part.astype(F32), extra)
        grads[h] = stack_rows(e, dct_ref[at, :], extra.astype(BF))

    def block(h, ib):
        pair, e = h // 2, h % 2
        at = slice(256 * ib, 256 * (ib + 1))
        to = slice(seq * e + 256 * ib, seq * e + 256 * (ib + 1))
        s = mm(keys[h], queries[h][:, at])
        dp = mm(values[h], grads[h][:, at])
        near, far = {}, {}
        for bj, piece in enumerate(near_bias(s, nb_ref, h, ib)):
            rows = slice(TILE * bj, TILE * (bj + 1))
            p = jnp.exp(piece)
            ds = p * dp[rows, :]
            p_ref[pair % 2, rows, to] = p.astype(BF)
            ds_ref[pair % 2, rows, to] = ds.astype(BF)
            for t in range(2):
                d = bj - (2 * ib + t)
                one = ds[:, TILE * t : TILE * (t + 1)]
                if abs(d) <= 1:
                    near[d] = near[d] + one if d in near else one
                else:
                    one = jnp.sum(one.reshape(TILE // 8, 8, TILE), axis=0)
                    side = 1 if d > 0 else 0
                    far[side] = far[side] + one if side in far else one
        for d, one in near.items():
            t_ref[3 * h + d + 1] += one
        for side, one in far.items():
            fsum_ref[2 * h + side] += one

    def finish(pair, part):
        slot = pair % 2
        cols = slice(TILE * pair, TILE * (pair + 1))
        if part < 2:
            src, rhs = ((p_ref, dc_ref[:, cols]), (ds_ref, q_ref[b, :, cols]))[part]
            one = jnp.where(lane < 64, mm(src[slot, :, :seq], rhs), mm(src[slot, :, seq:], rhs)).astype(BF)
            base = width * (2 - part)
            all_ref[here, base + TILE * pair : base + TILE * (pair + 1)] = one
        if part == 2:
            kt = turned[pair]
            dqt = [mm(kt[64 * e : 64 * (e + 1), :], ds_ref[slot, :, seq * e : seq * (e + 1)]) for e in range(2)]
            one = jnp.transpose(jnp.concatenate(dqt, axis=0).astype(BF))
            all_ref[here, TILE * pair : TILE * (pair + 1)] = one

    for pair in range(heads // 2):
        step = 0
        for e in range(2):
            prepare(2 * pair + e)
            for ib in range(seq // 256):
                block(2 * pair + e, ib)
                if pair > 0 and step < 3:
                    finish(pair - 1, step)
                step += 1
    for part in range(3):
        finish(heads // 2 - 1, part)
    done = send_rows(b, n, all_ref, all_hbm, out_sem)

    @pl.when(b == n - 1)
    def _():
        for c in late:
            c.wait()
        rows = ant_ref.shape[0] // 2
        out = None
        for i in range(n):
            one = mm(ct_ref[i], da_ref[seq * i : seq * (i + 1), :])
            out = one if out is None else out + one
        go_ref[:width, :] = out[:, :width].astype(BF)
        go_ref[width:, :] = out[:, width:].astype(BF)
        for ref, half in ((send_ref, 1 - core), (keep_ref, core)):
            at = pl.ds(pl.multiple_of(half * rows, rows), rows)
            ref[:, : 3 * width] = mm(ant_ref[at, :], all_ref[...]).astype(BF)
            ref[:, 3 * width :] = go_ref[at, :]
        turn = lax.broadcasted_iota(jnp.int32, (TILE, TILE), 0) + lax.broadcasted_iota(jnp.int32, (TILE, TILE), 1)
        turn = jnp.where(turn == TILE - 1, 1.0, 0.0).astype(BF)
        tiles = t_ref.shape[0]
        hi, lo, _ = split3(t_ref[...].reshape(tiles * TILE, TILE))
        back = mm(jnp.concatenate([hi, lo], axis=1), jnp.concatenate([turn, turn], axis=0))
        diag = []
        for t in range(tiles):
            x = jnp.concatenate([back[TILE * t : TILE * (t + 1)], jnp.zeros((TILE, TILE), F32)], axis=1)
            x = pltpu.roll(x, 0, 1, stride=1, stride_axis=0)
            diag.append(jnp.sum(x, axis=0, keepdims=True))
        lines = [jnp.concatenate(diag[3 * h : 3 * h + 3], axis=1) for h in range(heads)]
        lines.append(jnp.zeros((16 - heads, lines[0].shape[1]), F32))
        near = [mm(part, hot_ref[...]) for part in split3(jnp.concatenate(lines, axis=0))]
        spot = lax.broadcasted_iota(jnp.int32, (1, TILE), 1)
        for h in range(heads):
            one = near[0][h : h + 1] + near[1][h : h + 1] + near[2][h : h + 1]
            for side, bucket in ((0, BUCKETS // 2 - 1), (1, BUCKETS - 1)):
                far = jnp.sum(jnp.sum(fsum_ref[2 * h + side], axis=0, keepdims=True), axis=1, keepdims=True)
                one = one + jnp.where(spot == bucket, far, 0.0)
            table_ref[h : h + 1, :] = one
        for c in done:
            c.wait()


def send_rows(b, n, src, dst, sem):
    rows = src.shape[0] // n
    copies = [pltpu.make_async_copy(src.at[pl.ds(i * rows, rows)], dst.at[pl.ds(i * rows, rows)], sem.at[i]) for i in range(n)]
    for i, c in enumerate(copies):

        @pl.when(b == i)
        def _():
            c.start()

    return copies


def back_outs(n, seq, width, d):
    half = sds((d // 2, 4 * width), BF)
    outs = [sds((n * seq, 3 * width), BF), half, half, sds((8, TILE), F32)]
    return outs, [ANY] + [out_const(o.shape) for o in outs[1:]]


def back_scratch(n, seq, width, d):
    heads = width // 64
    return [
        pltpu.VMEM((seq, width), BF),
        pltpu.VMEM((width, seq), BF),
        pltpu.VMEM((3 * heads, TILE, TILE), F32),
        pltpu.VMEM((2 * heads, 8, TILE), F32),
        pltpu.VMEM((2, seq, 2 * seq), BF),
        pltpu.VMEM((2, seq, 2 * seq), BF),
        pltpu.VMEM((n * seq, 3 * width), BF),
        pltpu.VMEM((n * seq, d), BF),
        pltpu.VMEM((d, width), BF),
        pltpu.SemaphoreType.DMA((n,)),
    ]


def attn_bwd_kernel(lens, at_ref, da_blk, wo_ref, hot_ref, lse_ref, tf_ref, *refs):
    hbm, outs, scratch = refs[:7], refs[7:11], refs[11:21]
    bufs, sem = refs[21:28], refs[28]
    b = pl.program_id(0)
    n = da_blk.shape[0] * lse_ref.shape[0]
    copies = [pltpu.make_async_copy(x, y, sem.at[i]) for i, (x, y) in enumerate(zip(hbm, bufs))]

    @pl.when(b == 0)
    def _():
        for c in copies:
            c.start()
        for c in copies[:-1]:
            c.wait()

    q, qt, k, v, ct, nb, ant = bufs
    ins = (q, qt, k, v, ct, lse_ref, nb, tf_ref, ant, hot_ref)
    seq = da_blk.shape[1]
    scratch[7][pl.ds(pl.multiple_of(b * seq, seq), seq), :] = da_blk[0]
    attn_back(b, n, lens[b], at_ref[0] // 2, wo_ref[...], da_blk[0], ins, outs, scratch, copies[-1:])


def attn_bwd(lens, at, d_attn, wo, hot, lse, tf, *arrays):
    n, seq, d = d_attn.shape
    width = wo.shape[0]
    outs, specs = back_outs(n, seq, width, d)
    return pl.pallas_call(
        attn_bwd_kernel,
        grid=(n,),
        in_specs=[SMEM_SPEC, SMEM_SPEC, row_spec(d_attn.shape)]
        + [const_spec(x.shape) for x in (wo, hot, lse, tf)]
        + [ANY] * 7,
        out_specs=specs,
        out_shape=outs,
        scratch_shapes=back_scratch(n, seq, width, d)
        + [pltpu.VMEM(x.shape, x.dtype) for x in arrays]
        + [pltpu.SemaphoreType.DMA((7,))],
        compiler_params=params(),
        cost_estimate=cost(16),
        name="attn_bwd",
    )(lens, at, d_attn, wo, hot, lse, tf, *arrays)


def gelu_parts(v):
    v2 = v * v
    half = 0.5 + 0.5 * jnp.tanh(v * (GELU_A + (GELU_A * GELU_B) * v2))
    act = v * half
    return act, half + (act - act * half) * (2.0 * GELU_A + (6.0 * GELU_A * GELU_B) * v2)


def ffn_fwd_kernel(lens, at_ref, fin_ref, rs_ref, wi_ref, wu_ref, p0, p1, p2, p3, *refs):
    (act_ref, gp_ref, actb_ref, gpb_ref, asum_ref, rsum_ref) = refs[:6]
    (wib_ref, wu_buf, v_ref, sem1, sem2) = refs[6:]
    b = pl.program_id(0)
    late = join_copies(at_ref[0], (p0, p1, p2, p3), wib_ref, sem1) + [pltpu.make_async_copy(wu_ref, wu_buf, sem2)]

    @pl.when(b == 0)
    def _():
        run_copies(late)

    fin = fin_ref[0]
    seq = fin.shape[0]
    half = wi_ref.shape[1]
    chunk = v_ref.shape[2]
    length = lens[b]
    vrow = (lax.broadcasted_iota(jnp.int32, (8, seq), 1) < length).astype(F32).astype(BF)
    spot = lambda c: slice(c * chunk, (c + 1) * chunk)
    parts = [(w, a, g, c) for w, a, g in ((wi_ref, act_ref, gp_ref), (wib_ref, actb_ref, gpb_ref)) for c in range(half // chunk)]

    def project(t):
        w, _, _, c = parts[t]
        v_ref[t % 2] = mm(fin, w[:, spot(c)])

    project(0)
    for t, (_, a_ref, g_ref, c) in enumerate(parts):
        if t + 1 < len(parts):
            project(t + 1)
        for r in range(seq // TILE):
            rows = slice(TILE * r, TILE * (r + 1))
            act, slope = gelu_parts(v_ref[t % 2, rows, :])
            a_ref[0, rows, spot(c)] = act.astype(BF)
            g_ref[0, rows, spot(c)] = slope.astype(BF)
        asum_ref[0, :, spot(t)] = mm(vrow, a_ref[0, :, spot(c)])[:1]
    own = asum_ref[0, :, :half]
    hi = own.astype(BF)
    lo = (own - hi.astype(F32)).astype(BF)
    two_rows = jnp.concatenate([hi.astype(F32), lo.astype(F32), jnp.zeros((14, half), F32)], axis=0).astype(BF)
    branch = mm(two_rows, wu_buf[...])
    rsum_ref[0] = rs_ref[0] + branch[0:1] + branch[1:2]


def ffn_fwd(lens, at, fin, rsum, wi, wu, packs):
    n, seq, d = fin.shape
    half = wi.shape[1]
    wide = sds((n, seq, half), BF)
    outs = [wide, wide, wide, wide, sds((n, 1, 2 * half), F32), sds((n, 1, d), F32)]
    return pl.pallas_call(
        ffn_fwd_kernel,
        grid=(n,),
        in_specs=[SMEM_SPEC, SMEM_SPEC, row_spec(fin.shape), row_spec(rsum.shape), const_spec(wi.shape)] + [ANY] * 5,
        out_specs=[row_spec(o.shape) for o in outs],
        out_shape=outs,
        scratch_shapes=[
            pltpu.VMEM(wi.shape, BF),
            pltpu.VMEM(wu.shape, BF),
            pltpu.VMEM((2, seq, 512), F32),
            pltpu.SemaphoreType.DMA((4,)),
            pltpu.SemaphoreType.DMA,
        ],
        compiler_params=params(),
        cost_estimate=cost(16),
        name="ffn_fwd",
    )(lens, at, fin, rsum, wi, wu, *packs)


def pool_kernel(lens, at_ref, asum_ref, rs_ref, p0, p1, p2, p3, out_ref, wb_ref, sem):
    run_copies(join_copies(at_ref[0], (p0, p1, p2, p3), wb_ref, sem))
    n = asum_ref.shape[0]
    half = wb_ref.shape[0]
    rows = [asum_ref[i, :, half:] for i in range(n)]
    hi = [r.astype(BF) for r in rows]
    lo = [(r - h.astype(F32)).astype(BF) for r, h in zip(rows, hi)]
    pad = jnp.zeros((16 - 2 * n, half), F32)
    br = mm(jnp.concatenate([t.astype(F32) for t in hi + lo] + [pad], axis=0).astype(BF), wb_ref[...])
    for i in range(n):
        total = rs_ref[i] + br[i : i + 1] + br[n + i : n + i + 1]
        out_ref[i : i + 1, :] = total / lens[i].astype(F32)


def pool(lens, at, asum, rsum, packs):
    n, _, d = rsum.shape
    half = asum.shape[2] // 2
    vm = pl.BlockSpec(memory_space=pltpu.VMEM)
    return pl.pallas_call(
        pool_kernel,
        in_specs=[SMEM_SPEC, SMEM_SPEC, vm, vm] + [ANY] * 4,
        out_specs=vm,
        out_shape=sds((8, d), F32),
        scratch_shapes=[pltpu.VMEM((half, d), BF), pltpu.SemaphoreType.DMA((4,))],
        compiler_params=params(16),
        cost_estimate=cost(4),
        name="pool",
    )(lens, at, asum, rsum, *packs)


def loss_kernel(me_ref, at_ref, lens, pool_ref, q_ref, wp_ref, fint_hbm, gp_hbm, fn0, fn1, wi_hbm, wu_hbm, p0, p1, p2, p3, *refs):
    (loss_ref, row_ref, g_ref, drow_ref, demb_ref, send_ref, keep_ref) = refs[:7]
    (wu_ref, wb_ref, gp_ref, fnb_ref, wi_ref, ft_ref, gn_ref, v_ref, d_ref, sum_ref, sem, sem2) = refs[7:]
    copies = join_copies(at_ref[0], (p0, p1, p2, p3), wb_ref, sem)
    moves = [(wu_hbm, wu_ref), (wi_hbm, wi_ref), (gp_hbm, gp_ref)]
    moves.append((fint_hbm, ft_ref.at[:, pl.ds(0, fint_hbm.shape[1])]))
    moves += [(f, fnb_ref.at[pl.ds(i, 1)]) for i, f in enumerate((fn0, fn1))]
    loads = [pltpu.make_async_copy(a, b, sem2.at[i]) for i, (a, b) in enumerate(moves)]
    for c in [loads[0]] + copies + loads[1:]:
        c.start()
    d = wp_ref.shape[0]
    count = pool_ref.shape[0]
    pooled = pool_ref[...]
    qs = q_ref[:, :d]
    ints = q_ref[:, d : d + TILE].astype(F32)
    pos = (ints[:, 0:1] * 256.0 + ints[:, 1:2]).astype(jnp.int32)
    length = ints[:, 2:3] * 256.0 + ints[:, 3:4]
    wp = wp_ref[...]
    emb = mm(pooled, wp)
    inv = lax.rsqrt(jnp.sum(emb * emb, axis=-1, keepdims=True) + EPS)
    unit = (emb * inv).astype(BF)
    logits = mm(qs, unit, NT) / SHARPNESS
    top = jnp.max(logits, axis=-1, keepdims=True)
    total = top + jnp.log(jnp.sum(jnp.exp(logits - top), axis=-1, keepdims=True))
    hit = lax.broadcasted_iota(jnp.int32, (count, count), 1) == pos
    loss = total - jnp.sum(jnp.where(hit, logits, 0.0), axis=1, keepdims=True)
    d_logits = (LOSS_SCALE * (jnp.exp(logits - total) - jnp.where(hit, 1.0, 0.0))).astype(BF)
    d_unit = mm(d_logits, qs, TN) / SHARPNESS
    along = jnp.sum(emb * d_unit, axis=-1, keepdims=True)
    d_emb = (inv * d_unit - inv * inv * inv * along * emb).astype(BF)
    demb_ref[...] = d_emb
    rows = mm(d_emb, wp, NT) / length
    drow_ref[...] = rows.astype(BF)
    index = lax.broadcasted_iota(jnp.int32, (count, 1), 0)
    pick = lambda t, i: jnp.sum(jnp.where(index == i, t, 0.0), axis=0, keepdims=True)
    n, seq, half = gp_ref.shape
    own = [pick(rows, me_ref[i]) for i in range(n)]
    near = [pick(rows, me_ref[n + i]) for i in range(n)]
    lost = jnp.broadcast_to(loss, (count, TILE))
    pad = jnp.zeros((8 - n, d), F32)
    row_ref[...] = jnp.concatenate(own + [pad], axis=0)
    loss_ref[...] = jnp.concatenate([pick(lost, me_ref[i]) for i in range(n)] + [pad[:, :TILE]], axis=0)
    four = jnp.concatenate(own + near + [jnp.zeros((16 - 2 * n, d), F32)], axis=0).astype(BF)
    loads[0].wait()
    ga = mm(four, wu_ref[...], NT)
    gn_ref[...] = ga[:8]
    for c in copies:
        c.wait()
    g_ref[:, :half] = ga[:8]
    g_ref[:, half:] = mm(four, wb_ref[...], NT)[:8]
    for c in loads[1:]:
        c.wait()

    tokens = n * seq
    for i in range(n):
        valid = lax.broadcasted_iota(jnp.int32, (seq, TILE), 0) < lens[n + i]
        fin = (fnb_ref[i].astype(F32) * valid.astype(F32)[:, :1]).astype(BF)
        ft_ref[:, tokens + seq * i : tokens + seq * (i + 1)] = jnp.transpose(fin)
    chunk = v_ref.shape[3]
    steps = half // chunk
    spot = lambda c: slice(c * chunk, (c + 1) * chunk)

    def project(c):
        for i in range(n):
            v_ref[c % 2, i] = mm(fnb_ref[i], wi_ref[:, spot(c)])

    def scale(c):
        for i in range(n):
            at = slice(seq * i, seq * (i + 1))
            d_ref[c % 2, at, :] = (gp_ref[i, :, spot(c)].astype(F32) * gn_ref[i : i + 1, spot(c)]).astype(BF)
            for r in range(seq // TILE):
                part = slice(TILE * r, TILE * (r + 1))
                slope = gelu_parts(v_ref[c % 2, i, part, :])[1]
                one = slope * gn_ref[n + i : n + i + 1, spot(c)]
                base = tokens + seq * i + TILE * r
                d_ref[c % 2, base : base + TILE, :] = one.astype(BF)

    rows2 = d // 2
    core = at_ref[0] // 2
    project(0)
    scale(0)
    for c in range(steps):
        if c + 1 < steps:
            project(c + 1)
        sum_ref[...] = mm(ft_ref[...], d_ref[c % 2]).astype(BF)
        for ref, side in ((send_ref, 1 - core), (keep_ref, core)):
            ref[:, spot(c)] = sum_ref[pl.ds(pl.multiple_of(side * rows2, rows2), rows2), :]
        if c + 1 < steps:
            scale(c + 1)


def loss_all(me, at, lens4, pooled, queries, wp, fint, gp, fin_nb, wi, wu, packs):
    half, d = wu.shape
    n, seq, _ = gp.shape
    count = pooled.shape[0]
    chunk = 512
    vm = pl.BlockSpec(memory_space=pltpu.VMEM)
    return pl.pallas_call(
        loss_kernel,
        in_specs=[SMEM_SPEC] * 3 + [vm] * 3 + [ANY] * 10,
        out_specs=[vm] * 7,
        out_shape=[
            sds((8, TILE), F32),
            sds((8, d), F32),
            sds((8, 2 * half), F32),
            sds((count, d), BF),
            sds((count, d), BF),
            sds((d // 2, half), BF),
            sds((d // 2, half), BF),
        ],
        scratch_shapes=[
            pltpu.VMEM(wu.shape, BF),
            pltpu.VMEM(wu.shape, BF),
            pltpu.VMEM(gp.shape, BF),
            pltpu.VMEM((n, seq, d), BF),
            pltpu.VMEM(wi.shape, BF),
            pltpu.VMEM((d, 2 * n * seq), BF),
            pltpu.VMEM((8, half), F32),
            pltpu.VMEM((2, n, seq, chunk), F32),
            pltpu.VMEM((2, 2 * n * seq, chunk), BF),
            pltpu.VMEM((d, chunk), BF),
            pltpu.SemaphoreType.DMA((4,)),
            pltpu.SemaphoreType.DMA((6,)),
        ],
        compiler_params=params(),
        cost_estimate=cost(17),
        name="loss_inner",
    )(me, at, lens4, pooled, queries, wp, fint, gp, *fin_nb, wi, wu, *packs)


def mid_bwd_kernel(lens, at_ref, g_ref, row_ref, gain_ref, hot_ref, lse_ref, tf_ref, *refs):
    hbm, packs0, packs1 = refs[:11], refs[11:15], refs[15:19]
    (dres_hbm, dattn_hbm), outs, scratch = refs[19:21], refs[21:25], refs[25:35]
    bufs, (wib_ref, wob_ref, d_ref, dres_ref, sem, sem0, sem1, sem2) = refs[35:46], refs[46:]
    da_ref = scratch[7]
    wi_ref, gpa_ref, gpb_ref, res_all, q, qt, k, v, ct, nb, ant = bufs
    b = pl.program_id(0)
    n = lse_ref.shape[0]
    copies = [pltpu.make_async_copy(x, y, sem.at[i]) for i, (x, y) in enumerate(zip(hbm, bufs))]
    copies0 = out_copies(at_ref[0], packs0, wob_ref, sem0)
    copies1 = join_copies(at_ref[0], packs1, wib_ref, sem1)

    def first(group):
        @pl.when(b == 0)
        def _():
            for c in group:
                c.wait()

    @pl.when(b == 0)
    def _():
        for c in copies[:2] + copies1 + copies[2:4] + copies0 + copies[4:]:
            c.start()

    first(copies[:2])
    _, seq, d = res_all.shape
    half = wi_ref.shape[1]
    chunk = d_ref.shape[2]
    steps = half // chunk
    parts = [(gp, w, c) for gp, w in ((gpa_ref, wi_ref), (gpb_ref, wib_ref)) for c in range(steps)]

    def scale(t):
        gp, _, c = parts[t]
        g = g_ref[pl.ds(b, 1), t * chunk : (t + 1) * chunk]
        d_ref[t % 2] = (gp[b, :, c * chunk : (c + 1) * chunk].astype(F32) * g).astype(BF)

    d_two = None
    scale(0)
    for t, (_, w, c) in enumerate(parts):
        if t + 1 == steps:
            first(copies[2:4] + copies1)
        if t + 1 < len(parts):
            scale(t + 1)
        one = mm(d_ref[t % 2], w[:, c * chunk : (c + 1) * chunk], NT)
        d_two = one if d_two is None else d_two + one
    res = res_all[b]
    inv = lax.rsqrt(jnp.mean(res * res, axis=-1, keepdims=True) + EPS)
    scaled = d_two * gain_ref[...]
    along = jnp.sum(scaled * res, axis=-1, keepdims=True)
    valid = lax.broadcasted_iota(jnp.int32, (seq, TILE), 0) < lens[b]
    vcol = valid.astype(F32)[:, :1]
    inv = inv * vcol
    d_res = vcol * row_ref[pl.ds(b, 1), :] + scaled * inv - res * (inv * inv * inv * along / d)
    here = pl.ds(pl.multiple_of(b * seq, seq), seq)
    dres_ref[here, :] = d_res
    d_attn = d_res.astype(BF)
    da_ref[here, :] = d_attn
    done = send_rows(b, n, dres_ref, dres_hbm, sem2.at[0]) + send_rows(b, n, da_ref, dattn_hbm, sem2.at[1])
    first(copies0 + copies[4:-1])
    ins = (q, qt, k, v, ct, lse_ref, nb, tf_ref, ant, hot_ref)
    attn_back(b, n, lens[b], at_ref[0] // 2, wob_ref[...], d_attn, ins, outs, scratch, copies[-1:])

    @pl.when(b == n - 1)
    def _():
        for c in done:
            c.wait()


def mid_bwd(lens, at, g, row, gain, hot, lse, tf, arrays, packs0, packs1):
    wi, _, _, res = arrays[:4]
    n, seq, d = res.shape
    half = wi.shape[1]
    width = packs0[0].shape[1] // 3
    outs, specs = back_outs(n, seq, width, d)
    more = [sds((n * seq, d), F32), sds((n * seq, d), BF)]
    return pl.pallas_call(
        mid_bwd_kernel,
        grid=(n,),
        in_specs=[SMEM_SPEC, SMEM_SPEC]
        + [const_spec(x.shape) for x in (g, row)]
        + [const_spec((1, d))]
        + [const_spec(x.shape) for x in (hot, lse, tf)]
        + [ANY] * 19,
        out_specs=[ANY] * 2 + specs,
        out_shape=more + outs,
        scratch_shapes=back_scratch(n, seq, width, d)
        + [pltpu.VMEM(x.shape, x.dtype) for x in arrays]
        + [
            pltpu.VMEM((d, half), BF),
            pltpu.VMEM((width, d), BF),
            pltpu.VMEM((2, seq, 512), BF),
            pltpu.VMEM((n * seq, d), F32),
            pltpu.SemaphoreType.DMA((11,)),
            pltpu.SemaphoreType.DMA((12,)),
            pltpu.SemaphoreType.DMA((4,)),
            pltpu.SemaphoreType.DMA((2, n)),
        ],
        compiler_params=params(),
        cost_estimate=cost(32),
        name="mid_bwd",
    )(lens, at, g, row, gain.reshape(1, d), hot, lse, tf, *arrays, *packs0, *packs1)


def input_kernel(at_ref, x_ref, dres_ref, gain_ref, ta_ref, tb_ref, wq, wk, wv, p0, p1, p2, p3, out_ref, w_ref, sem):
    @pl.when(pl.program_id(0) == 0)
    def _():
        run_copies(join_copies(at_ref[0], (p0, p1, p2, p3), w_ref, sem))

    width = wq.shape[1]
    d_one = mm(tb_ref[...], w_ref[...], NT)
    for i, w in enumerate((wq, wk, wv)):
        d_one = d_one + mm(ta_ref[:, width * i : width * (i + 1)], w[...], NT)
    x = x_ref[0].astype(F32)
    inv = lax.rsqrt(jnp.mean(x * x, axis=-1, keepdims=True) + EPS)
    scaled = d_one * gain_ref[...]
    along = jnp.sum(scaled * x, axis=-1, keepdims=True)
    out_ref[0] = dres_ref[...] + scaled * inv - x * (inv * inv * inv * along / x.shape[1])


def input_part(at, x, dres, gain, tok_a, tok_b, wq, wk, wv, packs):
    n, seq, d = x.shape
    width = wq.shape[1]
    rows = lambda cols: pl.BlockSpec((seq, cols), lambda b: (b, 0))
    return pl.pallas_call(
        input_kernel,
        grid=(n,),
        in_specs=[SMEM_SPEC, row_spec(x.shape), rows(d), const_spec((1, d)), rows(3 * width), rows(3 * width)]
        + [const_spec(wq.shape)] * 3
        + [ANY] * 4,
        out_specs=row_spec(x.shape),
        out_shape=sds(x.shape, F32),
        scratch_shapes=[pltpu.VMEM((d, 3 * width), BF), pltpu.SemaphoreType.DMA((4,))],
        compiler_params=params(),
        cost_estimate=cost(12),
        name="input_part",
    )(at, x, dres, gain.reshape(1, d), tok_a, tok_b, wq, wk, wv, *packs)


def layer_kernel(at_ref, res_ref, aa_ref, ab_ref, w_ref, p0, p1, p2, p3, out_ref, wb_ref, sem):
    @pl.when(pl.program_id(0) == 0)
    def _():
        run_copies(join_copies(at_ref[0], (p0, p1, p2, p3), wb_ref, sem))

    out_ref[0] = (res_ref[0] + mm(aa_ref[0], w_ref[...]) + mm(ab_ref[0], wb_ref[...])).astype(BF)


def layer_part(at, res, act_a, act_b, wu, packs):
    n, seq, d = res.shape
    return pl.pallas_call(
        layer_kernel,
        grid=(n,),
        in_specs=[SMEM_SPEC, row_spec(res.shape), row_spec(act_a.shape), row_spec(act_b.shape), const_spec(wu.shape)]
        + [ANY] * 4,
        out_specs=row_spec(res.shape),
        out_shape=sds(res.shape, BF),
        scratch_shapes=[pltpu.VMEM(wu.shape, BF), pltpu.SemaphoreType.DMA((4,))],
        compiler_params=params(),
        cost_estimate=cost(12),
        name="layer_part",
    )(at, res, act_a, act_b, wu, *packs)


def gain_row(prod):
    ones = jnp.ones((16, prod.shape[1]), BF)
    return sum(mm(ones, part, NT)[:1] for part in split3(prod))


def inner_done_kernel(at_ref, own_ref, near_ref, w_ref, out_ref, gain_ref):
    rows = own_ref.shape[0]
    core = at_ref[0] // 2
    halves = [own_ref[...].astype(F32), near_ref[...].astype(F32)]
    for half in range(2):
        one = jnp.where(core == half, halves[0], halves[1])
        at = slice(rows * half, rows * (half + 1))
        out_ref[at, :] = one
        gain_ref[:, at] = jnp.broadcast_to(gain_row(one * w_ref[at, :].astype(F32)), (8, rows))


def inner_done(at, own, near, w):
    d, half = w.shape
    chunk = 512
    cols = lambda r: pl.BlockSpec((r, chunk), lambda c: (0, c))
    return pl.pallas_call(
        inner_done_kernel,
        grid=(half // chunk,),
        in_specs=[SMEM_SPEC, cols(d // 2), cols(d // 2), cols(d)],
        out_specs=[cols(d), pl.BlockSpec((8, d), lambda c: (c, 0))],
        out_shape=[sds((d, half), F32), sds((8 * (half // chunk), d), F32)],
        compiler_params=params(20),
        cost_estimate=cost(5),
        name="inner_done",
    )(at, own, near, w)


def attn_done_kernel(half_ref, sum_ref, wq, wk, wv, *refs):
    q_ref, k_ref, v_ref, o_ref, gain_ref = refs[-5:]
    width = wq.shape[1]
    total = None
    for i, (w, out) in enumerate(((wq, q_ref), (wk, k_ref), (wv, v_ref))):
        one = sum_ref[:, width * i : width * (i + 1)].astype(F32)
        out[...] = one
        prod = one * w[...].astype(F32)
        total = prod if total is None else total + prod
    o_ref[...] = sum_ref[:, 3 * width :].astype(F32)
    gain_ref[...] = jnp.broadcast_to(gain_row(total), gain_ref.shape)


def attn_done(half, sums, wq, wk, wv, into=()):
    d, width = wq.shape
    rows = d // 2
    grad = sds((d, width), F32)
    block = pl.BlockSpec((rows, width), lambda b, half: (half[0], 0))
    across = pl.BlockSpec((width, rows), lambda b, half: (0, half[0]))
    return pl.pallas_call(
        attn_done_kernel,
        grid_spec=pltpu.PrefetchScalarGridSpec(
            num_scalar_prefetch=1,
            grid=(1,),
            in_specs=[pl.BlockSpec(sums.shape, lambda b, half: (0, 0))] + [block] * 3 + [ANY] * len(into),
            out_specs=[block] * 3 + [across, pl.BlockSpec((8, rows), lambda b, half: (0, 0))],
        ),
        out_shape=[grad, grad, grad, sds((width, d), F32), sds((8, rows), F32)],
        input_output_aliases={5 + i: i for i in range(len(into))},
        compiler_params=params(20),
        cost_estimate=cost(3),
        name="attn_done",
    )(half, sums, wq, wk, wv, *into)


def after(*xs):
    return lax.optimization_barrier(xs)


def swap(x, axis, bit, size):
    return lax.ppermute(x, axis, [(i, i ^ bit) for i in range(size)])


class Place:
    def __init__(self, chips, tensor):
        self.chips, self.tensor = chips, tensor
        self.chip = lax.axis_index("chip")
        self.core = lax.axis_index("core")
        self.ti = lax.axis_index("tensor")

    def across(self, x):
        return swap(x, "tensor", 1, self.tensor)

    def core_swap(self, x):
        return swap(x, "core", 1, 2)

    def share(self, x):
        return lax.all_to_all(x, ("chip", "core", "tensor"), 0, 0, tiled=True)

    def side(self, mine):
        return swap(mine, "chip", 1, self.chips)

    def spread(self, mine, side):
        return [mine, side, self.core_swap(mine), self.core_swap(side)]

    def exchange(self, x):
        rows, width = x.shape
        return lax.all_to_all(x.reshape(self.chips, rows // self.chips, width), "chip", 0, 0, tiled=True)

    def add(self, got):
        return jnp.sum(got.astype(F32), axis=0).astype(BF)

    def gather(self, x):
        got = lax.all_to_all(jnp.broadcast_to(x[None], (self.chips,) + x.shape), "chip", 0, 0, tiled=True)
        return got.reshape(-1, x.shape[1])

    def total(self, x):
        for i in range(self.chips.bit_length() - 1):
            x = x + swap(x, "chip", 1 << i, self.chips)
        return x


def body(
    mesh_shape,
    hidden_in,
    lengths,
    queries,
    positives,
    gain_attn,
    w_query,
    w_key,
    w_value,
    w_out,
    rel_table,
    gain_ffn,
    w_inner,
    w_outer,
    w_proj,
):
    pc = Place(mesh_shape["chip"], mesh_shape["tensor"])
    n, seq, d = hidden_in.shape
    half = w_inner.shape[1]
    width = w_query.shape[1]
    buckets = rel_table.shape[0]
    lens = lax.dynamic_slice_in_dim(lengths, pc.ti * n, n, 0)
    near_lens = lax.dynamic_slice_in_dim(lengths, (1 - pc.ti) * n, n, 0)
    lens4 = jnp.concatenate([lens, near_lens])
    at = (2 * pc.core + (pc.chip & 1)).reshape(1)
    devices = pc.chips * 2 * pc.tensor
    hot_t = jnp.asarray(np.pad(diag_onehot(buckets, False).T, ((0, TILE - buckets), (0, 0))), BF)
    hot_back = jnp.asarray(np.pad(diag_onehot(buckets, True), ((0, 0), (0, TILE - buckets))), BF)

    turned = rel_table.T
    packs = pack_weights(at, turned, w_query, w_key, w_value, w_out, w_inner, w_outer)
    y_attn = pc.across(packs[0])

    qf = queries.astype(F32)
    q_unit = (qf * lax.rsqrt(jnp.sum(qf * qf, axis=-1, keepdims=True) + EPS)).astype(BF)
    ints = jnp.stack([positives // 256, positives % 256, lens // 256, lens % 256], axis=1)
    ints = jnp.pad(ints.astype(BF), ((0, 0), (0, TILE - 4)))
    q_all = jnp.concatenate([q_unit, ints], axis=1)

    an, ant, q_a, qt_a, k_a, v_a, ctx_a, ctxt_a, lse_a, nb_a, tf_a = attn_own(
        lens, hidden_in, gain_attn, w_query, w_key, w_value, turned, hot_t
    )
    y_attn, an, q_all, *packs = after(y_attn, an, q_all, *packs[1:])
    y_inner, y_outer = [pc.across(p) for p in packs]
    x_attn = pc.side(y_attn)
    q_all = pc.share(jnp.broadcast_to(q_all[None], (devices,) + q_all.shape))
    x_attn, q_all = after(x_attn, q_all)
    p_attn = pc.spread(y_attn, x_attn)
    y_inner, an = after(y_inner, an)
    x_inner = pc.side(y_inner)
    q_b, qt_b, k_b, v_b, ctxt_b, lse_b, nb_b, tf_b, res, fin, fint, rsum, *fins = attn_other(
        lens, at, an, hot_t, hidden_in, ctx_a, w_out, gain_ffn, p_attn
    )
    y_inner, x_inner, y_outer, fin, *fins = after(y_inner, x_inner, y_outer, fin, *fins)
    x_outer = pc.side(y_outer)
    p_inner = pc.spread(y_inner, x_inner)
    fin_nb = [pc.across(f) for f in fins]
    act_a, gp_a, act_b, gp_b, asum, rsum = ffn_fwd(lens, at, fin, rsum, w_inner, w_outer, p_inner)
    y_outer, x_outer, asum, fin_nb[0] = after(y_outer, x_outer, asum, fin_nb[0])
    p_outer = pc.spread(y_outer, x_outer)
    pooled = pool(lens, at, asum, rsum, p_outer)[:n].astype(BF)

    sums_a, sums_b = asum[:, 0, :half].astype(BF), asum[:, 0, half:].astype(BF)
    sums = jnp.where(pc.ti > 0, jnp.stack([sums_b, sums_a]), jnp.stack([sums_a, sums_b]))
    msg = jnp.concatenate([jnp.broadcast_to(pooled[None], (2,) + pooled.shape), sums], axis=2)
    msg = jnp.broadcast_to(msg[None], (2 * pc.chips,) + msg.shape).reshape((devices,) + msg.shape[1:])
    got = pc.share(msg).reshape(devices * n, -1)
    pooled = got[:, :d]
    base = (2 * pc.chip + pc.core) * pc.tensor * n
    me = jnp.stack([base + pc.ti * n, base + pc.ti * n + 1, base + (1 - pc.ti) * n, base + (1 - pc.ti) * n + 1])
    loss8, row8, g8, d_rows, d_emb, gi_send, gi_keep = loss_all(
        me, at, lens4, pooled, q_all.reshape(devices * n, -1), w_proj, fint, gp_a, fin_nb, w_inner, w_outer, p_outer
    )
    query_loss = loss8[:n, 0]

    inner_half, gp_a = after(gi_keep + pc.core_swap(gi_send), gp_a)
    inner_parts = pc.exchange(inner_half)
    arrays = [w_inner, gp_a, gp_b, res, q_b, qt_b, k_b, v_b, ctxt_b, nb_b, ant]
    d_res, d_attn, tok_b, send_b, keep_b, table_b = mid_bwd(
        lens, at, g8, row8, gain_ffn, hot_back, lse_b, tf_b, arrays, p_attn, p_inner
    )
    inner_part, d_attn = after(pc.add(inner_parts), d_attn)
    inner_all = pc.gather(inner_part)
    half_b, d_attn = after(keep_b + pc.core_swap(send_b), d_attn)
    far_part = pc.across(half_b)
    tok_a, send_a, keep_a, table_a = attn_bwd(
        lens, at, d_attn.reshape(n, seq, d), w_out, hot_back, lse_a, tf_a, q_a, qt_a, k_a, v_a, ctxt_a, nb_a, ant
    )
    proj_grad = mm(pooled, d_emb, TN)
    outer_grad = mm(got[:, d:], d_rows, TN)
    inner_all, far_part, far_table, send_a, proj_grad, outer_grad = after(
        inner_all, far_part, pc.across(table_b), send_a, proj_grad, outer_grad
    )
    table = table_a + far_table
    near_a, near_table = after(pc.core_swap(send_a), pc.core_swap(table))
    parts = pc.exchange(keep_a + far_part + near_a)
    input_grad = input_part(at, hidden_in, d_res, gain_attn, tok_a, tok_b, w_query, w_key, w_value, p_attn)
    inner_sum, gain_ffn_part = inner_done(at, inner_all, pc.core_swap(inner_all), w_inner)
    layer = layer_part(at, res, act_a, act_b, w_outer, p_outer)
    parts, input_grad, layer = after(parts, input_grad, layer)
    attn_all = pc.gather(pc.add(parts))
    table_sum = pc.total(table + near_table)
    gain_ffn_part = jnp.sum(gain_ffn_part[::8], axis=0)
    gain_ffn_grad = (gain_ffn_part + pc.across(gain_ffn_part)) / gain_ffn
    attn_all, gain_ffn_grad, table_sum, inner_sum = after(attn_all, gain_ffn_grad, table_sum, inner_sum)
    half = pc.core.reshape(1)
    near = pc.core_swap(attn_all)
    *grads, gain_own = attn_done(half, attn_all, w_query, w_key, w_value)
    near, *grads = after(near, *grads)
    gain_own = gain_own[0] + pc.across(gain_own[0])
    *grads, _ = attn_done(1 - half, near, w_query, w_key, w_value, grads)
    gain_own, *grads = after(gain_own, *grads)
    q_grad, k_grad, v_grad, out_grad = grads
    gain_near = pc.core_swap(gain_own)
    gain_attn_grad = jnp.where(
        pc.core > 0, jnp.concatenate([gain_near, gain_own]), jnp.concatenate([gain_own, gain_near])
    ) / gain_attn
    return (
        layer,
        query_loss,
        input_grad,
        gain_attn_grad,
        q_grad,
        k_grad,
        v_grad,
        out_grad,
        table_sum[: rel_table.shape[1], :buckets].T,
        gain_ffn_grad,
        inner_sum,
        outer_grad,
        proj_grad,
    )


def solution(mesh):
    dp, tensor = mesh.shape["dp"], mesh.shape["tensor"]
    fine = jax.sharding.Mesh(mesh.devices.reshape(dp // 2, 2, tensor), ("chip", "core", "tensor"))
    rows = ("chip", "core")
    both = rows + ("tensor",)
    return jax.shard_map(
        functools.partial(body, dict(fine.shape)),
        mesh=fine,
        in_specs=(
            P(both, None, None),
            P(rows),
            P(both, None),
            P(both),
            P(),
            P(None, "tensor"),
            P(None, "tensor"),
            P(None, "tensor"),
            P("tensor", None),
            P(None, "tensor"),
            P(),
            P(None, "tensor"),
            P("tensor", None),
            P(),
        ),
        out_specs=(
            P(both, None, None),
            P(both),
            P(both, None, None),
            P(),
            P(None, "tensor"),
            P(None, "tensor"),
            P(None, "tensor"),
            P("tensor", None),
            P(None, "tensor"),
            P(),
            P(None, "tensor"),
            P("tensor", None),
            P(),
        ),
        check_vma=False,
    )
```

```python
import functools

import numpy as np

import jax
import jax.numpy as jnp
from jax import lax
from jax.experimental import pallas as pl
from jax.experimental.pallas import tpu as pltpu
from jax.sharding import PartitionSpec as P

LARGE_STEPS = (12, 16, 23, 32, 46, 64, 91)
SHARPNESS = 0.02
LOSS_SCALE = 256.0
EPS = 1e-06
NEG = -1e30
BF = jnp.bfloat16
F32 = jnp.float32
TILE = 128
BUCKETS = 32
GELU_A = 0.7978845608028654
GELU_B = 0.044715
MIB = 1024 * 1024

NN = (((1,), (0,)), ((), ()))
NT = (((1,), (1,)), ((), ()))
TN = (((0,), (0,)), ((), ()))


def mm(a, b, dims=NN):
    return lax.dot_general(a, b, dims, preferred_element_type=F32)


def bucket_of(r):
    a = np.abs(r)
    far = 8 + sum((a >= t).astype(np.int32) for t in LARGE_STEPS)
    return np.where(r > 0, 16, 0) + np.where(a < 8, a, far)


def diag_onehot(buckets, back):
    lane = np.arange(2 * TILE)
    at = lane - TILE + 1 if back else TILE - 1 - lane
    idx = np.concatenate([bucket_of(TILE * d + at) for d in (-1, 0, 1)])
    hot = (idx[:, None] == np.arange(buckets)[None, :]).astype(np.float32)
    hot[2 * TILE - 1 :: 2 * TILE] = 0.0
    return hot


def params(mib=60):
    return pltpu.CompilerParams(vmem_limit_bytes=mib * MIB)


def cost(us):
    return pl.CostEstimate(flops=0, bytes_accessed=int(us * 3.6e6), transcendentals=0)

ANY = pl.BlockSpec(memory_space=pl.ANY)
SMEM_SPEC = pl.BlockSpec(memory_space=pltpu.SMEM)


def const_spec(shape):
    zeros = (0,) * len(shape)
    return pl.BlockSpec(tuple(shape), lambda b: zeros, pipeline_mode=pl.Buffered(1))


def out_const(shape):
    zeros = (0,) * len(shape)
    return pl.BlockSpec(tuple(shape), lambda b: zeros)


def row_spec(shape):
    tail = (0,) * (len(shape) - 1)
    return pl.BlockSpec((1,) + tuple(shape[1:]), lambda b: (b,) + tail)


def sds(shape, dtype):
    return jax.ShapeDtypeStruct(tuple(shape), dtype)


def split3(t):
    hi = t.astype(BF)
    rest = t - hi.astype(F32)
    mid = rest.astype(BF)
    return hi, mid, (rest - mid.astype(F32)).astype(BF)


def run_copies(copies):
    for c in copies:
        c.start()
    for c in copies:
        c.wait()


def out_pieces(width, d):
    rows, tall = width // 4, width // 6
    rest = rows - tall
    out = [((0, tall, 0, d), (0, tall, 0, d))]
    for i in range(2):
        out.append(((tall, rest, i * width, width), (i * rest, rest, d, width)))
    return out


def pack_kernel(at_ref, tab_ref, wq, wk, wv, wo, wi, wu, s0, s1, s2, sem):
    at = at_ref[0]
    d, width = wq.shape
    rows = d // 4

    def part(w, dst, i):
        count = w.shape[0] // 4
        src = w.at[pl.ds(pl.multiple_of(at * count, count), count)]
        return pltpu.make_async_copy(src, dst, sem.at[i])

    copies = [part(w, s0.at[pl.ds(0, rows), width * i : width * (i + 1)], i) for i, w in enumerate((wq, wk, wv))]
    copies += [part(wi, s1, 3), part(wu, s2, 4)]
    for i, (a, b) in enumerate(out_pieces(width, d)):
        src = wo.at[pl.ds(pl.multiple_of(at * (width // 4) + a[0], 32), a[1]), a[2] : a[2] + a[3]]
        dst = s0.at[pl.ds(rows + 16 + b[0], b[1]), b[2] : b[2] + b[3]]
        copies.append(pltpu.make_async_copy(src, dst, sem.at[5 + i]))
    for c in copies:
        c.start()
    s0[rows : rows + 16, :] = jnp.zeros((16, s0.shape[1]), BF)
    heads, buckets = tab_ref.shape
    for k, t in enumerate(split3(tab_ref[...])):
        s0[rows : rows + heads, TILE * k : TILE * k + buckets] = t
    for c in copies:
        c.wait()


def pack_weights(at, table, wq, wk, wv, wo, wi, wu):
    d, half = wi.shape
    width = wq.shape[1]
    vm = pl.BlockSpec(memory_space=pltpu.VMEM)
    return pl.pallas_call(
        pack_kernel,
        in_specs=[SMEM_SPEC, vm] + [ANY] * 6,
        out_specs=[vm] * 3,
        out_shape=[
            sds((d // 4 + 16 + width // 6, 3 * width), BF),
            sds((d // 4, half), BF),
            sds((half // 4, d), BF),
        ],
        scratch_shapes=[pltpu.SemaphoreType.DMA((8,))],
        compiler_params=params(),
        cost_estimate=cost(3),
        name="pack_weights",
    )(at, table, wq, wk, wv, wo, wi, wu)


def quarter_spots(at):
    core, xb = at // 2, at % 2
    return [at, 2 * core + 1 - xb, 2 * (1 - core) + xb, 2 * (1 - core) + 1 - xb]


def out_copies(at, packs, dst, sem):
    width, d = dst.shape
    base = d // 4 + 16
    out = []
    for i, (p, s) in enumerate(zip(packs, quarter_spots(at))):
        for j, (a, b) in enumerate(out_pieces(width, d)):
            src = p.at[pl.ds(base + b[0], b[1]), b[2] : b[2] + b[3]]
            to = dst.at[pl.ds(pl.multiple_of(s * (width // 4) + a[0], 32), a[1]), a[2] : a[2] + a[3]]
            out.append(pltpu.make_async_copy(src, to, sem.at[3 * i + j]))
    return out


def join_copies(at, packs, dst, sem):
    rows = dst.shape[0] // 4
    out = []
    for i, (p, s) in enumerate(zip(packs, quarter_spots(at))):
        to = dst.at[pl.ds(pl.multiple_of(s * rows, rows), rows)]
        out.append(pltpu.make_async_copy(p.at[pl.ds(0, rows)], to, sem.at[i]))
    return out


EXTRA = 16


def key_extras(length, rows):
    row = lax.broadcasted_iota(jnp.int32, (rows, TILE), 0)
    lane = lax.broadcasted_iota(jnp.int32, (rows, TILE), 1) & 63
    blk = (lane - 1) & 3
    hot = (lane >= 1) & (lane < 13) & (blk == row // TILE)
    one = ((lane == 0) & (row >= length)) | hot | ((lane >= 13) & (lane < EXTRA))
    return jnp.where(one, 1.0, 0.0)


def far_rows(tf_ref, h, seq):
    row = lax.broadcasted_iota(jnp.int32, (EXTRA, seq), 0)
    diff = ((row - 1) & 3) - lax.broadcasted_iota(jnp.int32, (EXTRA, seq), 1) // TILE
    out = jnp.where(row == 0, NEG, 0.0)
    last, mid = BUCKETS - 1, BUCKETS // 2 - 1
    for k in range(3):
        mine = (row >= 1 + 4 * k) & (row < 5 + 4 * k)
        out = out + jnp.where(mine & (diff >= 2), tf_ref[k, h : h + 1, last : last + 1], 0.0)
        out = out + jnp.where(mine & (diff <= -2), tf_ref[k, h : h + 1, mid : mid + 1], 0.0)
    return out


def stack_rows(e, main, extra):
    pad = jnp.zeros((64 - extra.shape[0], extra.shape[1]), BF)
    return jnp.concatenate([main, extra, pad] if e == 0 else [extra, pad, main], axis=0)


def near_bias(s, nb_ref, h, ib):
    rows = []
    for bj in range(s.shape[0] // TILE):
        parts = []
        for t in range(2):
            piece = s[TILE * bj : TILE * (bj + 1), TILE * t : TILE * (t + 1)]
            d = bj - (2 * ib + t)
            parts.append(piece + nb_ref[3 * h + d + 1] if abs(d) <= 1 else piece)
        rows.append(jnp.concatenate(parts, axis=1))
    return rows


def set_bias(parts, hot_ref, tf_ref, nb_ref):
    for k in range(3):
        tf_ref[k] = parts[k].astype(F32)
    hot = hot_ref[...]
    bv = mm(parts[0], hot) + mm(parts[1], hot) + mm(parts[2], hot)
    for t in range(nb_ref.shape[0]):
        h, k = t // 3, t % 3
        v = jnp.broadcast_to(bv[h : h + 1, 2 * TILE * k : 2 * TILE * (k + 1)], (TILE, 2 * TILE))
        nb_ref[t] = pltpu.roll(v, TILE + 1, 1, stride=1, stride_axis=0)[:, :TILE]


def attn_rows(an, length, ws, outs, nb_ref, tf_ref, s_ref, p_ref, between=None):
    q_ref, qt_ref, k_ref, v_ref, ctx_ref, ctxt_ref, lse_ref = outs
    seq = an.shape[0]
    width = q_ref.shape[2]
    for ref, w in zip((q_ref, k_ref), ws):
        ref[0] = mm(an, w[...]).astype(BF)
    kx = key_extras(length, seq)
    lane = lax.broadcasted_iota(jnp.int32, (seq, TILE), 1)
    blocks = [(h, ib) for h in range(width // 64) for ib in range(seq // 256)]
    keys, queries, values, tops, rows = {}, {}, {}, {}, {}

    def prepare(h):
        pair, e = h // 2, h % 2
        cols = slice(TILE * pair, TILE * (pair + 1))
        if e == 0:
            qt_ref[0, cols, :] = jnp.transpose(q_ref[0, :, cols])
        mine = lane < 64 if e == 0 else lane >= 64
        keys[h] = jnp.where(mine, k_ref[0, :, cols].astype(F32), kx).astype(BF)
        qt = qt_ref[0, 64 * h : 64 * (h + 1), :]
        queries[h] = stack_rows(e, qt, far_rows(tf_ref, h, seq).astype(BF))

    def start(t):
        h, ib = blocks[t]
        if ib == 0:
            prepare(h)
        s = mm(keys[h], queries[h][:, 256 * ib : 256 * (ib + 1)])
        return near_bias(s, nb_ref, h, ib)

    def score(t, bj, pieces):
        piece = pieces[bj]
        s_ref[t % 2, TILE * bj : TILE * (bj + 1), :] = piece
        m = jnp.max(piece.reshape(TILE // 8, 8, 256), axis=0)
        tops[t] = m if bj == 0 else jnp.maximum(tops[t], m)
        if bj == seq // TILE - 1:
            tops[t] = jnp.max(tops[t], axis=0, keepdims=True)

    def soft(t, bj):
        h, ib = blocks[t]
        at = slice(TILE * bj, TILE * (bj + 1))
        p_ref[h % 2, at, 256 * ib : 256 * (ib + 1)] = jnp.exp(s_ref[t % 2, at, :] - tops[t]).astype(BF)

    def combine(h):
        per = seq // 256
        top = jnp.concatenate([tops[per * h + i] for i in range(per)], axis=1)
        if h % 2 == 0:
            values[h // 2] = jnp.transpose(v_ref[0, :, TILE * (h // 2) : TILE * (h // 2 + 1)])
        vt = values[h // 2][64 * (h % 2) : 64 * (h % 2 + 1), :]
        got = mm(jnp.concatenate([vt, jnp.ones((16, seq), BF)], axis=0), p_ref[h % 2])
        total = got[64:65]
        lse_ref[0, h : h + 1, :] = top + jnp.log(total)
        rows[h] = got[:64] * (1.0 / total)
        if h % 2 == 1:
            pair = h // 2
            cols = slice(TILE * pair, TILE * (pair + 1))
            ct = jnp.concatenate([rows[h - 1], rows[h]], axis=0).astype(BF)
            ctxt_ref[0, cols, :] = ct
            ctx_ref[0, :, cols] = jnp.transpose(ct)

    for t in range(len(blocks) + 1):
        if t < len(blocks):
            pieces = start(t)
            for bj in range(seq // TILE):
                score(t, bj, pieces)
        if t == 0:
            v_ref[0] = mm(an, ws[2][...]).astype(BF)
        if t == 5 and between is not None:
            between()
        if t > 0:
            for bj in range(seq // TILE):
                soft(t - 1, bj)
            if blocks[t - 1][1] == seq // 256 - 1:
                combine(blocks[t - 1][0])


def attn_own_kernel(lens, x_ref, gain_ref, wq, wk, wv, tab_ref, hot_ref, an_ref, ant_ref, *refs):
    outs, (nb_ref, tf_ref, s_ref, p_ref) = refs[:7], refs[7:]
    b = pl.program_id(0)

    @pl.when(b == 0)
    def _():
        heads, buckets = tab_ref.shape
        wide = jnp.concatenate([tab_ref[...], jnp.zeros((heads, TILE - buckets), F32)], axis=1)
        wide = jnp.concatenate([wide, jnp.zeros((16 - heads, TILE), F32)], axis=0)
        set_bias(split3(wide), hot_ref, tf_ref, nb_ref)

    x = x_ref[0].astype(F32)
    inv = lax.rsqrt(jnp.mean(x * x, axis=-1, keepdims=True) + EPS)
    an = (x * inv * gain_ref[...]).astype(BF)
    an_ref[0] = an
    ant_ref[...] = jnp.transpose(an)
    attn_rows(an, lens[b], (wq, wk, wv), outs, nb_ref, tf_ref, s_ref, p_ref)


def attn_other_kernel(lens, at_ref, an_ref, hot_ref, gain_ref, x_hbm, ca_hbm, wo_hbm, p0, p1, p2, p3, *refs):
    outs, (nb_ref, tf_ref, res_ref, fin_ref, fint_ref, rsum_ref, f0_ref, f1_ref) = list(refs[:6]), refs[6:14]
    (s_ref, p_ref, w_ref, tab_ref, wb_ref, c_ref, x_ref, ca_ref, wo_ref, sem, sem1, sem2) = refs[14:]
    outs.insert(4, c_ref)
    b = pl.program_id(0)
    late = out_copies(at_ref[0], (p0, p1, p2, p3), wb_ref, sem1)
    moves = ((x_hbm, x_ref), (ca_hbm, ca_ref), (wo_hbm, wo_ref))
    more = [pltpu.make_async_copy(x, y, sem2.at[i]) for i, (x, y) in enumerate(moves)]

    @pl.when(b == 0)
    def _():
        rows = w_ref.shape[0] // 4
        copies = join_copies(at_ref[0], (p0, p1, p2, p3), w_ref, sem)
        copies.append(pltpu.make_async_copy(p0.at[pl.ds(rows, 16)], tab_ref, sem.at[4]))
        for c in copies + more + late:
            c.start()
        for c in copies:
            c.wait()
        parts = [tab_ref[:, TILE * k : TILE * (k + 1)] for k in range(3)]
        set_bias(parts, hot_ref, tf_ref, nb_ref)
        for c in more:
            c.wait()

    width = outs[0].shape[2]
    ws = [w_ref.at[:, width * k : width * (k + 1)] for k in range(3)]

    def between():
        res_ref[0] = x_ref[b].astype(F32) + mm(ca_ref[b], wo_ref[...])

    attn_rows(an_ref[0], lens[b], ws, outs, nb_ref, tf_ref, s_ref, p_ref, between)

    @pl.when(b == 0)
    def _():
        for c in late:
            c.wait()

    res = res_ref[0] + mm(outs[4][0], wb_ref[...])
    res_ref[0] = res
    inv = lax.rsqrt(jnp.mean(res * res, axis=-1, keepdims=True) + EPS)
    fin = (res * inv * gain_ref[...]).astype(BF)
    fin_ref[0] = fin
    for i, f_ref in enumerate((f0_ref, f1_ref)):

        @pl.when(b == i)
        def _():
            f_ref[0] = fin

    vcol = (lax.broadcasted_iota(jnp.int32, (res.shape[0], TILE), 0) < lens[b]).astype(F32)[:, :1]
    fint_ref[...] = jnp.transpose((fin.astype(F32) * vcol).astype(BF))
    rsum_ref[0] = jnp.sum(res * vcol, axis=0, keepdims=True)


def attn_outs(n, seq, width):
    heads = width // 64
    tok, turned = sds((n, seq, width), BF), sds((n, width, seq), BF)
    rows = [tok, turned, tok, tok, tok, turned, sds((n, 8, seq), F32)]
    flat = [sds((3 * heads, TILE, TILE), F32), sds((3, 16, TILE), F32)]
    scratch = [pltpu.VMEM((2, seq, 256), F32), pltpu.VMEM((2, seq, seq), BF)]
    return rows + flat, [row_spec(o.shape) for o in rows] + [out_const(o.shape) for o in flat], scratch


def attn_own(lens, x, gain, wq, wk, wv, table, hot):
    n, seq, d = x.shape
    outs, specs, scratch = attn_outs(n, seq, wq.shape[1])
    return pl.pallas_call(
        attn_own_kernel,
        grid=(n,),
        in_specs=[SMEM_SPEC, row_spec(x.shape), const_spec((1, d))]
        + [const_spec(wq.shape)] * 3
        + [const_spec(table.shape), const_spec(hot.shape)],
        out_specs=[row_spec(x.shape), pl.BlockSpec((d, seq), lambda b: (0, b))] + specs,
        out_shape=[sds((n, seq, d), BF), sds((d, n * seq), BF)] + outs,
        scratch_shapes=scratch,
        compiler_params=params(),
        cost_estimate=cost(12),
        name="attn_own",
    )(lens, x, gain.reshape(1, d), wq, wk, wv, table, hot)


def attn_other(lens, at, an, hot, x, ctx_a, wo, gain, packs):
    n, seq, d = an.shape
    width = wo.shape[0]
    outs, specs, scratch = attn_outs(n, seq, width)
    del outs[4], specs[4]
    more = [sds((n, seq, d), F32), sds((n, seq, d), BF), sds((d, n * seq), BF), sds((n, 1, d), F32)]
    more_specs = [row_spec(o.shape) for o in more]
    more_specs[2] = pl.BlockSpec((d, seq), lambda b: (0, b))
    more += [sds((1, seq, d), BF)] * n
    more_specs += [out_const((1, seq, d))] * n
    return pl.pallas_call(
        attn_other_kernel,
        grid=(n,),
        in_specs=[SMEM_SPEC, SMEM_SPEC, row_spec(an.shape), const_spec(hot.shape), const_spec((1, d))]
        + [ANY] * 7,
        out_specs=specs + more_specs,
        out_shape=outs + more,
        scratch_shapes=scratch
        + [
            pltpu.VMEM((d, 3 * width), BF),
            pltpu.VMEM((16, 3 * width), BF),
            pltpu.VMEM(wo.shape, BF),
            pltpu.VMEM((1, seq, width), BF),
            pltpu.VMEM(x.shape, BF),
            pltpu.VMEM(ctx_a.shape, BF),
            pltpu.VMEM(wo.shape, BF),
            pltpu.SemaphoreType.DMA((5,)),
            pltpu.SemaphoreType.DMA((12,)),
            pltpu.SemaphoreType.DMA((3,)),
        ],
        compiler_params=params(),
        cost_estimate=cost(15),
        name="attn_other",
    )(lens, at, an, hot, gain, x, ctx_a, wo, *packs)


def attn_back(b, n, length, core, w, d_attn, ins, outs, scratch, late):
    (q_ref, qt_ref, k_ref, v_ref, ct_ref, lse_ref, nb_ref, tf_ref, ant_ref, hot_ref) = ins
    (all_hbm, send_ref, keep_ref, table_ref) = outs
    (dc_ref, dct_ref, t_ref, fsum_ref, p_ref, ds_ref, all_ref, da_ref, go_ref, out_sem) = scratch
    seq, width = q_ref.shape[1], q_ref.shape[2]
    heads = width // 64
    nblk = seq // TILE
    here = pl.ds(pl.multiple_of(b * seq, seq), seq)

    @pl.when(b == 0)
    def _():
        t_ref[...] = jnp.zeros_like(t_ref)
        fsum_ref[...] = jnp.zeros_like(fsum_ref)
        table_ref[...] = jnp.zeros_like(table_ref)

    dct_ref[...] = mm(w, d_attn, NT).astype(BF)
    dc_ref[...] = jnp.transpose(dct_ref[...])
    kx = key_extras(length, seq)
    lane = lax.broadcasted_iota(jnp.int32, (seq, TILE), 1)
    vx = jnp.where((lane & 63) < 3, 1.0, 0.0)
    keys, values, queries, grads, turned = {}, {}, {}, {}, {}

    def prepare(h):
        pair, e = h // 2, h % 2
        cols = slice(TILE * pair, TILE * (pair + 1))
        mine = lane < 64 if e == 0 else lane >= 64
        if e == 0:
            turned[pair] = jnp.transpose(k_ref[b, :, cols])
        keys[h] = jnp.where(mine, k_ref[b, :, cols].astype(F32), kx).astype(BF)
        values[h] = jnp.where(mine, v_ref[b, :, cols].astype(F32), vx).astype(BF)
        at = slice(64 * h, 64 * (h + 1))
        lse = split3(-lse_ref[b, h : h + 1, :])
        extra = far_rows(tf_ref, h, seq)
        row = lax.broadcasted_iota(jnp.int32, (EXTRA, seq), 0)
        for k in range(3):
            extra = jnp.where(row == 13 + k, lse[k].astype(F32), extra)
        queries[h] = stack_rows(e, qt_ref[b, at, :], extra.astype(BF))
        along = jnp.sum(dct_ref[at, :].astype(F32) * ct_ref[b, at, :].astype(F32), axis=0, keepdims=True)
        extra = jnp.zeros((EXTRA, seq), F32)
        for k, part in enumerate(split3(-along)):
            extra = jnp.where(row == k, part.astype(F32), extra)
        grads[h] = stack_rows(e, dct_ref[at, :], extra.astype(BF))

    def block(h, ib):
        pair, e = h // 2, h % 2
        at = slice(256 * ib, 256 * (ib + 1))
        to = slice(seq * e + 256 * ib, seq * e + 256 * (ib + 1))
        s = mm(keys[h], queries[h][:, at])
        dp = mm(values[h], grads[h][:, at])
        near, far = {}, {}
        for bj, piece in enumerate(near_bias(s, nb_ref, h, ib)):
            rows = slice(TILE * bj, TILE * (bj + 1))
            p = jnp.exp(piece)
            ds = p * dp[rows, :]
            p_ref[pair % 2, rows, to] = p.astype(BF)
            ds_ref[pair % 2, rows, to] = ds.astype(BF)
            for t in range(2):
                d = bj - (2 * ib + t)
                one = ds[:, TILE * t : TILE * (t + 1)]
                if abs(d) <= 1:
                    near[d] = near[d] + one if d in near else one
                else:
                    one = jnp.sum(one.reshape(TILE // 8, 8, TILE), axis=0)
                    side = 1 if d > 0 else 0
                    far[side] = far[side] + one if side in far else one
        for d, one in near.items():
            t_ref[3 * h + d + 1] += one
        for side, one in far.items():
            fsum_ref[2 * h + side] += one

    def finish(pair, part):
        slot = pair % 2
        cols = slice(TILE * pair, TILE * (pair + 1))
        if part < 2:
            src, rhs = ((p_ref, dc_ref[:, cols]), (ds_ref, q_ref[b, :, cols]))[part]
            one = jnp.where(lane < 64, mm(src[slot, :, :seq], rhs), mm(src[slot, :, seq:], rhs)).astype(BF)
            base = width * (2 - part)
            all_ref[here, base + TILE * pair : base + TILE * (pair + 1)] = one
        if part == 2:
            kt = turned[pair]
            dqt = [mm(kt[64 * e : 64 * (e + 1), :], ds_ref[slot, :, seq * e : seq * (e + 1)]) for e in range(2)]
            one = jnp.transpose(jnp.concatenate(dqt, axis=0).astype(BF))
            all_ref[here, TILE * pair : TILE * (pair + 1)] = one

    for pair in range(heads // 2):
        step = 0
        for e in range(2):
            prepare(2 * pair + e)
            for ib in range(seq // 256):
                block(2 * pair + e, ib)
                if pair > 0 and step < 3:
                    finish(pair - 1, step)
                step += 1
    for part in range(3):
        finish(heads // 2 - 1, part)
    done = send_rows(b, n, all_ref, all_hbm, out_sem)

    @pl.when(b == n - 1)
    def _():
        for c in late:
            c.wait()
        rows = ant_ref.shape[0] // 2
        out = None
        for i in range(n):
            one = mm(ct_ref[i], da_ref[seq * i : seq * (i + 1), :])
            out = one if out is None else out + one
        go_ref[:width, :] = out[:, :width].astype(BF)
        go_ref[width:, :] = out[:, width:].astype(BF)
        for ref, half in ((send_ref, 1 - core), (keep_ref, core)):
            at = pl.ds(pl.multiple_of(half * rows, rows), rows)
            ref[:, : 3 * width] = mm(ant_ref[at, :], all_ref[...]).astype(BF)
            ref[:, 3 * width :] = go_ref[at, :]
        turn = lax.broadcasted_iota(jnp.int32, (TILE, TILE), 0) + lax.broadcasted_iota(jnp.int32, (TILE, TILE), 1)
        turn = jnp.where(turn == TILE - 1, 1.0, 0.0).astype(BF)
        tiles = t_ref.shape[0]
        hi, lo, _ = split3(t_ref[...].reshape(tiles * TILE, TILE))
        back = mm(jnp.concatenate([hi, lo], axis=1), jnp.concatenate([turn, turn], axis=0))
        diag = []
        for t in range(tiles):
            x = jnp.concatenate([back[TILE * t : TILE * (t + 1)], jnp.zeros((TILE, TILE), F32)], axis=1)
            x = pltpu.roll(x, 0, 1, stride=1, stride_axis=0)
            diag.append(jnp.sum(x, axis=0, keepdims=True))
        lines = [jnp.concatenate(diag[3 * h : 3 * h + 3], axis=1) for h in range(heads)]
        lines.append(jnp.zeros((16 - heads, lines[0].shape[1]), F32))
        near = [mm(part, hot_ref[...]) for part in split3(jnp.concatenate(lines, axis=0))]
        spot = lax.broadcasted_iota(jnp.int32, (1, TILE), 1)
        for h in range(heads):
            one = near[0][h : h + 1] + near[1][h : h + 1] + near[2][h : h + 1]
            for side, bucket in ((0, BUCKETS // 2 - 1), (1, BUCKETS - 1)):
                far = jnp.sum(jnp.sum(fsum_ref[2 * h + side], axis=0, keepdims=True), axis=1, keepdims=True)
                one = one + jnp.where(spot == bucket, far, 0.0)
            table_ref[h : h + 1, :] = one
        for c in done:
            c.wait()


def send_rows(b, n, src, dst, sem):
    rows = src.shape[0] // n
    copies = [pltpu.make_async_copy(src.at[pl.ds(i * rows, rows)], dst.at[pl.ds(i * rows, rows)], sem.at[i]) for i in range(n)]
    for i, c in enumerate(copies):

        @pl.when(b == i)
        def _():
            c.start()

    return copies


def back_outs(n, seq, width, d):
    half = sds((d // 2, 4 * width), BF)
    outs = [sds((n * seq, 3 * width), BF), half, half, sds((8, TILE), F32)]
    return outs, [ANY] + [out_const(o.shape) for o in outs[1:]]


def back_scratch(n, seq, width, d):
    heads = width // 64
    return [
        pltpu.VMEM((seq, width), BF),
        pltpu.VMEM((width, seq), BF),
        pltpu.VMEM((3 * heads, TILE, TILE), F32),
        pltpu.VMEM((2 * heads, 8, TILE), F32),
        pltpu.VMEM((2, seq, 2 * seq), BF),
        pltpu.VMEM((2, seq, 2 * seq), BF),
        pltpu.VMEM((n * seq, 3 * width), BF),
        pltpu.VMEM((n * seq, d), BF),
        pltpu.VMEM((d, width), BF),
        pltpu.SemaphoreType.DMA((n,)),
    ]


def attn_bwd_kernel(lens, at_ref, da_blk, wo_ref, hot_ref, lse_ref, tf_ref, *refs):
    hbm, outs, scratch = refs[:7], refs[7:11], refs[11:21]
    bufs, sem = refs[21:28], refs[28]
    b = pl.program_id(0)
    n = da_blk.shape[0] * lse_ref.shape[0]
    copies = [pltpu.make_async_copy(x, y, sem.at[i]) for i, (x, y) in enumerate(zip(hbm, bufs))]

    @pl.when(b == 0)
    def _():
        for c in copies:
            c.start()
        for c in copies[:-1]:
            c.wait()

    q, qt, k, v, ct, nb, ant = bufs
    ins = (q, qt, k, v, ct, lse_ref, nb, tf_ref, ant, hot_ref)
    seq = da_blk.shape[1]
    scratch[7][pl.ds(pl.multiple_of(b * seq, seq), seq), :] = da_blk[0]
    attn_back(b, n, lens[b], at_ref[0] // 2, wo_ref[...], da_blk[0], ins, outs, scratch, copies[-1:])


def attn_bwd(lens, at, d_attn, wo, hot, lse, tf, *arrays):
    n, seq, d = d_attn.shape
    width = wo.shape[0]
    outs, specs = back_outs(n, seq, width, d)
    return pl.pallas_call(
        attn_bwd_kernel,
        grid=(n,),
        in_specs=[SMEM_SPEC, SMEM_SPEC, row_spec(d_attn.shape)]
        + [const_spec(x.shape) for x in (wo, hot, lse, tf)]
        + [ANY] * 7,
        out_specs=specs,
        out_shape=outs,
        scratch_shapes=back_scratch(n, seq, width, d)
        + [pltpu.VMEM(x.shape, x.dtype) for x in arrays]
        + [pltpu.SemaphoreType.DMA((7,))],
        compiler_params=params(),
        cost_estimate=cost(16),
        name="attn_bwd",
    )(lens, at, d_attn, wo, hot, lse, tf, *arrays)


def gelu_parts(v):
    v2 = v * v
    half = 0.5 + 0.5 * jnp.tanh(v * (GELU_A + (GELU_A * GELU_B) * v2))
    act = v * half
    return act, half + (act - act * half) * (2.0 * GELU_A + (6.0 * GELU_A * GELU_B) * v2)


def ffn_fwd_kernel(lens, at_ref, fin_ref, rs_ref, wi_ref, wu_ref, p0, p1, p2, p3, *refs):
    (act_ref, gp_ref, actb_ref, gpb_ref, asum_ref, rsum_ref) = refs[:6]
    (wib_ref, wu_buf, v_ref, sem1, sem2) = refs[6:]
    b = pl.program_id(0)
    late = join_copies(at_ref[0], (p0, p1, p2, p3), wib_ref, sem1) + [pltpu.make_async_copy(wu_ref, wu_buf, sem2)]

    @pl.when(b == 0)
    def _():
        run_copies(late)

    fin = fin_ref[0]
    seq = fin.shape[0]
    half = wi_ref.shape[1]
    chunk = v_ref.shape[2]
    length = lens[b]
    vrow = (lax.broadcasted_iota(jnp.int32, (8, seq), 1) < length).astype(F32).astype(BF)
    spot = lambda c: slice(c * chunk, (c + 1) * chunk)
    parts = [(w, a, g, c) for w, a, g in ((wi_ref, act_ref, gp_ref), (wib_ref, actb_ref, gpb_ref)) for c in range(half // chunk)]

    def project(t):
        w, _, _, c = parts[t]
        v_ref[t % 2] = mm(fin, w[:, spot(c)])

    project(0)
    for t, (_, a_ref, g_ref, c) in enumerate(parts):
        if t + 1 < len(parts):
            project(t + 1)
        for r in range(seq // TILE):
            rows = slice(TILE * r, TILE * (r + 1))
            act, slope = gelu_parts(v_ref[t % 2, rows, :])
            a_ref[0, rows, spot(c)] = act.astype(BF)
            g_ref[0, rows, spot(c)] = slope.astype(BF)
        asum_ref[0, :, spot(t)] = mm(vrow, a_ref[0, :, spot(c)])[:1]
    own = asum_ref[0, :, :half]
    hi = own.astype(BF)
    lo = (own - hi.astype(F32)).astype(BF)
    two_rows = jnp.concatenate([hi.astype(F32), lo.astype(F32), jnp.zeros((14, half), F32)], axis=0).astype(BF)
    branch = mm(two_rows, wu_buf[...])
    rsum_ref[0] = rs_ref[0] + branch[0:1] + branch[1:2]


def ffn_fwd(lens, at, fin, rsum, wi, wu, packs):
    n, seq, d = fin.shape
    half = wi.shape[1]
    wide = sds((n, seq, half), BF)
    outs = [wide, wide, wide, wide, sds((n, 1, 2 * half), F32), sds((n, 1, d), F32)]
    return pl.pallas_call(
        ffn_fwd_kernel,
        grid=(n,),
        in_specs=[SMEM_SPEC, SMEM_SPEC, row_spec(fin.shape), row_spec(rsum.shape), const_spec(wi.shape)] + [ANY] * 5,
        out_specs=[row_spec(o.shape) for o in outs],
        out_shape=outs,
        scratch_shapes=[
            pltpu.VMEM(wi.shape, BF),
            pltpu.VMEM(wu.shape, BF),
            pltpu.VMEM((2, seq, 512), F32),
            pltpu.SemaphoreType.DMA((4,)),
            pltpu.SemaphoreType.DMA,
        ],
        compiler_params=params(),
        cost_estimate=cost(16),
        name="ffn_fwd",
    )(lens, at, fin, rsum, wi, wu, *packs)


def pool_kernel(lens, at_ref, asum_ref, rs_ref, p0, p1, p2, p3, out_ref, wb_ref, sem):
    run_copies(join_copies(at_ref[0], (p0, p1, p2, p3), wb_ref, sem))
    n = asum_ref.shape[0]
    half = wb_ref.shape[0]
    rows = [asum_ref[i, :, half:] for i in range(n)]
    hi = [r.astype(BF) for r in rows]
    lo = [(r - h.astype(F32)).astype(BF) for r, h in zip(rows, hi)]
    pad = jnp.zeros((16 - 2 * n, half), F32)
    br = mm(jnp.concatenate([t.astype(F32) for t in hi + lo] + [pad], axis=0).astype(BF), wb_ref[...])
    for i in range(n):
        total = rs_ref[i] + br[i : i + 1] + br[n + i : n + i + 1]
        out_ref[i : i + 1, :] = total / lens[i].astype(F32)


def pool(lens, at, asum, rsum, packs):
    n, _, d = rsum.shape
    half = asum.shape[2] // 2
    vm = pl.BlockSpec(memory_space=pltpu.VMEM)
    return pl.pallas_call(
        pool_kernel,
        in_specs=[SMEM_SPEC, SMEM_SPEC, vm, vm] + [ANY] * 4,
        out_specs=vm,
        out_shape=sds((8, d), F32),
        scratch_shapes=[pltpu.VMEM((half, d), BF), pltpu.SemaphoreType.DMA((4,))],
        compiler_params=params(16),
        cost_estimate=cost(4),
        name="pool",
    )(lens, at, asum, rsum, *packs)


def pre_kernel(lens, fint_ref, gp_ref, fn_ref, w_ref, out_ref, ft_ref, v_ref, s_ref):
    n, seq, _ = gp_ref.shape

    @pl.when(pl.program_id(0) == 0)
    def _():
        valid = lax.broadcasted_iota(jnp.int32, (seq, TILE), 0) < lens[n]
        ft_ref[...] = jnp.transpose((fn_ref[0].astype(F32) * valid.astype(F32)[:, :1]).astype(BF))

    v_ref[...] = mm(fn_ref[0], w_ref[...])
    for i in range(n):
        out_ref[i] = mm(fint_ref[:, seq * i : seq * (i + 1)], gp_ref[i]).astype(BF)
        for r in range(seq // TILE // n):
            at = slice(seq // n * i + TILE * r, seq // n * i + TILE * (r + 1))
            s_ref[at, :] = gelu_parts(v_ref[at, :])[1].astype(BF)
    out_ref[n] = mm(ft_ref[...], s_ref[...]).astype(BF)


def pre_inner(lens4, fint, gp, fn, wi):
    n, seq, half = gp.shape
    d = fint.shape[0]
    chunk = 512
    return pl.pallas_call(
        pre_kernel,
        grid=(half // chunk,),
        in_specs=[SMEM_SPEC, const_spec(fint.shape), pl.BlockSpec((n, seq, chunk), lambda c: (0, 0, c))]
        + [const_spec(fn.shape), pl.BlockSpec((d, chunk), lambda c: (0, c))],
        out_specs=pl.BlockSpec((n + 1, d, chunk), lambda c: (0, 0, c)),
        out_shape=sds((n + 1, d, half), BF),
        scratch_shapes=[pltpu.VMEM((d, seq), BF), pltpu.VMEM((seq, chunk), F32), pltpu.VMEM((seq, chunk), BF)],
        compiler_params=params(),
        cost_estimate=cost(9),
        name="pre_inner",
    )(lens4, fint, gp, fn, wi)


def loss_kernel(me_ref, at_ref, lens, pool_ref, q_ref, wp_hbm, pre_hbm, fn_hbm, wi_hbm, wu_hbm, *refs):
    (loss_ref, row_ref, g_ref, drow_ref, demb_ref, send_ref, keep_ref) = refs[:7]
    (wp_ref, wu_ref, pre_ref, fn_ref, wi_ref, ft_ref, gn_ref, v_ref, d_ref, sum_ref, sem) = refs[7:]
    moves = ((wp_hbm, wp_ref), (wu_hbm, wu_ref), (fn_hbm, fn_ref), (wi_hbm, wi_ref), (pre_hbm, pre_ref))
    loads = [pltpu.make_async_copy(a, b, sem.at[i]) for i, (a, b) in enumerate(moves)]
    for c in loads:
        c.start()
    loads[0].wait()
    d = wp_ref.shape[0]
    count = pool_ref.shape[0]
    pooled = pool_ref[...]
    qs = q_ref[:, :d]
    ints = q_ref[:, d : d + TILE].astype(F32)
    pos = (ints[:, 0:1] * 256.0 + ints[:, 1:2]).astype(jnp.int32)
    length = ints[:, 2:3] * 256.0 + ints[:, 3:4]
    wp = wp_ref[...]
    emb = mm(pooled, wp)
    inv = lax.rsqrt(jnp.sum(emb * emb, axis=-1, keepdims=True) + EPS)
    unit = (emb * inv).astype(BF)
    logits = mm(qs, unit, NT) / SHARPNESS
    top = jnp.max(logits, axis=-1, keepdims=True)
    total = top + jnp.log(jnp.sum(jnp.exp(logits - top), axis=-1, keepdims=True))
    hit = lax.broadcasted_iota(jnp.int32, (count, count), 1) == pos
    loss = total - jnp.sum(jnp.where(hit, logits, 0.0), axis=1, keepdims=True)
    d_logits = (LOSS_SCALE * (jnp.exp(logits - total) - jnp.where(hit, 1.0, 0.0))).astype(BF)
    d_unit = mm(d_logits, qs, TN) / SHARPNESS
    along = jnp.sum(emb * d_unit, axis=-1, keepdims=True)
    d_emb = (inv * d_unit - inv * inv * inv * along * emb).astype(BF)
    demb_ref[...] = d_emb
    rows = mm(d_emb, wp, NT) / length
    drow_ref[...] = rows.astype(BF)
    index = lax.broadcasted_iota(jnp.int32, (count, 1), 0)
    pick = lambda t, i: jnp.sum(jnp.where(index == i, t, 0.0), axis=0, keepdims=True)
    seq = fn_ref.shape[1]
    half = wi_ref.shape[1]
    n = pre_ref.shape[0] - 1
    own = [pick(rows, me_ref[i]) for i in range(n)]
    near = [pick(rows, me_ref[n + i]) for i in range(n)]
    lost = jnp.broadcast_to(loss, (count, TILE))
    pad = jnp.zeros((8 - n, d), F32)
    row_ref[...] = jnp.concatenate(own + [pad], axis=0)
    loss_ref[...] = jnp.concatenate([pick(lost, me_ref[i]) for i in range(n)] + [pad[:, :TILE]], axis=0)
    four = jnp.concatenate(own + near + [jnp.zeros((16 - 2 * n, d), F32)], axis=0).astype(BF)
    loads[1].wait()
    gn_ref[...] = mm(four, wu_ref[...], NT)[:8]
    g_ref[...] = gn_ref[...]
    for c in loads[2:]:
        c.wait()

    last = 2 * n - 1
    valid = lax.broadcasted_iota(jnp.int32, (seq, TILE), 0) < lens[last]
    ft_ref[...] = jnp.transpose((fn_ref[0].astype(F32) * valid.astype(F32)[:, :1]).astype(BF))
    chunk = v_ref.shape[2]
    steps = half // chunk
    spot = lambda c: slice(c * chunk, (c + 1) * chunk)
    rows2 = d // 2
    core = at_ref[0] // 2

    def project(c):
        v_ref[c % 2] = mm(fn_ref[0], wi_ref[:, spot(c)])

    def scale(c):
        for r in range(seq // TILE):
            at = slice(TILE * r, TILE * (r + 1))
            slope = gelu_parts(v_ref[c % 2, at, :])[1]
            d_ref[c % 2, at, :] = (slope * gn_ref[last : last + 1, spot(c)]).astype(BF)

    project(0)
    scale(0)
    for c in range(steps):
        if c + 1 < steps:
            project(c + 1)
        for r in range(d // TILE):
            at = slice(TILE * r, TILE * (r + 1))
            total = mm(ft_ref[at, :], d_ref[c % 2])
            for i in range(n + 1):
                total = total + pre_ref[i, at, spot(c)].astype(F32) * gn_ref[i : i + 1, spot(c)]
            sum_ref[at, :] = total.astype(BF)
        for ref, side in ((send_ref, 1 - core), (keep_ref, core)):
            ref[:, spot(c)] = sum_ref[pl.ds(pl.multiple_of(side * rows2, rows2), rows2), :]
        if c + 1 < steps:
            scale(c + 1)


def loss_all(me, at, lens4, pooled, queries, wp, pre, fn, wi, wu):
    half, d = wu.shape
    seq = fn.shape[1]
    count = pooled.shape[0]
    chunk = 512
    vm = pl.BlockSpec(memory_space=pltpu.VMEM)
    return pl.pallas_call(
        loss_kernel,
        in_specs=[SMEM_SPEC] * 3 + [vm] * 2 + [ANY] * 5,
        out_specs=[vm] * 7,
        out_shape=[
            sds((8, TILE), F32),
            sds((8, d), F32),
            sds((8, half), F32),
            sds((count, d), BF),
            sds((count, d), BF),
            sds((d // 2, half), BF),
            sds((d // 2, half), BF),
        ],
        scratch_shapes=[
            pltpu.VMEM(wp.shape, BF),
            pltpu.VMEM(wu.shape, BF),
            pltpu.VMEM(pre.shape, BF),
            pltpu.VMEM(fn.shape, BF),
            pltpu.VMEM(wi.shape, BF),
            pltpu.VMEM((d, seq), BF),
            pltpu.VMEM((8, half), F32),
            pltpu.VMEM((2, seq, chunk), F32),
            pltpu.VMEM((2, seq, chunk), BF),
            pltpu.VMEM((d, chunk), BF),
            pltpu.SemaphoreType.DMA((5,)),
        ],
        compiler_params=params(),
        cost_estimate=cost(12),
        name="loss_inner",
    )(me, at, lens4, pooled, queries, wp, pre, fn, wi, wu)


def mid_bwd_kernel(lens, at_ref, g_ref, row_ref, gain_ref, hot_ref, lse_ref, tf_ref, *refs):
    hbm, packs0, packs1, packs2 = refs[:11], refs[11:15], refs[15:19], refs[19:23]
    (dres_hbm, dattn_hbm), outs, scratch = refs[23:25], refs[25:29], refs[29:39]
    bufs, (wib_ref, wob_ref, wub_ref, gb_ref, d_ref, dres_ref, sem, sem0, sem1, sem2, sem3) = refs[39:50], refs[50:]
    da_ref = scratch[7]
    wi_ref, gpa_ref, gpb_ref, res_all, q, qt, k, v, ct, nb, ant = bufs
    b = pl.program_id(0)
    n = lse_ref.shape[0]
    copies = [pltpu.make_async_copy(x, y, sem.at[i]) for i, (x, y) in enumerate(zip(hbm, bufs))]
    copies0 = out_copies(at_ref[0], packs0, wob_ref, sem0)
    copies1 = join_copies(at_ref[0], packs1, wib_ref, sem1)
    copies1 += join_copies(at_ref[0], packs2, wub_ref, sem3)

    def first(group):
        @pl.when(b == 0)
        def _():
            for c in group:
                c.wait()

    @pl.when(b == 0)
    def _():
        for c in copies[:2] + copies1 + copies[2:4] + copies0 + copies[4:]:
            c.start()

    first(copies[:2])
    _, seq, d = res_all.shape
    half = wi_ref.shape[1]
    chunk = d_ref.shape[2]
    steps = half // chunk
    parts = [(gp, w, c) for gp, w in ((gpa_ref, wi_ref), (gpb_ref, wib_ref)) for c in range(steps)]

    def scale(t):
        gp, _, c = parts[t]
        g = (g_ref if t < steps else gb_ref)[pl.ds(b, 1), c * chunk : (c + 1) * chunk]
        d_ref[t % 2] = (gp[b, :, c * chunk : (c + 1) * chunk].astype(F32) * g).astype(BF)

    d_two = None
    scale(0)
    for t, (_, w, c) in enumerate(parts):
        if t + 1 == steps:
            first(copies[2:4] + copies1)

            @pl.when(b == 0)
            def _():
                rows = jnp.concatenate([row_ref[...], jnp.zeros_like(row_ref)], axis=0).astype(BF)
                gb_ref[...] = mm(rows, wub_ref[...], NT)[:8]

        if t + 1 < len(parts):
            scale(t + 1)
        one = mm(d_ref[t % 2], w[:, c * chunk : (c + 1) * chunk], NT)
        d_two = one if d_two is None else d_two + one
    res = res_all[b]
    inv = lax.rsqrt(jnp.mean(res * res, axis=-1, keepdims=True) + EPS)
    scaled = d_two * gain_ref[...]
    along = jnp.sum(scaled * res, axis=-1, keepdims=True)
    valid = lax.broadcasted_iota(jnp.int32, (seq, TILE), 0) < lens[b]
    vcol = valid.astype(F32)[:, :1]
    inv = inv * vcol
    d_res = vcol * row_ref[pl.ds(b, 1), :] + scaled * inv - res * (inv * inv * inv * along / d)
    here = pl.ds(pl.multiple_of(b * seq, seq), seq)
    dres_ref[here, :] = d_res
    d_attn = d_res.astype(BF)
    da_ref[here, :] = d_attn
    done = send_rows(b, n, dres_ref, dres_hbm, sem2.at[0]) + send_rows(b, n, da_ref, dattn_hbm, sem2.at[1])
    first(copies0 + copies[4:-1])
    ins = (q, qt, k, v, ct, lse_ref, nb, tf_ref, ant, hot_ref)
    attn_back(b, n, lens[b], at_ref[0] // 2, wob_ref[...], d_attn, ins, outs, scratch, copies[-1:])

    @pl.when(b == n - 1)
    def _():
        for c in done:
            c.wait()


def mid_bwd(lens, at, g, row, gain, hot, lse, tf, arrays, packs0, packs1, packs2):
    wi, _, _, res = arrays[:4]
    n, seq, d = res.shape
    half = wi.shape[1]
    width = packs0[0].shape[1] // 3
    outs, specs = back_outs(n, seq, width, d)
    more = [sds((n * seq, d), F32), sds((n * seq, d), BF)]
    return pl.pallas_call(
        mid_bwd_kernel,
        grid=(n,),
        in_specs=[SMEM_SPEC, SMEM_SPEC]
        + [const_spec(x.shape) for x in (g, row)]
        + [const_spec((1, d))]
        + [const_spec(x.shape) for x in (hot, lse, tf)]
        + [ANY] * 23,
        out_specs=[ANY] * 2 + specs,
        out_shape=more + outs,
        scratch_shapes=back_scratch(n, seq, width, d)
        + [pltpu.VMEM(x.shape, x.dtype) for x in arrays]
        + [
            pltpu.VMEM((d, half), BF),
            pltpu.VMEM((width, d), BF),
            pltpu.VMEM((half, d), BF),
            pltpu.VMEM((8, half), F32),
            pltpu.VMEM((2, seq, 512), BF),
            pltpu.VMEM((n * seq, d), F32),
            pltpu.SemaphoreType.DMA((11,)),
            pltpu.SemaphoreType.DMA((12,)),
            pltpu.SemaphoreType.DMA((4,)),
            pltpu.SemaphoreType.DMA((2, n)),
            pltpu.SemaphoreType.DMA((4,)),
        ],
        compiler_params=params(),
        cost_estimate=cost(32),
        name="mid_bwd",
    )(lens, at, g, row, gain.reshape(1, d), hot, lse, tf, *arrays, *packs0, *packs1, *packs2)


def input_kernel(at_ref, x_ref, dres_ref, gain_ref, ta_ref, tb_ref, wq, wk, wv, p0, p1, p2, p3, out_ref, w_ref, sem):
    @pl.when(pl.program_id(0) == 0)
    def _():
        run_copies(join_copies(at_ref[0], (p0, p1, p2, p3), w_ref, sem))

    width = wq.shape[1]
    d_one = mm(tb_ref[...], w_ref[...], NT)
    for i, w in enumerate((wq, wk, wv)):
        d_one = d_one + mm(ta_ref[:, width * i : width * (i + 1)], w[...], NT)
    x = x_ref[0].astype(F32)
    inv = lax.rsqrt(jnp.mean(x * x, axis=-1, keepdims=True) + EPS)
    scaled = d_one * gain_ref[...]
    along = jnp.sum(scaled * x, axis=-1, keepdims=True)
    out_ref[0] = dres_ref[...] + scaled * inv - x * (inv * inv * inv * along / x.shape[1])


def input_part(at, x, dres, gain, tok_a, tok_b, wq, wk, wv, packs):
    n, seq, d = x.shape
    width = wq.shape[1]
    rows = lambda cols: pl.BlockSpec((seq, cols), lambda b: (b, 0))
    return pl.pallas_call(
        input_kernel,
        grid=(n,),
        in_specs=[SMEM_SPEC, row_spec(x.shape), rows(d), const_spec((1, d)), rows(3 * width), rows(3 * width)]
        + [const_spec(wq.shape)] * 3
        + [ANY] * 4,
        out_specs=row_spec(x.shape),
        out_shape=sds(x.shape, F32),
        scratch_shapes=[pltpu.VMEM((d, 3 * width), BF), pltpu.SemaphoreType.DMA((4,))],
        compiler_params=params(),
        cost_estimate=cost(12),
        name="input_part",
    )(at, x, dres, gain.reshape(1, d), tok_a, tok_b, wq, wk, wv, *packs)


def layer_kernel(at_ref, res_ref, aa_ref, ab_ref, w_ref, p0, p1, p2, p3, out_ref, wb_ref, sem):
    @pl.when(pl.program_id(0) == 0)
    def _():
        run_copies(join_copies(at_ref[0], (p0, p1, p2, p3), wb_ref, sem))

    out_ref[0] = (res_ref[0] + mm(aa_ref[0], w_ref[...]) + mm(ab_ref[0], wb_ref[...])).astype(BF)


def layer_part(at, res, act_a, act_b, wu, packs):
    n, seq, d = res.shape
    return pl.pallas_call(
        layer_kernel,
        grid=(n,),
        in_specs=[SMEM_SPEC, row_spec(res.shape), row_spec(act_a.shape), row_spec(act_b.shape), const_spec(wu.shape)]
        + [ANY] * 4,
        out_specs=row_spec(res.shape),
        out_shape=sds(res.shape, BF),
        scratch_shapes=[pltpu.VMEM(wu.shape, BF), pltpu.SemaphoreType.DMA((4,))],
        compiler_params=params(),
        cost_estimate=cost(12),
        name="layer_part",
    )(at, res, act_a, act_b, wu, *packs)


def gain_row(prod):
    ones = jnp.ones((16, prod.shape[1]), BF)
    return sum(mm(ones, part, NT)[:1] for part in split3(prod))


def inner_done_kernel(at_ref, own_ref, near_ref, w_ref, out_ref, gain_ref):
    rows = own_ref.shape[0]
    core = at_ref[0] // 2
    halves = [own_ref[...].astype(F32), near_ref[...].astype(F32)]
    for half in range(2):
        one = jnp.where(core == half, halves[0], halves[1])
        at = slice(rows * half, rows * (half + 1))
        out_ref[at, :] = one
        gain_ref[:, at] = jnp.broadcast_to(gain_row(one * w_ref[at, :].astype(F32)), (8, rows))


def inner_done(at, own, near, w):
    d, half = w.shape
    chunk = 512
    cols = lambda r: pl.BlockSpec((r, chunk), lambda c: (0, c))
    return pl.pallas_call(
        inner_done_kernel,
        grid=(half // chunk,),
        in_specs=[SMEM_SPEC, cols(d // 2), cols(d // 2), cols(d)],
        out_specs=[cols(d), pl.BlockSpec((8, d), lambda c: (c, 0))],
        out_shape=[sds((d, half), F32), sds((8 * (half // chunk), d), F32)],
        compiler_params=params(20),
        cost_estimate=cost(5),
        name="inner_done",
    )(at, own, near, w)


def attn_done_kernel(half_ref, sum_ref, wq, wk, wv, *refs):
    q_ref, k_ref, v_ref, o_ref, gain_ref = refs[-5:]
    width = wq.shape[1]
    total = None
    for i, (w, out) in enumerate(((wq, q_ref), (wk, k_ref), (wv, v_ref))):
        one = sum_ref[:, width * i : width * (i + 1)].astype(F32)
        out[...] = one
        prod = one * w[...].astype(F32)
        total = prod if total is None else total + prod
    o_ref[...] = sum_ref[:, 3 * width :].astype(F32)
    gain_ref[...] = jnp.broadcast_to(gain_row(total), gain_ref.shape)


def attn_done(half, sums, wq, wk, wv, into=()):
    d, width = wq.shape
    rows = d // 2
    grad = sds((d, width), F32)
    block = pl.BlockSpec((rows, width), lambda b, half: (half[0], 0))
    across = pl.BlockSpec((width, rows), lambda b, half: (0, half[0]))
    return pl.pallas_call(
        attn_done_kernel,
        grid_spec=pltpu.PrefetchScalarGridSpec(
            num_scalar_prefetch=1,
            grid=(1,),
            in_specs=[pl.BlockSpec(sums.shape, lambda b, half: (0, 0))] + [block] * 3 + [ANY] * len(into),
            out_specs=[block] * 3 + [across, pl.BlockSpec((8, rows), lambda b, half: (0, 0))],
        ),
        out_shape=[grad, grad, grad, sds((width, d), F32), sds((8, rows), F32)],
        input_output_aliases={5 + i: i for i in range(len(into))},
        compiler_params=params(20),
        cost_estimate=cost(3),
        name="attn_done",
    )(half, sums, wq, wk, wv, *into)


def after(*xs):
    return lax.optimization_barrier(xs)


def swap(x, axis, bit, size):
    return lax.ppermute(x, axis, [(i, i ^ bit) for i in range(size)])


class Place:
    def __init__(self, chips, tensor):
        self.chips, self.tensor = chips, tensor
        self.chip = lax.axis_index("chip")
        self.core = lax.axis_index("core")
        self.ti = lax.axis_index("tensor")

    def across(self, x):
        return swap(x, "tensor", 1, self.tensor)

    def core_swap(self, x):
        return swap(x, "core", 1, 2)

    def share(self, x):
        return lax.all_to_all(x, ("chip", "core", "tensor"), 0, 0, tiled=True)

    def side(self, mine):
        return swap(mine, "chip", 1, self.chips)

    def spread(self, mine, side):
        return [mine, side, self.core_swap(mine), self.core_swap(side)]

    def exchange(self, x):
        rows, width = x.shape
        return lax.all_to_all(x.reshape(self.chips, rows // self.chips, width), "chip", 0, 0, tiled=True)

    def add(self, got):
        return jnp.sum(got.astype(F32), axis=0).astype(BF)

    def gather(self, x):
        got = lax.all_to_all(jnp.broadcast_to(x[None], (self.chips,) + x.shape), "chip", 0, 0, tiled=True)
        return got.reshape(-1, x.shape[1])

    def total(self, x):
        for i in range(self.chips.bit_length() - 1):
            x = x + swap(x, "chip", 1 << i, self.chips)
        return x


def body(
    mesh_shape,
    hidden_in,
    lengths,
    queries,
    positives,
    gain_attn,
    w_query,
    w_key,
    w_value,
    w_out,
    rel_table,
    gain_ffn,
    w_inner,
    w_outer,
    w_proj,
):
    pc = Place(mesh_shape["chip"], mesh_shape["tensor"])
    n, seq, d = hidden_in.shape
    half = w_inner.shape[1]
    width = w_query.shape[1]
    buckets = rel_table.shape[0]
    lens = lax.dynamic_slice_in_dim(lengths, pc.ti * n, n, 0)
    near_lens = lax.dynamic_slice_in_dim(lengths, (1 - pc.ti) * n, n, 0)
    lens4 = jnp.concatenate([lens, near_lens])
    at = (2 * pc.core + (pc.chip & 1)).reshape(1)
    devices = pc.chips * 2 * pc.tensor
    hot_t = jnp.asarray(np.pad(diag_onehot(buckets, False).T, ((0, TILE - buckets), (0, 0))), BF)
    hot_back = jnp.asarray(np.pad(diag_onehot(buckets, True), ((0, 0), (0, TILE - buckets))), BF)

    turned = rel_table.T
    packs = pack_weights(at, turned, w_query, w_key, w_value, w_out, w_inner, w_outer)
    y_attn = pc.across(packs[0])

    base = (2 * pc.chip + pc.core) * pc.tensor * n
    me = jnp.stack([base + pc.ti * n, base + pc.ti * n + 1, base + (1 - pc.ti) * n, base + (1 - pc.ti) * n + 1])

    qf = queries.astype(F32)
    q_unit = (qf * lax.rsqrt(jnp.sum(qf * qf, axis=-1, keepdims=True) + EPS)).astype(BF)
    ints = jnp.stack([positives // 256, positives % 256, lens // 256, lens % 256], axis=1)
    ints = jnp.pad(ints.astype(BF), ((0, 0), (0, TILE - 4)))
    q_all = jnp.concatenate([q_unit, ints], axis=1)

    an, ant, q_a, qt_a, k_a, v_a, ctx_a, ctxt_a, lse_a, nb_a, tf_a = attn_own(
        lens, hidden_in, gain_attn, w_query, w_key, w_value, turned, hot_t
    )
    y_attn, an, q_all, *packs = after(y_attn, an, q_all, *packs[1:])
    y_inner, y_outer = [pc.across(p) for p in packs]
    x_attn = pc.side(y_attn)
    q_all = pc.share(jnp.broadcast_to(q_all[None], (devices,) + q_all.shape))
    x_attn, q_all, lens4, me, gain_two = after(x_attn, q_all, lens4, me, gain_ffn.reshape(1, d))
    p_attn = pc.spread(y_attn, x_attn)
    y_inner, an = after(y_inner, an)
    x_inner = pc.side(y_inner)
    q_b, qt_b, k_b, v_b, ctxt_b, lse_b, nb_b, tf_b, res, fin, fint, rsum, *fins = attn_other(
        lens, at, an, hot_t, hidden_in, ctx_a, w_out, gain_two, p_attn
    )
    y_inner, x_inner, y_outer, fin, *fins = after(y_inner, x_inner, y_outer, fin, *fins)
    x_outer = pc.side(y_outer)
    p_inner = pc.spread(y_inner, x_inner)
    fin_nb = [pc.across(f) for f in fins]
    act_a, gp_a, act_b, gp_b, asum, rsum = ffn_fwd(lens, at, fin, rsum, w_inner, w_outer, p_inner)
    y_outer, x_outer, asum, fin_nb[0] = after(y_outer, x_outer, asum, fin_nb[0])
    p_outer = pc.spread(y_outer, x_outer)
    pooled = pool(lens, at, asum, rsum, p_outer)[:n].astype(BF)

    sums_a, sums_b = asum[:, 0, :half].astype(BF), asum[:, 0, half:].astype(BF)
    sums = jnp.where(pc.ti > 0, jnp.stack([sums_b, sums_a]), jnp.stack([sums_a, sums_b]))
    msg = jnp.concatenate([jnp.broadcast_to(pooled[None], (2,) + pooled.shape), sums], axis=2)
    msg = jnp.broadcast_to(msg[None], (2 * pc.chips,) + msg.shape).reshape((devices,) + msg.shape[1:])
    got, pre = after(pc.share(msg), pre_inner(lens4, fint, gp_a, fin_nb[0], w_inner))
    got = got.reshape(devices * n, -1)
    pooled = got[:, :d]
    loss8, row8, g8, d_rows, d_emb, gi_send, gi_keep = loss_all(
        me, at, lens4, pooled, q_all.reshape(devices * n, -1), w_proj, pre, fin_nb[1], w_inner, w_outer
    )
    query_loss = loss8[:n, 0]

    inner_half, gp_a = after(gi_keep + pc.core_swap(gi_send), gp_a)
    inner_parts = pc.exchange(inner_half)
    arrays = [w_inner, gp_a, gp_b, res, q_b, qt_b, k_b, v_b, ctxt_b, nb_b, ant]
    d_res, d_attn, tok_b, send_b, keep_b, table_b = mid_bwd(
        lens, at, g8, row8, gain_ffn, hot_back, lse_b, tf_b, arrays, p_attn, p_inner, p_outer
    )
    inner_part, d_attn = after(pc.add(inner_parts), d_attn)
    inner_all = pc.gather(inner_part)
    half_b, d_attn = after(keep_b + pc.core_swap(send_b), d_attn)
    far_part = pc.across(half_b)
    tok_a, send_a, keep_a, table_a = attn_bwd(
        lens, at, d_attn.reshape(n, seq, d), w_out, hot_back, lse_a, tf_a, q_a, qt_a, k_a, v_a, ctxt_a, nb_a, ant
    )
    proj_grad = mm(pooled, d_emb, TN)
    outer_grad = mm(got[:, d:], d_rows, TN)
    inner_all, far_part, far_table, send_a, proj_grad, outer_grad = after(
        inner_all, far_part, pc.across(table_b), send_a, proj_grad, outer_grad
    )
    table = table_a + far_table
    near_a, near_table = after(pc.core_swap(send_a), pc.core_swap(table))
    parts = pc.exchange(keep_a + far_part + near_a)
    input_grad = input_part(at, hidden_in, d_res, gain_attn, tok_a, tok_b, w_query, w_key, w_value, p_attn)
    inner_sum, gain_ffn_part = inner_done(at, inner_all, pc.core_swap(inner_all), w_inner)
    layer = layer_part(at, res, act_a, act_b, w_outer, p_outer)
    parts, input_grad, layer = after(parts, input_grad, layer)
    attn_all = pc.gather(pc.add(parts))
    table_sum = pc.total(table + near_table)
    gain_ffn_part = jnp.sum(gain_ffn_part[::8], axis=0)
    gain_ffn_grad = (gain_ffn_part + pc.across(gain_ffn_part)) / gain_ffn
    attn_all, gain_ffn_grad, table_sum, inner_sum, query_loss = after(
        attn_all, gain_ffn_grad, table_sum, inner_sum, query_loss
    )
    half = pc.core.reshape(1)
    near = pc.core_swap(attn_all)
    *grads, gain_own = attn_done(half, attn_all, w_query, w_key, w_value)
    near, *grads = after(near, *grads)
    gain_own = gain_own[0] + pc.across(gain_own[0])
    *grads, _ = attn_done(1 - half, near, w_query, w_key, w_value, grads)
    gain_own, *grads = after(gain_own, *grads)
    q_grad, k_grad, v_grad, out_grad = grads
    gain_near = pc.core_swap(gain_own)
    gain_attn_grad = jnp.where(
        pc.core > 0, jnp.concatenate([gain_near, gain_own]), jnp.concatenate([gain_own, gain_near])
    ) / gain_attn
    return (
        layer,
        query_loss,
        input_grad,
        gain_attn_grad,
        q_grad,
        k_grad,
        v_grad,
        out_grad,
        table_sum[: rel_table.shape[1], :buckets].T,
        gain_ffn_grad,
        inner_sum,
        outer_grad,
        proj_grad,
    )


def solution(mesh):
    dp, tensor = mesh.shape["dp"], mesh.shape["tensor"]
    fine = jax.sharding.Mesh(mesh.devices.reshape(dp // 2, 2, tensor), ("chip", "core", "tensor"))
    rows = ("chip", "core")
    both = rows + ("tensor",)
    return jax.shard_map(
        functools.partial(body, dict(fine.shape)),
        mesh=fine,
        in_specs=(
            P(both, None, None),
            P(rows),
            P(both, None),
            P(both),
            P(),
            P(None, "tensor"),
            P(None, "tensor"),
            P(None, "tensor"),
            P("tensor", None),
            P(None, "tensor"),
            P(),
            P(None, "tensor"),
            P("tensor", None),
            P(),
        ),
        out_specs=(
            P(both, None, None),
            P(both),
            P(both, None, None),
            P(),
            P(None, "tensor"),
            P(None, "tensor"),
            P(None, "tensor"),
            P("tensor", None),
            P(None, "tensor"),
            P(),
            P(None, "tensor"),
            P("tensor", None),
            P(),
        ),
        check_vma=False,
    )
```

```python
import functools

import numpy as np

import jax
import jax.numpy as jnp
from jax import lax
from jax.experimental import pallas as pl
from jax.experimental.pallas import tpu as pltpu
from jax.sharding import PartitionSpec as P

LARGE_STEPS = (12, 16, 23, 32, 46, 64, 91)
SHARPNESS = 0.02
LOSS_SCALE = 256.0
EPS = 1e-06
NEG = -1e30
BF = jnp.bfloat16
F32 = jnp.float32
TILE = 128
BUCKETS = 32
GELU_A = 0.7978845608028654
GELU_B = 0.044715
MIB = 1024 * 1024

NN = (((1,), (0,)), ((), ()))
NT = (((1,), (1,)), ((), ()))
TN = (((0,), (0,)), ((), ()))


def mm(a, b, dims=NN):
    return lax.dot_general(a, b, dims, preferred_element_type=F32)


def bucket_of(r):
    a = np.abs(r)
    far = 8 + sum((a >= t).astype(np.int32) for t in LARGE_STEPS)
    return np.where(r > 0, 16, 0) + np.where(a < 8, a, far)


def diag_onehot(buckets, back):
    lane = np.arange(2 * TILE)
    at = lane - TILE + 1 if back else TILE - 1 - lane
    idx = np.concatenate([bucket_of(TILE * d + at) for d in (-1, 0, 1)])
    hot = (idx[:, None] == np.arange(buckets)[None, :]).astype(np.float32)
    hot[2 * TILE - 1 :: 2 * TILE] = 0.0
    return hot


def params(mib=60):
    return pltpu.CompilerParams(vmem_limit_bytes=mib * MIB)


def cost(us):
    return pl.CostEstimate(flops=0, bytes_accessed=int(us * 3.6e6), transcendentals=0)

ANY = pl.BlockSpec(memory_space=pl.ANY)
SMEM_SPEC = pl.BlockSpec(memory_space=pltpu.SMEM)


def const_spec(shape):
    zeros = (0,) * len(shape)
    return pl.BlockSpec(tuple(shape), lambda b: zeros, pipeline_mode=pl.Buffered(1))


def out_const(shape):
    zeros = (0,) * len(shape)
    return pl.BlockSpec(tuple(shape), lambda b: zeros)


def row_spec(shape):
    tail = (0,) * (len(shape) - 1)
    return pl.BlockSpec((1,) + tuple(shape[1:]), lambda b: (b,) + tail)


def sds(shape, dtype):
    return jax.ShapeDtypeStruct(tuple(shape), dtype)


def split3(t):
    hi = t.astype(BF)
    rest = t - hi.astype(F32)
    mid = rest.astype(BF)
    return hi, mid, (rest - mid.astype(F32)).astype(BF)


def run_copies(copies):
    for c in copies:
        c.start()
    for c in copies:
        c.wait()


def out_pieces(width, d):
    rows, tall = width // 4, width // 6
    rest = rows - tall
    out = [((0, tall, 0, d), (0, tall, 0, d))]
    for i in range(2):
        out.append(((tall, rest, i * width, width), (i * rest, rest, d, width)))
    return out


def pack_kernel(at_ref, tab_ref, wq, wk, wv, wo, wi, wu, s0, s1, s2, sem):
    at = at_ref[0]
    d, width = wq.shape
    rows = d // 4

    def part(w, dst, i):
        count = w.shape[0] // 4
        src = w.at[pl.ds(pl.multiple_of(at * count, count), count)]
        return pltpu.make_async_copy(src, dst, sem.at[i])

    copies = [part(w, s0.at[pl.ds(0, rows), width * i : width * (i + 1)], i) for i, w in enumerate((wq, wk, wv))]
    copies += [part(wi, s1, 3), part(wu, s2, 4)]
    for i, (a, b) in enumerate(out_pieces(width, d)):
        src = wo.at[pl.ds(pl.multiple_of(at * (width // 4) + a[0], 32), a[1]), a[2] : a[2] + a[3]]
        dst = s0.at[pl.ds(rows + 16 + b[0], b[1]), b[2] : b[2] + b[3]]
        copies.append(pltpu.make_async_copy(src, dst, sem.at[5 + i]))
    for c in copies:
        c.start()
    s0[rows : rows + 16, :] = jnp.zeros((16, s0.shape[1]), BF)
    heads, buckets = tab_ref.shape
    for k, t in enumerate(split3(tab_ref[...])):
        s0[rows : rows + heads, TILE * k : TILE * k + buckets] = t
    for c in copies:
        c.wait()


def pack_weights(at, table, wq, wk, wv, wo, wi, wu):
    d, half = wi.shape
    width = wq.shape[1]
    vm = pl.BlockSpec(memory_space=pltpu.VMEM)
    return pl.pallas_call(
        pack_kernel,
        in_specs=[SMEM_SPEC, vm] + [ANY] * 6,
        out_specs=[vm] * 3,
        out_shape=[
            sds((d // 4 + 16 + width // 6, 3 * width), BF),
            sds((d // 4, half), BF),
            sds((half // 4, d), BF),
        ],
        scratch_shapes=[pltpu.SemaphoreType.DMA((8,))],
        compiler_params=params(),
        cost_estimate=cost(3),
        name="pack_weights",
    )(at, table, wq, wk, wv, wo, wi, wu)


def quarter_spots(at):
    core, xb = at // 2, at % 2
    return [at, 2 * core + 1 - xb, 2 * (1 - core) + xb, 2 * (1 - core) + 1 - xb]


def out_copies(at, packs, dst, sem):
    width, d = dst.shape
    base = d // 4 + 16
    out = []
    for i, (p, s) in enumerate(zip(packs, quarter_spots(at))):
        for j, (a, b) in enumerate(out_pieces(width, d)):
            src = p.at[pl.ds(base + b[0], b[1]), b[2] : b[2] + b[3]]
            to = dst.at[pl.ds(pl.multiple_of(s * (width // 4) + a[0], 32), a[1]), a[2] : a[2] + a[3]]
            out.append(pltpu.make_async_copy(src, to, sem.at[3 * i + j]))
    return out


def join_copies(at, packs, dst, sem):
    rows = dst.shape[0] // 4
    out = []
    for i, (p, s) in enumerate(zip(packs, quarter_spots(at))):
        to = dst.at[pl.ds(pl.multiple_of(s * rows, rows), rows)]
        out.append(pltpu.make_async_copy(p.at[pl.ds(0, rows)], to, sem.at[i]))
    return out


EXTRA = 16


def key_extras(length, rows):
    row = lax.broadcasted_iota(jnp.int32, (rows, TILE), 0)
    lane = lax.broadcasted_iota(jnp.int32, (rows, TILE), 1) & 63
    blk = (lane - 1) & 3
    hot = (lane >= 1) & (lane < 13) & (blk == row // TILE)
    one = ((lane == 0) & (row >= length)) | hot | ((lane >= 13) & (lane < EXTRA))
    return jnp.where(one, 1.0, 0.0)


def far_rows(tf_ref, h, seq):
    row = lax.broadcasted_iota(jnp.int32, (EXTRA, seq), 0)
    diff = ((row - 1) & 3) - lax.broadcasted_iota(jnp.int32, (EXTRA, seq), 1) // TILE
    out = jnp.where(row == 0, NEG, 0.0)
    last, mid = BUCKETS - 1, BUCKETS // 2 - 1
    for k in range(3):
        mine = (row >= 1 + 4 * k) & (row < 5 + 4 * k)
        out = out + jnp.where(mine & (diff >= 2), tf_ref[k, h : h + 1, last : last + 1], 0.0)
        out = out + jnp.where(mine & (diff <= -2), tf_ref[k, h : h + 1, mid : mid + 1], 0.0)
    return out


def stack_rows(e, main, extra):
    pad = jnp.zeros((64 - extra.shape[0], extra.shape[1]), BF)
    return jnp.concatenate([main, extra, pad] if e == 0 else [extra, pad, main], axis=0)


def near_bias(s, nb_ref, h, ib):
    rows = []
    for bj in range(s.shape[0] // TILE):
        parts = []
        for t in range(2):
            piece = s[TILE * bj : TILE * (bj + 1), TILE * t : TILE * (t + 1)]
            d = bj - (2 * ib + t)
            parts.append(piece + nb_ref[3 * h + d + 1] if abs(d) <= 1 else piece)
        rows.append(jnp.concatenate(parts, axis=1))
    return rows


def set_bias(parts, hot_ref, tf_ref, nb_ref):
    for k in range(3):
        tf_ref[k] = parts[k].astype(F32)
    hot = hot_ref[...]
    bv = mm(parts[0], hot) + mm(parts[1], hot) + mm(parts[2], hot)
    for t in range(nb_ref.shape[0]):
        h, k = t // 3, t % 3
        v = jnp.broadcast_to(bv[h : h + 1, 2 * TILE * k : 2 * TILE * (k + 1)], (TILE, 2 * TILE))
        nb_ref[t] = pltpu.roll(v, TILE + 1, 1, stride=1, stride_axis=0)[:, :TILE]


def attn_rows(an, length, ws, outs, nb_ref, tf_ref, s_ref, p_ref, between=None):
    q_ref, qt_ref, k_ref, v_ref, ctx_ref, ctxt_ref, lse_ref = outs
    seq = an.shape[0]
    width = q_ref.shape[2]
    for ref, w in zip((q_ref, k_ref), ws):
        ref[0] = mm(an, w[...]).astype(BF)
    kx = key_extras(length, seq)
    lane = lax.broadcasted_iota(jnp.int32, (seq, TILE), 1)
    blocks = [(h, ib) for h in range(width // 64) for ib in range(seq // 256)]
    keys, queries, values, tops, rows = {}, {}, {}, {}, {}

    def prepare(h):
        pair, e = h // 2, h % 2
        cols = slice(TILE * pair, TILE * (pair + 1))
        if e == 0:
            qt_ref[0, cols, :] = jnp.transpose(q_ref[0, :, cols])
        mine = lane < 64 if e == 0 else lane >= 64
        keys[h] = jnp.where(mine, k_ref[0, :, cols].astype(F32), kx).astype(BF)
        qt = qt_ref[0, 64 * h : 64 * (h + 1), :]
        queries[h] = stack_rows(e, qt, far_rows(tf_ref, h, seq).astype(BF))

    def start(t):
        h, ib = blocks[t]
        if ib == 0:
            prepare(h)
        s = mm(keys[h], queries[h][:, 256 * ib : 256 * (ib + 1)])
        return near_bias(s, nb_ref, h, ib)

    def score(t, bj, pieces):
        piece = pieces[bj]
        s_ref[t % 2, TILE * bj : TILE * (bj + 1), :] = piece
        m = jnp.max(piece.reshape(TILE // 8, 8, 256), axis=0)
        tops[t] = m if bj == 0 else jnp.maximum(tops[t], m)
        if bj == seq // TILE - 1:
            tops[t] = jnp.max(tops[t], axis=0, keepdims=True)

    def soft(t, bj):
        h, ib = blocks[t]
        at = slice(TILE * bj, TILE * (bj + 1))
        p_ref[h % 2, at, 256 * ib : 256 * (ib + 1)] = jnp.exp(s_ref[t % 2, at, :] - tops[t]).astype(BF)

    def combine(h):
        per = seq // 256
        top = jnp.concatenate([tops[per * h + i] for i in range(per)], axis=1)
        if h % 2 == 0:
            values[h // 2] = jnp.transpose(v_ref[0, :, TILE * (h // 2) : TILE * (h // 2 + 1)])
        vt = values[h // 2][64 * (h % 2) : 64 * (h % 2 + 1), :]
        got = mm(jnp.concatenate([vt, jnp.ones((16, seq), BF)], axis=0), p_ref[h % 2])
        total = got[64:65]
        lse_ref[0, h : h + 1, :] = top + jnp.log(total)
        rows[h] = got[:64] * (1.0 / total)
        if h % 2 == 1:
            pair = h // 2
            cols = slice(TILE * pair, TILE * (pair + 1))
            ct = jnp.concatenate([rows[h - 1], rows[h]], axis=0).astype(BF)
            ctxt_ref[0, cols, :] = ct
            ctx_ref[0, :, cols] = jnp.transpose(ct)

    for t in range(len(blocks) + 1):
        if t < len(blocks):
            pieces = start(t)
            for bj in range(seq // TILE):
                score(t, bj, pieces)
        if t == 0:
            v_ref[0] = mm(an, ws[2][...]).astype(BF)
        if t == 5 and between is not None:
            between()
        if t > 0:
            for bj in range(seq // TILE):
                soft(t - 1, bj)
            if blocks[t - 1][1] == seq // 256 - 1:
                combine(blocks[t - 1][0])


def attn_own_kernel(lens, x_ref, gain_ref, wq, wk, wv, tab_ref, hot_ref, an_ref, ant_ref, *refs):
    outs, (nb_ref, tf_ref, s_ref, p_ref) = refs[:7], refs[7:]
    b = pl.program_id(0)

    @pl.when(b == 0)
    def _():
        heads, buckets = tab_ref.shape
        wide = jnp.concatenate([tab_ref[...], jnp.zeros((heads, TILE - buckets), F32)], axis=1)
        wide = jnp.concatenate([wide, jnp.zeros((16 - heads, TILE), F32)], axis=0)
        set_bias(split3(wide), hot_ref, tf_ref, nb_ref)

    x = x_ref[0].astype(F32)
    inv = lax.rsqrt(jnp.mean(x * x, axis=-1, keepdims=True) + EPS)
    an = (x * inv * gain_ref[...]).astype(BF)
    an_ref[0] = an
    ant_ref[...] = jnp.transpose(an)
    attn_rows(an, lens[b], (wq, wk, wv), outs, nb_ref, tf_ref, s_ref, p_ref)


def attn_other_kernel(lens, at_ref, an_ref, hot_ref, gain_ref, x_hbm, ca_hbm, wo_hbm, p0, p1, p2, p3, *refs):
    outs, (nb_ref, tf_ref, res_ref, fin_ref, fint_ref, rsum_ref, f0_ref, f1_ref) = list(refs[:6]), refs[6:14]
    (s_ref, p_ref, w_ref, tab_ref, wb_ref, c_ref, x_ref, ca_ref, wo_ref, sem, sem1, sem2) = refs[14:]
    outs.insert(4, c_ref)
    b = pl.program_id(0)
    late = out_copies(at_ref[0], (p0, p1, p2, p3), wb_ref, sem1)
    moves = ((x_hbm, x_ref), (ca_hbm, ca_ref), (wo_hbm, wo_ref))
    more = [pltpu.make_async_copy(x, y, sem2.at[i]) for i, (x, y) in enumerate(moves)]

    @pl.when(b == 0)
    def _():
        rows = w_ref.shape[0] // 4
        copies = join_copies(at_ref[0], (p0, p1, p2, p3), w_ref, sem)
        copies.append(pltpu.make_async_copy(p0.at[pl.ds(rows, 16)], tab_ref, sem.at[4]))
        for c in copies + more + late:
            c.start()
        for c in copies:
            c.wait()
        parts = [tab_ref[:, TILE * k : TILE * (k + 1)] for k in range(3)]
        set_bias(parts, hot_ref, tf_ref, nb_ref)
        for c in more:
            c.wait()

    width = outs[0].shape[2]
    ws = [w_ref.at[:, width * k : width * (k + 1)] for k in range(3)]

    def between():
        res_ref[0] = x_ref[b].astype(F32) + mm(ca_ref[b], wo_ref[...])

    attn_rows(an_ref[0], lens[b], ws, outs, nb_ref, tf_ref, s_ref, p_ref, between)

    @pl.when(b == 0)
    def _():
        for c in late:
            c.wait()

    res = res_ref[0] + mm(outs[4][0], wb_ref[...])
    res_ref[0] = res
    inv = lax.rsqrt(jnp.mean(res * res, axis=-1, keepdims=True) + EPS)
    fin = (res * inv * gain_ref[...]).astype(BF)
    fin_ref[0] = fin
    for i, f_ref in enumerate((f0_ref, f1_ref)):

        @pl.when(b == i)
        def _():
            f_ref[0] = fin

    vcol = (lax.broadcasted_iota(jnp.int32, (res.shape[0], TILE), 0) < lens[b]).astype(F32)[:, :1]
    fint_ref[...] = jnp.transpose((fin.astype(F32) * vcol).astype(BF))
    rsum_ref[0] = jnp.sum(res * vcol, axis=0, keepdims=True)


def attn_outs(n, seq, width):
    heads = width // 64
    tok, turned = sds((n, seq, width), BF), sds((n, width, seq), BF)
    rows = [tok, turned, tok, tok, tok, turned, sds((n, 8, seq), F32)]
    flat = [sds((3 * heads, TILE, TILE), F32), sds((3, 16, TILE), F32)]
    scratch = [pltpu.VMEM((2, seq, 256), F32), pltpu.VMEM((2, seq, seq), BF)]
    return rows + flat, [row_spec(o.shape) for o in rows] + [out_const(o.shape) for o in flat], scratch


def attn_own(lens, x, gain, wq, wk, wv, table, hot):
    n, seq, d = x.shape
    outs, specs, scratch = attn_outs(n, seq, wq.shape[1])
    return pl.pallas_call(
        attn_own_kernel,
        grid=(n,),
        in_specs=[SMEM_SPEC, row_spec(x.shape), const_spec((1, d))]
        + [const_spec(wq.shape)] * 3
        + [const_spec(table.shape), const_spec(hot.shape)],
        out_specs=[row_spec(x.shape), pl.BlockSpec((d, seq), lambda b: (0, b))] + specs,
        out_shape=[sds((n, seq, d), BF), sds((d, n * seq), BF)] + outs,
        scratch_shapes=scratch,
        compiler_params=params(),
        cost_estimate=cost(12),
        name="attn_own",
    )(lens, x, gain.reshape(1, d), wq, wk, wv, table, hot)


def attn_other(lens, at, an, hot, x, ctx_a, wo, gain, packs):
    n, seq, d = an.shape
    width = wo.shape[0]
    outs, specs, scratch = attn_outs(n, seq, width)
    del outs[4], specs[4]
    more = [sds((n, seq, d), F32), sds((n, seq, d), BF), sds((d, n * seq), BF), sds((n, 1, d), F32)]
    more_specs = [row_spec(o.shape) for o in more]
    more_specs[2] = pl.BlockSpec((d, seq), lambda b: (0, b))
    more += [sds((1, seq, d), BF)] * n
    more_specs += [out_const((1, seq, d))] * n
    return pl.pallas_call(
        attn_other_kernel,
        grid=(n,),
        in_specs=[SMEM_SPEC, SMEM_SPEC, row_spec(an.shape), const_spec(hot.shape), const_spec((1, d))]
        + [ANY] * 7,
        out_specs=specs + more_specs,
        out_shape=outs + more,
        scratch_shapes=scratch
        + [
            pltpu.VMEM((d, 3 * width), BF),
            pltpu.VMEM((16, 3 * width), BF),
            pltpu.VMEM(wo.shape, BF),
            pltpu.VMEM((1, seq, width), BF),
            pltpu.VMEM(x.shape, BF),
            pltpu.VMEM(ctx_a.shape, BF),
            pltpu.VMEM(wo.shape, BF),
            pltpu.SemaphoreType.DMA((5,)),
            pltpu.SemaphoreType.DMA((12,)),
            pltpu.SemaphoreType.DMA((3,)),
        ],
        compiler_params=params(),
        cost_estimate=cost(15),
        name="attn_other",
    )(lens, at, an, hot, gain, x, ctx_a, wo, *packs)


def attn_back(b, n, length, core, w, d_attn, ins, outs, scratch, late):
    (q_ref, qt_ref, k_ref, v_ref, ct_ref, lse_ref, nb_ref, tf_ref, ant_ref, hot_ref) = ins
    (all_hbm, send_ref, keep_ref, table_ref) = outs
    (dc_ref, dct_ref, t_ref, fsum_ref, p_ref, ds_ref, all_ref, da_ref, go_ref, out_sem) = scratch
    seq, width = q_ref.shape[1], q_ref.shape[2]
    heads = width // 64
    nblk = seq // TILE
    here = pl.ds(pl.multiple_of(b * seq, seq), seq)

    @pl.when(b == 0)
    def _():
        t_ref[...] = jnp.zeros_like(t_ref)
        fsum_ref[...] = jnp.zeros_like(fsum_ref)
        table_ref[...] = jnp.zeros_like(table_ref)

    dct_ref[...] = mm(w, d_attn, NT).astype(BF)
    dc_ref[...] = jnp.transpose(dct_ref[...])
    kx = key_extras(length, seq)
    lane = lax.broadcasted_iota(jnp.int32, (seq, TILE), 1)
    vx = jnp.where((lane & 63) < 3, 1.0, 0.0)
    keys, values, queries, grads, turned = {}, {}, {}, {}, {}

    def prepare(h):
        pair, e = h // 2, h % 2
        cols = slice(TILE * pair, TILE * (pair + 1))
        mine = lane < 64 if e == 0 else lane >= 64
        if e == 0:
            turned[pair] = jnp.transpose(k_ref[b, :, cols])
        keys[h] = jnp.where(mine, k_ref[b, :, cols].astype(F32), kx).astype(BF)
        values[h] = jnp.where(mine, v_ref[b, :, cols].astype(F32), vx).astype(BF)
        at = slice(64 * h, 64 * (h + 1))
        lse = split3(-lse_ref[b, h : h + 1, :])
        extra = far_rows(tf_ref, h, seq)
        row = lax.broadcasted_iota(jnp.int32, (EXTRA, seq), 0)
        for k in range(3):
            extra = jnp.where(row == 13 + k, lse[k].astype(F32), extra)
        queries[h] = stack_rows(e, qt_ref[b, at, :], extra.astype(BF))
        along = jnp.sum(dct_ref[at, :].astype(F32) * ct_ref[b, at, :].astype(F32), axis=0, keepdims=True)
        extra = jnp.zeros((EXTRA, seq), F32)
        for k, part in enumerate(split3(-along)):
            extra = jnp.where(row == k, part.astype(F32), extra)
        grads[h] = stack_rows(e, dct_ref[at, :], extra.astype(BF))

    def block(h, ib):
        pair, e = h // 2, h % 2
        at = slice(256 * ib, 256 * (ib + 1))
        to = slice(seq * e + 256 * ib, seq * e + 256 * (ib + 1))
        s = mm(keys[h], queries[h][:, at])
        dp = mm(values[h], grads[h][:, at])
        near, far = {}, {}
        for bj, piece in enumerate(near_bias(s, nb_ref, h, ib)):
            rows = slice(TILE * bj, TILE * (bj + 1))
            p = jnp.exp(piece)
            ds = p * dp[rows, :]
            p_ref[pair % 2, rows, to] = p.astype(BF)
            ds_ref[pair % 2, rows, to] = ds.astype(BF)
            for t in range(2):
                d = bj - (2 * ib + t)
                one = ds[:, TILE * t : TILE * (t + 1)]
                if abs(d) <= 1:
                    near[d] = near[d] + one if d in near else one
                else:
                    one = jnp.sum(one.reshape(TILE // 8, 8, TILE), axis=0)
                    side = 1 if d > 0 else 0
                    far[side] = far[side] + one if side in far else one
        for d, one in near.items():
            t_ref[3 * h + d + 1] += one
        for side, one in far.items():
            fsum_ref[2 * h + side] += one

    def finish(pair, part):
        slot = pair % 2
        cols = slice(TILE * pair, TILE * (pair + 1))
        if part < 2:
            src, rhs = ((p_ref, dc_ref[:, cols]), (ds_ref, q_ref[b, :, cols]))[part]
            one = jnp.where(lane < 64, mm(src[slot, :, :seq], rhs), mm(src[slot, :, seq:], rhs)).astype(BF)
            base = width * (2 - part)
            all_ref[here, base + TILE * pair : base + TILE * (pair + 1)] = one
        if part == 2:
            kt = turned[pair]
            dqt = [mm(kt[64 * e : 64 * (e + 1), :], ds_ref[slot, :, seq * e : seq * (e + 1)]) for e in range(2)]
            one = jnp.transpose(jnp.concatenate(dqt, axis=0).astype(BF))
            all_ref[here, TILE * pair : TILE * (pair + 1)] = one

    for pair in range(heads // 2):
        step = 0
        for e in range(2):
            prepare(2 * pair + e)
            for ib in range(seq // 256):
                block(2 * pair + e, ib)
                if pair > 0 and step < 3:
                    finish(pair - 1, step)
                step += 1
    for part in range(3):
        finish(heads // 2 - 1, part)
    done = send_rows(b, n, all_ref, all_hbm, out_sem)

    @pl.when(b == n - 1)
    def _():
        for c in late:
            c.wait()
        rows = ant_ref.shape[0] // 2
        out = None
        for i in range(n):
            one = mm(ct_ref[i], da_ref[seq * i : seq * (i + 1), :])
            out = one if out is None else out + one
        go_ref[:width, :] = out[:, :width].astype(BF)
        go_ref[width:, :] = out[:, width:].astype(BF)
        for ref, half in ((send_ref, 1 - core), (keep_ref, core)):
            at = pl.ds(pl.multiple_of(half * rows, rows), rows)
            ref[:, : 3 * width] = mm(ant_ref[at, :], all_ref[...]).astype(BF)
            ref[:, 3 * width :] = go_ref[at, :]
        turn = lax.broadcasted_iota(jnp.int32, (TILE, TILE), 0) + lax.broadcasted_iota(jnp.int32, (TILE, TILE), 1)
        turn = jnp.where(turn == TILE - 1, 1.0, 0.0).astype(BF)
        tiles = t_ref.shape[0]
        hi, lo, _ = split3(t_ref[...].reshape(tiles * TILE, TILE))
        back = mm(jnp.concatenate([hi, lo], axis=1), jnp.concatenate([turn, turn], axis=0))
        diag = []
        for t in range(tiles):
            x = jnp.concatenate([back[TILE * t : TILE * (t + 1)], jnp.zeros((TILE, TILE), F32)], axis=1)
            x = pltpu.roll(x, 0, 1, stride=1, stride_axis=0)
            diag.append(jnp.sum(x, axis=0, keepdims=True))
        lines = [jnp.concatenate(diag[3 * h : 3 * h + 3], axis=1) for h in range(heads)]
        lines.append(jnp.zeros((16 - heads, lines[0].shape[1]), F32))
        near = [mm(part, hot_ref[...]) for part in split3(jnp.concatenate(lines, axis=0))]
        spot = lax.broadcasted_iota(jnp.int32, (1, TILE), 1)
        for h in range(heads):
            one = near[0][h : h + 1] + near[1][h : h + 1] + near[2][h : h + 1]
            for side, bucket in ((0, BUCKETS // 2 - 1), (1, BUCKETS - 1)):
                far = jnp.sum(jnp.sum(fsum_ref[2 * h + side], axis=0, keepdims=True), axis=1, keepdims=True)
                one = one + jnp.where(spot == bucket, far, 0.0)
            table_ref[h : h + 1, :] = one
        for c in done:
            c.wait()


def send_rows(b, n, src, dst, sem):
    rows = src.shape[0] // n
    copies = [pltpu.make_async_copy(src.at[pl.ds(i * rows, rows)], dst.at[pl.ds(i * rows, rows)], sem.at[i]) for i in range(n)]
    for i, c in enumerate(copies):

        @pl.when(b == i)
        def _():
            c.start()

    return copies


def back_outs(n, seq, width, d):
    half = sds((d // 2, 4 * width), BF)
    outs = [sds((n * seq, 3 * width), BF), half, half, sds((8, TILE), F32)]
    return outs, [ANY] + [out_const(o.shape) for o in outs[1:]]


def back_scratch(n, seq, width, d):
    heads = width // 64
    return [
        pltpu.VMEM((seq, width), BF),
        pltpu.VMEM((width, seq), BF),
        pltpu.VMEM((3 * heads, TILE, TILE), F32),
        pltpu.VMEM((2 * heads, 8, TILE), F32),
        pltpu.VMEM((2, seq, 2 * seq), BF),
        pltpu.VMEM((2, seq, 2 * seq), BF),
        pltpu.VMEM((n * seq, 3 * width), BF),
        pltpu.VMEM((n * seq, d), BF),
        pltpu.VMEM((d, width), BF),
        pltpu.SemaphoreType.DMA((n,)),
    ]


def attn_bwd_kernel(lens, at_ref, da_blk, wo_ref, hot_ref, lse_ref, tf_ref, *refs):
    hbm, outs, scratch = refs[:7], refs[7:11], refs[11:21]
    bufs, sem = refs[21:28], refs[28]
    b = pl.program_id(0)
    n = da_blk.shape[0] * lse_ref.shape[0]
    copies = [pltpu.make_async_copy(x, y, sem.at[i]) for i, (x, y) in enumerate(zip(hbm, bufs))]

    @pl.when(b == 0)
    def _():
        for c in copies:
            c.start()
        for c in copies[:-1]:
            c.wait()

    q, qt, k, v, ct, nb, ant = bufs
    ins = (q, qt, k, v, ct, lse_ref, nb, tf_ref, ant, hot_ref)
    seq = da_blk.shape[1]
    scratch[7][pl.ds(pl.multiple_of(b * seq, seq), seq), :] = da_blk[0]
    attn_back(b, n, lens[b], at_ref[0] // 2, wo_ref[...], da_blk[0], ins, outs, scratch, copies[-1:])


def attn_bwd(lens, at, d_attn, wo, hot, lse, tf, *arrays):
    n, seq, d = d_attn.shape
    width = wo.shape[0]
    outs, specs = back_outs(n, seq, width, d)
    return pl.pallas_call(
        attn_bwd_kernel,
        grid=(n,),
        in_specs=[SMEM_SPEC, SMEM_SPEC, row_spec(d_attn.shape)]
        + [const_spec(x.shape) for x in (wo, hot, lse, tf)]
        + [ANY] * 7,
        out_specs=specs,
        out_shape=outs,
        scratch_shapes=back_scratch(n, seq, width, d)
        + [pltpu.VMEM(x.shape, x.dtype) for x in arrays]
        + [pltpu.SemaphoreType.DMA((7,))],
        compiler_params=params(),
        cost_estimate=cost(16),
        name="attn_bwd",
    )(lens, at, d_attn, wo, hot, lse, tf, *arrays)


def gelu_parts(v):
    v2 = v * v
    half = 0.5 + 0.5 * jnp.tanh(v * (GELU_A + (GELU_A * GELU_B) * v2))
    act = v * half
    return act, half + (act - act * half) * (2.0 * GELU_A + (6.0 * GELU_A * GELU_B) * v2)


def ffn_fwd_kernel(lens, at_ref, fin_ref, rs_ref, wi_ref, wu_ref, p0, p1, p2, p3, *refs):
    (act_ref, gp_ref, actb_ref, gpb_ref, asum_ref, rsum_ref) = refs[:6]
    (wib_ref, wu_buf, v_ref, sem1, sem2) = refs[6:]
    b = pl.program_id(0)
    late = join_copies(at_ref[0], (p0, p1, p2, p3), wib_ref, sem1) + [pltpu.make_async_copy(wu_ref, wu_buf, sem2)]

    @pl.when(b == 0)
    def _():
        run_copies(late)

    fin = fin_ref[0]
    seq = fin.shape[0]
    half = wi_ref.shape[1]
    chunk = v_ref.shape[2]
    length = lens[b]
    vrow = (lax.broadcasted_iota(jnp.int32, (8, seq), 1) < length).astype(F32).astype(BF)
    spot = lambda c: slice(c * chunk, (c + 1) * chunk)
    parts = [(w, a, g, c) for w, a, g in ((wi_ref, act_ref, gp_ref), (wib_ref, actb_ref, gpb_ref)) for c in range(half // chunk)]

    def project(t):
        w, _, _, c = parts[t]
        v_ref[t % 2] = mm(fin, w[:, spot(c)])

    project(0)
    for t, (_, a_ref, g_ref, c) in enumerate(parts):
        if t + 1 < len(parts):
            project(t + 1)
        for r in range(seq // TILE):
            rows = slice(TILE * r, TILE * (r + 1))
            act, slope = gelu_parts(v_ref[t % 2, rows, :])
            a_ref[0, rows, spot(c)] = act.astype(BF)
            g_ref[0, rows, spot(c)] = slope.astype(BF)
        asum_ref[0, :, spot(t)] = mm(vrow, a_ref[0, :, spot(c)])[:1]
    own = asum_ref[0, :, :half]
    hi = own.astype(BF)
    lo = (own - hi.astype(F32)).astype(BF)
    two_rows = jnp.concatenate([hi.astype(F32), lo.astype(F32), jnp.zeros((14, half), F32)], axis=0).astype(BF)
    branch = mm(two_rows, wu_buf[...])
    rsum_ref[0] = rs_ref[0] + branch[0:1] + branch[1:2]


def ffn_fwd(lens, at, fin, rsum, wi, wu, packs):
    n, seq, d = fin.shape
    half = wi.shape[1]
    wide = sds((n, seq, half), BF)
    outs = [wide, wide, wide, wide, sds((n, 1, 2 * half), F32), sds((n, 1, d), F32)]
    return pl.pallas_call(
        ffn_fwd_kernel,
        grid=(n,),
        in_specs=[SMEM_SPEC, SMEM_SPEC, row_spec(fin.shape), row_spec(rsum.shape), const_spec(wi.shape)] + [ANY] * 5,
        out_specs=[row_spec(o.shape) for o in outs],
        out_shape=outs,
        scratch_shapes=[
            pltpu.VMEM(wi.shape, BF),
            pltpu.VMEM(wu.shape, BF),
            pltpu.VMEM((2, seq, 512), F32),
            pltpu.SemaphoreType.DMA((4,)),
            pltpu.SemaphoreType.DMA,
        ],
        compiler_params=params(),
        cost_estimate=cost(16),
        name="ffn_fwd",
    )(lens, at, fin, rsum, wi, wu, *packs)


def pool_kernel(lens, at_ref, asum_ref, rs_ref, p0, p1, p2, p3, out_ref, wb_ref, sem):
    run_copies(join_copies(at_ref[0], (p0, p1, p2, p3), wb_ref, sem))
    n = asum_ref.shape[0]
    half = wb_ref.shape[0]
    rows = [asum_ref[i, :, half:] for i in range(n)]
    hi = [r.astype(BF) for r in rows]
    lo = [(r - h.astype(F32)).astype(BF) for r, h in zip(rows, hi)]
    pad = jnp.zeros((16 - 2 * n, half), F32)
    br = mm(jnp.concatenate([t.astype(F32) for t in hi + lo] + [pad], axis=0).astype(BF), wb_ref[...])
    for i in range(n):
        total = rs_ref[i] + br[i : i + 1] + br[n + i : n + i + 1]
        out_ref[i : i + 1, :] = total / lens[i].astype(F32)


def pool(lens, at, asum, rsum, packs):
    n, _, d = rsum.shape
    half = asum.shape[2] // 2
    vm = pl.BlockSpec(memory_space=pltpu.VMEM)
    return pl.pallas_call(
        pool_kernel,
        in_specs=[SMEM_SPEC, SMEM_SPEC, vm, vm] + [ANY] * 4,
        out_specs=vm,
        out_shape=sds((8, d), F32),
        scratch_shapes=[pltpu.VMEM((half, d), BF), pltpu.SemaphoreType.DMA((4,))],
        compiler_params=params(16),
        cost_estimate=cost(4),
        name="pool",
    )(lens, at, asum, rsum, *packs)


def pre_kernel(lens, fint_ref, gp_ref, fn_ref, w_ref, out_ref, ft_ref, v_ref, s_ref):
    n, seq, _ = gp_ref.shape

    @pl.when(pl.program_id(0) == 0)
    def _():
        valid = lax.broadcasted_iota(jnp.int32, (seq, TILE), 0) < lens[n]
        ft_ref[...] = jnp.transpose((fn_ref[0].astype(F32) * valid.astype(F32)[:, :1]).astype(BF))

    v_ref[...] = mm(fn_ref[0], w_ref[...])
    for i in range(n):
        out_ref[i] = mm(fint_ref[:, seq * i : seq * (i + 1)], gp_ref[i]).astype(BF)
        for r in range(seq // TILE // n):
            at = slice(seq // n * i + TILE * r, seq // n * i + TILE * (r + 1))
            s_ref[at, :] = gelu_parts(v_ref[at, :])[1].astype(BF)
    out_ref[n] = mm(ft_ref[...], s_ref[...]).astype(BF)


def pre_inner(lens4, fint, gp, fn, wi):
    n, seq, half = gp.shape
    d = fint.shape[0]
    chunk = 512
    return pl.pallas_call(
        pre_kernel,
        grid=(half // chunk,),
        in_specs=[SMEM_SPEC, const_spec(fint.shape), pl.BlockSpec((n, seq, chunk), lambda c: (0, 0, c))]
        + [const_spec(fn.shape), pl.BlockSpec((d, chunk), lambda c: (0, c))],
        out_specs=pl.BlockSpec((n + 1, d, chunk), lambda c: (0, 0, c)),
        out_shape=sds((n + 1, d, half), BF),
        scratch_shapes=[pltpu.VMEM((d, seq), BF), pltpu.VMEM((seq, chunk), F32), pltpu.VMEM((seq, chunk), BF)],
        compiler_params=params(),
        cost_estimate=cost(9),
        name="pre_inner",
    )(lens4, fint, gp, fn, wi)


def loss_kernel(me_ref, at_ref, lens, pool_ref, q_ref, wp_hbm, pre_hbm, fn_hbm, wi_hbm, wu_hbm, *refs):
    (loss_ref, row_ref, g_ref, drow_ref, demb_ref, send_ref, keep_ref) = refs[:7]
    (wp_ref, wu_ref, pre_ref, fn_ref, wi_ref, ft_ref, gn_ref, v_ref, d_ref, sum_ref, sem) = refs[7:]
    moves = ((wp_hbm, wp_ref), (wu_hbm, wu_ref), (fn_hbm, fn_ref), (wi_hbm, wi_ref), (pre_hbm, pre_ref))
    loads = [pltpu.make_async_copy(a, b, sem.at[i]) for i, (a, b) in enumerate(moves)]
    for c in loads:
        c.start()
    loads[0].wait()
    d = wp_ref.shape[0]
    count = pool_ref.shape[0]
    pooled = pool_ref[...]
    qs = q_ref[:, :d]
    ints = q_ref[:, d : d + TILE].astype(F32)
    pos = (ints[:, 0:1] * 256.0 + ints[:, 1:2]).astype(jnp.int32)
    length = ints[:, 2:3] * 256.0 + ints[:, 3:4]
    wp = wp_ref[...]
    emb = mm(pooled, wp)
    inv = lax.rsqrt(jnp.sum(emb * emb, axis=-1, keepdims=True) + EPS)
    unit = (emb * inv).astype(BF)
    logits = mm(qs, unit, NT) / SHARPNESS
    top = jnp.max(logits, axis=-1, keepdims=True)
    total = top + jnp.log(jnp.sum(jnp.exp(logits - top), axis=-1, keepdims=True))
    hit = lax.broadcasted_iota(jnp.int32, (count, count), 1) == pos
    loss = total - jnp.sum(jnp.where(hit, logits, 0.0), axis=1, keepdims=True)
    d_logits = (LOSS_SCALE * (jnp.exp(logits - total) - jnp.where(hit, 1.0, 0.0))).astype(BF)
    d_unit = mm(d_logits, qs, TN) / SHARPNESS
    along = jnp.sum(emb * d_unit, axis=-1, keepdims=True)
    d_emb = (inv * d_unit - inv * inv * inv * along * emb).astype(BF)
    demb_ref[...] = d_emb
    rows = mm(d_emb, wp, NT) / length
    drow_ref[...] = rows.astype(BF)
    index = lax.broadcasted_iota(jnp.int32, (count, 1), 0)
    pick = lambda t, i: jnp.sum(jnp.where(index == i, t, 0.0), axis=0, keepdims=True)
    seq = fn_ref.shape[1]
    half = wi_ref.shape[1]
    n = pre_ref.shape[0] - 1
    own = [pick(rows, me_ref[i]) for i in range(n)]
    near = [pick(rows, me_ref[n + i]) for i in range(n)]
    lost = jnp.broadcast_to(loss, (count, TILE))
    pad = jnp.zeros((8 - n, d), F32)
    row_ref[...] = jnp.concatenate(own + [pad], axis=0)
    loss_ref[...] = jnp.concatenate([pick(lost, me_ref[i]) for i in range(n)] + [pad[:, :TILE]], axis=0)
    four = jnp.concatenate(own + near + [jnp.zeros((16 - 2 * n, d), F32)], axis=0).astype(BF)
    loads[1].wait()
    gn_ref[...] = mm(four, wu_ref[...], NT)[:8]
    g_ref[...] = gn_ref[...]
    for c in loads[2:]:
        c.wait()

    last = 2 * n - 1
    valid = lax.broadcasted_iota(jnp.int32, (seq, TILE), 0) < lens[last]
    ft_ref[...] = jnp.transpose((fn_ref[0].astype(F32) * valid.astype(F32)[:, :1]).astype(BF))
    chunk = v_ref.shape[2]
    steps = half // chunk
    spot = lambda c: slice(c * chunk, (c + 1) * chunk)
    rows2 = d // 2
    core = at_ref[0] // 2

    def project(c):
        v_ref[c % 2] = mm(fn_ref[0], wi_ref[:, spot(c)])

    def scale(c):
        for r in range(seq // TILE):
            at = slice(TILE * r, TILE * (r + 1))
            slope = gelu_parts(v_ref[c % 2, at, :])[1]
            d_ref[c % 2, at, :] = (slope * gn_ref[last : last + 1, spot(c)]).astype(BF)

    project(0)
    scale(0)
    for c in range(steps):
        if c + 1 < steps:
            project(c + 1)
        for r in range(d // TILE):
            at = slice(TILE * r, TILE * (r + 1))
            total = mm(ft_ref[at, :], d_ref[c % 2])
            for i in range(n + 1):
                total = total + pre_ref[i, at, spot(c)].astype(F32) * gn_ref[i : i + 1, spot(c)]
            sum_ref[at, :] = total.astype(BF)
        for ref, side in ((send_ref, 1 - core), (keep_ref, core)):
            ref[:, spot(c)] = sum_ref[pl.ds(pl.multiple_of(side * rows2, rows2), rows2), :]
        if c + 1 < steps:
            scale(c + 1)


def loss_all(me, at, lens4, pooled, queries, wp, pre, fn, wi, wu):
    half, d = wu.shape
    seq = fn.shape[1]
    count = pooled.shape[0]
    chunk = 512
    vm = pl.BlockSpec(memory_space=pltpu.VMEM)
    return pl.pallas_call(
        loss_kernel,
        in_specs=[SMEM_SPEC] * 3 + [vm] * 2 + [ANY] * 5,
        out_specs=[vm] * 7,
        out_shape=[
            sds((8, TILE), F32),
            sds((8, d), F32),
            sds((8, half), F32),
            sds((count, d), BF),
            sds((count, d), BF),
            sds((d // 2, half), BF),
            sds((d // 2, half), BF),
        ],
        scratch_shapes=[
            pltpu.VMEM(wp.shape, BF),
            pltpu.VMEM(wu.shape, BF),
            pltpu.VMEM(pre.shape, BF),
            pltpu.VMEM(fn.shape, BF),
            pltpu.VMEM(wi.shape, BF),
            pltpu.VMEM((d, seq), BF),
            pltpu.VMEM((8, half), F32),
            pltpu.VMEM((2, seq, chunk), F32),
            pltpu.VMEM((2, seq, chunk), BF),
            pltpu.VMEM((d, chunk), BF),
            pltpu.SemaphoreType.DMA((5,)),
        ],
        compiler_params=params(),
        cost_estimate=cost(12),
        name="loss_inner",
    )(me, at, lens4, pooled, queries, wp, pre, fn, wi, wu)


def mid_bwd_kernel(lens, at_ref, g_ref, row_ref, gain_ref, hot_ref, lse_ref, tf_ref, *refs):
    hbm, packs0, packs1, packs2 = refs[:11], refs[11:15], refs[15:19], refs[19:23]
    (dres_hbm, dattn_hbm), outs, scratch = refs[23:25], refs[25:29], refs[29:39]
    bufs, (wib_ref, wob_ref, wub_ref, gb_ref, d_ref, dres_ref, sem, sem0, sem1, sem2, sem3) = refs[39:50], refs[50:]
    da_ref = scratch[7]
    wi_ref, gpa_ref, gpb_ref, res_all, q, qt, k, v, ct, nb, ant = bufs
    b = pl.program_id(0)
    n = lse_ref.shape[0]
    copies = [pltpu.make_async_copy(x, y, sem.at[i]) for i, (x, y) in enumerate(zip(hbm, bufs))]
    copies0 = out_copies(at_ref[0], packs0, wob_ref, sem0)
    copies1 = join_copies(at_ref[0], packs1, wib_ref, sem1)
    copies1 += join_copies(at_ref[0], packs2, wub_ref, sem3)

    def first(group):
        @pl.when(b == 0)
        def _():
            for c in group:
                c.wait()

    @pl.when(b == 0)
    def _():
        for c in copies[:2] + copies1 + copies[2:4] + copies0 + copies[4:]:
            c.start()

    first(copies[:2])
    _, seq, d = res_all.shape
    half = wi_ref.shape[1]
    chunk = d_ref.shape[2]
    steps = half // chunk
    parts = [(gp, w, c) for gp, w in ((gpa_ref, wi_ref), (gpb_ref, wib_ref)) for c in range(steps)]

    def scale(t):
        gp, _, c = parts[t]
        g = (g_ref if t < steps else gb_ref)[pl.ds(b, 1), c * chunk : (c + 1) * chunk]
        d_ref[t % 2] = (gp[b, :, c * chunk : (c + 1) * chunk].astype(F32) * g).astype(BF)

    d_two = None
    scale(0)
    for t, (_, w, c) in enumerate(parts):
        if t + 1 == steps:
            first(copies[2:4] + copies1)

            @pl.when(b == 0)
            def _():
                rows = jnp.concatenate([row_ref[...], jnp.zeros_like(row_ref)], axis=0).astype(BF)
                gb_ref[...] = mm(rows, wub_ref[...], NT)[:8]

        if t + 1 < len(parts):
            scale(t + 1)
        one = mm(d_ref[t % 2], w[:, c * chunk : (c + 1) * chunk], NT)
        d_two = one if d_two is None else d_two + one
    res = res_all[b]
    inv = lax.rsqrt(jnp.mean(res * res, axis=-1, keepdims=True) + EPS)
    scaled = d_two * gain_ref[...]
    along = jnp.sum(scaled * res, axis=-1, keepdims=True)
    valid = lax.broadcasted_iota(jnp.int32, (seq, TILE), 0) < lens[b]
    vcol = valid.astype(F32)[:, :1]
    inv = inv * vcol
    d_res = vcol * row_ref[pl.ds(b, 1), :] + scaled * inv - res * (inv * inv * inv * along / d)
    here = pl.ds(pl.multiple_of(b * seq, seq), seq)
    dres_ref[here, :] = d_res
    d_attn = d_res.astype(BF)
    da_ref[here, :] = d_attn
    done = send_rows(b, n, dres_ref, dres_hbm, sem2.at[0]) + send_rows(b, n, da_ref, dattn_hbm, sem2.at[1])
    first(copies0 + copies[4:-1])
    ins = (q, qt, k, v, ct, lse_ref, nb, tf_ref, ant, hot_ref)
    attn_back(b, n, lens[b], at_ref[0] // 2, wob_ref[...], d_attn, ins, outs, scratch, copies[-1:])

    @pl.when(b == n - 1)
    def _():
        for c in done:
            c.wait()


def mid_bwd(lens, at, g, row, gain, hot, lse, tf, arrays, packs0, packs1, packs2):
    wi, _, _, res = arrays[:4]
    n, seq, d = res.shape
    half = wi.shape[1]
    width = packs0[0].shape[1] // 3
    outs, specs = back_outs(n, seq, width, d)
    more = [sds((n * seq, d), F32), sds((n * seq, d), BF)]
    return pl.pallas_call(
        mid_bwd_kernel,
        grid=(n,),
        in_specs=[SMEM_SPEC, SMEM_SPEC]
        + [const_spec(x.shape) for x in (g, row)]
        + [const_spec((1, d))]
        + [const_spec(x.shape) for x in (hot, lse, tf)]
        + [ANY] * 23,
        out_specs=[ANY] * 2 + specs,
        out_shape=more + outs,
        scratch_shapes=back_scratch(n, seq, width, d)
        + [pltpu.VMEM(x.shape, x.dtype) for x in arrays]
        + [
            pltpu.VMEM((d, half), BF),
            pltpu.VMEM((width, d), BF),
            pltpu.VMEM((half, d), BF),
            pltpu.VMEM((8, half), F32),
            pltpu.VMEM((2, seq, 512), BF),
            pltpu.VMEM((n * seq, d), F32),
            pltpu.SemaphoreType.DMA((11,)),
            pltpu.SemaphoreType.DMA((12,)),
            pltpu.SemaphoreType.DMA((4,)),
            pltpu.SemaphoreType.DMA((2, n)),
            pltpu.SemaphoreType.DMA((4,)),
        ],
        compiler_params=params(),
        cost_estimate=cost(32),
        name="mid_bwd",
    )(lens, at, g, row, gain.reshape(1, d), hot, lse, tf, *arrays, *packs0, *packs1, *packs2)


def input_kernel(at_ref, x_ref, dres_ref, gain_ref, ta_ref, tb_ref, wq, wk, wv, p0, p1, p2, p3, out_ref, w_ref, sem):
    @pl.when(pl.program_id(0) == 0)
    def _():
        run_copies(join_copies(at_ref[0], (p0, p1, p2, p3), w_ref, sem))

    width = wq.shape[1]
    d_one = mm(tb_ref[...], w_ref[...], NT)
    for i, w in enumerate((wq, wk, wv)):
        d_one = d_one + mm(ta_ref[:, width * i : width * (i + 1)], w[...], NT)
    x = x_ref[0].astype(F32)
    inv = lax.rsqrt(jnp.mean(x * x, axis=-1, keepdims=True) + EPS)
    scaled = d_one * gain_ref[...]
    along = jnp.sum(scaled * x, axis=-1, keepdims=True)
    out_ref[0] = dres_ref[...] + scaled * inv - x * (inv * inv * inv * along / x.shape[1])


def input_part(at, x, dres, gain, tok_a, tok_b, wq, wk, wv, packs):
    n, seq, d = x.shape
    width = wq.shape[1]
    rows = lambda cols: pl.BlockSpec((seq, cols), lambda b: (b, 0))
    return pl.pallas_call(
        input_kernel,
        grid=(n,),
        in_specs=[SMEM_SPEC, row_spec(x.shape), rows(d), const_spec((1, d)), rows(3 * width), rows(3 * width)]
        + [const_spec(wq.shape)] * 3
        + [ANY] * 4,
        out_specs=row_spec(x.shape),
        out_shape=sds(x.shape, F32),
        scratch_shapes=[pltpu.VMEM((d, 3 * width), BF), pltpu.SemaphoreType.DMA((4,))],
        compiler_params=params(),
        cost_estimate=cost(12),
        name="input_part",
    )(at, x, dres, gain.reshape(1, d), tok_a, tok_b, wq, wk, wv, *packs)


def layer_kernel(at_ref, res_ref, aa_ref, ab_ref, w_ref, p0, p1, p2, p3, out_ref, wb_ref, sem):
    @pl.when(pl.program_id(0) == 0)
    def _():
        run_copies(join_copies(at_ref[0], (p0, p1, p2, p3), wb_ref, sem))

    out_ref[0] = (res_ref[0] + mm(aa_ref[0], w_ref[...]) + mm(ab_ref[0], wb_ref[...])).astype(BF)


def layer_part(at, res, act_a, act_b, wu, packs):
    n, seq, d = res.shape
    return pl.pallas_call(
        layer_kernel,
        grid=(n,),
        in_specs=[SMEM_SPEC, row_spec(res.shape), row_spec(act_a.shape), row_spec(act_b.shape), const_spec(wu.shape)]
        + [ANY] * 4,
        out_specs=row_spec(res.shape),
        out_shape=sds(res.shape, BF),
        scratch_shapes=[pltpu.VMEM(wu.shape, BF), pltpu.SemaphoreType.DMA((4,))],
        compiler_params=params(),
        cost_estimate=cost(12),
        name="layer_part",
    )(at, res, act_a, act_b, wu, *packs)


def gain_row(prod):
    ones = jnp.ones((16, prod.shape[1]), BF)
    return sum(mm(ones, part, NT)[:1] for part in split3(prod))


def inner_done_kernel(at_ref, own_ref, near_ref, w_ref, out_ref, gain_ref):
    rows = own_ref.shape[0]
    core = at_ref[0] // 2
    halves = [own_ref[...].astype(F32), near_ref[...].astype(F32)]
    for half in range(2):
        one = jnp.where(core == half, halves[0], halves[1])
        at = slice(rows * half, rows * (half + 1))
        out_ref[at, :] = one
        gain_ref[:, at] = jnp.broadcast_to(gain_row(one * w_ref[at, :].astype(F32)), (8, rows))


def inner_done(at, own, near, w):
    d, half = w.shape
    chunk = 512
    cols = lambda r: pl.BlockSpec((r, chunk), lambda c: (0, c))
    return pl.pallas_call(
        inner_done_kernel,
        grid=(half // chunk,),
        in_specs=[SMEM_SPEC, cols(d // 2), cols(d // 2), cols(d)],
        out_specs=[cols(d), pl.BlockSpec((8, d), lambda c: (c, 0))],
        out_shape=[sds((d, half), F32), sds((8 * (half // chunk), d), F32)],
        compiler_params=params(20),
        cost_estimate=cost(5),
        name="inner_done",
    )(at, own, near, w)


def attn_done_kernel(half_ref, sum_ref, wq, wk, wv, *refs):
    q_ref, k_ref, v_ref, o_ref, gain_ref = refs[-5:]
    width = wq.shape[1]
    total = None
    for i, (w, out) in enumerate(((wq, q_ref), (wk, k_ref), (wv, v_ref))):
        one = sum_ref[:, width * i : width * (i + 1)].astype(F32)
        out[...] = one
        prod = one * w[...].astype(F32)
        total = prod if total is None else total + prod
    o_ref[...] = sum_ref[:, 3 * width :].astype(F32)
    gain_ref[...] = jnp.broadcast_to(gain_row(total), gain_ref.shape)


def attn_done(half, sums, wq, wk, wv, into=()):
    d, width = wq.shape
    rows = d // 2
    grad = sds((d, width), F32)
    block = pl.BlockSpec((rows, width), lambda b, half: (half[0], 0))
    across = pl.BlockSpec((width, rows), lambda b, half: (0, half[0]))
    return pl.pallas_call(
        attn_done_kernel,
        grid_spec=pltpu.PrefetchScalarGridSpec(
            num_scalar_prefetch=1,
            grid=(1,),
            in_specs=[pl.BlockSpec(sums.shape, lambda b, half: (0, 0))] + [block] * 3 + [ANY] * len(into),
            out_specs=[block] * 3 + [across, pl.BlockSpec((8, rows), lambda b, half: (0, 0))],
        ),
        out_shape=[grad, grad, grad, sds((width, d), F32), sds((8, rows), F32)],
        input_output_aliases={5 + i: i for i in range(len(into))},
        compiler_params=params(20),
        cost_estimate=cost(3),
        name="attn_done",
    )(half, sums, wq, wk, wv, *into)


def after(*xs):
    return lax.optimization_barrier(xs)


def swap(x, axis, bit, size):
    return lax.ppermute(x, axis, [(i, i ^ bit) for i in range(size)])


class Place:
    def __init__(self, chips, tensor):
        self.chips, self.tensor = chips, tensor
        self.chip = lax.axis_index("chip")
        self.core = lax.axis_index("core")
        self.ti = lax.axis_index("tensor")

    def across(self, x):
        return swap(x, "tensor", 1, self.tensor)

    def core_swap(self, x):
        return swap(x, "core", 1, 2)

    def share(self, x):
        return lax.all_to_all(x, ("chip", "core", "tensor"), 0, 0, tiled=True)

    def side(self, mine):
        return swap(mine, "chip", 1, self.chips)

    def spread(self, mine, side):
        return [mine, side, self.core_swap(mine), self.core_swap(side)]

    def exchange(self, x):
        rows, width = x.shape
        return lax.all_to_all(x.reshape(self.chips, rows // self.chips, width), "chip", 0, 0, tiled=True)

    def add(self, got):
        return jnp.sum(got.astype(F32), axis=0).astype(BF)

    def gather(self, x):
        got = lax.all_to_all(jnp.broadcast_to(x[None], (self.chips,) + x.shape), "chip", 0, 0, tiled=True)
        return got.reshape(-1, x.shape[1])

    def total(self, x):
        for i in range(self.chips.bit_length() - 1):
            x = x + swap(x, "chip", 1 << i, self.chips)
        return x


def body(
    mesh_shape,
    hidden_in,
    lengths,
    queries,
    positives,
    gain_attn,
    w_query,
    w_key,
    w_value,
    w_out,
    rel_table,
    gain_ffn,
    w_inner,
    w_outer,
    w_proj,
):
    pc = Place(mesh_shape["chip"], mesh_shape["tensor"])
    n, seq, d = hidden_in.shape
    half = w_inner.shape[1]
    width = w_query.shape[1]
    buckets = rel_table.shape[0]
    lens = lax.dynamic_slice_in_dim(lengths, pc.ti * n, n, 0)
    near_lens = lax.dynamic_slice_in_dim(lengths, (1 - pc.ti) * n, n, 0)
    lens4 = jnp.concatenate([lens, near_lens])
    at = (2 * pc.core + (pc.chip & 1)).reshape(1)
    devices = pc.chips * 2 * pc.tensor
    hot_t = jnp.asarray(np.pad(diag_onehot(buckets, False).T, ((0, TILE - buckets), (0, 0))), BF)
    hot_back = jnp.asarray(np.pad(diag_onehot(buckets, True), ((0, 0), (0, TILE - buckets))), BF)

    turned = rel_table.T
    packs = pack_weights(at, turned, w_query, w_key, w_value, w_out, w_inner, w_outer)
    y_attn = pc.across(packs[0])

    base = (2 * pc.chip + pc.core) * pc.tensor * n
    me = jnp.stack([base + pc.ti * n, base + pc.ti * n + 1, base + (1 - pc.ti) * n, base + (1 - pc.ti) * n + 1])

    qf = queries.astype(F32)
    q_unit = (qf * lax.rsqrt(jnp.sum(qf * qf, axis=-1, keepdims=True) + EPS)).astype(BF)
    ints = jnp.stack([positives // 256, positives % 256, lens // 256, lens % 256], axis=1)
    ints = jnp.pad(ints.astype(BF), ((0, 0), (0, TILE - 4)))
    q_all = jnp.concatenate([q_unit, ints], axis=1)

    an, ant, q_a, qt_a, k_a, v_a, ctx_a, ctxt_a, lse_a, nb_a, tf_a = attn_own(
        lens, hidden_in, gain_attn, w_query, w_key, w_value, turned, hot_t
    )
    y_attn, an, q_all, *packs = after(y_attn, an, q_all, *packs[1:])
    y_inner, y_outer = [pc.across(p) for p in packs]
    x_attn = pc.side(y_attn)
    q_all = pc.share(jnp.broadcast_to(q_all[None], (devices,) + q_all.shape))
    x_attn, q_all, lens4, me, gain_two = after(x_attn, q_all, lens4, me, gain_ffn.reshape(1, d))
    p_attn = pc.spread(y_attn, x_attn)
    y_inner, an = after(y_inner, an)
    x_inner = pc.side(y_inner)
    q_b, qt_b, k_b, v_b, ctxt_b, lse_b, nb_b, tf_b, res, fin, fint, rsum, *fins = attn_other(
        lens, at, an, hot_t, hidden_in, ctx_a, w_out, gain_two, p_attn
    )
    y_inner, x_inner, y_outer, fin, *fins = after(y_inner, x_inner, y_outer, fin, *fins)
    x_outer = pc.side(y_outer)
    p_inner = pc.spread(y_inner, x_inner)
    fin_nb = [pc.across(f) for f in fins]
    act_a, gp_a, act_b, gp_b, asum, rsum = ffn_fwd(lens, at, fin, rsum, w_inner, w_outer, p_inner)
    y_outer, x_outer, asum = after(y_outer, x_outer, asum)
    p_outer = pc.spread(y_outer, x_outer)
    pooled = pool(lens, at, asum, rsum, p_outer)[:n].astype(BF)

    sums_a, sums_b = asum[:, 0, :half].astype(BF), asum[:, 0, half:].astype(BF)
    sums = jnp.where(pc.ti > 0, jnp.stack([sums_b, sums_a]), jnp.stack([sums_a, sums_b]))
    msg = jnp.concatenate([jnp.broadcast_to(pooled[None], (2,) + pooled.shape), sums], axis=2)
    msg = jnp.broadcast_to(msg[None], (2 * pc.chips,) + msg.shape).reshape((devices,) + msg.shape[1:])
    msg, fin_nb[0] = after(msg, fin_nb[0])
    got, pre = after(pc.share(msg), pre_inner(lens4, fint, gp_a, fin_nb[0], w_inner))
    got = got.reshape(devices * n, -1)
    pooled = got[:, :d]
    loss8, row8, g8, d_rows, d_emb, gi_send, gi_keep = loss_all(
        me, at, lens4, pooled, q_all.reshape(devices * n, -1), w_proj, pre, fin_nb[1], w_inner, w_outer
    )
    query_loss = loss8[:n, 0]

    inner_half, gp_a = after(gi_keep + pc.core_swap(gi_send), gp_a)
    inner_parts = pc.exchange(inner_half)
    arrays = [w_inner, gp_a, gp_b, res, q_b, qt_b, k_b, v_b, ctxt_b, nb_b, ant]
    d_res, d_attn, tok_b, send_b, keep_b, table_b = mid_bwd(
        lens, at, g8, row8, gain_ffn, hot_back, lse_b, tf_b, arrays, p_attn, p_inner, p_outer
    )
    inner_part, d_attn = after(pc.add(inner_parts), d_attn)
    inner_all = pc.gather(inner_part)
    half_b, d_attn = after(keep_b + pc.core_swap(send_b), d_attn)
    far_part = pc.across(half_b)
    tok_a, send_a, keep_a, table_a = attn_bwd(
        lens, at, d_attn.reshape(n, seq, d), w_out, hot_back, lse_a, tf_a, q_a, qt_a, k_a, v_a, ctxt_a, nb_a, ant
    )
    proj_grad = mm(pooled, d_emb, TN)
    outer_grad = mm(got[:, d:], d_rows, TN)
    inner_all, far_part, far_table, send_a, proj_grad, outer_grad = after(
        inner_all, far_part, pc.across(table_b), send_a, proj_grad, outer_grad
    )
    table = table_a + far_table
    near_a, near_table = after(pc.core_swap(send_a), pc.core_swap(table))
    parts = pc.exchange(keep_a + far_part + near_a)
    input_grad = input_part(at, hidden_in, d_res, gain_attn, tok_a, tok_b, w_query, w_key, w_value, p_attn)
    inner_sum, gain_ffn_part = inner_done(at, inner_all, pc.core_swap(inner_all), w_inner)
    layer = layer_part(at, res, act_a, act_b, w_outer, p_outer)
    parts, input_grad, layer = after(parts, input_grad, layer)
    attn_all = pc.gather(pc.add(parts))
    table_sum = pc.total(table + near_table)
    gain_ffn_part = jnp.sum(gain_ffn_part[::8], axis=0)
    gain_ffn_grad = (gain_ffn_part + pc.across(gain_ffn_part)) / gain_ffn
    attn_all, gain_ffn_grad, table_sum, inner_sum, query_loss = after(
        attn_all, gain_ffn_grad, table_sum, inner_sum, query_loss
    )
    half = pc.core.reshape(1)
    near = pc.core_swap(attn_all)
    *grads, gain_own = attn_done(half, attn_all, w_query, w_key, w_value)
    near, *grads = after(near, *grads)
    gain_far = pc.across(gain_own[0])
    *grads, _ = attn_done(1 - half, near, w_query, w_key, w_value, grads)
    gain_far, *grads = after(gain_far, *grads)
    gain_own = gain_own[0] + gain_far
    q_grad, k_grad, v_grad, out_grad = grads
    gain_near = pc.core_swap(gain_own)
    gain_attn_grad = jnp.where(
        pc.core > 0, jnp.concatenate([gain_near, gain_own]), jnp.concatenate([gain_own, gain_near])
    ) / gain_attn
    return (
        layer,
        query_loss,
        input_grad,
        gain_attn_grad,
        q_grad,
        k_grad,
        v_grad,
        out_grad,
        table_sum[: rel_table.shape[1], :buckets].T,
        gain_ffn_grad,
        inner_sum,
        outer_grad,
        proj_grad,
    )


def solution(mesh):
    dp, tensor = mesh.shape["dp"], mesh.shape["tensor"]
    fine = jax.sharding.Mesh(mesh.devices.reshape(dp // 2, 2, tensor), ("chip", "core", "tensor"))
    rows = ("chip", "core")
    both = rows + ("tensor",)
    return jax.shard_map(
        functools.partial(body, dict(fine.shape)),
        mesh=fine,
        in_specs=(
            P(both, None, None),
            P(rows),
            P(both, None),
            P(both),
            P(),
            P(None, "tensor"),
            P(None, "tensor"),
            P(None, "tensor"),
            P("tensor", None),
            P(None, "tensor"),
            P(),
            P(None, "tensor"),
            P("tensor", None),
            P(),
        ),
        out_specs=(
            P(both, None, None),
            P(both),
            P(both, None, None),
            P(),
            P(None, "tensor"),
            P(None, "tensor"),
            P(None, "tensor"),
            P("tensor", None),
            P(None, "tensor"),
            P(),
            P(None, "tensor"),
            P("tensor", None),
            P(),
        ),
        check_vma=False,
    )
```

```python
import functools

import numpy as np

import jax
import jax.numpy as jnp
from jax import lax
from jax.experimental import pallas as pl
from jax.experimental.pallas import tpu as pltpu
from jax.sharding import PartitionSpec as P

LARGE_STEPS = (12, 16, 23, 32, 46, 64, 91)
SHARPNESS = 0.02
LOSS_SCALE = 256.0
EPS = 1e-06
NEG = -1e30
BF = jnp.bfloat16
F32 = jnp.float32
TILE = 128
BUCKETS = 32
GELU_A = 0.7978845608028654
GELU_B = 0.044715
MIB = 1024 * 1024

NN = (((1,), (0,)), ((), ()))
NT = (((1,), (1,)), ((), ()))
TN = (((0,), (0,)), ((), ()))


def mm(a, b, dims=NN):
    return lax.dot_general(a, b, dims, preferred_element_type=F32)


def bucket_of(r):
    a = np.abs(r)
    far = 8 + sum((a >= t).astype(np.int32) for t in LARGE_STEPS)
    return np.where(r > 0, 16, 0) + np.where(a < 8, a, far)


def diag_onehot(buckets, back):
    lane = np.arange(2 * TILE)
    at = lane - TILE + 1 if back else TILE - 1 - lane
    idx = np.concatenate([bucket_of(TILE * d + at) for d in (-1, 0, 1)])
    hot = (idx[:, None] == np.arange(buckets)[None, :]).astype(np.float32)
    hot[2 * TILE - 1 :: 2 * TILE] = 0.0
    return hot


def params(mib=60):
    return pltpu.CompilerParams(vmem_limit_bytes=mib * MIB)


def cost(us):
    return pl.CostEstimate(flops=0, bytes_accessed=int(us * 3.6e6), transcendentals=0)

ANY = pl.BlockSpec(memory_space=pl.ANY)
SMEM_SPEC = pl.BlockSpec(memory_space=pltpu.SMEM)


def const_spec(shape):
    zeros = (0,) * len(shape)
    return pl.BlockSpec(tuple(shape), lambda b: zeros, pipeline_mode=pl.Buffered(1))


def out_const(shape):
    zeros = (0,) * len(shape)
    return pl.BlockSpec(tuple(shape), lambda b: zeros)


def row_spec(shape):
    tail = (0,) * (len(shape) - 1)
    return pl.BlockSpec((1,) + tuple(shape[1:]), lambda b: (b,) + tail)


def sds(shape, dtype):
    return jax.ShapeDtypeStruct(tuple(shape), dtype)


def split3(t):
    hi = t.astype(BF)
    rest = t - hi.astype(F32)
    mid = rest.astype(BF)
    return hi, mid, (rest - mid.astype(F32)).astype(BF)


def run_copies(copies):
    for c in copies:
        c.start()
    for c in copies:
        c.wait()


def out_pieces(width, d):
    rows, tall = width // 4, width // 6
    rest = rows - tall
    out = [((0, tall, 0, d), (0, tall, 0, d))]
    for i in range(2):
        out.append(((tall, rest, i * width, width), (i * rest, rest, d, width)))
    return out


def pack_kernel(at_ref, tab_ref, wq, wk, wv, wo, wi, wu, s0, s1, s2, sem):
    at = at_ref[0]
    d, width = wq.shape
    rows = d // 4

    def part(w, dst, i):
        count = w.shape[0] // 4
        src = w.at[pl.ds(pl.multiple_of(at * count, count), count)]
        return pltpu.make_async_copy(src, dst, sem.at[i])

    copies = [part(w, s0.at[pl.ds(0, rows), width * i : width * (i + 1)], i) for i, w in enumerate((wq, wk, wv))]
    copies += [part(wi, s1, 3), part(wu, s2, 4)]
    for i, (a, b) in enumerate(out_pieces(width, d)):
        src = wo.at[pl.ds(pl.multiple_of(at * (width // 4) + a[0], 32), a[1]), a[2] : a[2] + a[3]]
        dst = s0.at[pl.ds(rows + 16 + b[0], b[1]), b[2] : b[2] + b[3]]
        copies.append(pltpu.make_async_copy(src, dst, sem.at[5 + i]))
    for c in copies:
        c.start()
    s0[rows : rows + 16, :] = jnp.zeros((16, s0.shape[1]), BF)
    heads, buckets = tab_ref.shape
    for k, t in enumerate(split3(tab_ref[...])):
        s0[rows : rows + heads, TILE * k : TILE * k + buckets] = t
    for c in copies:
        c.wait()


def pack_weights(at, table, wq, wk, wv, wo, wi, wu):
    d, half = wi.shape
    width = wq.shape[1]
    vm = pl.BlockSpec(memory_space=pltpu.VMEM)
    return pl.pallas_call(
        pack_kernel,
        in_specs=[SMEM_SPEC, vm] + [ANY] * 6,
        out_specs=[vm] * 3,
        out_shape=[
            sds((d // 4 + 16 + width // 6, 3 * width), BF),
            sds((d // 4, half), BF),
            sds((half // 4, d), BF),
        ],
        scratch_shapes=[pltpu.SemaphoreType.DMA((8,))],
        compiler_params=params(),
        cost_estimate=cost(3),
        name="pack_weights",
    )(at, table, wq, wk, wv, wo, wi, wu)


def quarter_spots(at):
    core, xb = at // 2, at % 2
    return [at, 2 * core + 1 - xb, 2 * (1 - core) + xb, 2 * (1 - core) + 1 - xb]


def out_copies(at, packs, dst, sem):
    width, d = dst.shape
    base = d // 4 + 16
    out = []
    for i, (p, s) in enumerate(zip(packs, quarter_spots(at))):
        for j, (a, b) in enumerate(out_pieces(width, d)):
            src = p.at[pl.ds(base + b[0], b[1]), b[2] : b[2] + b[3]]
            to = dst.at[pl.ds(pl.multiple_of(s * (width // 4) + a[0], 32), a[1]), a[2] : a[2] + a[3]]
            out.append(pltpu.make_async_copy(src, to, sem.at[3 * i + j]))
    return out


def join_copies(at, packs, dst, sem):
    rows = dst.shape[0] // 4
    out = []
    for i, (p, s) in enumerate(zip(packs, quarter_spots(at))):
        to = dst.at[pl.ds(pl.multiple_of(s * rows, rows), rows)]
        out.append(pltpu.make_async_copy(p.at[pl.ds(0, rows)], to, sem.at[i]))
    return out


EXTRA = 16


def key_extras(length, rows):
    row = lax.broadcasted_iota(jnp.int32, (rows, TILE), 0)
    lane = lax.broadcasted_iota(jnp.int32, (rows, TILE), 1) & 63
    blk = (lane - 1) & 3
    hot = (lane >= 1) & (lane < 13) & (blk == row // TILE)
    one = ((lane == 0) & (row >= length)) | hot | ((lane >= 13) & (lane < EXTRA))
    return jnp.where(one, 1.0, 0.0)


def far_rows(tf_ref, h, seq):
    row = lax.broadcasted_iota(jnp.int32, (EXTRA, seq), 0)
    diff = ((row - 1) & 3) - lax.broadcasted_iota(jnp.int32, (EXTRA, seq), 1) // TILE
    out = jnp.where(row == 0, NEG, 0.0)
    last, mid = BUCKETS - 1, BUCKETS // 2 - 1
    for k in range(3):
        mine = (row >= 1 + 4 * k) & (row < 5 + 4 * k)
        out = out + jnp.where(mine & (diff >= 2), tf_ref[k, h : h + 1, last : last + 1], 0.0)
        out = out + jnp.where(mine & (diff <= -2), tf_ref[k, h : h + 1, mid : mid + 1], 0.0)
    return out


def stack_rows(e, main, extra):
    pad = jnp.zeros((64 - extra.shape[0], extra.shape[1]), BF)
    return jnp.concatenate([main, extra, pad] if e == 0 else [extra, pad, main], axis=0)


def near_bias(s, nb_ref, h, ib):
    rows = []
    for bj in range(s.shape[0] // TILE):
        parts = []
        for t in range(2):
            piece = s[TILE * bj : TILE * (bj + 1), TILE * t : TILE * (t + 1)]
            d = bj - (2 * ib + t)
            parts.append(piece + nb_ref[3 * h + d + 1] if abs(d) <= 1 else piece)
        rows.append(jnp.concatenate(parts, axis=1))
    return rows


def set_bias(parts, hot_ref, tf_ref, nb_ref):
    for k in range(3):
        tf_ref[k] = parts[k].astype(F32)
    hot = hot_ref[...]
    bv = mm(parts[0], hot) + mm(parts[1], hot) + mm(parts[2], hot)
    for t in range(nb_ref.shape[0]):
        h, k = t // 3, t % 3
        v = jnp.broadcast_to(bv[h : h + 1, 2 * TILE * k : 2 * TILE * (k + 1)], (TILE, 2 * TILE))
        nb_ref[t] = pltpu.roll(v, TILE + 1, 1, stride=1, stride_axis=0)[:, :TILE]


def attn_rows(an, length, ws, outs, nb_ref, tf_ref, s_ref, p_ref, between=None):
    q_ref, qt_ref, k_ref, v_ref, ctx_ref, ctxt_ref, lse_ref = outs
    seq = an.shape[0]
    width = q_ref.shape[2]
    for ref, w in zip((q_ref, k_ref), ws):
        ref[0] = mm(an, w[...]).astype(BF)
    kx = key_extras(length, seq)
    lane = lax.broadcasted_iota(jnp.int32, (seq, TILE), 1)
    blocks = [(h, ib) for h in range(width // 64) for ib in range(seq // 256)]
    keys, queries, values, tops, rows = {}, {}, {}, {}, {}

    def prepare(h):
        pair, e = h // 2, h % 2
        cols = slice(TILE * pair, TILE * (pair + 1))
        if e == 0:
            qt_ref[0, cols, :] = jnp.transpose(q_ref[0, :, cols])
        mine = lane < 64 if e == 0 else lane >= 64
        keys[h] = jnp.where(mine, k_ref[0, :, cols].astype(F32), kx).astype(BF)
        qt = qt_ref[0, 64 * h : 64 * (h + 1), :]
        queries[h] = stack_rows(e, qt, far_rows(tf_ref, h, seq).astype(BF))

    def start(t):
        h, ib = blocks[t]
        if ib == 0:
            prepare(h)
        s = mm(keys[h], queries[h][:, 256 * ib : 256 * (ib + 1)])
        return near_bias(s, nb_ref, h, ib)

    def score(t, bj, pieces):
        piece = pieces[bj]
        s_ref[t % 2, TILE * bj : TILE * (bj + 1), :] = piece
        m = jnp.max(piece.reshape(TILE // 8, 8, 256), axis=0)
        tops[t] = m if bj == 0 else jnp.maximum(tops[t], m)
        if bj == seq // TILE - 1:
            tops[t] = jnp.max(tops[t], axis=0, keepdims=True)

    def soft(t, bj):
        h, ib = blocks[t]
        at = slice(TILE * bj, TILE * (bj + 1))
        p_ref[h % 2, at, 256 * ib : 256 * (ib + 1)] = jnp.exp(s_ref[t % 2, at, :] - tops[t]).astype(BF)

    def combine(h):
        per = seq // 256
        top = jnp.concatenate([tops[per * h + i] for i in range(per)], axis=1)
        if h % 2 == 0:
            values[h // 2] = jnp.transpose(v_ref[0, :, TILE * (h // 2) : TILE * (h // 2 + 1)])
        vt = values[h // 2][64 * (h % 2) : 64 * (h % 2 + 1), :]
        got = mm(jnp.concatenate([vt, jnp.ones((16, seq), BF)], axis=0), p_ref[h % 2])
        total = got[64:65]
        lse_ref[0, h : h + 1, :] = top + jnp.log(total)
        rows[h] = got[:64] * (1.0 / total)
        if h % 2 == 1:
            pair = h // 2
            cols = slice(TILE * pair, TILE * (pair + 1))
            ct = jnp.concatenate([rows[h - 1], rows[h]], axis=0).astype(BF)
            ctxt_ref[0, cols, :] = ct
            ctx_ref[0, :, cols] = jnp.transpose(ct)

    for t in range(len(blocks) + 1):
        if t < len(blocks):
            pieces = start(t)
            for bj in range(seq // TILE):
                score(t, bj, pieces)
        if t == 0:
            v_ref[0] = mm(an, ws[2][...]).astype(BF)
        if t == 5 and between is not None:
            between()
        if t > 0:
            for bj in range(seq // TILE):
                soft(t - 1, bj)
            if blocks[t - 1][1] == seq // 256 - 1:
                combine(blocks[t - 1][0])


def attn_own_kernel(lens, x_ref, gain_ref, wq, wk, wv, tab_ref, hot_ref, an_ref, ant_ref, *refs):
    outs, (nb_ref, tf_ref, s_ref, p_ref) = refs[:7], refs[7:]
    b = pl.program_id(0)

    @pl.when(b == 0)
    def _():
        heads, buckets = tab_ref.shape
        wide = jnp.concatenate([tab_ref[...], jnp.zeros((heads, TILE - buckets), F32)], axis=1)
        wide = jnp.concatenate([wide, jnp.zeros((16 - heads, TILE), F32)], axis=0)
        set_bias(split3(wide), hot_ref, tf_ref, nb_ref)

    x = x_ref[0].astype(F32)
    inv = lax.rsqrt(jnp.mean(x * x, axis=-1, keepdims=True) + EPS)
    an = (x * inv * gain_ref[...]).astype(BF)
    an_ref[0] = an
    ant_ref[...] = jnp.transpose(an)
    attn_rows(an, lens[b], (wq, wk, wv), outs, nb_ref, tf_ref, s_ref, p_ref)


def attn_other_kernel(lens, at_ref, an_ref, hot_ref, gain_ref, x_hbm, ca_hbm, wo_hbm, p0, p1, p2, p3, *refs):
    outs, (nb_ref, tf_ref, res_ref, fin_ref, fint_ref, rsum_ref, f0_ref, f1_ref) = list(refs[:6]), refs[6:14]
    (s_ref, p_ref, w_ref, tab_ref, wb_ref, c_ref, x_ref, ca_ref, wo_ref, sem, sem1, sem2) = refs[14:]
    outs.insert(4, c_ref)
    b = pl.program_id(0)
    late = out_copies(at_ref[0], (p0, p1, p2, p3), wb_ref, sem1)
    moves = ((x_hbm, x_ref), (ca_hbm, ca_ref), (wo_hbm, wo_ref))
    more = [pltpu.make_async_copy(x, y, sem2.at[i]) for i, (x, y) in enumerate(moves)]

    @pl.when(b == 0)
    def _():
        rows = w_ref.shape[0] // 4
        copies = join_copies(at_ref[0], (p0, p1, p2, p3), w_ref, sem)
        copies.append(pltpu.make_async_copy(p0.at[pl.ds(rows, 16)], tab_ref, sem.at[4]))
        for c in copies + more + late:
            c.start()
        for c in copies:
            c.wait()
        parts = [tab_ref[:, TILE * k : TILE * (k + 1)] for k in range(3)]
        set_bias(parts, hot_ref, tf_ref, nb_ref)
        for c in more:
            c.wait()

    width = outs[0].shape[2]
    ws = [w_ref.at[:, width * k : width * (k + 1)] for k in range(3)]

    def between():
        res_ref[0] = x_ref[b].astype(F32) + mm(ca_ref[b], wo_ref[...])

    attn_rows(an_ref[0], lens[b], ws, outs, nb_ref, tf_ref, s_ref, p_ref, between)

    @pl.when(b == 0)
    def _():
        for c in late:
            c.wait()

    res = res_ref[0] + mm(outs[4][0], wb_ref[...])
    res_ref[0] = res
    inv = lax.rsqrt(jnp.mean(res * res, axis=-1, keepdims=True) + EPS)
    fin = (res * inv * gain_ref[...]).astype(BF)
    fin_ref[0] = fin
    for i, f_ref in enumerate((f0_ref, f1_ref)):

        @pl.when(b == i)
        def _():
            f_ref[0] = fin

    vcol = (lax.broadcasted_iota(jnp.int32, (res.shape[0], TILE), 0) < lens[b]).astype(F32)[:, :1]
    fint_ref[...] = jnp.transpose((fin.astype(F32) * vcol).astype(BF))
    rsum_ref[0] = jnp.sum(res * vcol, axis=0, keepdims=True)


def attn_outs(n, seq, width):
    heads = width // 64
    tok, turned = sds((n, seq, width), BF), sds((n, width, seq), BF)
    rows = [tok, turned, tok, tok, tok, turned, sds((n, 8, seq), F32)]
    flat = [sds((3 * heads, TILE, TILE), F32), sds((3, 16, TILE), F32)]
    scratch = [pltpu.VMEM((2, seq, 256), F32), pltpu.VMEM((2, seq, seq), BF)]
    return rows + flat, [row_spec(o.shape) for o in rows] + [out_const(o.shape) for o in flat], scratch


def attn_own(lens, x, gain, wq, wk, wv, table, hot):
    n, seq, d = x.shape
    outs, specs, scratch = attn_outs(n, seq, wq.shape[1])
    return pl.pallas_call(
        attn_own_kernel,
        grid=(n,),
        in_specs=[SMEM_SPEC, row_spec(x.shape), const_spec((1, d))]
        + [const_spec(wq.shape)] * 3
        + [const_spec(table.shape), const_spec(hot.shape)],
        out_specs=[row_spec(x.shape), pl.BlockSpec((d, seq), lambda b: (0, b))] + specs,
        out_shape=[sds((n, seq, d), BF), sds((d, n * seq), BF)] + outs,
        scratch_shapes=scratch,
        compiler_params=params(),
        cost_estimate=cost(12),
        name="attn_own",
    )(lens, x, gain.reshape(1, d), wq, wk, wv, table, hot)


def attn_other(lens, at, an, hot, x, ctx_a, wo, gain, packs):
    n, seq, d = an.shape
    width = wo.shape[0]
    outs, specs, scratch = attn_outs(n, seq, width)
    del outs[4], specs[4]
    more = [sds((n, seq, d), F32), sds((n, seq, d), BF), sds((d, n * seq), BF), sds((n, 1, d), F32)]
    more_specs = [row_spec(o.shape) for o in more]
    more_specs[2] = pl.BlockSpec((d, seq), lambda b: (0, b))
    more += [sds((1, seq, d), BF)] * n
    more_specs += [out_const((1, seq, d))] * n
    return pl.pallas_call(
        attn_other_kernel,
        grid=(n,),
        in_specs=[SMEM_SPEC, SMEM_SPEC, row_spec(an.shape), const_spec(hot.shape), const_spec((1, d))]
        + [ANY] * 7,
        out_specs=specs + more_specs,
        out_shape=outs + more,
        scratch_shapes=scratch
        + [
            pltpu.VMEM((d, 3 * width), BF),
            pltpu.VMEM((16, 3 * width), BF),
            pltpu.VMEM(wo.shape, BF),
            pltpu.VMEM((1, seq, width), BF),
            pltpu.VMEM(x.shape, BF),
            pltpu.VMEM(ctx_a.shape, BF),
            pltpu.VMEM(wo.shape, BF),
            pltpu.SemaphoreType.DMA((5,)),
            pltpu.SemaphoreType.DMA((12,)),
            pltpu.SemaphoreType.DMA((3,)),
        ],
        compiler_params=params(),
        cost_estimate=cost(15),
        name="attn_other",
    )(lens, at, an, hot, gain, x, ctx_a, wo, *packs)


def attn_back(b, n, length, core, w, d_attn, ins, outs, scratch, late):
    (q_ref, qt_ref, k_ref, v_ref, ct_ref, lse_ref, nb_ref, tf_ref, ant_ref, hot_ref) = ins
    (all_hbm, send_ref, keep_ref, table_ref) = outs
    (dc_ref, dct_ref, t_ref, fsum_ref, p_ref, ds_ref, all_ref, da_ref, go_ref, out_sem) = scratch
    seq, width = q_ref.shape[1], q_ref.shape[2]
    heads = width // 64
    nblk = seq // TILE
    here = pl.ds(pl.multiple_of(b * seq, seq), seq)

    @pl.when(b == 0)
    def _():
        t_ref[...] = jnp.zeros_like(t_ref)
        fsum_ref[...] = jnp.zeros_like(fsum_ref)
        table_ref[...] = jnp.zeros_like(table_ref)

    dct_ref[...] = mm(w, d_attn, NT).astype(BF)
    dc_ref[...] = jnp.transpose(dct_ref[...])
    kx = key_extras(length, seq)
    lane = lax.broadcasted_iota(jnp.int32, (seq, TILE), 1)
    vx = jnp.where((lane & 63) < 3, 1.0, 0.0)
    keys, values, queries, grads, turned = {}, {}, {}, {}, {}

    def prepare(h):
        pair, e = h // 2, h % 2
        cols = slice(TILE * pair, TILE * (pair + 1))
        mine = lane < 64 if e == 0 else lane >= 64
        if e == 0:
            turned[pair] = jnp.transpose(k_ref[b, :, cols])
        keys[h] = jnp.where(mine, k_ref[b, :, cols].astype(F32), kx).astype(BF)
        values[h] = jnp.where(mine, v_ref[b, :, cols].astype(F32), vx).astype(BF)
        at = slice(64 * h, 64 * (h + 1))
        lse = split3(-lse_ref[b, h : h + 1, :])
        extra = far_rows(tf_ref, h, seq)
        row = lax.broadcasted_iota(jnp.int32, (EXTRA, seq), 0)
        for k in range(3):
            extra = jnp.where(row == 13 + k, lse[k].astype(F32), extra)
        queries[h] = stack_rows(e, qt_ref[b, at, :], extra.astype(BF))
        along = jnp.sum(dct_ref[at, :].astype(F32) * ct_ref[b, at, :].astype(F32), axis=0, keepdims=True)
        extra = jnp.zeros((EXTRA, seq), F32)
        for k, part in enumerate(split3(-along)):
            extra = jnp.where(row == k, part.astype(F32), extra)
        grads[h] = stack_rows(e, dct_ref[at, :], extra.astype(BF))

    def block(h, ib):
        pair, e = h // 2, h % 2
        at = slice(256 * ib, 256 * (ib + 1))
        to = slice(seq * e + 256 * ib, seq * e + 256 * (ib + 1))
        s = mm(keys[h], queries[h][:, at])
        dp = mm(values[h], grads[h][:, at])
        near, far = {}, {}
        for bj, piece in enumerate(near_bias(s, nb_ref, h, ib)):
            rows = slice(TILE * bj, TILE * (bj + 1))
            p = jnp.exp(piece)
            ds = p * dp[rows, :]
            p_ref[pair % 2, rows, to] = p.astype(BF)
            ds_ref[pair % 2, rows, to] = ds.astype(BF)
            for t in range(2):
                d = bj - (2 * ib + t)
                one = ds[:, TILE * t : TILE * (t + 1)]
                if abs(d) <= 1:
                    near[d] = near[d] + one if d in near else one
                else:
                    one = jnp.sum(one.reshape(TILE // 8, 8, TILE), axis=0)
                    side = 1 if d > 0 else 0
                    far[side] = far[side] + one if side in far else one
        for d, one in near.items():
            t_ref[3 * h + d + 1] += one
        for side, one in far.items():
            fsum_ref[2 * h + side] += one

    def finish(pair, part):
        slot = pair % 2
        cols = slice(TILE * pair, TILE * (pair + 1))
        if part < 2:
            src, rhs = ((p_ref, dc_ref[:, cols]), (ds_ref, q_ref[b, :, cols]))[part]
            one = jnp.where(lane < 64, mm(src[slot, :, :seq], rhs), mm(src[slot, :, seq:], rhs)).astype(BF)
            base = width * (2 - part)
            all_ref[here, base + TILE * pair : base + TILE * (pair + 1)] = one
        if part == 2:
            kt = turned[pair]
            dqt = [mm(kt[64 * e : 64 * (e + 1), :], ds_ref[slot, :, seq * e : seq * (e + 1)]) for e in range(2)]
            one = jnp.transpose(jnp.concatenate(dqt, axis=0).astype(BF))
            all_ref[here, TILE * pair : TILE * (pair + 1)] = one

    for pair in range(heads // 2):
        step = 0
        for e in range(2):
            prepare(2 * pair + e)
            for ib in range(seq // 256):
                block(2 * pair + e, ib)
                if pair > 0 and step < 3:
                    finish(pair - 1, step)
                step += 1
    for part in range(3):
        finish(heads // 2 - 1, part)
    done = send_rows(b, n, all_ref, all_hbm, out_sem)

    @pl.when(b == n - 1)
    def _():
        for c in late:
            c.wait()
        rows = ant_ref.shape[0] // 2
        out = None
        for i in range(n):
            one = mm(ct_ref[i], da_ref[seq * i : seq * (i + 1), :])
            out = one if out is None else out + one
        go_ref[:width, :] = out[:, :width].astype(BF)
        go_ref[width:, :] = out[:, width:].astype(BF)
        for ref, half in ((send_ref, 1 - core), (keep_ref, core)):
            at = pl.ds(pl.multiple_of(half * rows, rows), rows)
            ref[:, : 3 * width] = mm(ant_ref[at, :], all_ref[...]).astype(BF)
            ref[:, 3 * width :] = go_ref[at, :]
        turn = lax.broadcasted_iota(jnp.int32, (TILE, TILE), 0) + lax.broadcasted_iota(jnp.int32, (TILE, TILE), 1)
        turn = jnp.where(turn == TILE - 1, 1.0, 0.0).astype(BF)
        tiles = t_ref.shape[0]
        hi, lo, _ = split3(t_ref[...].reshape(tiles * TILE, TILE))
        back = mm(jnp.concatenate([hi, lo], axis=1), jnp.concatenate([turn, turn], axis=0))
        diag = []
        for t in range(tiles):
            x = jnp.concatenate([back[TILE * t : TILE * (t + 1)], jnp.zeros((TILE, TILE), F32)], axis=1)
            x = pltpu.roll(x, 0, 1, stride=1, stride_axis=0)
            diag.append(jnp.sum(x, axis=0, keepdims=True))
        lines = [jnp.concatenate(diag[3 * h : 3 * h + 3], axis=1) for h in range(heads)]
        lines.append(jnp.zeros((16 - heads, lines[0].shape[1]), F32))
        near = [mm(part, hot_ref[...]) for part in split3(jnp.concatenate(lines, axis=0))]
        spot = lax.broadcasted_iota(jnp.int32, (1, TILE), 1)
        for h in range(heads):
            one = near[0][h : h + 1] + near[1][h : h + 1] + near[2][h : h + 1]
            for side, bucket in ((0, BUCKETS // 2 - 1), (1, BUCKETS - 1)):
                far = jnp.sum(jnp.sum(fsum_ref[2 * h + side], axis=0, keepdims=True), axis=1, keepdims=True)
                one = one + jnp.where(spot == bucket, far, 0.0)
            table_ref[h : h + 1, :] = one
        for c in done:
            c.wait()


def send_rows(b, n, src, dst, sem):
    rows = src.shape[0] // n
    copies = [pltpu.make_async_copy(src.at[pl.ds(i * rows, rows)], dst.at[pl.ds(i * rows, rows)], sem.at[i]) for i in range(n)]
    for i, c in enumerate(copies):

        @pl.when(b == i)
        def _():
            c.start()

    return copies


def back_outs(n, seq, width, d):
    half = sds((d // 2, 4 * width), BF)
    outs = [sds((n * seq, 3 * width), BF), half, half, sds((8, TILE), F32)]
    return outs, [ANY] + [out_const(o.shape) for o in outs[1:]]


def back_scratch(n, seq, width, d):
    heads = width // 64
    return [
        pltpu.VMEM((seq, width), BF),
        pltpu.VMEM((width, seq), BF),
        pltpu.VMEM((3 * heads, TILE, TILE), F32),
        pltpu.VMEM((2 * heads, 8, TILE), F32),
        pltpu.VMEM((2, seq, 2 * seq), BF),
        pltpu.VMEM((2, seq, 2 * seq), BF),
        pltpu.VMEM((n * seq, 3 * width), BF),
        pltpu.VMEM((n * seq, d), BF),
        pltpu.VMEM((d, width), BF),
        pltpu.SemaphoreType.DMA((n,)),
    ]


def attn_bwd_kernel(lens, at_ref, da_blk, wo_ref, hot_ref, lse_ref, tf_ref, *refs):
    hbm, outs, scratch = refs[:7], refs[7:11], refs[11:21]
    bufs, sem = refs[21:28], refs[28]
    b = pl.program_id(0)
    n = da_blk.shape[0] * lse_ref.shape[0]
    copies = [pltpu.make_async_copy(x, y, sem.at[i]) for i, (x, y) in enumerate(zip(hbm, bufs))]

    @pl.when(b == 0)
    def _():
        for c in copies:
            c.start()
        for c in copies[:-1]:
            c.wait()

    q, qt, k, v, ct, nb, ant = bufs
    ins = (q, qt, k, v, ct, lse_ref, nb, tf_ref, ant, hot_ref)
    seq = da_blk.shape[1]
    scratch[7][pl.ds(pl.multiple_of(b * seq, seq), seq), :] = da_blk[0]
    attn_back(b, n, lens[b], at_ref[0] // 2, wo_ref[...], da_blk[0], ins, outs, scratch, copies[-1:])


def attn_bwd(lens, at, d_attn, wo, hot, lse, tf, *arrays):
    n, seq, d = d_attn.shape
    width = wo.shape[0]
    outs, specs = back_outs(n, seq, width, d)
    return pl.pallas_call(
        attn_bwd_kernel,
        grid=(n,),
        in_specs=[SMEM_SPEC, SMEM_SPEC, row_spec(d_attn.shape)]
        + [const_spec(x.shape) for x in (wo, hot, lse, tf)]
        + [ANY] * 7,
        out_specs=specs,
        out_shape=outs,
        scratch_shapes=back_scratch(n, seq, width, d)
        + [pltpu.VMEM(x.shape, x.dtype) for x in arrays]
        + [pltpu.SemaphoreType.DMA((7,))],
        compiler_params=params(),
        cost_estimate=cost(16),
        name="attn_bwd",
    )(lens, at, d_attn, wo, hot, lse, tf, *arrays)


def gelu_parts(v):
    v2 = v * v
    half = 0.5 + 0.5 * jnp.tanh(v * (GELU_A + (GELU_A * GELU_B) * v2))
    act = v * half
    return act, half + (act - act * half) * (2.0 * GELU_A + (6.0 * GELU_A * GELU_B) * v2)


def ffn_fwd_kernel(lens, at_ref, fin_ref, rs_ref, wi_ref, wu_ref, p0, p1, p2, p3, *refs):
    (act_ref, gp_ref, actb_ref, gpb_ref, asum_ref, rsum_ref) = refs[:6]
    (wib_ref, wu_buf, v_ref, sem1, sem2) = refs[6:]
    b = pl.program_id(0)
    late = join_copies(at_ref[0], (p0, p1, p2, p3), wib_ref, sem1) + [pltpu.make_async_copy(wu_ref, wu_buf, sem2)]

    @pl.when(b == 0)
    def _():
        run_copies(late)

    fin = fin_ref[0]
    seq = fin.shape[0]
    half = wi_ref.shape[1]
    chunk = v_ref.shape[2]
    length = lens[b]
    vrow = (lax.broadcasted_iota(jnp.int32, (8, seq), 1) < length).astype(F32).astype(BF)
    spot = lambda c: slice(c * chunk, (c + 1) * chunk)
    parts = [(w, a, g, c) for w, a, g in ((wi_ref, act_ref, gp_ref), (wib_ref, actb_ref, gpb_ref)) for c in range(half // chunk)]

    def project(t):
        w, _, _, c = parts[t]
        v_ref[t % 2] = mm(fin, w[:, spot(c)])

    project(0)
    for t, (_, a_ref, g_ref, c) in enumerate(parts):
        if t + 1 < len(parts):
            project(t + 1)
        for r in range(seq // TILE):
            rows = slice(TILE * r, TILE * (r + 1))
            act, slope = gelu_parts(v_ref[t % 2, rows, :])
            a_ref[0, rows, spot(c)] = act.astype(BF)
            g_ref[0, rows, spot(c)] = slope.astype(BF)
        asum_ref[0, :, spot(t)] = mm(vrow, a_ref[0, :, spot(c)])[:1]
    own = asum_ref[0, :, :half]
    hi = own.astype(BF)
    lo = (own - hi.astype(F32)).astype(BF)
    two_rows = jnp.concatenate([hi.astype(F32), lo.astype(F32), jnp.zeros((14, half), F32)], axis=0).astype(BF)
    branch = mm(two_rows, wu_buf[...])
    rsum_ref[0] = rs_ref[0] + branch[0:1] + branch[1:2]


def ffn_fwd(lens, at, fin, rsum, wi, wu, packs):
    n, seq, d = fin.shape
    half = wi.shape[1]
    wide = sds((n, seq, half), BF)
    outs = [wide, wide, wide, wide, sds((n, 1, 2 * half), F32), sds((n, 1, d), F32)]
    return pl.pallas_call(
        ffn_fwd_kernel,
        grid=(n,),
        in_specs=[SMEM_SPEC, SMEM_SPEC, row_spec(fin.shape), row_spec(rsum.shape), const_spec(wi.shape)] + [ANY] * 5,
        out_specs=[row_spec(o.shape) for o in outs],
        out_shape=outs,
        scratch_shapes=[
            pltpu.VMEM(wi.shape, BF),
            pltpu.VMEM(wu.shape, BF),
            pltpu.VMEM((2, seq, 512), F32),
            pltpu.SemaphoreType.DMA((4,)),
            pltpu.SemaphoreType.DMA,
        ],
        compiler_params=params(),
        cost_estimate=cost(16),
        name="ffn_fwd",
    )(lens, at, fin, rsum, wi, wu, *packs)


def pool_kernel(lens, at_ref, asum_ref, rs_ref, p0, p1, p2, p3, out_ref, wb_ref, sem):
    run_copies(join_copies(at_ref[0], (p0, p1, p2, p3), wb_ref, sem))
    n = asum_ref.shape[0]
    half = wb_ref.shape[0]
    rows = [asum_ref[i, :, half:] for i in range(n)]
    hi = [r.astype(BF) for r in rows]
    lo = [(r - h.astype(F32)).astype(BF) for r, h in zip(rows, hi)]
    pad = jnp.zeros((16 - 2 * n, half), F32)
    br = mm(jnp.concatenate([t.astype(F32) for t in hi + lo] + [pad], axis=0).astype(BF), wb_ref[...])
    for i in range(n):
        total = rs_ref[i] + br[i : i + 1] + br[n + i : n + i + 1]
        out_ref[i : i + 1, :] = total / lens[i].astype(F32)


def pool(lens, at, asum, rsum, packs):
    n, _, d = rsum.shape
    half = asum.shape[2] // 2
    vm = pl.BlockSpec(memory_space=pltpu.VMEM)
    return pl.pallas_call(
        pool_kernel,
        in_specs=[SMEM_SPEC, SMEM_SPEC, vm, vm] + [ANY] * 4,
        out_specs=vm,
        out_shape=sds((8, d), F32),
        scratch_shapes=[pltpu.VMEM((half, d), BF), pltpu.SemaphoreType.DMA((4,))],
        compiler_params=params(16),
        cost_estimate=cost(4),
        name="pool",
    )(lens, at, asum, rsum, *packs)


def pre_kernel(lens, fint_ref, gp_ref, fn_ref, w_ref, out_ref, ft_ref, v_ref, s_ref):
    n, seq, _ = gp_ref.shape

    @pl.when(pl.program_id(0) == 0)
    def _():
        valid = lax.broadcasted_iota(jnp.int32, (seq, TILE), 0) < lens[n]
        ft_ref[...] = jnp.transpose((fn_ref[0].astype(F32) * valid.astype(F32)[:, :1]).astype(BF))

    v_ref[...] = mm(fn_ref[0], w_ref[...])
    for i in range(n):
        out_ref[i] = mm(fint_ref[:, seq * i : seq * (i + 1)], gp_ref[i]).astype(BF)
        for r in range(seq // TILE // n):
            at = slice(seq // n * i + TILE * r, seq // n * i + TILE * (r + 1))
            s_ref[at, :] = gelu_parts(v_ref[at, :])[1].astype(BF)
    out_ref[n] = mm(ft_ref[...], s_ref[...]).astype(BF)


def pre_inner(lens4, fint, gp, fn, wi):
    n, seq, half = gp.shape
    d = fint.shape[0]
    chunk = 512
    return pl.pallas_call(
        pre_kernel,
        grid=(half // chunk,),
        in_specs=[SMEM_SPEC, const_spec(fint.shape), pl.BlockSpec((n, seq, chunk), lambda c: (0, 0, c))]
        + [const_spec(fn.shape), pl.BlockSpec((d, chunk), lambda c: (0, c))],
        out_specs=pl.BlockSpec((n + 1, d, chunk), lambda c: (0, 0, c)),
        out_shape=sds((n + 1, d, half), BF),
        scratch_shapes=[pltpu.VMEM((d, seq), BF), pltpu.VMEM((seq, chunk), F32), pltpu.VMEM((seq, chunk), BF)],
        compiler_params=params(),
        cost_estimate=cost(9),
        name="pre_inner",
    )(lens4, fint, gp, fn, wi)


def loss_kernel(me_ref, at_ref, lens, pool_ref, q_ref, wp_hbm, pre_hbm, fn_hbm, wi_hbm, wu_hbm, *refs):
    (loss_ref, row_ref, g_ref, drow_ref, demb_ref, send_ref, keep_ref) = refs[:7]
    (wp_ref, wu_ref, pre_ref, fn_ref, wi_ref, ft_ref, gn_ref, v_ref, d_ref, sum_ref, sem) = refs[7:]
    moves = ((wp_hbm, wp_ref), (wu_hbm, wu_ref), (fn_hbm, fn_ref), (wi_hbm, wi_ref), (pre_hbm, pre_ref))
    loads = [pltpu.make_async_copy(a, b, sem.at[i]) for i, (a, b) in enumerate(moves)]
    for c in loads:
        c.start()
    loads[0].wait()
    d = wp_ref.shape[0]
    count = pool_ref.shape[0]
    pooled = pool_ref[...]
    qs = q_ref[:, :d]
    ints = q_ref[:, d : d + TILE].astype(F32)
    pos = (ints[:, 0:1] * 256.0 + ints[:, 1:2]).astype(jnp.int32)
    length = ints[:, 2:3] * 256.0 + ints[:, 3:4]
    wp = wp_ref[...]
    emb = mm(pooled, wp)
    inv = lax.rsqrt(jnp.sum(emb * emb, axis=-1, keepdims=True) + EPS)
    unit = (emb * inv).astype(BF)
    logits = mm(qs, unit, NT) / SHARPNESS
    top = jnp.max(logits, axis=-1, keepdims=True)
    total = top + jnp.log(jnp.sum(jnp.exp(logits - top), axis=-1, keepdims=True))
    hit = lax.broadcasted_iota(jnp.int32, (count, count), 1) == pos
    loss = total - jnp.sum(jnp.where(hit, logits, 0.0), axis=1, keepdims=True)
    d_logits = (LOSS_SCALE * (jnp.exp(logits - total) - jnp.where(hit, 1.0, 0.0))).astype(BF)
    d_unit = mm(d_logits, qs, TN) / SHARPNESS
    along = jnp.sum(emb * d_unit, axis=-1, keepdims=True)
    d_emb = (inv * d_unit - inv * inv * inv * along * emb).astype(BF)
    demb_ref[...] = d_emb
    rows = mm(d_emb, wp, NT) / length
    drow_ref[...] = rows.astype(BF)
    index = lax.broadcasted_iota(jnp.int32, (count, 1), 0)
    pick = lambda t, i: jnp.sum(jnp.where(index == i, t, 0.0), axis=0, keepdims=True)
    seq = fn_ref.shape[1]
    half = wi_ref.shape[1]
    n = pre_ref.shape[0] - 1
    own = [pick(rows, me_ref[i]) for i in range(n)]
    near = [pick(rows, me_ref[n + i]) for i in range(n)]
    lost = jnp.broadcast_to(loss, (count, TILE))
    pad = jnp.zeros((8 - n, d), F32)
    row_ref[...] = jnp.concatenate(own + [pad], axis=0)
    loss_ref[...] = jnp.concatenate([pick(lost, me_ref[i]) for i in range(n)] + [pad[:, :TILE]], axis=0)
    four = jnp.concatenate(own + near + [jnp.zeros((16 - 2 * n, d), F32)], axis=0).astype(BF)
    loads[1].wait()
    gn_ref[...] = mm(four, wu_ref[...], NT)[:8]
    g_ref[...] = gn_ref[...]
    for c in loads[2:]:
        c.wait()

    last = 2 * n - 1
    valid = lax.broadcasted_iota(jnp.int32, (seq, TILE), 0) < lens[last]
    ft_ref[...] = jnp.transpose((fn_ref[0].astype(F32) * valid.astype(F32)[:, :1]).astype(BF))
    chunk = v_ref.shape[2]
    steps = half // chunk
    spot = lambda c: slice(c * chunk, (c + 1) * chunk)
    rows2 = d // 2
    core = at_ref[0] // 2

    def project(c):
        v_ref[c % 2] = mm(fn_ref[0], wi_ref[:, spot(c)])

    def scale(c):
        for r in range(seq // TILE):
            at = slice(TILE * r, TILE * (r + 1))
            slope = gelu_parts(v_ref[c % 2, at, :])[1]
            d_ref[c % 2, at, :] = (slope * gn_ref[last : last + 1, spot(c)]).astype(BF)

    project(0)
    scale(0)
    for c in range(steps):
        if c + 1 < steps:
            project(c + 1)
        for r in range(d // TILE):
            at = slice(TILE * r, TILE * (r + 1))
            total = mm(ft_ref[at, :], d_ref[c % 2])
            for i in range(n + 1):
                total = total + pre_ref[i, at, spot(c)].astype(F32) * gn_ref[i : i + 1, spot(c)]
            sum_ref[at, :] = total.astype(BF)
        for ref, side in ((send_ref, 1 - core), (keep_ref, core)):
            ref[:, spot(c)] = sum_ref[pl.ds(pl.multiple_of(side * rows2, rows2), rows2), :]
        if c + 1 < steps:
            scale(c + 1)


def loss_all(me, at, lens4, pooled, queries, wp, pre, fn, wi, wu):
    half, d = wu.shape
    seq = fn.shape[1]
    count = pooled.shape[0]
    chunk = 512
    vm = pl.BlockSpec(memory_space=pltpu.VMEM)
    return pl.pallas_call(
        loss_kernel,
        in_specs=[SMEM_SPEC] * 3 + [vm] * 2 + [ANY] * 5,
        out_specs=[vm] * 7,
        out_shape=[
            sds((8, TILE), F32),
            sds((8, d), F32),
            sds((8, half), F32),
            sds((count, d), BF),
            sds((count, d), BF),
            sds((d // 2, half), BF),
            sds((d // 2, half), BF),
        ],
        scratch_shapes=[
            pltpu.VMEM(wp.shape, BF),
            pltpu.VMEM(wu.shape, BF),
            pltpu.VMEM(pre.shape, BF),
            pltpu.VMEM(fn.shape, BF),
            pltpu.VMEM(wi.shape, BF),
            pltpu.VMEM((d, seq), BF),
            pltpu.VMEM((8, half), F32),
            pltpu.VMEM((2, seq, chunk), F32),
            pltpu.VMEM((2, seq, chunk), BF),
            pltpu.VMEM((d, chunk), BF),
            pltpu.SemaphoreType.DMA((5,)),
        ],
        compiler_params=params(44),
        cost_estimate=cost(12),
        name="loss_inner",
    )(me, at, lens4, pooled, queries, wp, pre, fn, wi, wu)


def mid_bwd_kernel(lens, at_ref, g_ref, row_ref, gain_ref, hot_ref, lse_ref, tf_ref, *refs):
    hbm, packs0, packs1, packs2 = refs[:11], refs[11:15], refs[15:19], refs[19:23]
    (dres_hbm, dattn_hbm), outs, scratch = refs[23:25], refs[25:29], refs[29:39]
    bufs, (wib_ref, wob_ref, wub_ref, gb_ref, d_ref, dres_ref, sem, sem0, sem1, sem2, sem3) = refs[39:50], refs[50:]
    da_ref = scratch[7]
    wi_ref, gpa_ref, gpb_ref, res_all, q, qt, k, v, ct, nb, ant = bufs
    b = pl.program_id(0)
    n = lse_ref.shape[0]
    copies = [pltpu.make_async_copy(x, y, sem.at[i]) for i, (x, y) in enumerate(zip(hbm, bufs))]
    copies0 = out_copies(at_ref[0], packs0, wob_ref, sem0)
    copies1 = join_copies(at_ref[0], packs1, wib_ref, sem1)
    copies1 += join_copies(at_ref[0], packs2, wub_ref, sem3)

    def first(group):
        @pl.when(b == 0)
        def _():
            for c in group:
                c.wait()

    @pl.when(b == 0)
    def _():
        for c in copies[:2] + copies1 + copies[2:4] + copies0 + copies[4:]:
            c.start()

    first(copies[:2])
    _, seq, d = res_all.shape
    half = wi_ref.shape[1]
    chunk = d_ref.shape[2]
    steps = half // chunk
    parts = [(gp, w, c) for gp, w in ((gpa_ref, wi_ref), (gpb_ref, wib_ref)) for c in range(steps)]

    def scale(t):
        gp, _, c = parts[t]
        g = (g_ref if t < steps else gb_ref)[pl.ds(b, 1), c * chunk : (c + 1) * chunk]
        d_ref[t % 2] = (gp[b, :, c * chunk : (c + 1) * chunk].astype(F32) * g).astype(BF)

    d_two = None
    scale(0)
    for t, (_, w, c) in enumerate(parts):
        if t + 1 == steps:
            first(copies[2:4] + copies1)

            @pl.when(b == 0)
            def _():
                rows = jnp.concatenate([row_ref[...], jnp.zeros_like(row_ref)], axis=0).astype(BF)
                gb_ref[...] = mm(rows, wub_ref[...], NT)[:8]

        if t + 1 < len(parts):
            scale(t + 1)
        one = mm(d_ref[t % 2], w[:, c * chunk : (c + 1) * chunk], NT)
        d_two = one if d_two is None else d_two + one
    res = res_all[b]
    inv = lax.rsqrt(jnp.mean(res * res, axis=-1, keepdims=True) + EPS)
    scaled = d_two * gain_ref[...]
    along = jnp.sum(scaled * res, axis=-1, keepdims=True)
    valid = lax.broadcasted_iota(jnp.int32, (seq, TILE), 0) < lens[b]
    vcol = valid.astype(F32)[:, :1]
    inv = inv * vcol
    d_res = vcol * row_ref[pl.ds(b, 1), :] + scaled * inv - res * (inv * inv * inv * along / d)
    here = pl.ds(pl.multiple_of(b * seq, seq), seq)
    dres_ref[here, :] = d_res
    d_attn = d_res.astype(BF)
    da_ref[here, :] = d_attn
    done = send_rows(b, n, dres_ref, dres_hbm, sem2.at[0]) + send_rows(b, n, da_ref, dattn_hbm, sem2.at[1])
    first(copies0 + copies[4:-1])
    ins = (q, qt, k, v, ct, lse_ref, nb, tf_ref, ant, hot_ref)
    attn_back(b, n, lens[b], at_ref[0] // 2, wob_ref[...], d_attn, ins, outs, scratch, copies[-1:])

    @pl.when(b == n - 1)
    def _():
        for c in done:
            c.wait()


def mid_bwd(lens, at, g, row, gain, hot, lse, tf, arrays, packs0, packs1, packs2):
    wi, _, _, res = arrays[:4]
    n, seq, d = res.shape
    half = wi.shape[1]
    width = packs0[0].shape[1] // 3
    outs, specs = back_outs(n, seq, width, d)
    more = [sds((n * seq, d), F32), sds((n * seq, d), BF)]
    return pl.pallas_call(
        mid_bwd_kernel,
        grid=(n,),
        in_specs=[SMEM_SPEC, SMEM_SPEC]
        + [const_spec(x.shape) for x in (g, row)]
        + [const_spec((1, d))]
        + [const_spec(x.shape) for x in (hot, lse, tf)]
        + [ANY] * 23,
        out_specs=[ANY] * 2 + specs,
        out_shape=more + outs,
        scratch_shapes=back_scratch(n, seq, width, d)
        + [pltpu.VMEM(x.shape, x.dtype) for x in arrays]
        + [
            pltpu.VMEM((d, half), BF),
            pltpu.VMEM((width, d), BF),
            pltpu.VMEM((half, d), BF),
            pltpu.VMEM((8, half), F32),
            pltpu.VMEM((2, seq, 512), BF),
            pltpu.VMEM((n * seq, d), F32),
            pltpu.SemaphoreType.DMA((11,)),
            pltpu.SemaphoreType.DMA((12,)),
            pltpu.SemaphoreType.DMA((4,)),
            pltpu.SemaphoreType.DMA((2, n)),
            pltpu.SemaphoreType.DMA((4,)),
        ],
        compiler_params=params(),
        cost_estimate=cost(32),
        name="mid_bwd",
    )(lens, at, g, row, gain.reshape(1, d), hot, lse, tf, *arrays, *packs0, *packs1, *packs2)


def input_kernel(at_ref, x_ref, dres_ref, gain_ref, ta_ref, tb_ref, wq, wk, wv, p0, p1, p2, p3, out_ref, w_ref, sem):
    @pl.when(pl.program_id(0) == 0)
    def _():
        run_copies(join_copies(at_ref[0], (p0, p1, p2, p3), w_ref, sem))

    width = wq.shape[1]
    d_one = mm(tb_ref[...], w_ref[...], NT)
    for i, w in enumerate((wq, wk, wv)):
        d_one = d_one + mm(ta_ref[:, width * i : width * (i + 1)], w[...], NT)
    x = x_ref[0].astype(F32)
    inv = lax.rsqrt(jnp.mean(x * x, axis=-1, keepdims=True) + EPS)
    scaled = d_one * gain_ref[...]
    along = jnp.sum(scaled * x, axis=-1, keepdims=True)
    out_ref[0] = dres_ref[...] + scaled * inv - x * (inv * inv * inv * along / x.shape[1])


def input_part(at, x, dres, gain, tok_a, tok_b, wq, wk, wv, packs):
    n, seq, d = x.shape
    width = wq.shape[1]
    rows = lambda cols: pl.BlockSpec((seq, cols), lambda b: (b, 0))
    return pl.pallas_call(
        input_kernel,
        grid=(n,),
        in_specs=[SMEM_SPEC, row_spec(x.shape), rows(d), const_spec((1, d)), rows(3 * width), rows(3 * width)]
        + [const_spec(wq.shape)] * 3
        + [ANY] * 4,
        out_specs=row_spec(x.shape),
        out_shape=sds(x.shape, F32),
        scratch_shapes=[pltpu.VMEM((d, 3 * width), BF), pltpu.SemaphoreType.DMA((4,))],
        compiler_params=params(),
        cost_estimate=cost(12),
        name="input_part",
    )(at, x, dres, gain.reshape(1, d), tok_a, tok_b, wq, wk, wv, *packs)


def layer_kernel(at_ref, res_ref, aa_ref, ab_ref, w_ref, p0, p1, p2, p3, out_ref, wb_ref, sem):
    @pl.when(pl.program_id(0) == 0)
    def _():
        run_copies(join_copies(at_ref[0], (p0, p1, p2, p3), wb_ref, sem))

    out_ref[0] = (res_ref[0] + mm(aa_ref[0], w_ref[...]) + mm(ab_ref[0], wb_ref[...])).astype(BF)


def layer_part(at, res, act_a, act_b, wu, packs):
    n, seq, d = res.shape
    return pl.pallas_call(
        layer_kernel,
        grid=(n,),
        in_specs=[SMEM_SPEC, row_spec(res.shape), row_spec(act_a.shape), row_spec(act_b.shape), const_spec(wu.shape)]
        + [ANY] * 4,
        out_specs=row_spec(res.shape),
        out_shape=sds(res.shape, BF),
        scratch_shapes=[pltpu.VMEM(wu.shape, BF), pltpu.SemaphoreType.DMA((4,))],
        compiler_params=params(),
        cost_estimate=cost(12),
        name="layer_part",
    )(at, res, act_a, act_b, wu, *packs)


def gain_row(prod):
    ones = jnp.ones((16, prod.shape[1]), BF)
    return sum(mm(ones, part, NT)[:1] for part in split3(prod))


def inner_done_kernel(at_ref, own_ref, near_ref, w_ref, out_ref, gain_ref):
    rows = own_ref.shape[0]
    core = at_ref[0] // 2
    halves = [own_ref[...].astype(F32), near_ref[...].astype(F32)]
    for half in range(2):
        one = jnp.where(core == half, halves[0], halves[1])
        at = slice(rows * half, rows * (half + 1))
        out_ref[at, :] = one
        gain_ref[:, at] = jnp.broadcast_to(gain_row(one * w_ref[at, :].astype(F32)), (8, rows))


def inner_done(at, own, near, w):
    d, half = w.shape
    chunk = 512
    cols = lambda r: pl.BlockSpec((r, chunk), lambda c: (0, c))
    return pl.pallas_call(
        inner_done_kernel,
        grid=(half // chunk,),
        in_specs=[SMEM_SPEC, cols(d // 2), cols(d // 2), cols(d)],
        out_specs=[cols(d), pl.BlockSpec((8, d), lambda c: (c, 0))],
        out_shape=[sds((d, half), F32), sds((8 * (half // chunk), d), F32)],
        compiler_params=params(20),
        cost_estimate=cost(5),
        name="inner_done",
    )(at, own, near, w)


def attn_done_kernel(half_ref, sum_ref, wq, wk, wv, *refs):
    q_ref, k_ref, v_ref, o_ref, gain_ref = refs[-5:]
    width = wq.shape[1]
    total = None
    for i, (w, out) in enumerate(((wq, q_ref), (wk, k_ref), (wv, v_ref))):
        one = sum_ref[:, width * i : width * (i + 1)].astype(F32)
        out[...] = one
        prod = one * w[...].astype(F32)
        total = prod if total is None else total + prod
    o_ref[...] = sum_ref[:, 3 * width :].astype(F32)
    gain_ref[...] = jnp.broadcast_to(gain_row(total), gain_ref.shape)


def attn_done(half, sums, wq, wk, wv, into=()):
    d, width = wq.shape
    rows = d // 2
    grad = sds((d, width), F32)
    block = pl.BlockSpec((rows, width), lambda b, half: (half[0], 0))
    across = pl.BlockSpec((width, rows), lambda b, half: (0, half[0]))
    return pl.pallas_call(
        attn_done_kernel,
        grid_spec=pltpu.PrefetchScalarGridSpec(
            num_scalar_prefetch=1,
            grid=(1,),
            in_specs=[pl.BlockSpec(sums.shape, lambda b, half: (0, 0))] + [block] * 3 + [ANY] * len(into),
            out_specs=[block] * 3 + [across, pl.BlockSpec((8, rows), lambda b, half: (0, 0))],
        ),
        out_shape=[grad, grad, grad, sds((width, d), F32), sds((8, rows), F32)],
        input_output_aliases={5 + i: i for i in range(len(into))},
        compiler_params=params(20),
        cost_estimate=cost(3),
        name="attn_done",
    )(half, sums, wq, wk, wv, *into)


def after(*xs):
    return lax.optimization_barrier(xs)


def swap(x, axis, bit, size):
    return lax.ppermute(x, axis, [(i, i ^ bit) for i in range(size)])


class Place:
    def __init__(self, chips, tensor):
        self.chips, self.tensor = chips, tensor
        self.chip = lax.axis_index("chip")
        self.core = lax.axis_index("core")
        self.ti = lax.axis_index("tensor")

    def across(self, x):
        return swap(x, "tensor", 1, self.tensor)

    def core_swap(self, x):
        return swap(x, "core", 1, 2)

    def share(self, x):
        return lax.all_to_all(x, ("chip", "core", "tensor"), 0, 0, tiled=True)

    def side(self, mine):
        return swap(mine, "chip", 1, self.chips)

    def spread(self, mine, side):
        return [mine, side, self.core_swap(mine), self.core_swap(side)]

    def exchange(self, x):
        rows, width = x.shape
        return lax.all_to_all(x.reshape(self.chips, rows // self.chips, width), "chip", 0, 0, tiled=True)

    def add(self, got):
        return jnp.sum(got.astype(F32), axis=0).astype(BF)

    def gather(self, x):
        got = lax.all_to_all(jnp.broadcast_to(x[None], (self.chips,) + x.shape), "chip", 0, 0, tiled=True)
        return got.reshape(-1, x.shape[1])

    def steps(self):
        return [1 << i for i in range(self.chips.bit_length() - 1)]

    def plus(self, x, bit):
        return x + swap(x, "chip", bit, self.chips)


def body(
    mesh_shape,
    hidden_in,
    lengths,
    queries,
    positives,
    gain_attn,
    w_query,
    w_key,
    w_value,
    w_out,
    rel_table,
    gain_ffn,
    w_inner,
    w_outer,
    w_proj,
):
    pc = Place(mesh_shape["chip"], mesh_shape["tensor"])
    n, seq, d = hidden_in.shape
    half = w_inner.shape[1]
    width = w_query.shape[1]
    buckets = rel_table.shape[0]
    lens = lax.dynamic_slice_in_dim(lengths, pc.ti * n, n, 0)
    near_lens = lax.dynamic_slice_in_dim(lengths, (1 - pc.ti) * n, n, 0)
    lens4 = jnp.concatenate([lens, near_lens])
    at = (2 * pc.core + (pc.chip & 1)).reshape(1)
    devices = pc.chips * 2 * pc.tensor
    hot_t = jnp.asarray(np.pad(diag_onehot(buckets, False).T, ((0, TILE - buckets), (0, 0))), BF)
    hot_back = jnp.asarray(np.pad(diag_onehot(buckets, True), ((0, 0), (0, TILE - buckets))), BF)

    turned = rel_table.T
    packs = pack_weights(at, turned, w_query, w_key, w_value, w_out, w_inner, w_outer)
    y_attn = pc.across(packs[0])

    base = (2 * pc.chip + pc.core) * pc.tensor * n
    me = jnp.stack([base + pc.ti * n, base + pc.ti * n + 1, base + (1 - pc.ti) * n, base + (1 - pc.ti) * n + 1])

    qf = queries.astype(F32)
    q_unit = (qf * lax.rsqrt(jnp.sum(qf * qf, axis=-1, keepdims=True) + EPS)).astype(BF)
    ints = jnp.stack([positives // 256, positives % 256, lens // 256, lens % 256], axis=1)
    ints = jnp.pad(ints.astype(BF), ((0, 0), (0, TILE - 4)))
    q_all = jnp.concatenate([q_unit, ints], axis=1)

    an, ant, q_a, qt_a, k_a, v_a, ctx_a, ctxt_a, lse_a, nb_a, tf_a = attn_own(
        lens, hidden_in, gain_attn, w_query, w_key, w_value, turned, hot_t
    )
    y_attn, an, q_all, *packs = after(y_attn, an, q_all, *packs[1:])
    y_inner, y_outer = [pc.across(p) for p in packs]
    x_attn = pc.side(y_attn)
    q_all = pc.share(jnp.broadcast_to(q_all[None], (devices,) + q_all.shape))
    x_attn, q_all, lens4, me, gain_two = after(x_attn, q_all, lens4, me, gain_ffn.reshape(1, d))
    p_attn = pc.spread(y_attn, x_attn)
    y_inner, an = after(y_inner, an)
    x_inner = pc.side(y_inner)
    q_b, qt_b, k_b, v_b, ctxt_b, lse_b, nb_b, tf_b, res, fin, fint, rsum, *fins = attn_other(
        lens, at, an, hot_t, hidden_in, ctx_a, w_out, gain_two, p_attn
    )
    y_inner, x_inner, y_outer, fin, *fins = after(y_inner, x_inner, y_outer, fin, *fins)
    x_outer = pc.side(y_outer)
    p_inner = pc.spread(y_inner, x_inner)
    fin_nb = [pc.across(f) for f in fins]
    act_a, gp_a, act_b, gp_b, asum, rsum = ffn_fwd(lens, at, fin, rsum, w_inner, w_outer, p_inner)
    y_outer, x_outer, asum = after(y_outer, x_outer, asum)
    p_outer = pc.spread(y_outer, x_outer)
    pooled = pool(lens, at, asum, rsum, p_outer)[:n].astype(BF)

    sums_a, sums_b = asum[:, 0, :half].astype(BF), asum[:, 0, half:].astype(BF)
    sums = jnp.where(pc.ti > 0, jnp.stack([sums_b, sums_a]), jnp.stack([sums_a, sums_b]))
    msg = jnp.concatenate([jnp.broadcast_to(pooled[None], (2,) + pooled.shape), sums], axis=2)
    msg = jnp.broadcast_to(msg[None], (2 * pc.chips,) + msg.shape).reshape((devices,) + msg.shape[1:])
    msg, fin_nb[0] = after(msg, fin_nb[0])
    got, pre = after(pc.share(msg), pre_inner(lens4, fint, gp_a, fin_nb[0], w_inner))
    got = got.reshape(devices * n, -1)
    pooled = got[:, :d]
    loss8, row8, g8, d_rows, d_emb, gi_send, gi_keep = loss_all(
        me, at, lens4, pooled, q_all.reshape(devices * n, -1), w_proj, pre, fin_nb[1], w_inner, w_outer
    )
    query_loss = loss8[:n, 0]

    inner_half, gp_a = after(gi_keep + pc.core_swap(gi_send), gp_a)
    inner_parts = pc.exchange(inner_half)
    arrays = [w_inner, gp_a, gp_b, res, q_b, qt_b, k_b, v_b, ctxt_b, nb_b, ant]
    d_res, d_attn, tok_b, send_b, keep_b, table_b = mid_bwd(
        lens, at, g8, row8, gain_ffn, hot_back, lse_b, tf_b, arrays, p_attn, p_inner, p_outer
    )
    inner_part, d_attn = after(pc.add(inner_parts), d_attn)
    inner_all = pc.gather(inner_part)
    half_b, d_attn = after(keep_b + pc.core_swap(send_b), d_attn)
    far_part = pc.across(half_b)
    tok_a, send_a, keep_a, table_a = attn_bwd(
        lens, at, d_attn.reshape(n, seq, d), w_out, hot_back, lse_a, tf_a, q_a, qt_a, k_a, v_a, ctxt_a, nb_a, ant
    )
    proj_grad = mm(pooled, d_emb, TN)
    outer_grad = mm(got[:, d:], d_rows, TN)
    inner_all, far_part, far_table, send_a, proj_grad, outer_grad = after(
        inner_all, far_part, pc.across(table_b), send_a, proj_grad, outer_grad
    )
    table = table_a + far_table
    near_a, near_table = after(pc.core_swap(send_a), pc.core_swap(table))
    parts = pc.exchange(keep_a + far_part + near_a)
    input_grad = input_part(at, hidden_in, d_res, gain_attn, tok_a, tok_b, w_query, w_key, w_value, p_attn)
    inner_sum, gain_ffn_part = inner_done(at, inner_all, pc.core_swap(inner_all), w_inner)
    layer = layer_part(at, res, act_a, act_b, w_outer, p_outer)
    parts, input_grad, layer = after(parts, input_grad, layer)
    attn_all = pc.gather(pc.add(parts))
    *early, late = pc.steps()
    table_sum = table + near_table
    for bit in early:
        table_sum = pc.plus(table_sum, bit)
    gain_ffn_part = jnp.sum(gain_ffn_part[::8], axis=0)
    gain_ffn_grad = (gain_ffn_part + pc.across(gain_ffn_part)) / gain_ffn
    attn_all, gain_ffn_grad, table_sum, inner_sum, query_loss = after(
        attn_all, gain_ffn_grad, table_sum, inner_sum, query_loss
    )
    table_sum = pc.plus(table_sum, late)
    half = pc.core.reshape(1)
    near = pc.core_swap(attn_all)
    *grads, gain_own = attn_done(half, attn_all, w_query, w_key, w_value)
    near, *grads = after(near, *grads)
    gain_far = pc.across(gain_own[0])
    *grads, _ = attn_done(1 - half, near, w_query, w_key, w_value, grads)
    gain_far, *grads = after(gain_far, *grads)
    gain_own = gain_own[0] + gain_far
    q_grad, k_grad, v_grad, out_grad = grads
    gain_near = pc.core_swap(gain_own)
    gain_attn_grad = jnp.where(
        pc.core > 0, jnp.concatenate([gain_near, gain_own]), jnp.concatenate([gain_own, gain_near])
    ) / gain_attn
    return (
        layer,
        query_loss,
        input_grad,
        gain_attn_grad,
        q_grad,
        k_grad,
        v_grad,
        out_grad,
        table_sum[: rel_table.shape[1], :buckets].T,
        gain_ffn_grad,
        inner_sum,
        outer_grad,
        proj_grad,
    )


def solution(mesh):
    dp, tensor = mesh.shape["dp"], mesh.shape["tensor"]
    fine = jax.sharding.Mesh(mesh.devices.reshape(dp // 2, 2, tensor), ("chip", "core", "tensor"))
    rows = ("chip", "core")
    both = rows + ("tensor",)
    return jax.shard_map(
        functools.partial(body, dict(fine.shape)),
        mesh=fine,
        in_specs=(
            P(both, None, None),
            P(rows),
            P(both, None),
            P(both),
            P(),
            P(None, "tensor"),
            P(None, "tensor"),
            P(None, "tensor"),
            P("tensor", None),
            P(None, "tensor"),
            P(),
            P(None, "tensor"),
            P("tensor", None),
            P(),
        ),
        out_specs=(
            P(both, None, None),
            P(both),
            P(both, None, None),
            P(),
            P(None, "tensor"),
            P(None, "tensor"),
            P(None, "tensor"),
            P("tensor", None),
            P(None, "tensor"),
            P(),
            P(None, "tensor"),
            P("tensor", None),
            P(),
        ),
        check_vma=False,
    )
```

```python
import functools

import numpy as np

import jax
import jax.numpy as jnp
from jax import lax
from jax.experimental import pallas as pl
from jax.experimental.pallas import tpu as pltpu
from jax.sharding import PartitionSpec as P

LARGE_STEPS = (12, 16, 23, 32, 46, 64, 91)
SHARPNESS = 0.02
LOSS_SCALE = 256.0
EPS = 1e-06
NEG = -1e30
BF = jnp.bfloat16
F32 = jnp.float32
TILE = 128
BUCKETS = 32
GELU_A = 0.7978845608028654
GELU_B = 0.044715
MIB = 1024 * 1024

NN = (((1,), (0,)), ((), ()))
NT = (((1,), (1,)), ((), ()))
TN = (((0,), (0,)), ((), ()))


def mm(a, b, dims=NN):
    return lax.dot_general(a, b, dims, preferred_element_type=F32)


def bucket_of(r):
    a = np.abs(r)
    far = 8 + sum((a >= t).astype(np.int32) for t in LARGE_STEPS)
    return np.where(r > 0, 16, 0) + np.where(a < 8, a, far)


def diag_onehot(buckets, back):
    lane = np.arange(2 * TILE)
    at = lane - TILE + 1 if back else TILE - 1 - lane
    idx = np.concatenate([bucket_of(TILE * d + at) for d in (-1, 0, 1)])
    hot = (idx[:, None] == np.arange(buckets)[None, :]).astype(np.float32)
    hot[2 * TILE - 1 :: 2 * TILE] = 0.0
    return hot


def params(mib=60):
    return pltpu.CompilerParams(vmem_limit_bytes=mib * MIB)


def cost(us):
    return pl.CostEstimate(flops=0, bytes_accessed=int(us * 3.6e6), transcendentals=0)

ANY = pl.BlockSpec(memory_space=pl.ANY)
SMEM_SPEC = pl.BlockSpec(memory_space=pltpu.SMEM)


def const_spec(shape):
    zeros = (0,) * len(shape)
    return pl.BlockSpec(tuple(shape), lambda b: zeros, pipeline_mode=pl.Buffered(1))


def out_const(shape):
    zeros = (0,) * len(shape)
    return pl.BlockSpec(tuple(shape), lambda b: zeros)


def row_spec(shape):
    tail = (0,) * (len(shape) - 1)
    return pl.BlockSpec((1,) + tuple(shape[1:]), lambda b: (b,) + tail)


def sds(shape, dtype):
    return jax.ShapeDtypeStruct(tuple(shape), dtype)


def split3(t):
    hi = t.astype(BF)
    rest = t - hi.astype(F32)
    mid = rest.astype(BF)
    return hi, mid, (rest - mid.astype(F32)).astype(BF)


def run_copies(copies):
    for c in copies:
        c.start()
    for c in copies:
        c.wait()


def out_pieces(width, d):
    rows, tall = width // 4, width // 6
    rest = rows - tall
    out = [((0, tall, 0, d), (0, tall, 0, d))]
    for i in range(2):
        out.append(((tall, rest, i * width, width), (i * rest, rest, d, width)))
    return out


def pack_kernel(at_ref, tab_ref, wq, wk, wv, wo, wi, wu, s0, s1, s2, sem):
    at = at_ref[0]
    d, width = wq.shape
    rows = d // 4

    def part(w, dst, i):
        count = w.shape[0] // 4
        src = w.at[pl.ds(pl.multiple_of(at * count, count), count)]
        return pltpu.make_async_copy(src, dst, sem.at[i])

    copies = [part(w, s0.at[pl.ds(0, rows), width * i : width * (i + 1)], i) for i, w in enumerate((wq, wk, wv))]
    copies += [part(wi, s1, 3), part(wu, s2, 4)]
    for i, (a, b) in enumerate(out_pieces(width, d)):
        src = wo.at[pl.ds(pl.multiple_of(at * (width // 4) + a[0], 32), a[1]), a[2] : a[2] + a[3]]
        dst = s0.at[pl.ds(rows + 16 + b[0], b[1]), b[2] : b[2] + b[3]]
        copies.append(pltpu.make_async_copy(src, dst, sem.at[5 + i]))
    for c in copies:
        c.start()
    s0[rows : rows + 16, :] = jnp.zeros((16, s0.shape[1]), BF)
    heads, buckets = tab_ref.shape
    for k, t in enumerate(split3(tab_ref[...])):
        s0[rows : rows + heads, TILE * k : TILE * k + buckets] = t
    for c in copies:
        c.wait()


def pack_weights(at, table, wq, wk, wv, wo, wi, wu):
    d, half = wi.shape
    width = wq.shape[1]
    vm = pl.BlockSpec(memory_space=pltpu.VMEM)
    return pl.pallas_call(
        pack_kernel,
        in_specs=[SMEM_SPEC, vm] + [ANY] * 6,
        out_specs=[vm] * 3,
        out_shape=[
            sds((d // 4 + 16 + width // 6, 3 * width), BF),
            sds((d // 4, half), BF),
            sds((half // 4, d), BF),
        ],
        scratch_shapes=[pltpu.SemaphoreType.DMA((8,))],
        compiler_params=params(),
        cost_estimate=cost(3),
        name="pack_weights",
    )(at, table, wq, wk, wv, wo, wi, wu)


def quarter_spots(at):
    core, xb = at // 2, at % 2
    return [at, 2 * core + 1 - xb, 2 * (1 - core) + xb, 2 * (1 - core) + 1 - xb]


def out_copies(at, packs, dst, sem):
    width, d = dst.shape
    base = d // 4 + 16
    out = []
    for i, (p, s) in enumerate(zip(packs, quarter_spots(at))):
        for j, (a, b) in enumerate(out_pieces(width, d)):
            src = p.at[pl.ds(base + b[0], b[1]), b[2] : b[2] + b[3]]
            to = dst.at[pl.ds(pl.multiple_of(s * (width // 4) + a[0], 32), a[1]), a[2] : a[2] + a[3]]
            out.append(pltpu.make_async_copy(src, to, sem.at[3 * i + j]))
    return out


def join_copies(at, packs, dst, sem):
    rows = dst.shape[0] // 4
    out = []
    for i, (p, s) in enumerate(zip(packs, quarter_spots(at))):
        to = dst.at[pl.ds(pl.multiple_of(s * rows, rows), rows)]
        out.append(pltpu.make_async_copy(p.at[pl.ds(0, rows)], to, sem.at[i]))
    return out


EXTRA = 16


def key_extras(length, rows):
    row = lax.broadcasted_iota(jnp.int32, (rows, TILE), 0)
    lane = lax.broadcasted_iota(jnp.int32, (rows, TILE), 1) & 63
    blk = (lane - 1) & 3
    hot = (lane >= 1) & (lane < 13) & (blk == row // TILE)
    one = ((lane == 0) & (row >= length)) | hot | ((lane >= 13) & (lane < EXTRA))
    return jnp.where(one, 1.0, 0.0)


def far_rows(tf_ref, h, seq):
    row = lax.broadcasted_iota(jnp.int32, (EXTRA, seq), 0)
    diff = ((row - 1) & 3) - lax.broadcasted_iota(jnp.int32, (EXTRA, seq), 1) // TILE
    out = jnp.where(row == 0, NEG, 0.0)
    last, mid = BUCKETS - 1, BUCKETS // 2 - 1
    for k in range(3):
        mine = (row >= 1 + 4 * k) & (row < 5 + 4 * k)
        out = out + jnp.where(mine & (diff >= 2), tf_ref[k, h : h + 1, last : last + 1], 0.0)
        out = out + jnp.where(mine & (diff <= -2), tf_ref[k, h : h + 1, mid : mid + 1], 0.0)
    return out


def stack_rows(e, main, extra):
    pad = jnp.zeros((64 - extra.shape[0], extra.shape[1]), BF)
    return jnp.concatenate([main, extra, pad] if e == 0 else [extra, pad, main], axis=0)


def near_bias(s, nb_ref, h, ib):
    rows = []
    for bj in range(s.shape[0] // TILE):
        parts = []
        for t in range(2):
            piece = s[TILE * bj : TILE * (bj + 1), TILE * t : TILE * (t + 1)]
            d = bj - (2 * ib + t)
            parts.append(piece + nb_ref[3 * h + d + 1] if abs(d) <= 1 else piece)
        rows.append(jnp.concatenate(parts, axis=1))
    return rows


def set_bias(parts, hot_ref, tf_ref, nb_ref):
    for k in range(3):
        tf_ref[k] = parts[k].astype(F32)
    hot = hot_ref[...]
    bv = mm(parts[0], hot) + mm(parts[1], hot) + mm(parts[2], hot)
    for t in range(nb_ref.shape[0]):
        h, k = t // 3, t % 3
        v = jnp.broadcast_to(bv[h : h + 1, 2 * TILE * k : 2 * TILE * (k + 1)], (TILE, 2 * TILE))
        nb_ref[t] = pltpu.roll(v, TILE + 1, 1, stride=1, stride_axis=0)[:, :TILE]


def attn_rows(an, length, ws, outs, nb_ref, tf_ref, s_ref, p_ref, between=None):
    q_ref, qt_ref, k_ref, v_ref, ctx_ref, ctxt_ref, lse_ref = outs
    seq = an.shape[0]
    width = q_ref.shape[2]
    for ref, w in zip((q_ref, k_ref), ws):
        ref[0] = mm(an, w[...]).astype(BF)
    kx = key_extras(length, seq)
    lane = lax.broadcasted_iota(jnp.int32, (seq, TILE), 1)
    blocks = [(h, ib) for h in range(width // 64) for ib in range(seq // 256)]
    keys, queries, values, tops, rows = {}, {}, {}, {}, {}

    def prepare(h):
        pair, e = h // 2, h % 2
        cols = slice(TILE * pair, TILE * (pair + 1))
        if e == 0:
            qt_ref[0, cols, :] = jnp.transpose(q_ref[0, :, cols])
        mine = lane < 64 if e == 0 else lane >= 64
        keys[h] = jnp.where(mine, k_ref[0, :, cols].astype(F32), kx).astype(BF)
        qt = qt_ref[0, 64 * h : 64 * (h + 1), :]
        queries[h] = stack_rows(e, qt, far_rows(tf_ref, h, seq).astype(BF))

    def start(t):
        h, ib = blocks[t]
        if ib == 0:
            prepare(h)
        s = mm(keys[h], queries[h][:, 256 * ib : 256 * (ib + 1)])
        return near_bias(s, nb_ref, h, ib)

    def score(t, bj, pieces):
        piece = pieces[bj]
        s_ref[t % 2, TILE * bj : TILE * (bj + 1), :] = piece
        m = jnp.max(piece.reshape(TILE // 8, 8, 256), axis=0)
        tops[t] = m if bj == 0 else jnp.maximum(tops[t], m)
        if bj == seq // TILE - 1:
            tops[t] = jnp.max(tops[t], axis=0, keepdims=True)

    def soft(t, bj):
        h, ib = blocks[t]
        at = slice(TILE * bj, TILE * (bj + 1))
        p_ref[h % 2, at, 256 * ib : 256 * (ib + 1)] = jnp.exp(s_ref[t % 2, at, :] - tops[t]).astype(BF)

    def combine(h):
        per = seq // 256
        top = jnp.concatenate([tops[per * h + i] for i in range(per)], axis=1)
        if h % 2 == 0:
            values[h // 2] = jnp.transpose(v_ref[0, :, TILE * (h // 2) : TILE * (h // 2 + 1)])
        vt = values[h // 2][64 * (h % 2) : 64 * (h % 2 + 1), :]
        got = mm(jnp.concatenate([vt, jnp.ones((16, seq), BF)], axis=0), p_ref[h % 2])
        total = got[64:65]
        lse_ref[0, h : h + 1, :] = top + jnp.log(total)
        rows[h] = got[:64] * (1.0 / total)
        if h % 2 == 1:
            pair = h // 2
            cols = slice(TILE * pair, TILE * (pair + 1))
            ct = jnp.concatenate([rows[h - 1], rows[h]], axis=0).astype(BF)
            ctxt_ref[0, cols, :] = ct
            ctx_ref[0, :, cols] = jnp.transpose(ct)

    for t in range(len(blocks) + 1):
        if t < len(blocks):
            pieces = start(t)
            for bj in range(seq // TILE):
                score(t, bj, pieces)
        if t == 0:
            v_ref[0] = mm(an, ws[2][...]).astype(BF)
        if t == 5 and between is not None:
            between()
        if t > 0:
            for bj in range(seq // TILE):
                soft(t - 1, bj)
            if blocks[t - 1][1] == seq // 256 - 1:
                combine(blocks[t - 1][0])


def attn_own_kernel(lens, x_ref, gain_ref, wq, wk, wv, tab_ref, hot_ref, an_ref, ant_ref, *refs):
    outs, (nb_ref, tf_ref, s_ref, p_ref) = refs[:7], refs[7:]
    b = pl.program_id(0)

    @pl.when(b == 0)
    def _():
        heads, buckets = tab_ref.shape
        wide = jnp.concatenate([tab_ref[...], jnp.zeros((heads, TILE - buckets), F32)], axis=1)
        wide = jnp.concatenate([wide, jnp.zeros((16 - heads, TILE), F32)], axis=0)
        set_bias(split3(wide), hot_ref, tf_ref, nb_ref)

    x = x_ref[0].astype(F32)
    inv = lax.rsqrt(jnp.mean(x * x, axis=-1, keepdims=True) + EPS)
    an = (x * inv * gain_ref[...]).astype(BF)
    an_ref[0] = an
    ant_ref[...] = jnp.transpose(an)
    attn_rows(an, lens[b], (wq, wk, wv), outs, nb_ref, tf_ref, s_ref, p_ref)


def attn_other_kernel(lens, at_ref, an_ref, hot_ref, gain_ref, x_hbm, ca_hbm, wo_hbm, p0, p1, p2, p3, *refs):
    outs, (nb_ref, tf_ref, res_ref, fin_ref, fint_ref, rsum_ref, f0_ref, f1_ref) = list(refs[:6]), refs[6:14]
    (s_ref, p_ref, w_ref, tab_ref, wb_ref, c_ref, x_ref, ca_ref, wo_ref, sem, sem1, sem2) = refs[14:]
    outs.insert(4, c_ref)
    b = pl.program_id(0)
    late = out_copies(at_ref[0], (p0, p1, p2, p3), wb_ref, sem1)
    moves = ((x_hbm, x_ref), (ca_hbm, ca_ref), (wo_hbm, wo_ref))
    more = [pltpu.make_async_copy(x, y, sem2.at[i]) for i, (x, y) in enumerate(moves)]

    @pl.when(b == 0)
    def _():
        rows = w_ref.shape[0] // 4
        copies = join_copies(at_ref[0], (p0, p1, p2, p3), w_ref, sem)
        copies.append(pltpu.make_async_copy(p0.at[pl.ds(rows, 16)], tab_ref, sem.at[4]))
        for c in copies + more + late:
            c.start()
        for c in copies:
            c.wait()
        parts = [tab_ref[:, TILE * k : TILE * (k + 1)] for k in range(3)]
        set_bias(parts, hot_ref, tf_ref, nb_ref)
        for c in more:
            c.wait()

    width = outs[0].shape[2]
    ws = [w_ref.at[:, width * k : width * (k + 1)] for k in range(3)]

    def between():
        res_ref[0] = x_ref[b].astype(F32) + mm(ca_ref[b], wo_ref[...])

    attn_rows(an_ref[0], lens[b], ws, outs, nb_ref, tf_ref, s_ref, p_ref, between)

    @pl.when(b == 0)
    def _():
        for c in late:
            c.wait()

    res = res_ref[0] + mm(outs[4][0], wb_ref[...])
    res_ref[0] = res
    inv = lax.rsqrt(jnp.mean(res * res, axis=-1, keepdims=True) + EPS)
    fin = (res * inv * gain_ref[...]).astype(BF)
    fin_ref[0] = fin
    for i, f_ref in enumerate((f0_ref, f1_ref)):

        @pl.when(b == i)
        def _():
            f_ref[0] = fin

    vcol = (lax.broadcasted_iota(jnp.int32, (res.shape[0], TILE), 0) < lens[b]).astype(F32)[:, :1]
    fint_ref[...] = jnp.transpose((fin.astype(F32) * vcol).astype(BF))
    rsum_ref[0] = jnp.sum(res * vcol, axis=0, keepdims=True)


def attn_outs(n, seq, width):
    heads = width // 64
    tok, turned = sds((n, seq, width), BF), sds((n, width, seq), BF)
    rows = [tok, turned, tok, tok, tok, turned, sds((n, 8, seq), F32)]
    flat = [sds((3 * heads, TILE, TILE), F32), sds((3, 16, TILE), F32)]
    scratch = [pltpu.VMEM((2, seq, 256), F32), pltpu.VMEM((2, seq, seq), BF)]
    return rows + flat, [row_spec(o.shape) for o in rows] + [out_const(o.shape) for o in flat], scratch


def attn_own(lens, x, gain, wq, wk, wv, table, hot):
    n, seq, d = x.shape
    outs, specs, scratch = attn_outs(n, seq, wq.shape[1])
    return pl.pallas_call(
        attn_own_kernel,
        grid=(n,),
        in_specs=[SMEM_SPEC, row_spec(x.shape), const_spec((1, d))]
        + [const_spec(wq.shape)] * 3
        + [const_spec(table.shape), const_spec(hot.shape)],
        out_specs=[row_spec(x.shape), pl.BlockSpec((d, seq), lambda b: (0, b))] + specs,
        out_shape=[sds((n, seq, d), BF), sds((d, n * seq), BF)] + outs,
        scratch_shapes=scratch,
        compiler_params=params(),
        cost_estimate=cost(12),
        name="attn_own",
    )(lens, x, gain.reshape(1, d), wq, wk, wv, table, hot)


def attn_other(lens, at, an, hot, x, ctx_a, wo, gain, packs):
    n, seq, d = an.shape
    width = wo.shape[0]
    outs, specs, scratch = attn_outs(n, seq, width)
    del outs[4], specs[4]
    more = [sds((n, seq, d), F32), sds((n, seq, d), BF), sds((d, n * seq), BF), sds((n, 1, d), F32)]
    more_specs = [row_spec(o.shape) for o in more]
    more_specs[2] = pl.BlockSpec((d, seq), lambda b: (0, b))
    more += [sds((1, seq, d), BF)] * n
    more_specs += [out_const((1, seq, d))] * n
    return pl.pallas_call(
        attn_other_kernel,
        grid=(n,),
        in_specs=[SMEM_SPEC, SMEM_SPEC, row_spec(an.shape), const_spec(hot.shape), const_spec((1, d))]
        + [ANY] * 7,
        out_specs=specs + more_specs,
        out_shape=outs + more,
        scratch_shapes=scratch
        + [
            pltpu.VMEM((d, 3 * width), BF),
            pltpu.VMEM((16, 3 * width), BF),
            pltpu.VMEM(wo.shape, BF),
            pltpu.VMEM((1, seq, width), BF),
            pltpu.VMEM(x.shape, BF),
            pltpu.VMEM(ctx_a.shape, BF),
            pltpu.VMEM(wo.shape, BF),
            pltpu.SemaphoreType.DMA((5,)),
            pltpu.SemaphoreType.DMA((12,)),
            pltpu.SemaphoreType.DMA((3,)),
        ],
        compiler_params=params(),
        cost_estimate=cost(15),
        name="attn_other",
    )(lens, at, an, hot, gain, x, ctx_a, wo, *packs)


def attn_back(b, n, length, core, w, d_attn, ins, outs, scratch, late):
    (q_ref, qt_ref, k_ref, v_ref, ct_ref, lse_ref, nb_ref, tf_ref, ant_ref, hot_ref) = ins
    (all_hbm, send_ref, keep_ref, table_ref) = outs
    (dc_ref, dct_ref, t_ref, fsum_ref, p_ref, ds_ref, all_ref, da_ref, go_ref, out_sem) = scratch
    seq, width = q_ref.shape[1], q_ref.shape[2]
    heads = width // 64
    nblk = seq // TILE
    here = pl.ds(pl.multiple_of(b * seq, seq), seq)

    @pl.when(b == 0)
    def _():
        t_ref[...] = jnp.zeros_like(t_ref)
        fsum_ref[...] = jnp.zeros_like(fsum_ref)
        table_ref[...] = jnp.zeros_like(table_ref)

    dct_ref[...] = mm(w, d_attn, NT).astype(BF)
    dc_ref[...] = jnp.transpose(dct_ref[...])
    kx = key_extras(length, seq)
    lane = lax.broadcasted_iota(jnp.int32, (seq, TILE), 1)
    vx = jnp.where((lane & 63) < 3, 1.0, 0.0)
    keys, values, queries, grads, turned = {}, {}, {}, {}, {}

    def prepare(h):
        pair, e = h // 2, h % 2
        cols = slice(TILE * pair, TILE * (pair + 1))
        mine = lane < 64 if e == 0 else lane >= 64
        if e == 0:
            turned[pair] = jnp.transpose(k_ref[b, :, cols])
        keys[h] = jnp.where(mine, k_ref[b, :, cols].astype(F32), kx).astype(BF)
        values[h] = jnp.where(mine, v_ref[b, :, cols].astype(F32), vx).astype(BF)
        at = slice(64 * h, 64 * (h + 1))
        lse = split3(-lse_ref[b, h : h + 1, :])
        extra = far_rows(tf_ref, h, seq)
        row = lax.broadcasted_iota(jnp.int32, (EXTRA, seq), 0)
        for k in range(3):
            extra = jnp.where(row == 13 + k, lse[k].astype(F32), extra)
        queries[h] = stack_rows(e, qt_ref[b, at, :], extra.astype(BF))
        along = jnp.sum(dct_ref[at, :].astype(F32) * ct_ref[b, at, :].astype(F32), axis=0, keepdims=True)
        extra = jnp.zeros((EXTRA, seq), F32)
        for k, part in enumerate(split3(-along)):
            extra = jnp.where(row == k, part.astype(F32), extra)
        grads[h] = stack_rows(e, dct_ref[at, :], extra.astype(BF))

    def block(h, ib):
        pair, e = h // 2, h % 2
        at = slice(256 * ib, 256 * (ib + 1))
        to = slice(seq * e + 256 * ib, seq * e + 256 * (ib + 1))
        s = mm(keys[h], queries[h][:, at])
        dp = mm(values[h], grads[h][:, at])
        near, far = {}, {}
        for bj, piece in enumerate(near_bias(s, nb_ref, h, ib)):
            rows = slice(TILE * bj, TILE * (bj + 1))
            p = jnp.exp(piece)
            ds = p * dp[rows, :]
            p_ref[pair % 2, rows, to] = p.astype(BF)
            ds_ref[pair % 2, rows, to] = ds.astype(BF)
            for t in range(2):
                d = bj - (2 * ib + t)
                one = ds[:, TILE * t : TILE * (t + 1)]
                if abs(d) <= 1:
                    near[d] = near[d] + one if d in near else one
                else:
                    one = jnp.sum(one.reshape(TILE // 8, 8, TILE), axis=0)
                    side = 1 if d > 0 else 0
                    far[side] = far[side] + one if side in far else one
        for d, one in near.items():
            t_ref[3 * h + d + 1] += one
        for side, one in far.items():
            fsum_ref[2 * h + side] += one

    def finish(pair, part):
        slot = pair % 2
        cols = slice(TILE * pair, TILE * (pair + 1))
        if part < 2:
            src, rhs = ((p_ref, dc_ref[:, cols]), (ds_ref, q_ref[b, :, cols]))[part]
            one = jnp.where(lane < 64, mm(src[slot, :, :seq], rhs), mm(src[slot, :, seq:], rhs)).astype(BF)
            base = width * (2 - part)
            all_ref[here, base + TILE * pair : base + TILE * (pair + 1)] = one
        if part == 2:
            kt = turned[pair]
            dqt = [mm(kt[64 * e : 64 * (e + 1), :], ds_ref[slot, :, seq * e : seq * (e + 1)]) for e in range(2)]
            one = jnp.transpose(jnp.concatenate(dqt, axis=0).astype(BF))
            all_ref[here, TILE * pair : TILE * (pair + 1)] = one

    for pair in range(heads // 2):
        step = 0
        for e in range(2):
            prepare(2 * pair + e)
            for ib in range(seq // 256):
                block(2 * pair + e, ib)
                if pair > 0 and step < 3:
                    finish(pair - 1, step)
                step += 1
    for part in range(3):
        finish(heads // 2 - 1, part)
    done = send_rows(b, n, all_ref, all_hbm, out_sem)

    @pl.when(b == n - 1)
    def _():
        for c in late:
            c.wait()
        rows = ant_ref.shape[0] // 2
        out = None
        for i in range(n):
            one = mm(ct_ref[i], da_ref[seq * i : seq * (i + 1), :])
            out = one if out is None else out + one
        go_ref[:width, :] = out[:, :width].astype(BF)
        go_ref[width:, :] = out[:, width:].astype(BF)
        for ref, half in ((send_ref, 1 - core), (keep_ref, core)):
            at = pl.ds(pl.multiple_of(half * rows, rows), rows)
            ref[:, : 3 * width] = mm(ant_ref[at, :], all_ref[...]).astype(BF)
            ref[:, 3 * width :] = go_ref[at, :]
        turn = lax.broadcasted_iota(jnp.int32, (TILE, TILE), 0) + lax.broadcasted_iota(jnp.int32, (TILE, TILE), 1)
        turn = jnp.where(turn == TILE - 1, 1.0, 0.0).astype(BF)
        tiles = t_ref.shape[0]
        hi, lo, _ = split3(t_ref[...].reshape(tiles * TILE, TILE))
        back = mm(jnp.concatenate([hi, lo], axis=1), jnp.concatenate([turn, turn], axis=0))
        diag = []
        for t in range(tiles):
            x = jnp.concatenate([back[TILE * t : TILE * (t + 1)], jnp.zeros((TILE, TILE), F32)], axis=1)
            x = pltpu.roll(x, 0, 1, stride=1, stride_axis=0)
            diag.append(jnp.sum(x, axis=0, keepdims=True))
        lines = [jnp.concatenate(diag[3 * h : 3 * h + 3], axis=1) for h in range(heads)]
        lines.append(jnp.zeros((16 - heads, lines[0].shape[1]), F32))
        near = [mm(part, hot_ref[...]) for part in split3(jnp.concatenate(lines, axis=0))]
        spot = lax.broadcasted_iota(jnp.int32, (1, TILE), 1)
        for h in range(heads):
            one = near[0][h : h + 1] + near[1][h : h + 1] + near[2][h : h + 1]
            for side, bucket in ((0, BUCKETS // 2 - 1), (1, BUCKETS - 1)):
                far = jnp.sum(jnp.sum(fsum_ref[2 * h + side], axis=0, keepdims=True), axis=1, keepdims=True)
                one = one + jnp.where(spot == bucket, far, 0.0)
            table_ref[h : h + 1, :] = one
        for c in done:
            c.wait()


def send_rows(b, n, src, dst, sem):
    rows = src.shape[0] // n
    copies = [pltpu.make_async_copy(src.at[pl.ds(i * rows, rows)], dst.at[pl.ds(i * rows, rows)], sem.at[i]) for i in range(n)]
    for i, c in enumerate(copies):

        @pl.when(b == i)
        def _():
            c.start()

    return copies


def back_outs(n, seq, width, d):
    half = sds((d // 2, 4 * width), BF)
    outs = [sds((n * seq, 3 * width), BF), half, half, sds((8, TILE), F32)]
    return outs, [ANY] + [out_const(o.shape) for o in outs[1:]]


def back_scratch(n, seq, width, d):
    heads = width // 64
    return [
        pltpu.VMEM((seq, width), BF),
        pltpu.VMEM((width, seq), BF),
        pltpu.VMEM((3 * heads, TILE, TILE), F32),
        pltpu.VMEM((2 * heads, 8, TILE), F32),
        pltpu.VMEM((2, seq, 2 * seq), BF),
        pltpu.VMEM((2, seq, 2 * seq), BF),
        pltpu.VMEM((n * seq, 3 * width), BF),
        pltpu.VMEM((n * seq, d), BF),
        pltpu.VMEM((d, width), BF),
        pltpu.SemaphoreType.DMA((n,)),
    ]


def attn_bwd_kernel(lens, at_ref, da_blk, wo_ref, hot_ref, lse_ref, tf_ref, *refs):
    hbm, outs, scratch = refs[:7], refs[7:11], refs[11:21]
    bufs, sem = refs[21:28], refs[28]
    b = pl.program_id(0)
    n = da_blk.shape[0] * lse_ref.shape[0]
    copies = [pltpu.make_async_copy(x, y, sem.at[i]) for i, (x, y) in enumerate(zip(hbm, bufs))]

    @pl.when(b == 0)
    def _():
        for c in copies:
            c.start()
        for c in copies[:-1]:
            c.wait()

    q, qt, k, v, ct, nb, ant = bufs
    ins = (q, qt, k, v, ct, lse_ref, nb, tf_ref, ant, hot_ref)
    seq = da_blk.shape[1]
    scratch[7][pl.ds(pl.multiple_of(b * seq, seq), seq), :] = da_blk[0]
    attn_back(b, n, lens[b], at_ref[0] // 2, wo_ref[...], da_blk[0], ins, outs, scratch, copies[-1:])


def attn_bwd(lens, at, d_attn, wo, hot, lse, tf, *arrays):
    n, seq, d = d_attn.shape
    width = wo.shape[0]
    outs, specs = back_outs(n, seq, width, d)
    return pl.pallas_call(
        attn_bwd_kernel,
        grid=(n,),
        in_specs=[SMEM_SPEC, SMEM_SPEC, row_spec(d_attn.shape)]
        + [const_spec(x.shape) for x in (wo, hot, lse, tf)]
        + [ANY] * 7,
        out_specs=specs,
        out_shape=outs,
        scratch_shapes=back_scratch(n, seq, width, d)
        + [pltpu.VMEM(x.shape, x.dtype) for x in arrays]
        + [pltpu.SemaphoreType.DMA((7,))],
        compiler_params=params(),
        cost_estimate=cost(16),
        name="attn_bwd",
    )(lens, at, d_attn, wo, hot, lse, tf, *arrays)


def gelu_parts(v):
    v2 = v * v
    half = 0.5 + 0.5 * jnp.tanh(v * (GELU_A + (GELU_A * GELU_B) * v2))
    act = v * half
    return act, half + (act - act * half) * (2.0 * GELU_A + (6.0 * GELU_A * GELU_B) * v2)


def ffn_fwd_kernel(lens, at_ref, fin_ref, rs_ref, wi_ref, wu_ref, p0, p1, p2, p3, *refs):
    (act_ref, gp_ref, actb_ref, gpb_ref, asum_ref, rsum_ref) = refs[:6]
    (wib_ref, wu_buf, v_ref, sem1, sem2) = refs[6:]
    b = pl.program_id(0)
    late = join_copies(at_ref[0], (p0, p1, p2, p3), wib_ref, sem1) + [pltpu.make_async_copy(wu_ref, wu_buf, sem2)]

    @pl.when(b == 0)
    def _():
        run_copies(late)

    fin = fin_ref[0]
    seq = fin.shape[0]
    half = wi_ref.shape[1]
    chunk = v_ref.shape[2]
    length = lens[b]
    vrow = (lax.broadcasted_iota(jnp.int32, (8, seq), 1) < length).astype(F32).astype(BF)
    spot = lambda c: slice(c * chunk, (c + 1) * chunk)
    parts = [(w, a, g, c) for w, a, g in ((wi_ref, act_ref, gp_ref), (wib_ref, actb_ref, gpb_ref)) for c in range(half // chunk)]

    def project(t):
        w, _, _, c = parts[t]
        v_ref[t % 2] = mm(fin, w[:, spot(c)])

    project(0)
    for t, (_, a_ref, g_ref, c) in enumerate(parts):
        if t + 1 < len(parts):
            project(t + 1)
        for r in range(seq // TILE):
            rows = slice(TILE * r, TILE * (r + 1))
            act, slope = gelu_parts(v_ref[t % 2, rows, :])
            a_ref[0, rows, spot(c)] = act.astype(BF)
            g_ref[0, rows, spot(c)] = slope.astype(BF)
        asum_ref[0, :, spot(t)] = mm(vrow, a_ref[0, :, spot(c)])[:1]
    own = asum_ref[0, :, :half]
    hi = own.astype(BF)
    lo = (own - hi.astype(F32)).astype(BF)
    two_rows = jnp.concatenate([hi.astype(F32), lo.astype(F32), jnp.zeros((14, half), F32)], axis=0).astype(BF)
    branch = mm(two_rows, wu_buf[...])
    rsum_ref[0] = rs_ref[0] + branch[0:1] + branch[1:2]


def ffn_fwd(lens, at, fin, rsum, wi, wu, packs):
    n, seq, d = fin.shape
    half = wi.shape[1]
    wide = sds((n, seq, half), BF)
    outs = [wide, wide, wide, wide, sds((n, 1, 2 * half), F32), sds((n, 1, d), F32)]
    return pl.pallas_call(
        ffn_fwd_kernel,
        grid=(n,),
        in_specs=[SMEM_SPEC, SMEM_SPEC, row_spec(fin.shape), row_spec(rsum.shape), const_spec(wi.shape)] + [ANY] * 5,
        out_specs=[row_spec(o.shape) for o in outs],
        out_shape=outs,
        scratch_shapes=[
            pltpu.VMEM(wi.shape, BF),
            pltpu.VMEM(wu.shape, BF),
            pltpu.VMEM((2, seq, 512), F32),
            pltpu.SemaphoreType.DMA((4,)),
            pltpu.SemaphoreType.DMA,
        ],
        compiler_params=params(),
        cost_estimate=cost(16),
        name="ffn_fwd",
    )(lens, at, fin, rsum, wi, wu, *packs)


def pool_kernel(lens, at_ref, asum_ref, rs_ref, p0, p1, p2, p3, out_ref, wb_ref, sem):
    run_copies(join_copies(at_ref[0], (p0, p1, p2, p3), wb_ref, sem))
    n = asum_ref.shape[0]
    half = wb_ref.shape[0]
    rows = [asum_ref[i, :, half:] for i in range(n)]
    hi = [r.astype(BF) for r in rows]
    lo = [(r - h.astype(F32)).astype(BF) for r, h in zip(rows, hi)]
    pad = jnp.zeros((16 - 2 * n, half), F32)
    br = mm(jnp.concatenate([t.astype(F32) for t in hi + lo] + [pad], axis=0).astype(BF), wb_ref[...])
    for i in range(n):
        total = rs_ref[i] + br[i : i + 1] + br[n + i : n + i + 1]
        out_ref[i : i + 1, :] = total / lens[i].astype(F32)


def pool(lens, at, asum, rsum, packs):
    n, _, d = rsum.shape
    half = asum.shape[2] // 2
    vm = pl.BlockSpec(memory_space=pltpu.VMEM)
    return pl.pallas_call(
        pool_kernel,
        in_specs=[SMEM_SPEC, SMEM_SPEC, vm, vm] + [ANY] * 4,
        out_specs=vm,
        out_shape=sds((8, d), F32),
        scratch_shapes=[pltpu.VMEM((half, d), BF), pltpu.SemaphoreType.DMA((4,))],
        compiler_params=params(16),
        cost_estimate=cost(4),
        name="pool",
    )(lens, at, asum, rsum, *packs)


def pre_kernel(lens, fint_ref, gp_ref, fn_ref, w_ref, out_ref, ft_ref, v_ref, s_ref):
    n, seq, _ = gp_ref.shape

    @pl.when(pl.program_id(0) == 0)
    def _():
        valid = lax.broadcasted_iota(jnp.int32, (seq, TILE), 0) < lens[n]
        ft_ref[...] = jnp.transpose((fn_ref[0].astype(F32) * valid.astype(F32)[:, :1]).astype(BF))

    v_ref[...] = mm(fn_ref[0], w_ref[...])
    for i in range(n):
        out_ref[i] = mm(fint_ref[:, seq * i : seq * (i + 1)], gp_ref[i]).astype(BF)
        for r in range(seq // TILE // n):
            at = slice(seq // n * i + TILE * r, seq // n * i + TILE * (r + 1))
            s_ref[at, :] = gelu_parts(v_ref[at, :])[1].astype(BF)
    out_ref[n] = mm(ft_ref[...], s_ref[...]).astype(BF)


def pre_inner(lens4, fint, gp, fn, wi):
    n, seq, half = gp.shape
    d = fint.shape[0]
    chunk = 512
    return pl.pallas_call(
        pre_kernel,
        grid=(half // chunk,),
        in_specs=[SMEM_SPEC, const_spec(fint.shape), pl.BlockSpec((n, seq, chunk), lambda c: (0, 0, c))]
        + [const_spec(fn.shape), pl.BlockSpec((d, chunk), lambda c: (0, c))],
        out_specs=pl.BlockSpec((n + 1, d, chunk), lambda c: (0, 0, c)),
        out_shape=sds((n + 1, d, half), BF),
        scratch_shapes=[pltpu.VMEM((d, seq), BF), pltpu.VMEM((seq, chunk), F32), pltpu.VMEM((seq, chunk), BF)],
        compiler_params=params(),
        cost_estimate=cost(9),
        name="pre_inner",
    )(lens4, fint, gp, fn, wi)


def loss_kernel(me_ref, at_ref, lens, pool_ref, q_ref, wp_hbm, pre_hbm, fn_hbm, wi_hbm, wu_hbm, *refs):
    (loss_ref, row_ref, g_ref, drow_ref, demb_ref, send_ref, keep_ref) = refs[:7]
    (wp_ref, wu_ref, pre_ref, fn_ref, wi_ref, ft_ref, gn_ref, v_ref, d_ref, sum_ref, sem) = refs[7:]
    moves = ((wp_hbm, wp_ref), (wu_hbm, wu_ref), (fn_hbm, fn_ref), (wi_hbm, wi_ref), (pre_hbm, pre_ref))
    loads = [pltpu.make_async_copy(a, b, sem.at[i]) for i, (a, b) in enumerate(moves)]
    for c in loads:
        c.start()
    loads[0].wait()
    d = wp_ref.shape[0]
    count = pool_ref.shape[0]
    pooled = pool_ref[...]
    qs = q_ref[:, :d]
    ints = q_ref[:, d : d + TILE].astype(F32)
    pos = (ints[:, 0:1] * 256.0 + ints[:, 1:2]).astype(jnp.int32)
    length = ints[:, 2:3] * 256.0 + ints[:, 3:4]
    wp = wp_ref[...]
    emb = mm(pooled, wp)
    inv = lax.rsqrt(jnp.sum(emb * emb, axis=-1, keepdims=True) + EPS)
    unit = (emb * inv).astype(BF)
    logits = mm(qs, unit, NT) / SHARPNESS
    top = jnp.max(logits, axis=-1, keepdims=True)
    total = top + jnp.log(jnp.sum(jnp.exp(logits - top), axis=-1, keepdims=True))
    hit = lax.broadcasted_iota(jnp.int32, (count, count), 1) == pos
    loss = total - jnp.sum(jnp.where(hit, logits, 0.0), axis=1, keepdims=True)
    d_logits = (LOSS_SCALE * (jnp.exp(logits - total) - jnp.where(hit, 1.0, 0.0))).astype(BF)
    d_unit = mm(d_logits, qs, TN) / SHARPNESS
    along = jnp.sum(emb * d_unit, axis=-1, keepdims=True)
    d_emb = (inv * d_unit - inv * inv * inv * along * emb).astype(BF)
    demb_ref[...] = d_emb
    rows = mm(d_emb, wp, NT) / length
    drow_ref[...] = rows.astype(BF)
    index = lax.broadcasted_iota(jnp.int32, (count, 1), 0)
    pick = lambda t, i: jnp.sum(jnp.where(index == i, t, 0.0), axis=0, keepdims=True)
    seq = fn_ref.shape[1]
    half = wi_ref.shape[1]
    n = pre_ref.shape[0] - 1
    own = [pick(rows, me_ref[i]) for i in range(n)]
    near = [pick(rows, me_ref[n + i]) for i in range(n)]
    lost = jnp.broadcast_to(loss, (count, TILE))
    pad = jnp.zeros((8 - n, d), F32)
    row_ref[...] = jnp.concatenate(own + [pad], axis=0)
    loss_ref[...] = jnp.concatenate([pick(lost, me_ref[i]) for i in range(n)] + [pad[:, :TILE]], axis=0)
    four = jnp.concatenate(own + near + [jnp.zeros((16 - 2 * n, d), F32)], axis=0).astype(BF)
    loads[1].wait()
    gn_ref[...] = mm(four, wu_ref[...], NT)[:8]
    g_ref[...] = gn_ref[...]
    for c in loads[2:]:
        c.wait()

    last = 2 * n - 1
    valid = lax.broadcasted_iota(jnp.int32, (seq, TILE), 0) < lens[last]
    ft_ref[...] = jnp.transpose((fn_ref[0].astype(F32) * valid.astype(F32)[:, :1]).astype(BF))
    chunk = v_ref.shape[2]
    steps = half // chunk
    spot = lambda c: slice(c * chunk, (c + 1) * chunk)
    rows2 = d // 2
    core = at_ref[0] // 2

    def project(c):
        v_ref[c % 2] = mm(fn_ref[0], wi_ref[:, spot(c)])

    def scale(c):
        for r in range(seq // TILE):
            at = slice(TILE * r, TILE * (r + 1))
            slope = gelu_parts(v_ref[c % 2, at, :])[1]
            d_ref[c % 2, at, :] = (slope * gn_ref[last : last + 1, spot(c)]).astype(BF)

    project(0)
    scale(0)
    for c in range(steps):
        if c + 1 < steps:
            project(c + 1)
        for r in range(d // TILE):
            at = slice(TILE * r, TILE * (r + 1))
            total = mm(ft_ref[at, :], d_ref[c % 2])
            for i in range(n + 1):
                total = total + pre_ref[i, at, spot(c)].astype(F32) * gn_ref[i : i + 1, spot(c)]
            sum_ref[at, :] = total.astype(BF)
        for ref, side in ((send_ref, 1 - core), (keep_ref, core)):
            ref[:, spot(c)] = sum_ref[pl.ds(pl.multiple_of(side * rows2, rows2), rows2), :]
        if c + 1 < steps:
            scale(c + 1)


def loss_all(me, at, lens4, pooled, queries, wp, pre, fn, wi, wu):
    half, d = wu.shape
    seq = fn.shape[1]
    count = pooled.shape[0]
    chunk = 512
    vm = pl.BlockSpec(memory_space=pltpu.VMEM)
    return pl.pallas_call(
        loss_kernel,
        in_specs=[SMEM_SPEC] * 3 + [vm] * 2 + [ANY] * 5,
        out_specs=[vm] * 7,
        out_shape=[
            sds((8, TILE), F32),
            sds((8, d), F32),
            sds((8, half), F32),
            sds((count, d), BF),
            sds((count, d), BF),
            sds((d // 2, half), BF),
            sds((d // 2, half), BF),
        ],
        scratch_shapes=[
            pltpu.VMEM(wp.shape, BF),
            pltpu.VMEM(wu.shape, BF),
            pltpu.VMEM(pre.shape, BF),
            pltpu.VMEM(fn.shape, BF),
            pltpu.VMEM(wi.shape, BF),
            pltpu.VMEM((d, seq), BF),
            pltpu.VMEM((8, half), F32),
            pltpu.VMEM((2, seq, chunk), F32),
            pltpu.VMEM((2, seq, chunk), BF),
            pltpu.VMEM((d, chunk), BF),
            pltpu.SemaphoreType.DMA((5,)),
        ],
        compiler_params=params(44),
        cost_estimate=cost(12),
        name="loss_inner",
    )(me, at, lens4, pooled, queries, wp, pre, fn, wi, wu)


def mid_bwd_kernel(lens, at_ref, g_ref, row_ref, gain_ref, hot_ref, lse_ref, tf_ref, *refs):
    hbm, packs0, packs1, packs2 = refs[:11], refs[11:15], refs[15:19], refs[19:23]
    (dres_hbm, dattn_hbm), outs, scratch = refs[23:25], refs[25:29], refs[29:39]
    bufs, (wib_ref, wob_ref, wub_ref, gb_ref, d_ref, dres_ref, sem, sem0, sem1, sem2, sem3) = refs[39:50], refs[50:]
    da_ref = scratch[7]
    wi_ref, gpa_ref, gpb_ref, res_all, q, qt, k, v, ct, nb, ant = bufs
    b = pl.program_id(0)
    n = lse_ref.shape[0]
    copies = [pltpu.make_async_copy(x, y, sem.at[i]) for i, (x, y) in enumerate(zip(hbm, bufs))]
    copies0 = out_copies(at_ref[0], packs0, wob_ref, sem0)
    copies1 = join_copies(at_ref[0], packs1, wib_ref, sem1)
    copies1 += join_copies(at_ref[0], packs2, wub_ref, sem3)

    def first(group):
        @pl.when(b == 0)
        def _():
            for c in group:
                c.wait()

    @pl.when(b == 0)
    def _():
        for c in copies[:2] + copies1 + copies[2:4] + copies0 + copies[4:]:
            c.start()

    first(copies[:2])
    _, seq, d = res_all.shape
    half = wi_ref.shape[1]
    chunk = d_ref.shape[2]
    steps = half // chunk
    parts = [(gp, w, c) for gp, w in ((gpa_ref, wi_ref), (gpb_ref, wib_ref)) for c in range(steps)]

    def scale(t):
        gp, _, c = parts[t]
        g = (g_ref if t < steps else gb_ref)[pl.ds(b, 1), c * chunk : (c + 1) * chunk]
        d_ref[t % 2] = (gp[b, :, c * chunk : (c + 1) * chunk].astype(F32) * g).astype(BF)

    d_two = None
    scale(0)
    for t, (_, w, c) in enumerate(parts):
        if t + 1 == steps:
            first(copies[2:4] + copies1)

            @pl.when(b == 0)
            def _():
                rows = jnp.concatenate([row_ref[...], jnp.zeros_like(row_ref)], axis=0).astype(BF)
                gb_ref[...] = mm(rows, wub_ref[...], NT)[:8]

        if t + 1 < len(parts):
            scale(t + 1)
        one = mm(d_ref[t % 2], w[:, c * chunk : (c + 1) * chunk], NT)
        d_two = one if d_two is None else d_two + one
    res = res_all[b]
    inv = lax.rsqrt(jnp.mean(res * res, axis=-1, keepdims=True) + EPS)
    scaled = d_two * gain_ref[...]
    along = jnp.sum(scaled * res, axis=-1, keepdims=True)
    valid = lax.broadcasted_iota(jnp.int32, (seq, TILE), 0) < lens[b]
    vcol = valid.astype(F32)[:, :1]
    inv = inv * vcol
    d_res = vcol * row_ref[pl.ds(b, 1), :] + scaled * inv - res * (inv * inv * inv * along / d)
    here = pl.ds(pl.multiple_of(b * seq, seq), seq)
    dres_ref[here, :] = d_res
    d_attn = d_res.astype(BF)
    da_ref[here, :] = d_attn
    done = send_rows(b, n, dres_ref, dres_hbm, sem2.at[0]) + send_rows(b, n, da_ref, dattn_hbm, sem2.at[1])
    first(copies0 + copies[4:-1])
    ins = (q, qt, k, v, ct, lse_ref, nb, tf_ref, ant, hot_ref)
    attn_back(b, n, lens[b], at_ref[0] // 2, wob_ref[...], d_attn, ins, outs, scratch, copies[-1:])

    @pl.when(b == n - 1)
    def _():
        for c in done:
            c.wait()


def mid_bwd(lens, at, g, row, gain, hot, lse, tf, arrays, packs0, packs1, packs2):
    wi, _, _, res = arrays[:4]
    n, seq, d = res.shape
    half = wi.shape[1]
    width = packs0[0].shape[1] // 3
    outs, specs = back_outs(n, seq, width, d)
    more = [sds((n * seq, d), F32), sds((n * seq, d), BF)]
    return pl.pallas_call(
        mid_bwd_kernel,
        grid=(n,),
        in_specs=[SMEM_SPEC, SMEM_SPEC]
        + [const_spec(x.shape) for x in (g, row)]
        + [const_spec((1, d))]
        + [const_spec(x.shape) for x in (hot, lse, tf)]
        + [ANY] * 23,
        out_specs=[ANY] * 2 + specs,
        out_shape=more + outs,
        scratch_shapes=back_scratch(n, seq, width, d)
        + [pltpu.VMEM(x.shape, x.dtype) for x in arrays]
        + [
            pltpu.VMEM((d, half), BF),
            pltpu.VMEM((width, d), BF),
            pltpu.VMEM((half, d), BF),
            pltpu.VMEM((8, half), F32),
            pltpu.VMEM((2, seq, 512), BF),
            pltpu.VMEM((n * seq, d), F32),
            pltpu.SemaphoreType.DMA((11,)),
            pltpu.SemaphoreType.DMA((12,)),
            pltpu.SemaphoreType.DMA((4,)),
            pltpu.SemaphoreType.DMA((2, n)),
            pltpu.SemaphoreType.DMA((4,)),
        ],
        compiler_params=params(),
        cost_estimate=cost(32),
        name="mid_bwd",
    )(lens, at, g, row, gain.reshape(1, d), hot, lse, tf, *arrays, *packs0, *packs1, *packs2)


def input_kernel(at_ref, x_ref, dres_ref, gain_ref, ta_ref, tb_ref, wq, wk, wv, p0, p1, p2, p3, out_ref, w_ref, sem):
    @pl.when(pl.program_id(0) == 0)
    def _():
        run_copies(join_copies(at_ref[0], (p0, p1, p2, p3), w_ref, sem))

    width = wq.shape[1]
    d_one = mm(tb_ref[...], w_ref[...], NT)
    for i, w in enumerate((wq, wk, wv)):
        d_one = d_one + mm(ta_ref[:, width * i : width * (i + 1)], w[...], NT)
    x = x_ref[0].astype(F32)
    inv = lax.rsqrt(jnp.mean(x * x, axis=-1, keepdims=True) + EPS)
    scaled = d_one * gain_ref[...]
    along = jnp.sum(scaled * x, axis=-1, keepdims=True)
    out_ref[0] = dres_ref[...] + scaled * inv - x * (inv * inv * inv * along / x.shape[1])


def input_part(at, x, dres, gain, tok_a, tok_b, wq, wk, wv, packs):
    n, seq, d = x.shape
    width = wq.shape[1]
    rows = lambda cols: pl.BlockSpec((seq, cols), lambda b: (b, 0))
    return pl.pallas_call(
        input_kernel,
        grid=(n,),
        in_specs=[SMEM_SPEC, row_spec(x.shape), rows(d), const_spec((1, d)), rows(3 * width), rows(3 * width)]
        + [const_spec(wq.shape)] * 3
        + [ANY] * 4,
        out_specs=row_spec(x.shape),
        out_shape=sds(x.shape, F32),
        scratch_shapes=[pltpu.VMEM((d, 3 * width), BF), pltpu.SemaphoreType.DMA((4,))],
        compiler_params=params(),
        cost_estimate=cost(12),
        name="input_part",
    )(at, x, dres, gain.reshape(1, d), tok_a, tok_b, wq, wk, wv, *packs)


def layer_kernel(at_ref, res_ref, aa_ref, ab_ref, w_ref, p0, p1, p2, p3, out_ref, wb_ref, sem):
    @pl.when(pl.program_id(0) == 0)
    def _():
        run_copies(join_copies(at_ref[0], (p0, p1, p2, p3), wb_ref, sem))

    out_ref[0] = (res_ref[0] + mm(aa_ref[0], w_ref[...]) + mm(ab_ref[0], wb_ref[...])).astype(BF)


def layer_part(at, res, act_a, act_b, wu, packs):
    n, seq, d = res.shape
    return pl.pallas_call(
        layer_kernel,
        grid=(n,),
        in_specs=[SMEM_SPEC, row_spec(res.shape), row_spec(act_a.shape), row_spec(act_b.shape), const_spec(wu.shape)]
        + [ANY] * 4,
        out_specs=row_spec(res.shape),
        out_shape=sds(res.shape, BF),
        scratch_shapes=[pltpu.VMEM(wu.shape, BF), pltpu.SemaphoreType.DMA((4,))],
        compiler_params=params(),
        cost_estimate=cost(12),
        name="layer_part",
    )(at, res, act_a, act_b, wu, *packs)


def gain_row(prod):
    ones = jnp.ones((16, prod.shape[1]), BF)
    return sum(mm(ones, part, NT)[:1] for part in split3(prod))


def inner_done_kernel(at_ref, own_ref, near_ref, w_ref, out_ref, gain_ref):
    rows = own_ref.shape[0]
    core = at_ref[0] // 2
    halves = [own_ref[...].astype(F32), near_ref[...].astype(F32)]
    for half in range(2):
        one = jnp.where(core == half, halves[0], halves[1])
        at = slice(rows * half, rows * (half + 1))
        out_ref[at, :] = one
        gain_ref[:, at] = jnp.broadcast_to(gain_row(one * w_ref[at, :].astype(F32)), (8, rows))


def inner_done(at, own, near, w):
    d, half = w.shape
    chunk = 512
    cols = lambda r: pl.BlockSpec((r, chunk), lambda c: (0, c))
    return pl.pallas_call(
        inner_done_kernel,
        grid=(half // chunk,),
        in_specs=[SMEM_SPEC, cols(d // 2), cols(d // 2), cols(d)],
        out_specs=[cols(d), pl.BlockSpec((8, d), lambda c: (c, 0))],
        out_shape=[sds((d, half), F32), sds((8 * (half // chunk), d), F32)],
        compiler_params=params(20),
        cost_estimate=cost(5),
        name="inner_done",
    )(at, own, near, w)


def attn_done_kernel(half_ref, sum_ref, wq, wk, wv, *refs):
    q_ref, k_ref, v_ref, o_ref, gain_ref = refs[-5:]
    width = wq.shape[1]
    total = None
    for i, (w, out) in enumerate(((wq, q_ref), (wk, k_ref), (wv, v_ref))):
        one = sum_ref[:, width * i : width * (i + 1)].astype(F32)
        out[...] = one
        prod = one * w[...].astype(F32)
        total = prod if total is None else total + prod
    o_ref[...] = sum_ref[:, 3 * width :].astype(F32)
    gain_ref[...] = jnp.broadcast_to(gain_row(total), gain_ref.shape)


def attn_done(half, sums, wq, wk, wv, into=()):
    d, width = wq.shape
    rows = d // 2
    grad = sds((d, width), F32)
    block = pl.BlockSpec((rows, width), lambda b, half: (half[0], 0))
    across = pl.BlockSpec((width, rows), lambda b, half: (0, half[0]))
    return pl.pallas_call(
        attn_done_kernel,
        grid_spec=pltpu.PrefetchScalarGridSpec(
            num_scalar_prefetch=1,
            grid=(1,),
            in_specs=[pl.BlockSpec(sums.shape, lambda b, half: (0, 0))] + [block] * 3 + [ANY] * len(into),
            out_specs=[block] * 3 + [across, pl.BlockSpec((8, rows), lambda b, half: (0, 0))],
        ),
        out_shape=[grad, grad, grad, sds((width, d), F32), sds((8, rows), F32)],
        input_output_aliases={5 + i: i for i in range(len(into))},
        compiler_params=params(20),
        cost_estimate=cost(3),
        name="attn_done",
    )(half, sums, wq, wk, wv, *into)


def after(*xs):
    return lax.optimization_barrier(xs)


def swap(x, axis, bit, size):
    return lax.ppermute(x, axis, [(i, i ^ bit) for i in range(size)])


class Place:
    def __init__(self, chips, tensor):
        self.chips, self.tensor = chips, tensor
        self.chip = lax.axis_index("chip")
        self.core = lax.axis_index("core")
        self.ti = lax.axis_index("tensor")

    def across(self, x):
        return swap(x, "tensor", 1, self.tensor)

    def core_swap(self, x):
        return swap(x, "core", 1, 2)

    def share(self, x):
        return lax.all_to_all(x, ("chip", "core", "tensor"), 0, 0, tiled=True)

    def side(self, mine):
        return swap(mine, "chip", 1, self.chips)

    def spread(self, mine, side):
        return [mine, side, self.core_swap(mine), self.core_swap(side)]

    def exchange(self, x):
        rows, width = x.shape
        return lax.all_to_all(x.reshape(self.chips, rows // self.chips, width), "chip", 0, 0, tiled=True)

    def add(self, got):
        return jnp.sum(got.astype(F32), axis=0).astype(BF)

    def gather(self, x):
        got = lax.all_to_all(jnp.broadcast_to(x[None], (self.chips,) + x.shape), "chip", 0, 0, tiled=True)
        return got.reshape(-1, x.shape[1])

    def steps(self):
        return [1 << i for i in range(self.chips.bit_length() - 1)]

    def plus(self, x, bit):
        return x + swap(x, "chip", bit, self.chips)


def body(
    mesh_shape,
    hidden_in,
    lengths,
    queries,
    positives,
    gain_attn,
    w_query,
    w_key,
    w_value,
    w_out,
    rel_table,
    gain_ffn,
    w_inner,
    w_outer,
    w_proj,
):
    pc = Place(mesh_shape["chip"], mesh_shape["tensor"])
    n, seq, d = hidden_in.shape
    half = w_inner.shape[1]
    width = w_query.shape[1]
    buckets = rel_table.shape[0]
    lens = lax.dynamic_slice_in_dim(lengths, pc.ti * n, n, 0)
    near_lens = lax.dynamic_slice_in_dim(lengths, (1 - pc.ti) * n, n, 0)
    lens4 = jnp.concatenate([lens, near_lens])
    at = (2 * pc.core + (pc.chip & 1)).reshape(1)
    devices = pc.chips * 2 * pc.tensor
    hot_t = jnp.asarray(np.pad(diag_onehot(buckets, False).T, ((0, TILE - buckets), (0, 0))), BF)
    hot_back = jnp.asarray(np.pad(diag_onehot(buckets, True), ((0, 0), (0, TILE - buckets))), BF)

    turned = rel_table.T
    packs = pack_weights(at, turned, w_query, w_key, w_value, w_out, w_inner, w_outer)
    y_attn = pc.across(packs[0])

    base = (2 * pc.chip + pc.core) * pc.tensor * n
    me = jnp.stack([base + pc.ti * n, base + pc.ti * n + 1, base + (1 - pc.ti) * n, base + (1 - pc.ti) * n + 1])

    qf = queries.astype(F32)
    q_unit = (qf * lax.rsqrt(jnp.sum(qf * qf, axis=-1, keepdims=True) + EPS)).astype(BF)
    ints = jnp.stack([positives // 256, positives % 256, lens // 256, lens % 256], axis=1)
    ints = jnp.pad(ints.astype(BF), ((0, 0), (0, TILE - 4)))
    q_all = jnp.concatenate([q_unit, ints], axis=1)

    an, ant, q_a, qt_a, k_a, v_a, ctx_a, ctxt_a, lse_a, nb_a, tf_a = attn_own(
        lens, hidden_in, gain_attn, w_query, w_key, w_value, turned, hot_t
    )
    y_attn, an, q_all, *packs = after(y_attn, an, q_all, *packs[1:])
    y_inner, y_outer = [pc.across(p) for p in packs]
    x_attn = pc.side(y_attn)
    q_all = pc.share(jnp.broadcast_to(q_all[None], (devices,) + q_all.shape))
    x_attn, q_all, lens4, me, gain_two = after(x_attn, q_all, lens4, me, gain_ffn.reshape(1, d))
    p_attn = pc.spread(y_attn, x_attn)
    y_inner, an = after(y_inner, an)
    x_inner = pc.side(y_inner)
    q_b, qt_b, k_b, v_b, ctxt_b, lse_b, nb_b, tf_b, res, fin, fint, rsum, *fins = attn_other(
        lens, at, an, hot_t, hidden_in, ctx_a, w_out, gain_two, p_attn
    )
    y_inner, x_inner, y_outer, fin, *fins = after(y_inner, x_inner, y_outer, fin, *fins)
    x_outer = pc.side(y_outer)
    p_inner = pc.spread(y_inner, x_inner)
    fin_nb = [pc.across(f) for f in fins]
    act_a, gp_a, act_b, gp_b, asum, rsum = ffn_fwd(lens, at, fin, rsum, w_inner, w_outer, p_inner)
    y_outer, x_outer, asum = after(y_outer, x_outer, asum)
    p_outer = pc.spread(y_outer, x_outer)
    pooled = pool(lens, at, asum, rsum, p_outer)[:n].astype(BF)

    sums_a, sums_b = asum[:, 0, :half].astype(BF), asum[:, 0, half:].astype(BF)
    sums = jnp.where(pc.ti > 0, jnp.stack([sums_b, sums_a]), jnp.stack([sums_a, sums_b]))
    msg = jnp.concatenate([jnp.broadcast_to(pooled[None], (2,) + pooled.shape), sums], axis=2)
    msg = jnp.broadcast_to(msg[None], (2 * pc.chips,) + msg.shape).reshape((devices,) + msg.shape[1:])
    msg, fin_nb[0] = after(msg, fin_nb[0])
    got, pre = after(pc.share(msg), pre_inner(lens4, fint, gp_a, fin_nb[0], w_inner))
    got = got.reshape(devices * n, -1)
    pooled = got[:, :d]
    loss8, row8, g8, d_rows, d_emb, gi_send, gi_keep = loss_all(
        me, at, lens4, pooled, q_all.reshape(devices * n, -1), w_proj, pre, fin_nb[1], w_inner, w_outer
    )
    query_loss = loss8[:n, 0]

    inner_half, gp_a = after(gi_keep + pc.core_swap(gi_send), gp_a)
    inner_parts = pc.exchange(inner_half)
    arrays = [w_inner, gp_a, gp_b, res, q_b, qt_b, k_b, v_b, ctxt_b, nb_b, ant]
    d_res, d_attn, tok_b, send_b, keep_b, table_b = mid_bwd(
        lens, at, g8, row8, gain_ffn, hot_back, lse_b, tf_b, arrays, p_attn, p_inner, p_outer
    )
    inner_part, d_attn = after(pc.add(inner_parts), d_attn)
    inner_all = pc.gather(inner_part)
    half_b, d_attn = after(keep_b + pc.core_swap(send_b), d_attn)
    far_part = pc.across(half_b)
    tok_a, send_a, keep_a, table_a = attn_bwd(
        lens, at, d_attn.reshape(n, seq, d), w_out, hot_back, lse_a, tf_a, q_a, qt_a, k_a, v_a, ctxt_a, nb_a, ant
    )
    proj_grad = mm(pooled, d_emb, TN)
    outer_grad = mm(got[:, d:], d_rows, TN)
    inner_all, far_part, far_table, proj_grad, outer_grad = after(
        inner_all, far_part, pc.across(table_b), proj_grad, outer_grad
    )
    table = table_a + far_table
    near_a, near_table = after(pc.core_swap(send_a), pc.core_swap(table))
    parts = pc.exchange(keep_a + far_part + near_a)
    input_grad = input_part(at, hidden_in, d_res, gain_attn, tok_a, tok_b, w_query, w_key, w_value, p_attn)
    inner_sum, gain_ffn_part = inner_done(at, inner_all, pc.core_swap(inner_all), w_inner)
    layer = layer_part(at, res, act_a, act_b, w_outer, p_outer)
    parts, input_grad, layer = after(parts, input_grad, layer)
    attn_all = pc.gather(pc.add(parts))
    *early, late = pc.steps()
    table_sum = table + near_table
    for bit in early:
        table_sum = pc.plus(table_sum, bit)
    gain_ffn_part = jnp.sum(gain_ffn_part[::8], axis=0)
    gain_ffn_grad = (gain_ffn_part + pc.across(gain_ffn_part)) / gain_ffn
    attn_all, gain_ffn_grad, table_sum, inner_sum, query_loss = after(
        attn_all, gain_ffn_grad, table_sum, inner_sum, query_loss
    )
    table_sum = pc.plus(table_sum, late)
    half = pc.core.reshape(1)
    near = pc.core_swap(attn_all)
    *grads, gain_own = attn_done(half, attn_all, w_query, w_key, w_value)
    near, *grads = after(near, *grads)
    gain_far = pc.across(gain_own[0])
    *grads, _ = attn_done(1 - half, near, w_query, w_key, w_value, grads)
    gain_far, *grads = after(gain_far, *grads)
    gain_own = gain_own[0] + gain_far
    q_grad, k_grad, v_grad, out_grad = grads
    gain_near = pc.core_swap(gain_own)
    gain_attn_grad = jnp.where(
        pc.core > 0, jnp.concatenate([gain_near, gain_own]), jnp.concatenate([gain_own, gain_near])
    ) / gain_attn
    return (
        layer,
        query_loss,
        input_grad,
        gain_attn_grad,
        q_grad,
        k_grad,
        v_grad,
        out_grad,
        table_sum[: rel_table.shape[1], :buckets].T,
        gain_ffn_grad,
        inner_sum,
        outer_grad,
        proj_grad,
    )


def solution(mesh):
    dp, tensor = mesh.shape["dp"], mesh.shape["tensor"]
    fine = jax.sharding.Mesh(mesh.devices.reshape(dp // 2, 2, tensor), ("chip", "core", "tensor"))
    rows = ("chip", "core")
    both = rows + ("tensor",)
    return jax.shard_map(
        functools.partial(body, dict(fine.shape)),
        mesh=fine,
        in_specs=(
            P(both, None, None),
            P(rows),
            P(both, None),
            P(both),
            P(),
            P(None, "tensor"),
            P(None, "tensor"),
            P(None, "tensor"),
            P("tensor", None),
            P(None, "tensor"),
            P(),
            P(None, "tensor"),
            P("tensor", None),
            P(),
        ),
        out_specs=(
            P(both, None, None),
            P(both),
            P(both, None, None),
            P(),
            P(None, "tensor"),
            P(None, "tensor"),
            P(None, "tensor"),
            P("tensor", None),
            P(None, "tensor"),
            P(),
            P(None, "tensor"),
            P("tensor", None),
            P(),
        ),
        check_vma=False,
    )
```
